32 devices in a mesh: group: 2 (over x), attn: 8 (over z, y), expert: 2 (over core).
Axes of the slice: x: 2, y: 2, z: 4, core: 2. Of those that a mesh axis runs over, the one named last changes fastest.
Arguments:
- queries: bfloat16 [64, 6144], P(('group', 'attn'), 'expert'), parts along dimension 0, may hold values from -5 to 5
- key_cache: bfloat16 [64, 512, 1024], P(('group', 'attn'), None, 'expert'), parts along dimension 0, may hold values from -5 to 5
- value_cache: bfloat16 [64, 512, 1024], P(('group', 'attn'), None, 'expert'), parts along dimension 0, may hold values from -6 to 6
- new_key: bfloat16 [64, 1024], P(('group', 'attn'), 'expert'), parts along dimension 0, may hold values from -6 to 6
- new_value: bfloat16 [64, 1024], P(('group', 'attn'), 'expert'), parts along dimension 0, may hold values from -6 to 6
- cache_length: int32 [64], P(('group', 'attn')), parts along dimension 0, may hold values from 2 to 512, as said below
- residual: bfloat16 [64, 6144], P('group', 'attn'), parts along dimension 0, may hold values from -3 to 3
- out_weight: bfloat16 [6144, 6144], P('expert', 'attn'), may hold values from -0.5 to 0.5
- ln_gain: float32 [6144], P('attn'), may hold values from 0.1 to 1.9
- gate_weight: bfloat16 [6144, 2688], P(None, ('attn', 'expert')), may hold values from -0.078125 to 0.078125
- up_weight: bfloat16 [6144, 2688], P(None, ('attn', 'expert')), may hold values from -0.078125 to 0.078125
- down_weight: bfloat16 [2688, 6144], P(('attn', 'expert')), may hold values from -0.15625 to 0.15625
- routes: int32 [64, 4], P('group'), parts along dimension 0, may hold values from 0 to 15, as said below
- route_weight: float32 [64, 4], P('group'), parts along dimension 0, may hold values from 0.05 to 0.6
Outputs:
- attn_stream: bfloat16 [64, 6144], P('group', 'attn'), parts along dimension 0
- expert_out: bfloat16 [64, 6144], P('group', 'attn'), parts along dimension 0
The draws below stay inside these ranges and needn't reach their ends.
There are 2 independent parts, one for each index of `group`. The reference program is written for one: setup_inputs(seed, part) draws one part's arguments, and reference() takes and returns one part's arrays. A program takes and returns all parts, laid end to end along the dimension named above; an argument that names none is the same for every part. Nothing has to cross between parts.
Inputs may be any that keep to these rules, and one draw needn't show every extreme that they name: `routes`: each row names 4 different experts; of the held experts none is named by more than 16 rows, and one of them by exactly 16. `cache_length`: some request has all 512 positions filled.
All inputs are finite; a program needn't handle non-finite values.
Results may differ from the reference program's by a relative error of at most 0.015.
Values may be sent and summed in bfloat16 or wider, within the bound.
No kernel may reach another device: no remote copies, remote signals or barrier semaphores. Data moves between devices by JAX's collectives and lax.ppermute only.
A program may use at most 128 MiB of HBM per device.

```python
import math
import jax
import jax.numpy as jnp
from jax import lax

D = 6144
HEADS = 48
KV_HEADS = 8
HEAD_DIM = 128
EXPERTS = 16
TOP = 4
HELD = 2
FF_DEV = 168
LEN = 512
R_TOTAL = 32
CAP = 16
NSH = 8
EXPERT_FF = 1344


def draw_queries(key, part):
    key = jax.random.fold_in(key, 11)
    width = HEADS * HEAD_DIM
    values = jnp.clip(jax.random.normal(key, (R_TOTAL, width), jnp.float32), -4.0, 4.0)
    return values.astype(jnp.bfloat16)


def draw_key_cache(key, part):
    key = jax.random.fold_in(key, 23)
    width = KV_HEADS * HEAD_DIM
    values = jnp.clip(jax.random.normal(key, (R_TOTAL, LEN, width), jnp.float32), -4.0, 4.0)
    return values.astype(jnp.bfloat16)


def draw_cache_length(key, part):
    key = jax.random.fold_in(key, 37)
    lengths = jax.random.randint(key, (R_TOTAL,), 2, LEN + 1, jnp.int32)
    fullest = jax.random.randint(jax.random.fold_in(key, 5), (), 0, R_TOTAL, jnp.int32)
    return lengths.at[fullest].set(LEN)


def draw_routes(key, part):
    key = jax.random.fold_in(key, 53)
    experts_row = jnp.arange(EXPERTS, dtype=jnp.int32)
    base = jax.random.randint(jax.random.fold_in(key, 1), (R_TOTAL, EXPERTS), 0, 1000, jnp.int32)
    scores = base * EXPERTS + experts_row[None, :]
    lead = jax.random.randint(jax.random.fold_in(key, 2), (), 0, HELD, jnp.int32)
    row_ids = jnp.arange(R_TOTAL, dtype=jnp.int32)
    for expert_id in range(HELD):
        drawn = jax.random.randint(jax.random.fold_in(key, 10 + expert_id), (), CAP // 4, CAP + 1, jnp.int32)
        count = jnp.where(lead == expert_id, CAP, drawn)
        ranks = jax.random.permutation(jax.random.fold_in(key, 30 + expert_id), row_ids)
        picked = ranks < count
        column = jnp.where(picked, 2000000 + expert_id, -1 - expert_id)
        scores = scores.at[:, expert_id].set(column)
    _, chosen = lax.top_k(scores, TOP)
    return chosen.astype(jnp.int32)


def shard_levels(key, extent, split, least, top_value):
    level, own = 1.0, jax.random.fold_in(key, 6)
    for dim, blocks in split:
        steps = jnp.exp(jax.random.uniform(jax.random.fold_in(own, dim), (blocks,), jnp.float32, least / len(split), top_value / len(split)))
        level = level * jnp.repeat(steps, extent[dim] // blocks).reshape([-1 if axis == dim else 1 for axis in range(len(extent))])
    return level


def gaussian(stream_key, extent, deviation, bound, pieces=(), kind=jnp.bfloat16):
    values = deviation * jax.random.normal(stream_key, extent, jnp.float32)
    if pieces:
        values = values * shard_levels(stream_key, extent, pieces, -0.22, 0.18)
    return jnp.clip(values, -bound, bound).astype(kind)


def setup_inputs(seed: int = 0, part: int = 0) -> dict:
    arg_keys = jax.random.split(jax.random.key(seed), 15)
    part_keys = jax.random.split(jax.random.fold_in(arg_keys[14], part), 15)
    return {
        "queries": draw_queries(jax.random.fold_in(jax.random.fold_in(arg_keys[14], part), 71), part),
        "key_cache": draw_key_cache(jax.random.fold_in(jax.random.fold_in(arg_keys[14], part), 71), part),
        "value_cache": gaussian(part_keys[2], (R_TOTAL, LEN, KV_HEADS * HEAD_DIM), 1.0, 6.0, ((0, 8), (2, 2))),
        "new_key": gaussian(part_keys[3], (R_TOTAL, KV_HEADS * HEAD_DIM), 1.0, 6.0, ((0, 8), (1, 2))),
        "new_value": gaussian(part_keys[4], (R_TOTAL, KV_HEADS * HEAD_DIM), 1.0, 6.0, ((0, 8), (1, 2))),
        "cache_length": draw_cache_length(jax.random.fold_in(jax.random.fold_in(arg_keys[14], part), 71), part),
        "residual": gaussian(part_keys[6], (R_TOTAL, D), 0.5, 3.0, ((1, 8),)),
        "out_weight": gaussian(arg_keys[7], (HEADS * HEAD_DIM, D), HEAD_DIM ** -0.5, 0.5, ((0, 2), (1, 8))),
        "ln_gain": jnp.clip(1.0 + 0.18 * jax.random.normal(arg_keys[8], (D,), jnp.float32), 0.1, 1.9),
        "gate_weight": gaussian(arg_keys[9], (D, HELD * EXPERT_FF), D ** -0.5, 0.078125, ((1, 16),)),
        "up_weight": gaussian(arg_keys[10], (D, HELD * EXPERT_FF), D ** -0.5, 0.078125, ((1, 16),)),
        "down_weight": gaussian(arg_keys[11], (HELD * EXPERT_FF, D), EXPERT_FF ** -0.5, 0.15625, ((0, 16),)),
        "routes": draw_routes(jax.random.fold_in(jax.random.fold_in(arg_keys[14], part), 71), part),
        "route_weight": jnp.clip(jax.random.uniform(part_keys[13], (R_TOTAL, TOP), jnp.float32, 0.05, 0.6), 0.05, 0.6),
    }


NEG_FILL = -1e+30
EPSILON = 1e-05

def rounded(value):
    return lax.optimization_barrier(value.astype(jnp.bfloat16)).astype(jnp.float32)

def attend_single(operands):
    query_row, key_rows, value_rows, own_key, own_value, length = operands
    group = HEADS // KV_HEADS
    query_heads = query_row.astype(jnp.float32).reshape(KV_HEADS, group, HEAD_DIM)
    key_heads = key_rows.astype(jnp.float32).reshape(LEN, KV_HEADS, HEAD_DIM)
    value_heads = value_rows.astype(jnp.float32).reshape(LEN, KV_HEADS, HEAD_DIM)
    own_keys = own_key.astype(jnp.float32).reshape(KV_HEADS, HEAD_DIM)
    own_values = own_value.astype(jnp.float32).reshape(KV_HEADS, HEAD_DIM)
    scale = 1.0 / math.sqrt(HEAD_DIM)
    past = jnp.einsum('kgd,lkd->kgl', query_heads, key_heads) * scale
    valid = jnp.arange(LEN, dtype=jnp.int32) < length
    past = jnp.where(valid[None, None, :], past, NEG_FILL)
    own = jnp.einsum('kgd,kd->kg', query_heads, own_keys) * scale
    largest = jnp.maximum(lax.optimization_barrier(jnp.max(past, axis=2)), own)
    past_weight = jnp.exp(past - largest[:, :, None])
    own_weight = jnp.exp(own - largest)
    total = lax.optimization_barrier(jnp.sum(past_weight, axis=2)) + own_weight
    past_prob = rounded(past_weight / total[:, :, None])
    own_prob = rounded(own_weight / total)
    result = jnp.einsum('kgl,lkd->kgd', past_prob, value_heads)
    result = result + own_prob[:, :, None] * own_values[:, None, :]
    return result.reshape(HEADS * HEAD_DIM).astype(jnp.bfloat16)

def slot_table(routes, capacity, row_count):
    flat = routes.reshape(-1)
    onehot = (flat[:, None] == jnp.arange(EXPERTS, dtype=jnp.int32)[None, :]).astype(jnp.int32)
    before = jnp.cumsum(onehot, axis=0) - onehot
    slots = lax.optimization_barrier(jnp.sum(before * onehot, axis=1)).astype(jnp.int32)
    owners = (jnp.arange(flat.shape[0], dtype=jnp.int32) // TOP).astype(jnp.int32)
    table = jnp.full((HELD, capacity), row_count, jnp.int32).at[flat, slots].set(owners, mode='drop')
    return (slots.reshape(routes.shape), table)

def reference(queries, key_cache, value_cache, new_key, new_value, cache_length, residual, out_weight, ln_gain, gate_weight, up_weight, down_weight, routes, route_weight):
    attended = lax.map(attend_single, (queries, key_cache, value_cache, new_key, new_value, cache_length))
    stream_sum = residual.astype(jnp.float32) + jnp.dot(attended, out_weight, preferred_element_type=jnp.float32)
    attn_stream = stream_sum.astype(jnp.bfloat16)
    stream_wide = attn_stream.astype(jnp.float32)
    row_mean = lax.optimization_barrier(jnp.sum(stream_wide, axis=1, keepdims=True)) / D
    row_var = lax.optimization_barrier(jnp.sum(stream_wide * stream_wide, axis=1, keepdims=True)) / D - row_mean * row_mean
    normed = ((stream_wide - row_mean) * lax.rsqrt(row_var + EPSILON) * ln_gain[None, :]).astype(jnp.bfloat16)
    slots, table = slot_table(routes, CAP, R_TOTAL)

    def run_expert(expert_id):
        start = (expert_id * EXPERT_FF).astype(jnp.int32)
        rows_in = jnp.take(normed, table[expert_id], axis=0, mode='fill', fill_value=0)
        gate_cols = lax.dynamic_slice_in_dim(gate_weight, start, EXPERT_FF, 1)
        up_cols = lax.dynamic_slice_in_dim(up_weight, start, EXPERT_FF, 1)
        down_rows = lax.dynamic_slice_in_dim(down_weight, start, EXPERT_FF, 0)
        gate_val = jnp.dot(rows_in, gate_cols, preferred_element_type=jnp.float32)
        up_val = jnp.dot(rows_in, up_cols, preferred_element_type=jnp.float32)
        hidden = (jax.nn.silu(gate_val) * up_val).astype(jnp.bfloat16)
        summed = jnp.zeros((CAP, D), jnp.float32)
        for block_index in range(NSH):
            low = block_index * FF_DEV
            piece = jnp.dot(hidden[:, low:low + FF_DEV], down_rows[low:low + FF_DEV], preferred_element_type=jnp.float32)
            summed = summed + rounded(piece)
        return summed
    outputs = lax.map(run_expert, jnp.arange(HELD, dtype=jnp.int32))
    held = routes < HELD
    expert_pick = jnp.minimum(routes, HELD - 1).astype(jnp.int32)
    slot_pick = jnp.minimum(slots, CAP - 1).astype(jnp.int32)
    picked = outputs[expert_pick, slot_pick]
    weights = jnp.where(held, route_weight, 0.0)
    expert_out = lax.optimization_barrier(jnp.sum(weights[:, :, None] * picked, axis=1)).astype(jnp.bfloat16)
    return (attn_stream, expert_out)
```

```python
import math

import jax
import jax.numpy as jnp
from jax import lax
from jax.sharding import PartitionSpec as P

D = 6144
HEADS = 48
KV_HEADS = 8
HEAD_DIM = 128
EXPERTS = 16
TOP = 4
HELD = 2


NEG_FILL = -1e30
EPSILON = 1e-05


def attend_local(queries, key_cache, value_cache, new_key, new_value, cache_length):
    row_count = queries.shape[0]
    kv_local = new_key.shape[1] // HEAD_DIM
    group = HEADS // KV_HEADS
    length_max = key_cache.shape[1]
    query_heads = queries.reshape(row_count, kv_local, group, HEAD_DIM)
    key_heads = key_cache.reshape(row_count, length_max, kv_local, HEAD_DIM)
    value_heads = value_cache.reshape(row_count, length_max, kv_local, HEAD_DIM)
    own_keys = new_key.reshape(row_count, kv_local, HEAD_DIM)
    own_values = new_value.reshape(row_count, kv_local, HEAD_DIM)
    scale = 1.0 / math.sqrt(HEAD_DIM)
    past = (
        jnp.einsum("rkgd,rlkd->rkgl", query_heads, key_heads, preferred_element_type=jnp.float32)
        * scale
    )
    valid = jnp.arange(length_max, dtype=jnp.int32)[None, :] < cache_length[:, None]
    past = jnp.where(valid[:, None, None, :], past, NEG_FILL)
    own = (
        jnp.einsum("rkgd,rkd->rkg", query_heads, own_keys, preferred_element_type=jnp.float32)
        * scale
    )
    largest = jnp.maximum(jnp.max(past, axis=3), own)
    past_weight = jnp.exp(past - largest[..., None])
    own_weight = jnp.exp(own - largest)
    total = jnp.sum(past_weight, axis=3) + own_weight
    past_prob = (past_weight / total[..., None]).astype(jnp.bfloat16)
    own_prob = (own_weight / total).astype(jnp.bfloat16)
    result = jnp.einsum(
        "rkgl,rlkd->rkgd", past_prob, value_heads, preferred_element_type=jnp.float32
    )
    result = (
        result
        + own_prob.astype(jnp.float32)[..., None] * own_values.astype(jnp.float32)[:, :, None, :]
    )
    return result.reshape(row_count, kv_local * group * HEAD_DIM).astype(jnp.bfloat16)


def selection(routes, route_weight, capacity):
    row_count = routes.shape[0]
    experts = jnp.arange(HELD, dtype=jnp.int32)
    match = routes[None, :, :] == experts[:, None, None]
    hit = jnp.any(match, axis=2)
    row_weight = jnp.sum(jnp.where(match, route_weight[None], 0.0), axis=2)
    earlier = jnp.arange(row_count)[:, None] < jnp.arange(row_count)[None, :]
    slot = jnp.sum(jnp.where(earlier[None] & hit[:, :, None], 1, 0), axis=1)
    taken = hit[:, None, :] & (slot[:, None, :] == jnp.arange(capacity, dtype=jnp.int32)[None, :, None])
    slot_weight = jnp.sum(jnp.where(taken, row_weight[:, None, :], 0.0), axis=2)
    return taken, slot_weight


def gather_attn(block):
    count = lax.axis_size("attn")
    copies = jnp.broadcast_to(block[None], (count,) + block.shape)
    return lax.all_to_all(copies, "attn", split_axis=0, concat_axis=0, tiled=True)


def pair_sum(block):
    return block + lax.ppermute(block, "expert", [(0, 1), (1, 0)])


def shards(
    queries,
    key_cache,
    value_cache,
    new_key,
    new_value,
    cache_length,
    residual,
    out_weight,
    ln_gain,
    gate_weight,
    up_weight,
    down_weight,
    routes,
    route_weight,
):
    attn_count = lax.axis_size("attn")
    core_count = lax.axis_size("expert")
    sharers = attn_count * core_count // HELD
    my_expert = (lax.axis_index("attn") * core_count + lax.axis_index("expert")) // sharers
    dest_expert = [index * core_count // sharers for index in range(attn_count)]
    row_count = routes.shape[0]
    capacity = row_count * TOP // EXPERTS * 2
    cols = residual.shape[1]

    taken, slot_weight = selection(routes, route_weight, capacity)
    pick = taken.astype(jnp.bfloat16)

    gains = gather_attn(ln_gain)

    attended = attend_local(queries, key_cache, value_cache, new_key, new_value, cache_length)
    whole = gather_attn(attended).reshape(row_count, -1)
    partial_proj = jnp.dot(whole, out_weight, preferred_element_type=jnp.float32)
    head_total = pair_sum(partial_proj)
    attn_stream = (residual.astype(jnp.float32) + head_total).astype(jnp.bfloat16)

    chosen = jnp.einsum(
        "esr,rd->esd", pick, attn_stream, preferred_element_type=jnp.float32
    ).astype(jnp.bfloat16)
    outgoing = jnp.stack([chosen[index] for index in dest_expert])
    rows = lax.all_to_all(outgoing, "attn", split_axis=0, concat_axis=0, tiled=True)
    wide = rows.astype(jnp.float32)
    row_mean = jnp.sum(wide, axis=(0, 2)) / D
    row_var = jnp.sum(wide * wide, axis=(0, 2)) / D - row_mean * row_mean
    normed = (
        (wide - row_mean[None, :, None])
        * lax.rsqrt(row_var + EPSILON)[None, :, None]
        * gains.reshape(attn_count, 1, cols)
    ).astype(jnp.bfloat16)
    gate_val = jnp.einsum(
        "asd,adf->sf", normed, gate_weight.reshape(attn_count, cols, -1),
        preferred_element_type=jnp.float32,
    )
    up_val = jnp.einsum(
        "asd,adf->sf", normed, up_weight.reshape(attn_count, cols, -1),
        preferred_element_type=jnp.float32,
    )
    hidden = (jax.nn.silu(gate_val) * up_val).astype(jnp.bfloat16)
    piece = jnp.dot(hidden, down_weight, preferred_element_type=jnp.float32)
    mine = jnp.take(slot_weight, my_expert, axis=0)
    piece = (piece * mine[:, None]).astype(jnp.bfloat16)
    returned = lax.all_to_all(
        piece.reshape(capacity, attn_count, cols).swapaxes(0, 1),
        "attn", split_axis=0, concat_axis=0, tiled=True,
    )
    spread = jnp.stack([pick[index] for index in dest_expert])
    combined = jnp.einsum(
        "asr,asd->rd", spread, returned, preferred_element_type=jnp.float32
    )
    expert_out = pair_sum(combined).astype(jnp.bfloat16)
    return (attn_stream, expert_out)


def solution(mesh):
    return jax.shard_map(
        shards,
        mesh=mesh,
        in_specs=(
            P(("group", "attn"), "expert"),
            P(("group", "attn"), None, "expert"),
            P(("group", "attn"), None, "expert"),
            P(("group", "attn"), "expert"),
            P(("group", "attn"), "expert"),
            P(("group", "attn")),
            P("group", "attn"),
            P("expert", "attn"),
            P("attn"),
            P(None, ("attn", "expert")),
            P(None, ("attn", "expert")),
            P(("attn", "expert"), None),
            P("group", None),
            P("group", None),
        ),
        out_specs=(P("group", "attn"), P("group", "attn")),
        check_vma=False,
    )
```

```python
import functools
import math

import jax
import jax.numpy as jnp
from jax import lax
from jax.experimental import pallas as pl
from jax.experimental.pallas import tpu as pltpu
from jax.sharding import PartitionSpec as P

D = 6144
HEADS = 48
KV_HEADS = 8
HEAD_DIM = 128
EXPERTS = 16
TOP = 4
HELD = 2


NEG_FILL = -1e30
EPSILON = 1e-05


def attend_local(queries, key_cache, value_cache, new_key, new_value, cache_length):
    row_count = queries.shape[0]
    kv_local = new_key.shape[1] // HEAD_DIM
    group = HEADS // KV_HEADS
    length_max = key_cache.shape[1]
    query_heads = queries.reshape(row_count, kv_local, group, HEAD_DIM)
    key_heads = key_cache.reshape(row_count, length_max, kv_local, HEAD_DIM)
    value_heads = value_cache.reshape(row_count, length_max, kv_local, HEAD_DIM)
    own_keys = new_key.reshape(row_count, kv_local, HEAD_DIM)
    own_values = new_value.reshape(row_count, kv_local, HEAD_DIM)
    scale = 1.0 / math.sqrt(HEAD_DIM)
    past = (
        jnp.einsum("rkgd,rlkd->rkgl", query_heads, key_heads, preferred_element_type=jnp.float32)
        * scale
    )
    valid = jnp.arange(length_max, dtype=jnp.int32)[None, :] < cache_length[:, None]
    past = jnp.where(valid[:, None, None, :], past, NEG_FILL)
    own = (
        jnp.einsum("rkgd,rkd->rkg", query_heads, own_keys, preferred_element_type=jnp.float32)
        * scale
    )
    largest = jnp.maximum(jnp.max(past, axis=3), own)
    past_weight = jnp.exp(past - largest[..., None])
    own_weight = jnp.exp(own - largest)
    total = jnp.sum(past_weight, axis=3) + own_weight
    past_prob = (past_weight / total[..., None]).astype(jnp.bfloat16)
    own_prob = (own_weight / total).astype(jnp.bfloat16)
    result = jnp.einsum(
        "rkgl,rlkd->rkgd", past_prob, value_heads, preferred_element_type=jnp.float32
    )
    result = (
        result
        + own_prob.astype(jnp.float32)[..., None] * own_values.astype(jnp.float32)[:, :, None, :]
    )
    return result.reshape(row_count, kv_local * group * HEAD_DIM).astype(jnp.bfloat16)


def selection(routes, route_weight, capacity):
    row_count = routes.shape[0]
    experts = jnp.arange(HELD, dtype=jnp.int32)
    match = routes[None, :, :] == experts[:, None, None]
    hit = jnp.any(match, axis=2)
    row_weight = jnp.sum(jnp.where(match, route_weight[None], 0.0), axis=2)
    earlier = jnp.arange(row_count)[:, None] < jnp.arange(row_count)[None, :]
    slot = jnp.sum(jnp.where(earlier[None] & hit[:, :, None], 1, 0), axis=1)
    taken = hit[:, None, :] & (slot[:, None, :] == jnp.arange(capacity, dtype=jnp.int32)[None, :, None])
    slot_weight = jnp.sum(jnp.where(taken, row_weight[:, None, :], 0.0), axis=2)
    return taken, slot_weight


def gather_attn(block):
    count = lax.axis_size("attn")
    copies = jnp.broadcast_to(block[None], (count,) + block.shape)
    return lax.all_to_all(copies, "attn", split_axis=0, concat_axis=0, tiled=True)


def pair_sum(block):
    return block + lax.ppermute(block, "expert", [(0, 1), (1, 0)])


def shards_plain(
    queries,
    key_cache,
    value_cache,
    new_key,
    new_value,
    cache_length,
    residual,
    out_weight,
    ln_gain,
    gate_weight,
    up_weight,
    down_weight,
    routes,
    route_weight,
):
    attn_count = lax.axis_size("attn")
    core_count = lax.axis_size("expert")
    sharers = attn_count * core_count // HELD
    my_expert = (lax.axis_index("attn") * core_count + lax.axis_index("expert")) // sharers
    dest_expert = [index * core_count // sharers for index in range(attn_count)]
    row_count = routes.shape[0]
    capacity = row_count * TOP // EXPERTS * 2
    cols = residual.shape[1]

    taken, slot_weight = selection(routes, route_weight, capacity)
    pick = taken.astype(jnp.bfloat16)

    gains = gather_attn(ln_gain)

    attended = attend_local(queries, key_cache, value_cache, new_key, new_value, cache_length)
    whole = gather_attn(attended).reshape(row_count, -1)
    partial_proj = jnp.dot(whole, out_weight, preferred_element_type=jnp.float32)
    head_total = pair_sum(partial_proj)
    attn_stream = (residual.astype(jnp.float32) + head_total).astype(jnp.bfloat16)

    chosen = jnp.einsum(
        "esr,rd->esd", pick, attn_stream, preferred_element_type=jnp.float32
    ).astype(jnp.bfloat16)
    outgoing = jnp.stack([chosen[index] for index in dest_expert])
    rows = lax.all_to_all(outgoing, "attn", split_axis=0, concat_axis=0, tiled=True)
    wide = rows.astype(jnp.float32)
    row_mean = jnp.sum(wide, axis=(0, 2)) / D
    row_var = jnp.sum(wide * wide, axis=(0, 2)) / D - row_mean * row_mean
    normed = (
        (wide - row_mean[None, :, None])
        * lax.rsqrt(row_var + EPSILON)[None, :, None]
        * gains.reshape(attn_count, 1, cols)
    ).astype(jnp.bfloat16)
    gate_val = jnp.einsum(
        "asd,adf->sf", normed, gate_weight.reshape(attn_count, cols, -1),
        preferred_element_type=jnp.float32,
    )
    up_val = jnp.einsum(
        "asd,adf->sf", normed, up_weight.reshape(attn_count, cols, -1),
        preferred_element_type=jnp.float32,
    )
    hidden = (jax.nn.silu(gate_val) * up_val).astype(jnp.bfloat16)
    piece = jnp.dot(hidden, down_weight, preferred_element_type=jnp.float32)
    mine = jnp.take(slot_weight, my_expert, axis=0)
    piece = (piece * mine[:, None]).astype(jnp.bfloat16)
    returned = lax.all_to_all(
        piece.reshape(capacity, attn_count, cols).swapaxes(0, 1),
        "attn", split_axis=0, concat_axis=0, tiled=True,
    )
    spread = jnp.stack([pick[index] for index in dest_expert])
    combined = jnp.einsum(
        "asr,asd->rd", spread, returned, preferred_element_type=jnp.float32
    )
    expert_out = pair_sum(combined).astype(jnp.bfloat16)
    return (attn_stream, expert_out)


MIB = 1024 * 1024
VMEM_SPEC = pl.BlockSpec(memory_space=pltpu.VMEM)
SMEM_SPEC = pl.BlockSpec(memory_space=pltpu.SMEM)
ANY_SPEC = pl.BlockSpec(memory_space=pl.ANY)


def call(kernel, outs, in_specs, scratch, flops, nbytes, vmem_mib):
    single = not isinstance(outs, (list, tuple))
    return pl.pallas_call(
        kernel,
        out_shape=outs,
        in_specs=in_specs,
        out_specs=VMEM_SPEC if single else [VMEM_SPEC] * len(outs),
        scratch_shapes=scratch,
        cost_estimate=pl.CostEstimate(flops=flops, bytes_accessed=nbytes, transcendentals=0),
        compiler_params=pltpu.CompilerParams(vmem_limit_bytes=vmem_mib * MIB),
    )


def attend_kernel(
    length_ref, query_ref, key_hbm, value_hbm, own_key_ref, own_value_ref, out_ref,
    key_buf, value_buf, query_rows, key_rows, value_rows, result_rows, key_sem, value_sem,
):
    row_count, length_max = key_hbm.shape[0], key_hbm.shape[1]
    kv_local = own_key_ref.shape[1] // HEAD_DIM
    group = HEADS // KV_HEADS
    block = group * row_count
    key_copies = [
        pltpu.make_async_copy(key_hbm.at[r], key_buf.at[r], key_sem.at[r]) for r in range(row_count)
    ]
    value_copies = [
        pltpu.make_async_copy(value_hbm.at[r], value_buf.at[r], value_sem.at[r])
        for r in range(row_count)
    ]
    for copy in key_copies + value_copies:
        copy.start()
    for g in range(kv_local):
        lanes = slice(g * HEAD_DIM, (g + 1) * HEAD_DIM)
        own_key = own_key_ref[:, lanes].astype(jnp.float32)
        own_value = own_value_ref[:, lanes].astype(jnp.float32)
        for i in range(group):
            head = g * group + i
            rows = pl.ds(g * block + i * row_count, row_count)
            query_rows[rows, :] = query_ref[
                :, head * HEAD_DIM : (head + 1) * HEAD_DIM
            ].astype(jnp.float32)
            key_rows[rows, :] = own_key
            value_rows[rows, :] = own_value
    scale = 1.0 / math.sqrt(HEAD_DIM)
    pair_rows = 2 * block
    request = lax.broadcasted_iota(jnp.int32, (pair_rows, 1), 0) % row_count
    lengths = jnp.zeros((pair_rows, 1), jnp.int32)
    for r in range(row_count):
        lengths = jnp.where(request == r, length_ref[r], lengths)
    position = lax.broadcasted_iota(jnp.int32, (pair_rows, length_max), 1)
    valid = position < lengths
    pairs = kv_local // 2
    past = [jnp.zeros((pair_rows, length_max), jnp.float32) for _ in range(pairs)]
    packed = []
    for p in range(pairs):
        rows = query_rows[pl.ds(p * pair_rows, pair_rows), :]
        lower = rows[:block].astype(jnp.bfloat16)
        upper = rows[block:].astype(jnp.bfloat16)
        zero = jnp.zeros_like(lower)
        packed.append(
            jnp.concatenate(
                [
                    jnp.concatenate([lower, zero], axis=1),
                    jnp.concatenate([zero, upper], axis=1),
                ],
                axis=0,
            )
        )
    for r in range(row_count):
        key_copies[r].wait()
        for p in range(pairs):
            keys = key_buf[r, :, p * 2 * HEAD_DIM : (p + 1) * 2 * HEAD_DIM]
            scores = lax.dot_general(
                packed[p], keys, (((1,), (1,)), ((), ())), preferred_element_type=jnp.float32
            )
            past[p] = jnp.where(request == r, scores, past[p])
    probs, own_probs = [], []
    for p in range(pairs):
        rows = pl.ds(p * pair_rows, pair_rows)
        scores = jnp.where(valid, past[p] * scale, NEG_FILL)
        own = jnp.sum(query_rows[rows, :] * key_rows[rows, :], axis=1, keepdims=True) * scale
        largest = jnp.maximum(jnp.max(scores, axis=1, keepdims=True), own)
        weight = jnp.exp(scores - largest)
        own_weight = jnp.exp(own - largest)
        total = jnp.sum(weight, axis=1, keepdims=True) + own_weight
        probs.append((weight / total).astype(jnp.bfloat16))
        own_probs.append((own_weight / total).astype(jnp.bfloat16).astype(jnp.float32))
    sums = [jnp.zeros((pair_rows, 2 * HEAD_DIM), jnp.float32) for _ in range(pairs)]
    for r in range(row_count):
        value_copies[r].wait()
        for p in range(pairs):
            values = value_buf[r, :, p * 2 * HEAD_DIM : (p + 1) * 2 * HEAD_DIM]
            product = jnp.dot(probs[p], values, preferred_element_type=jnp.float32)
            sums[p] = jnp.where(request == r, product, sums[p])
    for p in range(pairs):
        rows = pl.ds(p * pair_rows, pair_rows)
        own_part = own_probs[p] * value_rows[rows, :]
        lower = sums[p][:block, :HEAD_DIM] + own_part[:block]
        upper = sums[p][block:, HEAD_DIM:] + own_part[block:]
        result_rows[pl.ds(p * pair_rows, block), :] = lower
        result_rows[pl.ds(p * pair_rows + block, block), :] = upper
    for head in range(kv_local * group):
        out_ref[:, head * HEAD_DIM : (head + 1) * HEAD_DIM] = result_rows[
            pl.ds(head * row_count, row_count), :
        ].astype(jnp.bfloat16)


def attend(queries, key_cache, value_cache, new_key, new_value, cache_length):
    row_count = queries.shape[0]
    heads = queries.shape[1] // HEAD_DIM
    table = pltpu.VMEM((heads * row_count, HEAD_DIM), jnp.float32)
    nbytes = 2 * key_cache.size * 2
    return call(
        attend_kernel,
        jax.ShapeDtypeStruct(queries.shape, jnp.bfloat16),
        [SMEM_SPEC, VMEM_SPEC, ANY_SPEC, ANY_SPEC, VMEM_SPEC, VMEM_SPEC],
        [
            pltpu.VMEM(key_cache.shape, jnp.bfloat16),
            pltpu.VMEM(value_cache.shape, jnp.bfloat16),
            table, table, table, table,
            pltpu.SemaphoreType.DMA((row_count,)),
            pltpu.SemaphoreType.DMA((row_count,)),
        ],
        4 * key_cache.size * 6, nbytes, 12,
    )(cache_length, queries, key_cache, value_cache, new_key, new_value)


def project_kernel(count, chunks, place_ref, *refs):
    pieces, weight_hbm, out_ref, stack, weight_buf, sem = (
        refs[:count], refs[count], refs[count + 1], refs[count + 2], refs[count + 3], refs[count + 4],
    )
    height = weight_hbm.shape[0] // chunks
    copies = [
        pltpu.make_async_copy(
            weight_hbm.at[pl.ds(c * height, height)],
            weight_buf.at[pl.ds(c * height, height)],
            sem.at[c],
        )
        for c in range(chunks)
    ]
    for copy in copies:
        copy.start()
    rows = pieces[0].shape[0]
    total = rows * count
    for k in range(count):
        stack[pl.ds(k * rows, rows), :] = pieces[k][...].astype(jnp.float32)
    place = place_ref[0]
    target = lax.broadcasted_iota(jnp.int32, (total, total), 0)
    source = lax.broadcasted_iota(jnp.int32, (total, total), 1)
    owner = place - source // rows
    owner = jnp.where(owner < 0, owner + count, owner)
    order = (target == owner * rows + source % rows).astype(jnp.bfloat16)
    whole = jnp.dot(
        order, stack[...].astype(jnp.bfloat16), preferred_element_type=jnp.float32
    ).astype(jnp.bfloat16)
    result = None
    for c in range(chunks):
        copies[c].wait()
        part = jnp.dot(
            whole[:, c * height : (c + 1) * height],
            weight_buf[pl.ds(c * height, height), :],
            preferred_element_type=jnp.float32,
        )
        result = part if result is None else result + part
    out_ref[...] = result


def project(place, pieces, out_weight):
    count = len(pieces)
    rows, depth = pieces[0].shape
    cols = out_weight.shape[1]
    chunks = 6
    return call(
        functools.partial(project_kernel, count, chunks),
        jax.ShapeDtypeStruct((rows * count, cols), jnp.float32),
        [SMEM_SPEC] + [VMEM_SPEC] * count + [ANY_SPEC],
        [
            pltpu.VMEM((rows * count, depth), jnp.float32),
            pltpu.VMEM(out_weight.shape, jnp.bfloat16),
            pltpu.SemaphoreType.DMA((chunks,)),
        ],
        2 * rows * count * out_weight.size, out_weight.size * 2, 10,
    )(place, *pieces, out_weight)


def expert_rows(routes, expert, capacity):
    row_count = routes.shape[1]
    hit = jnp.max((routes == expert).astype(jnp.float32), axis=0, keepdims=True)
    earlier = lax.broadcasted_iota(jnp.int32, (row_count, row_count), 0) < lax.broadcasted_iota(
        jnp.int32, (row_count, row_count), 1
    )
    slot = jnp.dot(
        jnp.broadcast_to(hit, (8, row_count)).astype(jnp.bfloat16),
        earlier.astype(jnp.bfloat16),
        preferred_element_type=jnp.float32,
    )[:1]
    place = lax.broadcasted_iota(jnp.int32, (capacity, row_count), 0).astype(jnp.float32)
    return jnp.where((slot == place) & (hit > 0.5), 1.0, 0.0)


def wrapped(value, count):
    value = jnp.where(value < 0, value + count, value)
    return jnp.where(value >= count, value - count, value)


def pick_kernel(count, cores, capacity, place_ref, mine_ref, other_ref, residual_ref, routes_ref,
                stream_ref, *out_refs):
    stream = (
        residual_ref[...].astype(jnp.float32) + (mine_ref[...] + other_ref[...])
    ).astype(jnp.bfloat16)
    stream_ref[...] = stream
    routes = routes_ref[...]
    chosen = [
        jnp.dot(
            expert_rows(routes, e, capacity).astype(jnp.bfloat16),
            stream,
            preferred_element_type=jnp.float32,
        )
        for e in range(HELD)
    ]
    sharers = count * cores // HELD
    for k in range(count):
        dest = wrapped(place_ref[0] + k, count)
        out_refs[k][...] = jnp.where(
            dest * cores < sharers, chosen[0], chosen[1]
        ).astype(jnp.bfloat16)


def pick(place, cores, count, capacity, mine, other, residual, routes):
    rows, cols = mine.shape
    return call(
        functools.partial(pick_kernel, count, cores, capacity),
        [jax.ShapeDtypeStruct((rows, cols), jnp.bfloat16)]
        + [jax.ShapeDtypeStruct((capacity, cols), jnp.bfloat16)] * count,
        [SMEM_SPEC] + [VMEM_SPEC] * 4,
        [],
        2 * HELD * capacity * rows * cols, rows * cols * 12, 4,
    )(place, mine, other, residual, routes)


def expert_kernel(count, cores, place_ref, routes_ref, weight_ref, *refs):
    pieces, gains = refs[:count], refs[count : 2 * count]
    gate_hbm, up_hbm, down_hbm = refs[2 * count : 2 * count + 3]
    outs = refs[2 * count + 3 : 3 * count + 3]
    gate_buf, up_buf, down_buf, sem = refs[3 * count + 3 :]
    capacity, cols = pieces[0].shape
    place = place_ref[0]
    copies = []
    for k in range(count):
        source = pl.ds(pl.multiple_of(wrapped(place - k, count) * cols, 128), cols)
        copies.append(
            (
                pltpu.make_async_copy(gate_hbm.at[:, source], gate_buf.at[k], sem.at[0, k]),
                pltpu.make_async_copy(up_hbm.at[:, source], up_buf.at[k], sem.at[1, k]),
            )
        )
    returns = []
    for k in range(count):
        target = pl.ds(pl.multiple_of(wrapped(place + k, count) * cols, 128), cols)
        returns.append(
            pltpu.make_async_copy(down_hbm.at[:, target], down_buf.at[k], sem.at[2, k])
        )
    for pair in copies:
        pair[0].start()
        pair[1].start()
    for copy in returns:
        copy.start()
    sharers = count * cores // HELD
    expert = jnp.where(place * cores < sharers, 0, 1)
    routes = routes_ref[...]
    taken = expert_rows(routes, expert, capacity)
    row_weight = jnp.sum(
        jnp.where(routes == expert, weight_ref[...], 0.0), axis=0, keepdims=True
    )
    slot_weight = jnp.sum(taken * row_weight, axis=1, keepdims=True)
    wide = [piece[...].astype(jnp.float32) for piece in pieces]
    first = wide[0]
    second = wide[0] * wide[0]
    for value in wide[1:]:
        first = first + value
        second = second + value * value
    row_mean = jnp.sum(first, axis=1, keepdims=True) / D
    row_var = jnp.sum(second, axis=1, keepdims=True) / D - row_mean * row_mean
    inverse = lax.rsqrt(row_var + EPSILON)
    contract = (((1,), (1,)), ((), ()))
    gate_val = up_val = None
    for k in range(count):
        normed = ((wide[k] - row_mean) * inverse * gains[k][...]).astype(jnp.bfloat16)
        copies[k][0].wait()
        gate_part = lax.dot_general(
            normed, gate_buf[k], contract, preferred_element_type=jnp.float32
        )
        copies[k][1].wait()
        up_part = lax.dot_general(
            normed, up_buf[k], contract, preferred_element_type=jnp.float32
        )
        gate_val = gate_part if gate_val is None else gate_val + gate_part
        up_val = up_part if up_val is None else up_val + up_part
    hidden = (gate_val / (1.0 + jnp.exp(-gate_val)) * up_val).astype(jnp.bfloat16)
    for k in range(count):
        returns[k].wait()
        outs[k][...] = (
            jnp.dot(hidden, down_buf[k], preferred_element_type=jnp.float32) * slot_weight
        ).astype(jnp.bfloat16)


def run_experts(place, cores, routes, route_weight, pieces, gains, gate, up, down):
    count = len(pieces)
    capacity, cols = pieces[0].shape
    hidden = gate.shape[0]
    buf = pltpu.VMEM((count, hidden, cols), jnp.bfloat16)
    return call(
        functools.partial(expert_kernel, count, cores),
        [jax.ShapeDtypeStruct((capacity, cols), jnp.bfloat16)] * count,
        [SMEM_SPEC] + [VMEM_SPEC] * (2 + 2 * count) + [ANY_SPEC] * 3,
        [buf, buf, buf, pltpu.SemaphoreType.DMA((3, count))],
        6 * capacity * gate.size, gate.size * 6, 14,
    )(place, routes, route_weight, *pieces, *gains, gate, up, down)


def combine_kernel(count, cores, place_ref, routes_ref, *refs):
    pieces, out_ref = refs[:count], refs[count]
    capacity = pieces[0].shape[0]
    sharers = count * cores // HELD
    routes = routes_ref[...]
    taken = [expert_rows(routes, e, capacity) for e in range(HELD)]
    spread = []
    for k in range(count):
        source = wrapped(place_ref[0] - k, count)
        spread.append(jnp.where(source * cores < sharers, taken[0], taken[1]))
    out_ref[...] = lax.dot_general(
        jnp.concatenate(spread, axis=0).astype(jnp.bfloat16),
        jnp.concatenate([piece[...] for piece in pieces], axis=0),
        (((0,), (0,)), ((), ())),
        preferred_element_type=jnp.float32,
    )


def combine(place, cores, routes, pieces):
    count = len(pieces)
    capacity, cols = pieces[0].shape
    rows = routes.shape[1]
    return call(
        functools.partial(combine_kernel, count, cores),
        jax.ShapeDtypeStruct((rows, cols), jnp.float32),
        [SMEM_SPEC] + [VMEM_SPEC] * (1 + count),
        [],
        2 * rows * capacity * count * cols, (count * capacity * 2 + rows * 4) * cols, 4,
    )(place, routes, *pieces)


def shifted(block, count, distance):
    pairs = [(index, (index + distance) % count) for index in range(count)]
    return lax.ppermute(block, "attn", pairs)


def swap(block):
    return lax.ppermute(block, "expert", [(0, 1), (1, 0)])


def shards(
    queries,
    key_cache,
    value_cache,
    new_key,
    new_value,
    cache_length,
    residual,
    out_weight,
    ln_gain,
    gate_weight,
    up_weight,
    down_weight,
    routes,
    route_weight,
):
    count = lax.axis_size("attn")
    cores = lax.axis_size("expert")
    row_count = routes.shape[0]
    capacity = row_count * TOP // EXPERTS * 2
    place = lax.axis_index("attn").astype(jnp.int32).reshape(1)
    routes = routes.T
    route_weight = route_weight.T

    gain = ln_gain.reshape(1, -1)
    gains = [gain] + [shifted(gain, count, k) for k in range(1, count)]

    attended = attend(queries, key_cache, value_cache, new_key, new_value, cache_length)
    pieces = [attended] + [shifted(attended, count, k) for k in range(1, count)]
    mine = project(place, pieces, out_weight)
    other = swap(mine)
    attn_stream, *chosen = pick(
        place, cores, count, capacity, mine, other, residual, routes
    )
    rows = [chosen[0]] + [shifted(chosen[k], count, k) for k in range(1, count)]
    outgoing = run_experts(
        place, cores, routes, route_weight, rows, gains,
        gate_weight.T, up_weight.T, down_weight,
    )
    returned = [outgoing[0]] + [shifted(outgoing[k], count, k) for k in range(1, count)]
    combined = combine(place, cores, routes, returned)
    expert_out = (combined + swap(combined)).astype(jnp.bfloat16)
    return (attn_stream, expert_out)


def solution(mesh):
    cols = D // mesh.shape["attn"]
    return jax.shard_map(
        shards if cols % 128 == 0 else shards_plain,
        mesh=mesh,
        in_specs=(
            P(("group", "attn"), "expert"),
            P(("group", "attn"), None, "expert"),
            P(("group", "attn"), None, "expert"),
            P(("group", "attn"), "expert"),
            P(("group", "attn"), "expert"),
            P(("group", "attn")),
            P("group", "attn"),
            P("expert", "attn"),
            P("attn"),
            P(None, ("attn", "expert")),
            P(None, ("attn", "expert")),
            P(("attn", "expert"), None),
            P("group", None),
            P("group", None),
        ),
        out_specs=(P("group", "attn"), P("group", "attn")),
        check_vma=False,
    )
```

```python
import functools
import math

import jax
import jax.numpy as jnp
from jax import lax
from jax.experimental import pallas as pl
from jax.experimental.pallas import tpu as pltpu
from jax.sharding import PartitionSpec as P

D = 6144
HEADS = 48
KV_HEADS = 8
HEAD_DIM = 128
EXPERTS = 16
TOP = 4
HELD = 2


NEG_FILL = -1e30
EPSILON = 1e-05


def attend_local(queries, key_cache, value_cache, new_key, new_value, cache_length):
    row_count = queries.shape[0]
    kv_local = new_key.shape[1] // HEAD_DIM
    group = HEADS // KV_HEADS
    length_max = key_cache.shape[1]
    query_heads = queries.reshape(row_count, kv_local, group, HEAD_DIM)
    key_heads = key_cache.reshape(row_count, length_max, kv_local, HEAD_DIM)
    value_heads = value_cache.reshape(row_count, length_max, kv_local, HEAD_DIM)
    own_keys = new_key.reshape(row_count, kv_local, HEAD_DIM)
    own_values = new_value.reshape(row_count, kv_local, HEAD_DIM)
    scale = 1.0 / math.sqrt(HEAD_DIM)
    past = (
        jnp.einsum("rkgd,rlkd->rkgl", query_heads, key_heads, preferred_element_type=jnp.float32)
        * scale
    )
    valid = jnp.arange(length_max, dtype=jnp.int32)[None, :] < cache_length[:, None]
    past = jnp.where(valid[:, None, None, :], past, NEG_FILL)
    own = (
        jnp.einsum("rkgd,rkd->rkg", query_heads, own_keys, preferred_element_type=jnp.float32)
        * scale
    )
    largest = jnp.maximum(jnp.max(past, axis=3), own)
    past_weight = jnp.exp(past - largest[..., None])
    own_weight = jnp.exp(own - largest)
    total = jnp.sum(past_weight, axis=3) + own_weight
    past_prob = (past_weight / total[..., None]).astype(jnp.bfloat16)
    own_prob = (own_weight / total).astype(jnp.bfloat16)
    result = jnp.einsum(
        "rkgl,rlkd->rkgd", past_prob, value_heads, preferred_element_type=jnp.float32
    )
    result = (
        result
        + own_prob.astype(jnp.float32)[..., None] * own_values.astype(jnp.float32)[:, :, None, :]
    )
    return result.reshape(row_count, kv_local * group * HEAD_DIM).astype(jnp.bfloat16)


def selection(routes, route_weight, capacity):
    row_count = routes.shape[0]
    experts = jnp.arange(HELD, dtype=jnp.int32)
    match = routes[None, :, :] == experts[:, None, None]
    hit = jnp.any(match, axis=2)
    row_weight = jnp.sum(jnp.where(match, route_weight[None], 0.0), axis=2)
    earlier = jnp.arange(row_count)[:, None] < jnp.arange(row_count)[None, :]
    slot = jnp.sum(jnp.where(earlier[None] & hit[:, :, None], 1, 0), axis=1)
    taken = hit[:, None, :] & (slot[:, None, :] == jnp.arange(capacity, dtype=jnp.int32)[None, :, None])
    slot_weight = jnp.sum(jnp.where(taken, row_weight[:, None, :], 0.0), axis=2)
    return taken, slot_weight


def gather_attn(block):
    count = lax.axis_size("attn")
    copies = jnp.broadcast_to(block[None], (count,) + block.shape)
    return lax.all_to_all(copies, "attn", split_axis=0, concat_axis=0, tiled=True)


def pair_sum(block):
    return block + lax.ppermute(block, "expert", [(0, 1), (1, 0)])


def shards_plain(
    queries,
    key_cache,
    value_cache,
    new_key,
    new_value,
    cache_length,
    residual,
    out_weight,
    ln_gain,
    gate_weight,
    up_weight,
    down_weight,
    routes,
    route_weight,
):
    attn_count = lax.axis_size("attn")
    core_count = lax.axis_size("expert")
    sharers = attn_count * core_count // HELD
    my_expert = (lax.axis_index("attn") * core_count + lax.axis_index("expert")) // sharers
    dest_expert = [index * core_count // sharers for index in range(attn_count)]
    row_count = routes.shape[0]
    capacity = row_count * TOP // EXPERTS * 2
    cols = residual.shape[1]

    taken, slot_weight = selection(routes, route_weight, capacity)
    pick = taken.astype(jnp.bfloat16)

    gains = gather_attn(ln_gain)

    attended = attend_local(queries, key_cache, value_cache, new_key, new_value, cache_length)
    whole = gather_attn(attended).reshape(row_count, -1)
    partial_proj = jnp.dot(whole, out_weight, preferred_element_type=jnp.float32)
    head_total = pair_sum(partial_proj)
    attn_stream = (residual.astype(jnp.float32) + head_total).astype(jnp.bfloat16)

    chosen = jnp.einsum(
        "esr,rd->esd", pick, attn_stream, preferred_element_type=jnp.float32
    ).astype(jnp.bfloat16)
    outgoing = jnp.stack([chosen[index] for index in dest_expert])
    rows = lax.all_to_all(outgoing, "attn", split_axis=0, concat_axis=0, tiled=True)
    wide = rows.astype(jnp.float32)
    row_mean = jnp.sum(wide, axis=(0, 2)) / D
    row_var = jnp.sum(wide * wide, axis=(0, 2)) / D - row_mean * row_mean
    normed = (
        (wide - row_mean[None, :, None])
        * lax.rsqrt(row_var + EPSILON)[None, :, None]
        * gains.reshape(attn_count, 1, cols)
    ).astype(jnp.bfloat16)
    gate_val = jnp.einsum(
        "asd,adf->sf", normed, gate_weight.reshape(attn_count, cols, -1),
        preferred_element_type=jnp.float32,
    )
    up_val = jnp.einsum(
        "asd,adf->sf", normed, up_weight.reshape(attn_count, cols, -1),
        preferred_element_type=jnp.float32,
    )
    hidden = (jax.nn.silu(gate_val) * up_val).astype(jnp.bfloat16)
    piece = jnp.dot(hidden, down_weight, preferred_element_type=jnp.float32)
    mine = jnp.take(slot_weight, my_expert, axis=0)
    piece = (piece * mine[:, None]).astype(jnp.bfloat16)
    returned = lax.all_to_all(
        piece.reshape(capacity, attn_count, cols).swapaxes(0, 1),
        "attn", split_axis=0, concat_axis=0, tiled=True,
    )
    spread = jnp.stack([pick[index] for index in dest_expert])
    combined = jnp.einsum(
        "asr,asd->rd", spread, returned, preferred_element_type=jnp.float32
    )
    expert_out = pair_sum(combined).astype(jnp.bfloat16)
    return (attn_stream, expert_out)


MIB = 1024 * 1024
VMEM_SPEC = pl.BlockSpec(memory_space=pltpu.VMEM)
SMEM_SPEC = pl.BlockSpec(memory_space=pltpu.SMEM)
HBM_SPEC = pl.BlockSpec(memory_space=pltpu.HBM)


def call(kernel, outs, in_specs, scratch, flops, nbytes, vmem_mib):
    single = not isinstance(outs, (list, tuple))
    return pl.pallas_call(
        kernel,
        out_shape=outs,
        in_specs=in_specs,
        out_specs=VMEM_SPEC if single else [VMEM_SPEC] * len(outs),
        scratch_shapes=scratch,
        cost_estimate=pl.CostEstimate(flops=flops, bytes_accessed=nbytes, transcendentals=0),
        compiler_params=pltpu.CompilerParams(vmem_limit_bytes=vmem_mib * MIB),
    )


def attend_kernel(
    length_ref, query_hbm, key_hbm, value_hbm, own_key_hbm, own_value_hbm, gain_hbm, out_ref,
    query_ref, key_buf, value_buf, own_key_ref, own_value_ref, gain_ref,
    query_rows, key_rows, value_rows, result_rows, key_sem, value_sem, small_sem,
):
    row_count, length_max = key_hbm.shape[0], key_hbm.shape[1]
    kv_local = own_key_ref.shape[1] // HEAD_DIM
    group = HEADS // KV_HEADS
    block = group * row_count
    key_copies = [
        pltpu.make_async_copy(key_hbm.at[r], key_buf.at[r], key_sem.at[r]) for r in range(row_count)
    ]
    value_copies = [
        pltpu.make_async_copy(value_hbm.at[r], value_buf.at[r], value_sem.at[r])
        for r in range(row_count)
    ]
    small_copies = [
        pltpu.make_async_copy(source, target, small_sem.at[index])
        for index, (source, target) in enumerate(
            (
                (query_hbm, query_ref),
                (own_key_hbm, own_key_ref),
                (own_value_hbm, own_value_ref),
                (gain_hbm, gain_ref),
            )
        )
    ]
    for copy in small_copies + key_copies + value_copies:
        copy.start()
    for copy in small_copies:
        copy.wait()
    for g in range(kv_local):
        lanes = slice(g * HEAD_DIM, (g + 1) * HEAD_DIM)
        own_key = own_key_ref[:, lanes].astype(jnp.float32)
        own_value = own_value_ref[:, lanes].astype(jnp.float32)
        for i in range(group):
            head = g * group + i
            rows = pl.ds(g * block + i * row_count, row_count)
            query_rows[rows, :] = query_ref[
                :, head * HEAD_DIM : (head + 1) * HEAD_DIM
            ].astype(jnp.float32)
            key_rows[rows, :] = own_key
            value_rows[rows, :] = own_value
    scale = 1.0 / math.sqrt(HEAD_DIM)
    pair_rows = 2 * block
    request = lax.broadcasted_iota(jnp.int32, (pair_rows, 1), 0) % row_count
    lengths = jnp.zeros((pair_rows, 1), jnp.int32)
    for r in range(row_count):
        lengths = jnp.where(request == r, length_ref[r], lengths)
    position = lax.broadcasted_iota(jnp.int32, (pair_rows, length_max), 1)
    valid = position < lengths
    pairs = kv_local // 2
    past = [jnp.zeros((pair_rows, length_max), jnp.float32) for _ in range(pairs)]
    packed = []
    for p in range(pairs):
        rows = query_rows[pl.ds(p * pair_rows, pair_rows), :]
        lower = rows[:block].astype(jnp.bfloat16)
        upper = rows[block:].astype(jnp.bfloat16)
        zero = jnp.zeros_like(lower)
        packed.append(
            jnp.concatenate(
                [
                    jnp.concatenate([lower, zero], axis=1),
                    jnp.concatenate([zero, upper], axis=1),
                ],
                axis=0,
            )
        )
    for r in range(row_count):
        key_copies[r].wait()
        for p in range(pairs):
            keys = key_buf[r, :, p * 2 * HEAD_DIM : (p + 1) * 2 * HEAD_DIM]
            scores = lax.dot_general(
                packed[p], keys, (((1,), (1,)), ((), ())), preferred_element_type=jnp.float32
            )
            past[p] = jnp.where(request == r, scores, past[p])
    probs, own_probs = [], []
    for p in range(pairs):
        rows = pl.ds(p * pair_rows, pair_rows)
        scores = jnp.where(valid, past[p] * scale, NEG_FILL)
        own = jnp.sum(query_rows[rows, :] * key_rows[rows, :], axis=1, keepdims=True) * scale
        largest = jnp.maximum(jnp.max(scores, axis=1, keepdims=True), own)
        weight = jnp.exp(scores - largest)
        own_weight = jnp.exp(own - largest)
        total = jnp.sum(weight, axis=1, keepdims=True) + own_weight
        probs.append((weight / total).astype(jnp.bfloat16))
        own_probs.append((own_weight / total).astype(jnp.bfloat16).astype(jnp.float32))
    sums = [jnp.zeros((pair_rows, 2 * HEAD_DIM), jnp.float32) for _ in range(pairs)]
    for r in range(row_count):
        value_copies[r].wait()
        for p in range(pairs):
            values = value_buf[r, :, p * 2 * HEAD_DIM : (p + 1) * 2 * HEAD_DIM]
            product = jnp.dot(probs[p], values, preferred_element_type=jnp.float32)
            sums[p] = jnp.where(request == r, product, sums[p])
    for p in range(pairs):
        rows = pl.ds(p * pair_rows, pair_rows)
        own_part = own_probs[p] * value_rows[rows, :]
        lower = sums[p][:block, :HEAD_DIM] + own_part[:block]
        upper = sums[p][block:, HEAD_DIM:] + own_part[block:]
        result_rows[pl.ds(p * pair_rows, block), :] = lower
        result_rows[pl.ds(p * pair_rows + block, block), :] = upper
    width = query_hbm.shape[1]
    for head in range(kv_local * group):
        rows = result_rows[pl.ds(head * row_count, row_count), :].astype(jnp.bfloat16)
        for index in range(out_ref.shape[0]):
            out_ref[index, :, head * HEAD_DIM : (head + 1) * HEAD_DIM] = rows
    half = gain_ref.shape[1] // 2
    row = lax.broadcasted_iota(jnp.int32, (row_count, half), 0)
    left = jnp.broadcast_to(gain_ref[:, :half], (row_count, half))
    right = jnp.broadcast_to(gain_ref[:, half:], (row_count, half))
    gain = jnp.where(row % 2 == 0, left, right)
    upper = gain.astype(jnp.bfloat16).astype(jnp.float32)
    parts = jnp.where(row < 2, upper, gain - upper).astype(jnp.bfloat16)
    for index in range(out_ref.shape[0]):
        out_ref[index, :, width:] = parts


def attend(count, queries, key_cache, value_cache, new_key, new_value, cache_length, gain):
    row_count, width = queries.shape
    heads = width // HEAD_DIM
    table = pltpu.VMEM((heads * row_count, HEAD_DIM), jnp.float32)
    nbytes = 2 * key_cache.size * 2
    return call(
        attend_kernel,
        jax.ShapeDtypeStruct((count, row_count, width + gain.shape[1] // 2), jnp.bfloat16),
        [SMEM_SPEC] + [HBM_SPEC] * 6,
        [
            pltpu.VMEM(queries.shape, jnp.bfloat16),
            pltpu.VMEM(key_cache.shape, jnp.bfloat16),
            pltpu.VMEM(value_cache.shape, jnp.bfloat16),
            pltpu.VMEM(new_key.shape, jnp.bfloat16),
            pltpu.VMEM(new_value.shape, jnp.bfloat16),
            pltpu.VMEM(gain.shape, jnp.float32),
            table, table, table, table,
            pltpu.SemaphoreType.DMA((row_count,)),
            pltpu.SemaphoreType.DMA((row_count,)),
            pltpu.SemaphoreType.DMA((4,)),
        ],
        4 * key_cache.size * 6, nbytes, 12,
    )(cache_length, queries, key_cache, value_cache, new_key, new_value, gain)


def project_kernel(chunks, pieces, weight_hbm, out_ref, gain_ref, stack, weight_buf, sem):
    height = weight_hbm.shape[0] // chunks
    copies = [
        pltpu.make_async_copy(
            weight_hbm.at[pl.ds(c * height, height)],
            weight_buf.at[pl.ds(c * height, height)],
            sem.at[c],
        )
        for c in range(chunks)
    ]
    for copy in copies:
        copy.start()
    count, rows, _ = pieces.shape
    width = weight_hbm.shape[0]
    half = gain_ref.shape[1] // 2
    for k in range(count):
        stack[pl.ds(k * rows, rows), :] = pieces[k, :, :width].astype(jnp.float32)
        parts = pieces[k, :, width:].astype(jnp.float32)
        gain_ref[pl.ds(k, 1), :half] = parts[0:1] + parts[2:3]
        gain_ref[pl.ds(k, 1), half:] = parts[1:2] + parts[3:4]
    result = None
    for c in range(chunks):
        copies[c].wait()
        part = jnp.dot(
            stack[:, pl.ds(c * height, height)].astype(jnp.bfloat16),
            weight_buf[pl.ds(c * height, height), :],
            preferred_element_type=jnp.float32,
        )
        result = part if result is None else result + part
    out_ref[...] = result


def project(pieces, out_weight):
    count, rows, _ = pieces.shape
    depth, cols = out_weight.shape
    chunks = 6
    return call(
        functools.partial(project_kernel, chunks),
        [
            jax.ShapeDtypeStruct((rows * count, cols), jnp.float32),
            jax.ShapeDtypeStruct((count, cols), jnp.float32),
        ],
        [VMEM_SPEC, HBM_SPEC],
        [
            pltpu.VMEM((rows * count, depth), jnp.float32),
            pltpu.VMEM(out_weight.shape, jnp.bfloat16),
            pltpu.SemaphoreType.DMA((chunks,)),
        ],
        2 * rows * count * out_weight.size, out_weight.size * 2, 10,
    )(pieces, out_weight)


def expert_rows(routes, expert, capacity):
    row_count = routes.shape[1]
    hit = jnp.max((routes == expert).astype(jnp.float32), axis=0, keepdims=True)
    earlier = lax.broadcasted_iota(jnp.int32, (row_count, row_count), 0) < lax.broadcasted_iota(
        jnp.int32, (row_count, row_count), 1
    )
    slot = jnp.dot(
        jnp.broadcast_to(hit, (8, row_count)).astype(jnp.bfloat16),
        earlier.astype(jnp.bfloat16),
        preferred_element_type=jnp.float32,
    )[:1]
    place = lax.broadcasted_iota(jnp.int32, (capacity, row_count), 0).astype(jnp.float32)
    return jnp.where((slot == place) & (hit > 0.5), 1.0, 0.0)


def pick_kernel(cores, mine_ref, other_ref, residual_ref, routes_ref, stream_ref, out_ref):
    count, capacity, _ = out_ref.shape
    stream = (
        residual_ref[...].astype(jnp.float32) + (mine_ref[...] + other_ref[...])
    ).astype(jnp.bfloat16)
    stream_ref[...] = stream
    routes = routes_ref[...]
    chosen = [
        jnp.dot(
            expert_rows(routes, e, capacity).astype(jnp.bfloat16),
            stream,
            preferred_element_type=jnp.float32,
        ).astype(jnp.bfloat16)
        for e in range(HELD)
    ]
    sharers = count * cores // HELD
    for k in range(count):
        out_ref[k] = chosen[k * cores // sharers]


def pick(cores, count, capacity, mine, other, residual, routes):
    rows, cols = mine.shape
    return call(
        functools.partial(pick_kernel, cores),
        [
            jax.ShapeDtypeStruct((rows, cols), jnp.bfloat16),
            jax.ShapeDtypeStruct((count, capacity, cols), jnp.bfloat16),
        ],
        [VMEM_SPEC] * 4,
        [],
        2 * HELD * capacity * rows * cols, rows * cols * 12, 4,
    )(mine, other, residual, routes)


def expert_kernel(cores, place_ref, routes_ref, weight_ref, pieces, gains, gate_hbm, up_hbm,
                  down_hbm, out_ref, gate_buf, up_buf, down_buf, sem):
    count, capacity, cols = pieces.shape
    copies, returns = [], []
    for k in range(count):
        block = pl.ds(k * cols, cols)
        copies.append(
            (
                pltpu.make_async_copy(gate_hbm.at[:, block], gate_buf.at[k], sem.at[0, k]),
                pltpu.make_async_copy(up_hbm.at[:, block], up_buf.at[k], sem.at[1, k]),
            )
        )
        returns.append(
            pltpu.make_async_copy(down_hbm.at[:, block], down_buf.at[k], sem.at[2, k])
        )
    for pair in copies:
        pair[0].start()
        pair[1].start()
    for copy in returns:
        copy.start()
    sharers = count * cores // HELD
    expert = jnp.where(place_ref[0] * cores < sharers, 0, 1)
    routes = routes_ref[...]
    taken = expert_rows(routes, expert, capacity)
    row_weight = jnp.sum(
        jnp.where(routes == expert, weight_ref[...], 0.0), axis=0, keepdims=True
    )
    slot_weight = jnp.sum(taken * row_weight, axis=1, keepdims=True)
    first = second = 0.0
    for k in range(count):
        wide = pieces[k].astype(jnp.float32)
        first = first + wide
        second = second + wide * wide
    row_mean = jnp.sum(first, axis=1, keepdims=True) / D
    row_var = jnp.sum(second, axis=1, keepdims=True) / D - row_mean * row_mean
    inverse = lax.rsqrt(row_var + EPSILON)
    contract = (((1,), (1,)), ((), ()))
    gate_val = up_val = 0.0
    for k in range(count):
        wide = pieces[k].astype(jnp.float32)
        normed = ((wide - row_mean) * inverse * gains[pl.ds(k, 1), :]).astype(jnp.bfloat16)
        copies[k][0].wait()
        gate_val = gate_val + lax.dot_general(
            gate_buf[k], normed, contract, preferred_element_type=jnp.float32
        )
        copies[k][1].wait()
        up_val = up_val + lax.dot_general(
            up_buf[k], normed, contract, preferred_element_type=jnp.float32
        )
    hidden = (gate_val / (1.0 + jnp.exp(-gate_val)) * up_val).T.astype(jnp.bfloat16)
    for k in range(count):
        returns[k].wait()
        out_ref[k] = (
            jnp.dot(hidden, down_buf[k], preferred_element_type=jnp.float32) * slot_weight
        ).astype(jnp.bfloat16)


def run_experts(place, cores, routes, route_weight, pieces, gains, gate, up, down):
    count, capacity, cols = pieces.shape
    hidden = gate.shape[0]
    buf = pltpu.VMEM((count, hidden, cols), jnp.bfloat16)
    return call(
        functools.partial(expert_kernel, cores),
        jax.ShapeDtypeStruct((count, capacity, cols), jnp.bfloat16),
        [SMEM_SPEC] + [VMEM_SPEC] * 4 + [HBM_SPEC] * 3,
        [buf, buf, buf, pltpu.SemaphoreType.DMA((3, count))],
        6 * capacity * gate.size, gate.size * 6, 14,
    )(place, routes, route_weight, pieces, gains, gate, up, down)


def combine_kernel(cores, routes_ref, pieces, out_ref):
    count, capacity, cols = pieces.shape
    sharers = count * cores // HELD
    routes = routes_ref[...]
    taken = [expert_rows(routes, e, capacity) for e in range(HELD)]
    spread = [taken[k * cores // sharers] for k in range(count)]
    out_ref[...] = lax.dot_general(
        jnp.concatenate(spread, axis=0).astype(jnp.bfloat16),
        pieces[...].reshape(count * capacity, cols),
        (((0,), (0,)), ((), ())),
        preferred_element_type=jnp.float32,
    )


def combine(cores, routes, pieces):
    count, capacity, cols = pieces.shape
    rows = routes.shape[1]
    return call(
        functools.partial(combine_kernel, cores),
        jax.ShapeDtypeStruct((rows, cols), jnp.float32),
        [VMEM_SPEC] * 2,
        [],
        2 * rows * capacity * count * cols, (count * capacity * 2 + rows * 4) * cols, 4,
    )(routes, pieces)


def exchange(blocks):
    return lax.all_to_all(blocks, "attn", split_axis=0, concat_axis=0, tiled=True)


def swap(block):
    return lax.ppermute(block, "expert", [(0, 1), (1, 0)])


def shards(
    queries,
    key_cache,
    value_cache,
    new_key,
    new_value,
    cache_length,
    residual,
    out_weight,
    ln_gain,
    gate_weight,
    up_weight,
    down_weight,
    routes,
    route_weight,
):
    count = lax.axis_size("attn")
    cores = lax.axis_size("expert")
    capacity = routes.shape[0] * TOP // EXPERTS * 2
    place = lax.axis_index("attn").astype(jnp.int32).reshape(1)
    routes = routes.T
    route_weight = route_weight.T

    attended = exchange(
        attend(
            count, queries, key_cache, value_cache, new_key, new_value, cache_length,
            ln_gain.reshape(1, -1),
        )
    )
    mine, gains = project(attended, out_weight)
    attn_stream, chosen = pick(cores, count, capacity, mine, swap(mine), residual, routes)
    outgoing = run_experts(
        place, cores, routes, route_weight, exchange(chosen), gains,
        gate_weight.T, up_weight.T, down_weight,
    )
    combined = combine(cores, routes, exchange(outgoing))
    expert_out = (combined + swap(combined)).astype(jnp.bfloat16)
    return (attn_stream, expert_out)


def solution(mesh):
    cols = D // mesh.shape["attn"]
    return jax.shard_map(
        shards if cols % 256 == 0 else shards_plain,
        mesh=mesh,
        in_specs=(
            P(("group", "attn"), "expert"),
            P(("group", "attn"), None, "expert"),
            P(("group", "attn"), None, "expert"),
            P(("group", "attn"), "expert"),
            P(("group", "attn"), "expert"),
            P(("group", "attn")),
            P("group", "attn"),
            P("expert", "attn"),
            P("attn"),
            P(None, ("attn", "expert")),
            P(None, ("attn", "expert")),
            P(("attn", "expert"), None),
            P("group", None),
            P("group", None),
        ),
        out_specs=(P("group", "attn"), P("group", "attn")),
        check_vma=False,
    )
```

```python
import functools
import math

import jax
import jax.numpy as jnp
from jax import lax
from jax.experimental import pallas as pl
from jax.experimental.pallas import tpu as pltpu
from jax.sharding import PartitionSpec as P

D = 6144
HEADS = 48
KV_HEADS = 8
HEAD_DIM = 128
EXPERTS = 16
TOP = 4
HELD = 2


NEG_FILL = -1e30
EPSILON = 1e-05


def attend_local(queries, key_cache, value_cache, new_key, new_value, cache_length):
    row_count = queries.shape[0]
    kv_local = new_key.shape[1] // HEAD_DIM
    group = HEADS // KV_HEADS
    length_max = key_cache.shape[1]
    query_heads = queries.reshape(row_count, kv_local, group, HEAD_DIM)
    key_heads = key_cache.reshape(row_count, length_max, kv_local, HEAD_DIM)
    value_heads = value_cache.reshape(row_count, length_max, kv_local, HEAD_DIM)
    own_keys = new_key.reshape(row_count, kv_local, HEAD_DIM)
    own_values = new_value.reshape(row_count, kv_local, HEAD_DIM)
    scale = 1.0 / math.sqrt(HEAD_DIM)
    past = (
        jnp.einsum("rkgd,rlkd->rkgl", query_heads, key_heads, preferred_element_type=jnp.float32)
        * scale
    )
    valid = jnp.arange(length_max, dtype=jnp.int32)[None, :] < cache_length[:, None]
    past = jnp.where(valid[:, None, None, :], past, NEG_FILL)
    own = (
        jnp.einsum("rkgd,rkd->rkg", query_heads, own_keys, preferred_element_type=jnp.float32)
        * scale
    )
    largest = jnp.maximum(jnp.max(past, axis=3), own)
    past_weight = jnp.exp(past - largest[..., None])
    own_weight = jnp.exp(own - largest)
    total = jnp.sum(past_weight, axis=3) + own_weight
    past_prob = (past_weight / total[..., None]).astype(jnp.bfloat16)
    own_prob = (own_weight / total).astype(jnp.bfloat16)
    result = jnp.einsum(
        "rkgl,rlkd->rkgd", past_prob, value_heads, preferred_element_type=jnp.float32
    )
    result = (
        result
        + own_prob.astype(jnp.float32)[..., None] * own_values.astype(jnp.float32)[:, :, None, :]
    )
    return result.reshape(row_count, kv_local * group * HEAD_DIM).astype(jnp.bfloat16)


def selection(routes, route_weight, capacity):
    row_count = routes.shape[0]
    experts = jnp.arange(HELD, dtype=jnp.int32)
    match = routes[None, :, :] == experts[:, None, None]
    hit = jnp.any(match, axis=2)
    row_weight = jnp.sum(jnp.where(match, route_weight[None], 0.0), axis=2)
    earlier = jnp.arange(row_count)[:, None] < jnp.arange(row_count)[None, :]
    slot = jnp.sum(jnp.where(earlier[None] & hit[:, :, None], 1, 0), axis=1)
    taken = hit[:, None, :] & (slot[:, None, :] == jnp.arange(capacity, dtype=jnp.int32)[None, :, None])
    slot_weight = jnp.sum(jnp.where(taken, row_weight[:, None, :], 0.0), axis=2)
    return taken, slot_weight


def gather_attn(block):
    count = lax.axis_size("attn")
    copies = jnp.broadcast_to(block[None], (count,) + block.shape)
    return lax.all_to_all(copies, "attn", split_axis=0, concat_axis=0, tiled=True)


def pair_sum(block):
    return block + lax.ppermute(block, "expert", [(0, 1), (1, 0)])


def shards_plain(
    queries,
    key_cache,
    value_cache,
    new_key,
    new_value,
    cache_length,
    residual,
    out_weight,
    ln_gain,
    gate_weight,
    up_weight,
    down_weight,
    routes,
    route_weight,
):
    attn_count = lax.axis_size("attn")
    core_count = lax.axis_size("expert")
    sharers = attn_count * core_count // HELD
    my_expert = (lax.axis_index("attn") * core_count + lax.axis_index("expert")) // sharers
    dest_expert = [index * core_count // sharers for index in range(attn_count)]
    row_count = routes.shape[0]
    capacity = row_count * TOP // EXPERTS * 2
    cols = residual.shape[1]

    taken, slot_weight = selection(routes, route_weight, capacity)
    pick = taken.astype(jnp.bfloat16)

    gains = gather_attn(ln_gain)

    attended = attend_local(queries, key_cache, value_cache, new_key, new_value, cache_length)
    whole = gather_attn(attended).reshape(row_count, -1)
    partial_proj = jnp.dot(whole, out_weight, preferred_element_type=jnp.float32)
    head_total = pair_sum(partial_proj)
    attn_stream = (residual.astype(jnp.float32) + head_total).astype(jnp.bfloat16)

    chosen = jnp.einsum(
        "esr,rd->esd", pick, attn_stream, preferred_element_type=jnp.float32
    ).astype(jnp.bfloat16)
    outgoing = jnp.stack([chosen[index] for index in dest_expert])
    rows = lax.all_to_all(outgoing, "attn", split_axis=0, concat_axis=0, tiled=True)
    wide = rows.astype(jnp.float32)
    row_mean = jnp.sum(wide, axis=(0, 2)) / D
    row_var = jnp.sum(wide * wide, axis=(0, 2)) / D - row_mean * row_mean
    normed = (
        (wide - row_mean[None, :, None])
        * lax.rsqrt(row_var + EPSILON)[None, :, None]
        * gains.reshape(attn_count, 1, cols)
    ).astype(jnp.bfloat16)
    gate_val = jnp.einsum(
        "asd,adf->sf", normed, gate_weight.reshape(attn_count, cols, -1),
        preferred_element_type=jnp.float32,
    )
    up_val = jnp.einsum(
        "asd,adf->sf", normed, up_weight.reshape(attn_count, cols, -1),
        preferred_element_type=jnp.float32,
    )
    hidden = (jax.nn.silu(gate_val) * up_val).astype(jnp.bfloat16)
    piece = jnp.dot(hidden, down_weight, preferred_element_type=jnp.float32)
    mine = jnp.take(slot_weight, my_expert, axis=0)
    piece = (piece * mine[:, None]).astype(jnp.bfloat16)
    returned = lax.all_to_all(
        piece.reshape(capacity, attn_count, cols).swapaxes(0, 1),
        "attn", split_axis=0, concat_axis=0, tiled=True,
    )
    spread = jnp.stack([pick[index] for index in dest_expert])
    combined = jnp.einsum(
        "asr,asd->rd", spread, returned, preferred_element_type=jnp.float32
    )
    expert_out = pair_sum(combined).astype(jnp.bfloat16)
    return (attn_stream, expert_out)


MIB = 1024 * 1024
ATTEND_MIB = 58_000_000 / MIB
EXCHANGE_FLOPS = 10**10
VMEM_SPEC = pl.BlockSpec(memory_space=pltpu.VMEM)
SMEM_SPEC = pl.BlockSpec(memory_space=pltpu.SMEM)
HBM_SPEC = pl.BlockSpec(memory_space=pltpu.HBM)


def call(kernel, outs, in_specs, scratch, flops, nbytes, vmem_mib):
    single = not isinstance(outs, (list, tuple))
    return pl.pallas_call(
        kernel,
        out_shape=outs,
        in_specs=in_specs,
        out_specs=VMEM_SPEC if single else [VMEM_SPEC] * len(outs),
        scratch_shapes=scratch,
        cost_estimate=pl.CostEstimate(flops=flops, bytes_accessed=nbytes, transcendentals=0),
        compiler_params=pltpu.CompilerParams(vmem_limit_bytes=int(vmem_mib * MIB)),
    )


def attend_kernel(
    length_ref, query_hbm, key_hbm, value_hbm, own_key_hbm, own_value_hbm, gain_hbm, out_ref,
    query_ref, key_buf, value_buf, own_key_ref, own_value_ref, gain_ref,
    query_rows, key_rows, value_rows, result_rows, key_sem, value_sem, small_sem,
):
    row_count, length_max = key_hbm.shape[0], key_hbm.shape[1]
    kv_local = own_key_ref.shape[1] // HEAD_DIM
    group = HEADS // KV_HEADS
    block = group * row_count
    key_copies = [
        pltpu.make_async_copy(key_hbm.at[r], key_buf.at[r], key_sem.at[r]) for r in range(row_count)
    ]
    value_copies = [
        pltpu.make_async_copy(value_hbm.at[r], value_buf.at[r], value_sem.at[r])
        for r in range(row_count)
    ]
    small_copies = [
        pltpu.make_async_copy(source, target, small_sem.at[index])
        for index, (source, target) in enumerate(
            (
                (query_hbm, query_ref),
                (own_key_hbm, own_key_ref),
                (own_value_hbm, own_value_ref),
                (gain_hbm, gain_ref),
            )
        )
    ]
    for copy in small_copies + key_copies + value_copies:
        copy.start()
    for copy in small_copies:
        copy.wait()
    for g in range(kv_local):
        lanes = slice(g * HEAD_DIM, (g + 1) * HEAD_DIM)
        own_key = own_key_ref[:, lanes].astype(jnp.float32)
        own_value = own_value_ref[:, lanes].astype(jnp.float32)
        for i in range(group):
            head = g * group + i
            rows = pl.ds(g * block + i * row_count, row_count)
            query_rows[rows, :] = query_ref[
                :, head * HEAD_DIM : (head + 1) * HEAD_DIM
            ].astype(jnp.float32)
            key_rows[rows, :] = own_key
            value_rows[rows, :] = own_value
    scale = 1.0 / math.sqrt(HEAD_DIM)
    pair_rows = 2 * block
    request = lax.broadcasted_iota(jnp.int32, (pair_rows, 1), 0) % row_count
    lengths = jnp.zeros((pair_rows, 1), jnp.int32)
    for r in range(row_count):
        lengths = jnp.where(request == r, length_ref[r], lengths)
    position = lax.broadcasted_iota(jnp.int32, (pair_rows, length_max), 1)
    valid = position < lengths
    pairs = kv_local // 2
    past = [jnp.zeros((pair_rows, length_max), jnp.float32) for _ in range(pairs)]
    packed = []
    for p in range(pairs):
        rows = query_rows[pl.ds(p * pair_rows, pair_rows), :]
        lower = rows[:block].astype(jnp.bfloat16)
        upper = rows[block:].astype(jnp.bfloat16)
        zero = jnp.zeros_like(lower)
        packed.append(
            jnp.concatenate(
                [
                    jnp.concatenate([lower, zero], axis=1),
                    jnp.concatenate([zero, upper], axis=1),
                ],
                axis=0,
            )
        )
    for r in range(row_count):
        key_copies[r].wait()
        for p in range(pairs):
            keys = key_buf[r, :, p * 2 * HEAD_DIM : (p + 1) * 2 * HEAD_DIM]
            scores = lax.dot_general(
                packed[p], keys, (((1,), (1,)), ((), ())), preferred_element_type=jnp.float32
            )
            past[p] = jnp.where(request == r, scores, past[p])
    probs, own_probs = [], []
    for p in range(pairs):
        rows = pl.ds(p * pair_rows, pair_rows)
        scores = jnp.where(valid, past[p] * scale, NEG_FILL)
        own = jnp.sum(query_rows[rows, :] * key_rows[rows, :], axis=1, keepdims=True) * scale
        largest = jnp.maximum(jnp.max(scores, axis=1, keepdims=True), own)
        weight = jnp.exp(scores - largest)
        own_weight = jnp.exp(own - largest)
        total = jnp.sum(weight, axis=1, keepdims=True) + own_weight
        probs.append((weight / total).astype(jnp.bfloat16))
        own_probs.append((own_weight / total).astype(jnp.bfloat16).astype(jnp.float32))
    sums = [jnp.zeros((pair_rows, 2 * HEAD_DIM), jnp.float32) for _ in range(pairs)]
    for r in range(row_count):
        value_copies[r].wait()
        for p in range(pairs):
            values = value_buf[r, :, p * 2 * HEAD_DIM : (p + 1) * 2 * HEAD_DIM]
            product = jnp.dot(probs[p], values, preferred_element_type=jnp.float32)
            sums[p] = jnp.where(request == r, product, sums[p])
    for p in range(pairs):
        rows = pl.ds(p * pair_rows, pair_rows)
        own_part = own_probs[p] * value_rows[rows, :]
        lower = sums[p][:block, :HEAD_DIM] + own_part[:block]
        upper = sums[p][block:, HEAD_DIM:] + own_part[block:]
        result_rows[pl.ds(p * pair_rows, block), :] = lower
        result_rows[pl.ds(p * pair_rows + block, block), :] = upper
    width = query_hbm.shape[1]
    for head in range(kv_local * group):
        rows = result_rows[pl.ds(head * row_count, row_count), :].astype(jnp.bfloat16)
        for index in range(out_ref.shape[0]):
            out_ref[index, :, head * HEAD_DIM : (head + 1) * HEAD_DIM] = rows
    gain_row = gain_ref[...].reshape(1, -1)
    half = gain_row.shape[1] // 2
    row = lax.broadcasted_iota(jnp.int32, (row_count, half), 0)
    left = jnp.broadcast_to(gain_row[:, :half], (row_count, half))
    right = jnp.broadcast_to(gain_row[:, half:], (row_count, half))
    gain = jnp.where(row % 2 == 0, left, right)
    upper = gain.astype(jnp.bfloat16).astype(jnp.float32)
    parts = jnp.where(row < 2, upper, gain - upper).astype(jnp.bfloat16)
    for index in range(out_ref.shape[0]):
        out_ref[index, :, width:] = parts


def attend(count, queries, key_cache, value_cache, new_key, new_value, cache_length, gain):
    row_count, width = queries.shape
    heads = width // HEAD_DIM
    table = pltpu.VMEM((heads * row_count, HEAD_DIM), jnp.float32)
    nbytes = 2 * key_cache.size * 2
    return call(
        attend_kernel,
        jax.ShapeDtypeStruct((count, row_count, width + gain.shape[0] // 2), jnp.bfloat16),
        [SMEM_SPEC] + [HBM_SPEC] * 6,
        [
            pltpu.VMEM(queries.shape, jnp.bfloat16),
            pltpu.VMEM(key_cache.shape, jnp.bfloat16),
            pltpu.VMEM(value_cache.shape, jnp.bfloat16),
            pltpu.VMEM(new_key.shape, jnp.bfloat16),
            pltpu.VMEM(new_value.shape, jnp.bfloat16),
            pltpu.VMEM(gain.shape, jnp.float32),
            table, table, table, table,
            pltpu.SemaphoreType.DMA((row_count,)),
            pltpu.SemaphoreType.DMA((row_count,)),
            pltpu.SemaphoreType.DMA((4,)),
        ],
        4 * key_cache.size * 6, nbytes, ATTEND_MIB,
    )(cache_length, queries, key_cache, value_cache, new_key, new_value, gain)


def project_kernel(pieces, weight_ref, out_ref, gain_ref, stack):
    count, rows, _ = pieces.shape
    width = weight_ref.shape[0]
    half = gain_ref.shape[1] // 2
    for k in range(count):
        stack[pl.ds(k * rows, rows), :] = pieces[k, :, :width].astype(jnp.float32)
        parts = pieces[k, :, width:].astype(jnp.float32)
        gain_ref[pl.ds(k, 1), :half] = parts[0:1] + parts[2:3]
        gain_ref[pl.ds(k, 1), half:] = parts[1:2] + parts[3:4]
    out_ref[...] = jnp.dot(
        stack[...].astype(jnp.bfloat16), weight_ref[...], preferred_element_type=jnp.float32
    )


def project(pieces, out_weight):
    count, rows, _ = pieces.shape
    depth, cols = out_weight.shape
    return call(
        project_kernel,
        [
            jax.ShapeDtypeStruct((rows * count, cols), jnp.float32),
            jax.ShapeDtypeStruct((count, cols), jnp.float32),
        ],
        [VMEM_SPEC, VMEM_SPEC],
        [pltpu.VMEM((rows * count, depth), jnp.float32)],
        2 * rows * count * out_weight.size, out_weight.size * 2, 10,
    )(pieces, out_weight)


def expert_rows(routes, expert, capacity):
    row_count = routes.shape[1]
    hit = jnp.max((routes == expert).astype(jnp.float32), axis=0, keepdims=True)
    earlier = lax.broadcasted_iota(jnp.int32, (row_count, row_count), 0) < lax.broadcasted_iota(
        jnp.int32, (row_count, row_count), 1
    )
    slot = jnp.dot(
        jnp.broadcast_to(hit, (8, row_count)).astype(jnp.bfloat16),
        earlier.astype(jnp.bfloat16),
        preferred_element_type=jnp.float32,
    )[:1]
    place = lax.broadcasted_iota(jnp.int32, (capacity, row_count), 0).astype(jnp.float32)
    return jnp.where((slot == place) & (hit > 0.5), 1.0, 0.0)


def pick_kernel(cores, place_ref, mine_ref, other_ref, residual_ref, routes_ref, weight_ref,
                stream_ref, out_ref, slot_ref):
    count, capacity, _ = out_ref.shape
    stream = (
        residual_ref[...].astype(jnp.float32) + (mine_ref[...] + other_ref[...])
    ).astype(jnp.bfloat16)
    stream_ref[...] = stream
    routes = routes_ref[...]
    sharers = count * cores // HELD
    taken = [expert_rows(routes, e, capacity) for e in range(HELD)]
    chosen = [
        jnp.dot(
            taken[e].astype(jnp.bfloat16), stream, preferred_element_type=jnp.float32
        ).astype(jnp.bfloat16)
        for e in range(HELD)
    ]
    for k in range(count):
        out_ref[k] = chosen[k * cores // sharers]
    first = place_ref[0] * cores < sharers
    expert = jnp.where(first, 0, 1)
    row_weight = jnp.sum(
        jnp.where(routes == expert, weight_ref[...], 0.0), axis=0, keepdims=True
    )
    mine = jnp.where(first, taken[0], taken[1])
    slot_ref[...] = jnp.broadcast_to(
        jnp.sum(mine * row_weight, axis=1, keepdims=True), slot_ref.shape
    )


def pick(place, cores, count, capacity, mine, other, residual, routes, route_weight):
    rows, cols = mine.shape
    return call(
        functools.partial(pick_kernel, cores),
        [
            jax.ShapeDtypeStruct((rows, cols), jnp.bfloat16),
            jax.ShapeDtypeStruct((count, capacity, cols), jnp.bfloat16),
            jax.ShapeDtypeStruct((capacity, 128), jnp.float32),
        ],
        [SMEM_SPEC] + [VMEM_SPEC] * 5,
        [],
        EXCHANGE_FLOPS, rows * cols * 12, 4,
    )(place, mine, other, residual, routes, route_weight)


def expert_kernel(slot_ref, pieces, gains, gate_ref, up_ref, down_ref, out_ref):
    count, capacity, cols = pieces.shape
    first = second = 0.0
    for k in range(count):
        wide = pieces[k].astype(jnp.float32)
        first = first + wide
        second = second + wide * wide
    row_mean = jnp.sum(first, axis=1, keepdims=True) / D
    row_var = jnp.sum(second, axis=1, keepdims=True) / D - row_mean * row_mean
    inverse = lax.rsqrt(row_var + EPSILON)
    contract = (((1,), (1,)), ((), ()))
    gate_val = up_val = 0.0
    for k in range(count):
        block = slice(k * cols, (k + 1) * cols)
        wide = pieces[k].astype(jnp.float32)
        normed = ((wide - row_mean) * inverse * gains[pl.ds(k, 1), :]).astype(jnp.bfloat16)
        gate_val = gate_val + lax.dot_general(
            gate_ref[:, block], normed, contract, preferred_element_type=jnp.float32
        )
        up_val = up_val + lax.dot_general(
            up_ref[:, block], normed, contract, preferred_element_type=jnp.float32
        )
    hidden = (gate_val / (1.0 + jnp.exp(-gate_val)) * up_val).T.astype(jnp.bfloat16)
    slot_weight = slot_ref[:, :1]
    for k in range(count):
        block = slice(k * cols, (k + 1) * cols)
        out_ref[k] = (
            jnp.dot(hidden, down_ref[:, block], preferred_element_type=jnp.float32) * slot_weight
        ).astype(jnp.bfloat16)


def run_experts(slots, pieces, gains, gate, up, down):
    return call(
        expert_kernel,
        jax.ShapeDtypeStruct(pieces.shape, jnp.bfloat16),
        [VMEM_SPEC] * 6,
        [],
        6 * pieces.shape[1] * gate.size, gate.size * 6, 14,
    )(slots, pieces, gains, gate, up, down)


def combine_kernel(cores, routes_ref, pieces, out_ref):
    count, capacity, cols = pieces.shape
    sharers = count * cores // HELD
    routes = routes_ref[...]
    taken = [expert_rows(routes, e, capacity) for e in range(HELD)]
    spread = [taken[k * cores // sharers] for k in range(count)]
    out_ref[...] = lax.dot_general(
        jnp.concatenate(spread, axis=0).astype(jnp.bfloat16),
        pieces[...].reshape(count * capacity, cols),
        (((0,), (0,)), ((), ())),
        preferred_element_type=jnp.float32,
    )


def combine(cores, routes, pieces):
    count, capacity, cols = pieces.shape
    rows = routes.shape[1]
    return call(
        functools.partial(combine_kernel, cores),
        jax.ShapeDtypeStruct((rows, cols), jnp.float32),
        [VMEM_SPEC] * 2,
        [],
        2 * rows * capacity * count * cols, (count * capacity * 2 + rows * 4) * cols, 4,
    )(routes, pieces)


def exchange(blocks):
    return lax.all_to_all(blocks, "attn", split_axis=0, concat_axis=0, tiled=True)


def swap(block):
    return lax.ppermute(block, "expert", [(0, 1), (1, 0)])


def shards(
    queries,
    key_cache,
    value_cache,
    new_key,
    new_value,
    cache_length,
    residual,
    out_weight,
    ln_gain,
    gate_weight,
    up_weight,
    down_weight,
    routes,
    route_weight,
):
    count = lax.axis_size("attn")
    cores = lax.axis_size("expert")
    capacity = routes.shape[0] * TOP // EXPERTS * 2
    place = lax.axis_index("attn").astype(jnp.int32).reshape(1)
    routes = routes.T
    route_weight = route_weight.T

    attended = exchange(
        attend(
            count, queries, key_cache, value_cache, new_key, new_value, cache_length,
            ln_gain,
        )
    )
    mine, gains = project(attended, out_weight)
    attn_stream, chosen, slots = pick(
        place, cores, count, capacity, mine, swap(mine), residual, routes, route_weight
    )
    outgoing = run_experts(
        slots, exchange(chosen), gains, gate_weight.T, up_weight.T, down_weight
    )
    combined = combine(cores, routes, exchange(outgoing))
    expert_out = (combined + swap(combined)).astype(jnp.bfloat16)
    return (attn_stream, expert_out)


def solution(mesh):
    cols = D // mesh.shape["attn"]
    return jax.shard_map(
        shards if cols % 256 == 0 else shards_plain,
        mesh=mesh,
        in_specs=(
            P(("group", "attn"), "expert"),
            P(("group", "attn"), None, "expert"),
            P(("group", "attn"), None, "expert"),
            P(("group", "attn"), "expert"),
            P(("group", "attn"), "expert"),
            P(("group", "attn")),
            P("group", "attn"),
            P("expert", "attn"),
            P("attn"),
            P(None, ("attn", "expert")),
            P(None, ("attn", "expert")),
            P(("attn", "expert"), None),
            P("group", None),
            P("group", None),
        ),
        out_specs=(P("group", "attn"), P("group", "attn")),
        check_vma=False,
    )
```

```python
import functools
import math

import jax
import jax.numpy as jnp
from jax import lax
from jax.experimental import pallas as pl
from jax.experimental.pallas import tpu as pltpu
from jax.sharding import PartitionSpec as P

D = 6144
HEADS = 48
KV_HEADS = 8
HEAD_DIM = 128
EXPERTS = 16
TOP = 4
HELD = 2


NEG_FILL = -1e30
EPSILON = 1e-05


def attend_local(queries, key_cache, value_cache, new_key, new_value, cache_length):
    row_count = queries.shape[0]
    kv_local = new_key.shape[1] // HEAD_DIM
    group = HEADS // KV_HEADS
    length_max = key_cache.shape[1]
    query_heads = queries.reshape(row_count, kv_local, group, HEAD_DIM)
    key_heads = key_cache.reshape(row_count, length_max, kv_local, HEAD_DIM)
    value_heads = value_cache.reshape(row_count, length_max, kv_local, HEAD_DIM)
    own_keys = new_key.reshape(row_count, kv_local, HEAD_DIM)
    own_values = new_value.reshape(row_count, kv_local, HEAD_DIM)
    scale = 1.0 / math.sqrt(HEAD_DIM)
    past = (
        jnp.einsum("rkgd,rlkd->rkgl", query_heads, key_heads, preferred_element_type=jnp.float32)
        * scale
    )
    valid = jnp.arange(length_max, dtype=jnp.int32)[None, :] < cache_length[:, None]
    past = jnp.where(valid[:, None, None, :], past, NEG_FILL)
    own = (
        jnp.einsum("rkgd,rkd->rkg", query_heads, own_keys, preferred_element_type=jnp.float32)
        * scale
    )
    largest = jnp.maximum(jnp.max(past, axis=3), own)
    past_weight = jnp.exp(past - largest[..., None])
    own_weight = jnp.exp(own - largest)
    total = jnp.sum(past_weight, axis=3) + own_weight
    past_prob = (past_weight / total[..., None]).astype(jnp.bfloat16)
    own_prob = (own_weight / total).astype(jnp.bfloat16)
    result = jnp.einsum(
        "rkgl,rlkd->rkgd", past_prob, value_heads, preferred_element_type=jnp.float32
    )
    result = (
        result
        + own_prob.astype(jnp.float32)[..., None] * own_values.astype(jnp.float32)[:, :, None, :]
    )
    return result.reshape(row_count, kv_local * group * HEAD_DIM).astype(jnp.bfloat16)


def selection(routes, route_weight, capacity):
    row_count = routes.shape[0]
    experts = jnp.arange(HELD, dtype=jnp.int32)
    match = routes[None, :, :] == experts[:, None, None]
    hit = jnp.any(match, axis=2)
    row_weight = jnp.sum(jnp.where(match, route_weight[None], 0.0), axis=2)
    earlier = jnp.arange(row_count)[:, None] < jnp.arange(row_count)[None, :]
    slot = jnp.sum(jnp.where(earlier[None] & hit[:, :, None], 1, 0), axis=1)
    taken = hit[:, None, :] & (slot[:, None, :] == jnp.arange(capacity, dtype=jnp.int32)[None, :, None])
    slot_weight = jnp.sum(jnp.where(taken, row_weight[:, None, :], 0.0), axis=2)
    return taken, slot_weight


def gather_attn(block):
    count = lax.axis_size("attn")
    copies = jnp.broadcast_to(block[None], (count,) + block.shape)
    return lax.all_to_all(copies, "attn", split_axis=0, concat_axis=0, tiled=True)


def pair_sum(block):
    return block + lax.ppermute(block, "expert", [(0, 1), (1, 0)])


def shards_plain(
    queries,
    key_cache,
    value_cache,
    new_key,
    new_value,
    cache_length,
    residual,
    out_weight,
    ln_gain,
    gate_weight,
    up_weight,
    down_weight,
    routes,
    route_weight,
):
    attn_count = lax.axis_size("attn")
    core_count = lax.axis_size("expert")
    sharers = attn_count * core_count // HELD
    my_expert = (lax.axis_index("attn") * core_count + lax.axis_index("expert")) // sharers
    dest_expert = [index * core_count // sharers for index in range(attn_count)]
    row_count = routes.shape[0]
    capacity = row_count * TOP // EXPERTS * 2
    cols = residual.shape[1]

    taken, slot_weight = selection(routes, route_weight, capacity)
    pick = taken.astype(jnp.bfloat16)

    gains = gather_attn(ln_gain)

    attended = attend_local(queries, key_cache, value_cache, new_key, new_value, cache_length)
    whole = gather_attn(attended).reshape(row_count, -1)
    partial_proj = jnp.dot(whole, out_weight, preferred_element_type=jnp.float32)
    head_total = pair_sum(partial_proj)
    attn_stream = (residual.astype(jnp.float32) + head_total).astype(jnp.bfloat16)

    chosen = jnp.einsum(
        "esr,rd->esd", pick, attn_stream, preferred_element_type=jnp.float32
    ).astype(jnp.bfloat16)
    outgoing = jnp.stack([chosen[index] for index in dest_expert])
    rows = lax.all_to_all(outgoing, "attn", split_axis=0, concat_axis=0, tiled=True)
    wide = rows.astype(jnp.float32)
    row_mean = jnp.sum(wide, axis=(0, 2)) / D
    row_var = jnp.sum(wide * wide, axis=(0, 2)) / D - row_mean * row_mean
    normed = (
        (wide - row_mean[None, :, None])
        * lax.rsqrt(row_var + EPSILON)[None, :, None]
        * gains.reshape(attn_count, 1, cols)
    ).astype(jnp.bfloat16)
    gate_val = jnp.einsum(
        "asd,adf->sf", normed, gate_weight.reshape(attn_count, cols, -1),
        preferred_element_type=jnp.float32,
    )
    up_val = jnp.einsum(
        "asd,adf->sf", normed, up_weight.reshape(attn_count, cols, -1),
        preferred_element_type=jnp.float32,
    )
    hidden = (jax.nn.silu(gate_val) * up_val).astype(jnp.bfloat16)
    piece = jnp.dot(hidden, down_weight, preferred_element_type=jnp.float32)
    mine = jnp.take(slot_weight, my_expert, axis=0)
    piece = (piece * mine[:, None]).astype(jnp.bfloat16)
    returned = lax.all_to_all(
        piece.reshape(capacity, attn_count, cols).swapaxes(0, 1),
        "attn", split_axis=0, concat_axis=0, tiled=True,
    )
    spread = jnp.stack([pick[index] for index in dest_expert])
    combined = jnp.einsum(
        "asr,asd->rd", spread, returned, preferred_element_type=jnp.float32
    )
    expert_out = pair_sum(combined).astype(jnp.bfloat16)
    return (attn_stream, expert_out)


MIB = 1024 * 1024
ATTEND_MIB = 58_000_000 / MIB
EXCHANGE_FLOPS = 10**10
VMEM_SPEC = pl.BlockSpec(memory_space=pltpu.VMEM)
SMEM_SPEC = pl.BlockSpec(memory_space=pltpu.SMEM)
HBM_SPEC = pl.BlockSpec(memory_space=pltpu.HBM)


def call(kernel, outs, in_specs, scratch, flops, nbytes, vmem_mib):
    single = not isinstance(outs, (list, tuple))
    return pl.pallas_call(
        kernel,
        out_shape=outs,
        in_specs=in_specs,
        out_specs=VMEM_SPEC if single else [VMEM_SPEC] * len(outs),
        scratch_shapes=scratch,
        cost_estimate=pl.CostEstimate(flops=flops, bytes_accessed=nbytes, transcendentals=0),
        compiler_params=pltpu.CompilerParams(vmem_limit_bytes=int(vmem_mib * MIB)),
    )


def attend_kernel(
    length_ref, query_hbm, key_hbm, value_hbm, own_key_hbm, own_value_hbm, gain_hbm, out_ref,
    query_ref, key_buf, value_buf, own_key_ref, own_value_ref, gain_ref,
    query_rows, key_rows, value_rows, result_rows, key_sem, value_sem, small_sem,
):
    row_count, length_max = key_hbm.shape[0], key_hbm.shape[1]
    kv_local = own_key_ref.shape[1] // HEAD_DIM
    group = HEADS // KV_HEADS
    block = group * row_count
    key_copies = [
        pltpu.make_async_copy(key_hbm.at[r], key_buf.at[r], key_sem.at[r]) for r in range(row_count)
    ]
    value_copies = [
        pltpu.make_async_copy(value_hbm.at[r], value_buf.at[r], value_sem.at[r])
        for r in range(row_count)
    ]
    small_copies = [
        pltpu.make_async_copy(source, target, small_sem.at[index])
        for index, (source, target) in enumerate(
            (
                (query_hbm, query_ref),
                (own_key_hbm, own_key_ref),
                (own_value_hbm, own_value_ref),
                (gain_hbm, gain_ref),
            )
        )
    ]
    for copy in small_copies + key_copies + value_copies:
        copy.start()
    for copy in small_copies:
        copy.wait()
    for g in range(kv_local):
        lanes = slice(g * HEAD_DIM, (g + 1) * HEAD_DIM)
        own_key = own_key_ref[:, lanes].astype(jnp.float32)
        own_value = own_value_ref[:, lanes].astype(jnp.float32)
        for i in range(group):
            head = g * group + i
            rows = pl.ds(g * block + i * row_count, row_count)
            query_rows[rows, :] = query_ref[
                :, head * HEAD_DIM : (head + 1) * HEAD_DIM
            ].astype(jnp.float32)
            key_rows[rows, :] = own_key
            value_rows[rows, :] = own_value
    scale = 1.0 / math.sqrt(HEAD_DIM)
    pair_rows = 2 * block
    request = lax.broadcasted_iota(jnp.int32, (pair_rows, 1), 0) % row_count
    lengths = jnp.zeros((pair_rows, 1), jnp.int32)
    for r in range(row_count):
        lengths = jnp.where(request == r, length_ref[r], lengths)
    position = lax.broadcasted_iota(jnp.int32, (pair_rows, length_max), 1)
    valid = position < lengths
    pairs = kv_local // 2
    past = [jnp.zeros((pair_rows, length_max), jnp.float32) for _ in range(pairs)]
    packed = []
    for p in range(pairs):
        rows = query_rows[pl.ds(p * pair_rows, pair_rows), :]
        lower = rows[:block].astype(jnp.bfloat16)
        upper = rows[block:].astype(jnp.bfloat16)
        zero = jnp.zeros_like(lower)
        packed.append(
            jnp.concatenate(
                [
                    jnp.concatenate([lower, zero], axis=1),
                    jnp.concatenate([zero, upper], axis=1),
                ],
                axis=0,
            )
        )
    for r in range(row_count):
        key_copies[r].wait()
        for p in range(pairs):
            keys = key_buf[r, :, p * 2 * HEAD_DIM : (p + 1) * 2 * HEAD_DIM]
            scores = lax.dot_general(
                packed[p], keys, (((1,), (1,)), ((), ())), preferred_element_type=jnp.float32
            )
            past[p] = jnp.where(request == r, scores, past[p])
    probs, own_probs = [], []
    for p in range(pairs):
        rows = pl.ds(p * pair_rows, pair_rows)
        scores = jnp.where(valid, past[p] * scale, NEG_FILL)
        own = jnp.sum(query_rows[rows, :] * key_rows[rows, :], axis=1, keepdims=True) * scale
        largest = jnp.maximum(jnp.max(scores, axis=1, keepdims=True), own)
        weight = jnp.exp(scores - largest)
        own_weight = jnp.exp(own - largest)
        total = jnp.sum(weight, axis=1, keepdims=True) + own_weight
        probs.append((weight / total).astype(jnp.bfloat16))
        own_probs.append((own_weight / total).astype(jnp.bfloat16).astype(jnp.float32))
    sums = [jnp.zeros((pair_rows, 2 * HEAD_DIM), jnp.float32) for _ in range(pairs)]
    for r in range(row_count):
        value_copies[r].wait()
        for p in range(pairs):
            values = value_buf[r, :, p * 2 * HEAD_DIM : (p + 1) * 2 * HEAD_DIM]
            product = jnp.dot(probs[p], values, preferred_element_type=jnp.float32)
            sums[p] = jnp.where(request == r, product, sums[p])
    for p in range(pairs):
        rows = pl.ds(p * pair_rows, pair_rows)
        own_part = own_probs[p] * value_rows[rows, :]
        lower = sums[p][:block, :HEAD_DIM] + own_part[:block]
        upper = sums[p][block:, HEAD_DIM:] + own_part[block:]
        result_rows[pl.ds(p * pair_rows, block), :] = lower
        result_rows[pl.ds(p * pair_rows + block, block), :] = upper
    width = query_hbm.shape[1]
    for head in range(kv_local * group):
        rows = result_rows[pl.ds(head * row_count, row_count), :].astype(jnp.bfloat16)
        for index in range(out_ref.shape[0]):
            out_ref[index, :, head * HEAD_DIM : (head + 1) * HEAD_DIM] = rows
    gain_row = gain_ref[...].reshape(1, -1)
    half = gain_row.shape[1] // 2
    row = lax.broadcasted_iota(jnp.int32, (row_count, half), 0)
    left = jnp.broadcast_to(gain_row[:, :half], (row_count, half))
    right = jnp.broadcast_to(gain_row[:, half:], (row_count, half))
    gain = jnp.where(row % 2 == 0, left, right)
    upper = gain.astype(jnp.bfloat16).astype(jnp.float32)
    parts = jnp.where(row < 2, upper, gain - upper).astype(jnp.bfloat16)
    for index in range(out_ref.shape[0]):
        out_ref[index, :, width:] = parts


def attend(count, queries, key_cache, value_cache, new_key, new_value, cache_length, gain):
    row_count, width = queries.shape
    heads = width // HEAD_DIM
    table = pltpu.VMEM((heads * row_count, HEAD_DIM), jnp.float32)
    nbytes = 2 * key_cache.size * 2
    return call(
        attend_kernel,
        jax.ShapeDtypeStruct((count, row_count, width + gain.shape[0] // 2), jnp.bfloat16),
        [SMEM_SPEC] + [HBM_SPEC] * 6,
        [
            pltpu.VMEM(queries.shape, jnp.bfloat16),
            pltpu.VMEM(key_cache.shape, jnp.bfloat16),
            pltpu.VMEM(value_cache.shape, jnp.bfloat16),
            pltpu.VMEM(new_key.shape, jnp.bfloat16),
            pltpu.VMEM(new_value.shape, jnp.bfloat16),
            pltpu.VMEM(gain.shape, jnp.float32),
            table, table, table, table,
            pltpu.SemaphoreType.DMA((row_count,)),
            pltpu.SemaphoreType.DMA((row_count,)),
            pltpu.SemaphoreType.DMA((4,)),
        ],
        4 * key_cache.size * 6, nbytes, ATTEND_MIB,
    )(cache_length, queries, key_cache, value_cache, new_key, new_value, gain)


def project_kernel(pieces, weight_ref, out_ref, gain_ref, stack):
    count, rows, _ = pieces.shape
    width = weight_ref.shape[0]
    half = gain_ref.shape[1] // 2
    for k in range(count):
        stack[pl.ds(k * rows, rows), :] = pieces[k, :, :width].astype(jnp.float32)
        parts = pieces[k, :, width:].astype(jnp.float32)
        gain_ref[pl.ds(k, 1), :half] = parts[0:1] + parts[2:3]
        gain_ref[pl.ds(k, 1), half:] = parts[1:2] + parts[3:4]
    out_ref[...] = jnp.dot(
        stack[...].astype(jnp.bfloat16), weight_ref[...], preferred_element_type=jnp.float32
    )


def project(pieces, out_weight):
    count, rows, _ = pieces.shape
    depth, cols = out_weight.shape
    return call(
        project_kernel,
        [
            jax.ShapeDtypeStruct((rows * count, cols), jnp.float32),
            jax.ShapeDtypeStruct((count, cols), jnp.float32),
        ],
        [VMEM_SPEC, VMEM_SPEC],
        [pltpu.VMEM((rows * count, depth), jnp.float32)],
        2 * rows * count * out_weight.size, out_weight.size * 2, 10,
    )(pieces, out_weight)


def expert_rows(routes, expert, capacity):
    row_count = routes.shape[1]
    hit = jnp.max((routes == expert).astype(jnp.float32), axis=0, keepdims=True)
    earlier = lax.broadcasted_iota(jnp.int32, (row_count, row_count), 0) < lax.broadcasted_iota(
        jnp.int32, (row_count, row_count), 1
    )
    slot = jnp.dot(
        jnp.broadcast_to(hit, (8, row_count)).astype(jnp.bfloat16),
        earlier.astype(jnp.bfloat16),
        preferred_element_type=jnp.float32,
    )[:1]
    place = lax.broadcasted_iota(jnp.int32, (capacity, row_count), 0).astype(jnp.float32)
    return jnp.where((slot == place) & (hit > 0.5), 1.0, 0.0)


def own_half(core, left, right):
    return jnp.where(core == 0, left, right)


def pick_kernel(cores, place_ref, mine_ref, other_ref, residual_ref, routes_ref, weight_ref,
                stream_ref, out_ref, slot_ref):
    count, capacity, half = out_ref.shape
    stream = (
        residual_ref[...].astype(jnp.float32) + (mine_ref[...] + other_ref[...])
    ).astype(jnp.bfloat16)
    stream_ref[...] = stream
    routes = routes_ref[...]
    sharers = count * cores // HELD
    taken = [expert_rows(routes, e, capacity) for e in range(HELD)]
    chosen = [
        jnp.dot(
            taken[e].astype(jnp.bfloat16), stream, preferred_element_type=jnp.float32
        ).astype(jnp.bfloat16)
        for e in range(HELD)
    ]
    core = place_ref[1]
    chosen = [own_half(core, rows[:, :half], rows[:, half:]) for rows in chosen]
    for k in range(count):
        out_ref[k] = chosen[k * cores // sharers]
    first = place_ref[0] * cores < sharers
    expert = jnp.where(first, 0, 1)
    row_weight = jnp.sum(
        jnp.where(routes == expert, weight_ref[...], 0.0), axis=0, keepdims=True
    )
    mine = jnp.where(first, taken[0], taken[1])
    slot_ref[...] = jnp.broadcast_to(
        jnp.sum(mine * row_weight, axis=1, keepdims=True), slot_ref.shape
    )


def pick(place, cores, count, capacity, mine, other, residual, routes, route_weight):
    rows, cols = mine.shape
    return call(
        functools.partial(pick_kernel, cores),
        [
            jax.ShapeDtypeStruct((rows, cols), jnp.bfloat16),
            jax.ShapeDtypeStruct((count, capacity, cols // 2), jnp.bfloat16),
            jax.ShapeDtypeStruct((capacity, 128), jnp.float32),
        ],
        [SMEM_SPEC] + [VMEM_SPEC] * 5,
        [],
        EXCHANGE_FLOPS, rows * cols * 12, 4,
    )(place, mine, other, residual, routes, route_weight)


def expert_kernel(place_ref, slot_ref, mine_ref, other_ref, gains, gate_ref, up_ref, down_ref,
                  keep_ref, give_ref):
    count, capacity, half = mine_ref.shape
    core = place_ref[1]
    blocks = []
    for k in range(count):
        mine, other = mine_ref[k], other_ref[k]
        blocks.append(own_half(core, mine, other).astype(jnp.float32))
        blocks.append(own_half(core, other, mine).astype(jnp.float32))
    first = second = 0.0
    for wide in blocks:
        first = first + wide
        second = second + wide * wide
    row_mean = jnp.sum(first, axis=1, keepdims=True) / D
    row_var = jnp.sum(second, axis=1, keepdims=True) / D - row_mean * row_mean
    inverse = lax.rsqrt(row_var + EPSILON)
    contract = (((1,), (1,)), ((), ()))
    gate_val = up_val = 0.0
    for k in range(count):
        columns = slice(2 * k * half, 2 * (k + 1) * half)
        wide = jnp.concatenate(blocks[2 * k : 2 * k + 2], axis=1)
        normed = ((wide - row_mean) * inverse * gains[pl.ds(k, 1), :]).astype(jnp.bfloat16)
        gate_val = gate_val + lax.dot_general(
            gate_ref[:, columns], normed, contract, preferred_element_type=jnp.float32
        )
        up_val = up_val + lax.dot_general(
            up_ref[:, columns], normed, contract, preferred_element_type=jnp.float32
        )
    hidden = (gate_val / (1.0 + jnp.exp(-gate_val)) * up_val).T.astype(jnp.bfloat16)
    slot_weight = slot_ref[:, :1]
    for k in range(count):
        columns = slice(2 * k * half, 2 * (k + 1) * half)
        piece = (
            jnp.dot(hidden, down_ref[:, columns], preferred_element_type=jnp.float32)
            * slot_weight
        ).astype(jnp.bfloat16)
        keep_ref[k] = own_half(core, piece[:, :half], piece[:, half:])
        give_ref[k] = own_half(core, piece[:, half:], piece[:, :half])


def run_experts(place, slots, mine, other, gains, gate, up, down):
    return call(
        expert_kernel,
        [jax.ShapeDtypeStruct(mine.shape, jnp.bfloat16)] * 2,
        [SMEM_SPEC] + [VMEM_SPEC] * 7,
        [],
        6 * mine.shape[1] * gate.size, gate.size * 6, 14,
    )(place, slots, mine, other, gains, gate, up, down)


def add_kernel(keep_ref, given_ref, out_ref):
    out_ref[...] = (
        keep_ref[...].astype(jnp.float32) + given_ref[...].astype(jnp.float32)
    ).astype(jnp.bfloat16)


def add(keep, given):
    return call(
        add_kernel,
        jax.ShapeDtypeStruct(keep.shape, jnp.bfloat16),
        [VMEM_SPEC] * 2,
        [],
        keep.size, keep.size * 6, 4,
    )(keep, given)


def combine_kernel(cores, routes_ref, pieces, out_ref):
    count, capacity, half = pieces.shape
    sharers = count * cores // HELD
    routes = routes_ref[...]
    taken = [expert_rows(routes, e, capacity) for e in range(HELD)]
    spread = [taken[k * cores // sharers] for k in range(count)]
    out_ref[...] = lax.dot_general(
        jnp.concatenate(spread, axis=0).astype(jnp.bfloat16),
        pieces[...].reshape(count * capacity, half),
        (((0,), (0,)), ((), ())),
        preferred_element_type=jnp.float32,
    ).astype(jnp.bfloat16)


def combine(cores, routes, pieces):
    count, capacity, half = pieces.shape
    rows = routes.shape[1]
    return call(
        functools.partial(combine_kernel, cores),
        jax.ShapeDtypeStruct((rows, half), jnp.bfloat16),
        [VMEM_SPEC] * 2,
        [],
        2 * rows * capacity * count * half, (count * capacity + rows) * 2 * half, 4,
    )(routes, pieces)


def join_kernel(place_ref, mine_ref, other_ref, out_ref):
    half = mine_ref.shape[1]
    core = place_ref[1]
    mine, other = mine_ref[...], other_ref[...]
    out_ref[:, :half] = own_half(core, mine, other)
    out_ref[:, half:] = own_half(core, other, mine)


def join(place, mine, other):
    rows, half = mine.shape
    return call(
        join_kernel,
        jax.ShapeDtypeStruct((rows, 2 * half), jnp.bfloat16),
        [SMEM_SPEC] + [VMEM_SPEC] * 2,
        [],
        rows * half, rows * half * 8, 4,
    )(place, mine, other)


def exchange(blocks):
    return lax.all_to_all(blocks, "attn", split_axis=0, concat_axis=0, tiled=True)


def swap(block):
    return lax.ppermute(block, "expert", [(0, 1), (1, 0)])


def shards(
    queries,
    key_cache,
    value_cache,
    new_key,
    new_value,
    cache_length,
    residual,
    out_weight,
    ln_gain,
    gate_weight,
    up_weight,
    down_weight,
    routes,
    route_weight,
):
    count = lax.axis_size("attn")
    cores = lax.axis_size("expert")
    capacity = routes.shape[0] * TOP // EXPERTS * 2
    place = jnp.stack([lax.axis_index("attn"), lax.axis_index("expert")]).astype(jnp.int32)
    routes = routes.T
    route_weight = route_weight.T

    attended = exchange(
        attend(
            count, queries, key_cache, value_cache, new_key, new_value, cache_length,
            ln_gain,
        )
    )
    mine, gains = project(attended, out_weight)
    attn_stream, chosen, slots = pick(
        place, cores, count, capacity, mine, swap(mine), residual, routes, route_weight
    )
    arrived = exchange(chosen)
    keep, give = run_experts(
        place, slots, arrived, swap(arrived), gains, gate_weight.T, up_weight.T, down_weight
    )
    combined = combine(cores, routes, exchange(add(keep, swap(give))))
    expert_out = join(place, combined, swap(combined))
    return (attn_stream, expert_out)


def solution(mesh):
    cols = D // mesh.shape["attn"]
    return jax.shard_map(
        shards if cols % 256 == 0 else shards_plain,
        mesh=mesh,
        in_specs=(
            P(("group", "attn"), "expert"),
            P(("group", "attn"), None, "expert"),
            P(("group", "attn"), None, "expert"),
            P(("group", "attn"), "expert"),
            P(("group", "attn"), "expert"),
            P(("group", "attn")),
            P("group", "attn"),
            P("expert", "attn"),
            P("attn"),
            P(None, ("attn", "expert")),
            P(None, ("attn", "expert")),
            P(("attn", "expert"), None),
            P("group", None),
            P("group", None),
        ),
        out_specs=(P("group", "attn"), P("group", "attn")),
        check_vma=False,
    )
```

```python
import functools
import math

import jax
import jax.numpy as jnp
from jax import lax
from jax.experimental import pallas as pl
from jax.experimental.pallas import tpu as pltpu
from jax.sharding import PartitionSpec as P

D = 6144
HEADS = 48
KV_HEADS = 8
HEAD_DIM = 128
EXPERTS = 16
TOP = 4
HELD = 2


NEG_FILL = -1e30
EPSILON = 1e-05


def attend_local(queries, key_cache, value_cache, new_key, new_value, cache_length):
    row_count = queries.shape[0]
    kv_local = new_key.shape[1] // HEAD_DIM
    group = HEADS // KV_HEADS
    length_max = key_cache.shape[1]
    query_heads = queries.reshape(row_count, kv_local, group, HEAD_DIM)
    key_heads = key_cache.reshape(row_count, length_max, kv_local, HEAD_DIM)
    value_heads = value_cache.reshape(row_count, length_max, kv_local, HEAD_DIM)
    own_keys = new_key.reshape(row_count, kv_local, HEAD_DIM)
    own_values = new_value.reshape(row_count, kv_local, HEAD_DIM)
    scale = 1.0 / math.sqrt(HEAD_DIM)
    past = (
        jnp.einsum("rkgd,rlkd->rkgl", query_heads, key_heads, preferred_element_type=jnp.float32)
        * scale
    )
    valid = jnp.arange(length_max, dtype=jnp.int32)[None, :] < cache_length[:, None]
    past = jnp.where(valid[:, None, None, :], past, NEG_FILL)
    own = (
        jnp.einsum("rkgd,rkd->rkg", query_heads, own_keys, preferred_element_type=jnp.float32)
        * scale
    )
    largest = jnp.maximum(jnp.max(past, axis=3), own)
    past_weight = jnp.exp(past - largest[..., None])
    own_weight = jnp.exp(own - largest)
    total = jnp.sum(past_weight, axis=3) + own_weight
    past_prob = (past_weight / total[..., None]).astype(jnp.bfloat16)
    own_prob = (own_weight / total).astype(jnp.bfloat16)
    result = jnp.einsum(
        "rkgl,rlkd->rkgd", past_prob, value_heads, preferred_element_type=jnp.float32
    )
    result = (
        result
        + own_prob.astype(jnp.float32)[..., None] * own_values.astype(jnp.float32)[:, :, None, :]
    )
    return result.reshape(row_count, kv_local * group * HEAD_DIM).astype(jnp.bfloat16)


def selection(routes, route_weight, capacity):
    row_count = routes.shape[0]
    experts = jnp.arange(HELD, dtype=jnp.int32)
    match = routes[None, :, :] == experts[:, None, None]
    hit = jnp.any(match, axis=2)
    row_weight = jnp.sum(jnp.where(match, route_weight[None], 0.0), axis=2)
    earlier = jnp.arange(row_count)[:, None] < jnp.arange(row_count)[None, :]
    slot = jnp.sum(jnp.where(earlier[None] & hit[:, :, None], 1, 0), axis=1)
    taken = hit[:, None, :] & (slot[:, None, :] == jnp.arange(capacity, dtype=jnp.int32)[None, :, None])
    slot_weight = jnp.sum(jnp.where(taken, row_weight[:, None, :], 0.0), axis=2)
    return taken, slot_weight


def gather_attn(block):
    count = lax.axis_size("attn")
    copies = jnp.broadcast_to(block[None], (count,) + block.shape)
    return lax.all_to_all(copies, "attn", split_axis=0, concat_axis=0, tiled=True)


def pair_sum(block):
    return block + lax.ppermute(block, "expert", [(0, 1), (1, 0)])


def shards_plain(
    queries,
    key_cache,
    value_cache,
    new_key,
    new_value,
    cache_length,
    residual,
    out_weight,
    ln_gain,
    gate_weight,
    up_weight,
    down_weight,
    routes,
    route_weight,
):
    attn_count = lax.axis_size("attn")
    core_count = lax.axis_size("expert")
    sharers = attn_count * core_count // HELD
    my_expert = (lax.axis_index("attn") * core_count + lax.axis_index("expert")) // sharers
    dest_expert = [index * core_count // sharers for index in range(attn_count)]
    row_count = routes.shape[0]
    capacity = row_count * TOP // EXPERTS * 2
    cols = residual.shape[1]

    taken, slot_weight = selection(routes, route_weight, capacity)
    pick = taken.astype(jnp.bfloat16)

    gains = gather_attn(ln_gain)

    attended = attend_local(queries, key_cache, value_cache, new_key, new_value, cache_length)
    whole = gather_attn(attended).reshape(row_count, -1)
    partial_proj = jnp.dot(whole, out_weight, preferred_element_type=jnp.float32)
    head_total = pair_sum(partial_proj)
    attn_stream = (residual.astype(jnp.float32) + head_total).astype(jnp.bfloat16)

    chosen = jnp.einsum(
        "esr,rd->esd", pick, attn_stream, preferred_element_type=jnp.float32
    ).astype(jnp.bfloat16)
    outgoing = jnp.stack([chosen[index] for index in dest_expert])
    rows = lax.all_to_all(outgoing, "attn", split_axis=0, concat_axis=0, tiled=True)
    wide = rows.astype(jnp.float32)
    row_mean = jnp.sum(wide, axis=(0, 2)) / D
    row_var = jnp.sum(wide * wide, axis=(0, 2)) / D - row_mean * row_mean
    normed = (
        (wide - row_mean[None, :, None])
        * lax.rsqrt(row_var + EPSILON)[None, :, None]
        * gains.reshape(attn_count, 1, cols)
    ).astype(jnp.bfloat16)
    gate_val = jnp.einsum(
        "asd,adf->sf", normed, gate_weight.reshape(attn_count, cols, -1),
        preferred_element_type=jnp.float32,
    )
    up_val = jnp.einsum(
        "asd,adf->sf", normed, up_weight.reshape(attn_count, cols, -1),
        preferred_element_type=jnp.float32,
    )
    hidden = (jax.nn.silu(gate_val) * up_val).astype(jnp.bfloat16)
    piece = jnp.dot(hidden, down_weight, preferred_element_type=jnp.float32)
    mine = jnp.take(slot_weight, my_expert, axis=0)
    piece = (piece * mine[:, None]).astype(jnp.bfloat16)
    returned = lax.all_to_all(
        piece.reshape(capacity, attn_count, cols).swapaxes(0, 1),
        "attn", split_axis=0, concat_axis=0, tiled=True,
    )
    spread = jnp.stack([pick[index] for index in dest_expert])
    combined = jnp.einsum(
        "asr,asd->rd", spread, returned, preferred_element_type=jnp.float32
    )
    expert_out = pair_sum(combined).astype(jnp.bfloat16)
    return (attn_stream, expert_out)


MIB = 1024 * 1024
ATTEND_MIB = 58_000_000 / MIB
EXCHANGE_FLOPS = 10**10
VMEM_SPEC = pl.BlockSpec(memory_space=pltpu.VMEM)
SMEM_SPEC = pl.BlockSpec(memory_space=pltpu.SMEM)
HBM_SPEC = pl.BlockSpec(memory_space=pltpu.HBM)


def call(kernel, outs, in_specs, scratch, flops, nbytes, vmem_mib):
    single = not isinstance(outs, (list, tuple))
    return pl.pallas_call(
        kernel,
        out_shape=outs,
        in_specs=in_specs,
        out_specs=VMEM_SPEC if single else [VMEM_SPEC] * len(outs),
        scratch_shapes=scratch,
        cost_estimate=pl.CostEstimate(flops=flops, bytes_accessed=nbytes, transcendentals=0),
        compiler_params=pltpu.CompilerParams(vmem_limit_bytes=int(vmem_mib * MIB)),
    )


def attend_kernel(
    length_ref, query_hbm, key_hbm, value_hbm, own_key_hbm, own_value_hbm, gain_hbm, out_ref,
    query_ref, key_buf, value_buf, own_key_ref, own_value_ref, gain_ref,
    query_table, own_table, value_rows, result_rows, key_sem, value_sem, small_sem,
):
    row_count, length_max = key_hbm.shape[0], key_hbm.shape[1]
    kv_local = own_key_hbm.shape[1] // HEAD_DIM
    group = HEADS // KV_HEADS
    block = group * row_count
    total_rows = kv_local * block
    small_copies = [
        pltpu.make_async_copy(source, target, small_sem.at[index])
        for index, (source, target) in enumerate(
            (
                (query_hbm, query_ref),
                (own_key_hbm, own_key_ref),
                (own_value_hbm, own_value_ref),
                (gain_hbm, gain_ref),
            )
        )
    ]
    key_copies = [
        pltpu.make_async_copy(key_hbm.at[r], key_buf.at[r], key_sem.at[r]) for r in range(row_count)
    ]
    value_copies = [
        pltpu.make_async_copy(value_hbm.at[r], value_buf.at[r], value_sem.at[r])
        for r in range(row_count)
    ]
    for copy in small_copies + key_copies + value_copies:
        copy.start()
    query_table[...] = jnp.zeros_like(query_table)
    own_table[...] = jnp.zeros_like(own_table)
    lane = lax.broadcasted_iota(jnp.int32, (1, total_rows), 1) % row_count
    lengths = jnp.zeros((1, total_rows), jnp.int32)
    for r in range(row_count):
        lengths = jnp.where(lane == r, length_ref[r], lengths)
    position = lax.broadcasted_iota(jnp.int32, (length_max, total_rows), 0)
    for copy in small_copies:
        copy.wait()
    own_table[pl.ds(0, row_count), :] = own_key_ref[...].astype(jnp.float32)
    for g in range(kv_local):
        lanes = slice(g * HEAD_DIM, (g + 1) * HEAD_DIM)
        own_value = own_value_ref[:, lanes].astype(jnp.float32)
        for i in range(group):
            head = g * group + i
            rows = pl.ds(g * block + i * row_count, row_count)
            query_table[rows, lanes] = query_ref[
                :, head * HEAD_DIM : (head + 1) * HEAD_DIM
            ].astype(jnp.float32)
            value_rows[rows, :] = own_value
    queries = query_table[...].astype(jnp.bfloat16)
    contract = (((1,), (1,)), ((), ()))
    scale = 1.0 / math.sqrt(HEAD_DIM)
    own_scores = lax.dot_general(
        own_table[...].astype(jnp.bfloat16), queries, contract, preferred_element_type=jnp.float32
    )
    own_row = lax.broadcasted_iota(jnp.int32, own_scores.shape, 0)
    own = jnp.sum(jnp.where(own_row == lane, own_scores, 0.0), axis=0, keepdims=True) * scale
    past = None
    for r in range(row_count):
        key_copies[r].wait()
        scores = lax.dot_general(
            key_buf[r], queries, contract, preferred_element_type=jnp.float32
        )
        past = scores if past is None else jnp.where(lane == r, scores, past)
    past = jnp.where(position < lengths, past * scale, NEG_FILL)
    largest = jnp.maximum(jnp.max(past, axis=0, keepdims=True), own)
    weight = jnp.exp(past - largest)
    own_weight = jnp.exp(own - largest)
    inverse = 1.0 / (jnp.sum(weight, axis=0, keepdims=True) + own_weight)
    probs = (weight * inverse).T.astype(jnp.bfloat16)
    own_prob = (own_weight * inverse).astype(jnp.bfloat16).astype(jnp.float32)
    own_prob = jnp.broadcast_to(own_prob, (8, total_rows)).T[:, :1]
    own_part = own_prob * value_rows[...]
    request = lax.broadcasted_iota(jnp.int32, (block, 1), 0) % row_count
    sums = [own_part[g * block : (g + 1) * block] for g in range(kv_local)]
    for r in range(row_count):
        value_copies[r].wait()
        for g in range(0, kv_local, 2):
            product = jnp.dot(
                probs[g * block : (g + 2) * block],
                value_buf[r, :, g * HEAD_DIM : (g + 2) * HEAD_DIM],
                preferred_element_type=jnp.float32,
            )
            sums[g] = sums[g] + jnp.where(request == r, product[:block, :HEAD_DIM], 0.0)
            sums[g + 1] = sums[g + 1] + jnp.where(request == r, product[block:, HEAD_DIM:], 0.0)
    for g in range(kv_local):
        result_rows[pl.ds(g * block, block), :] = sums[g]
    width = query_hbm.shape[1]
    for head in range(kv_local * group):
        out_ref[:, head * HEAD_DIM : (head + 1) * HEAD_DIM] = result_rows[
            pl.ds(head * row_count, row_count), :
        ].astype(jnp.bfloat16)
    gain_row = gain_ref[...].reshape(1, -1)
    half = gain_row.shape[1] // 2
    row = lax.broadcasted_iota(jnp.int32, (row_count, half), 0)
    left = jnp.broadcast_to(gain_row[:, :half], (row_count, half))
    right = jnp.broadcast_to(gain_row[:, half:], (row_count, half))
    gain = jnp.where(row % 2 == 0, left, right)
    upper = gain.astype(jnp.bfloat16).astype(jnp.float32)
    out_ref[:, width:] = jnp.where(row < 2, upper, gain - upper).astype(jnp.bfloat16)


def attend(queries, key_cache, value_cache, new_key, new_value, cache_length, gain):
    row_count, width = queries.shape
    total_rows = width // HEAD_DIM * row_count
    table = pltpu.VMEM((total_rows, HEAD_DIM), jnp.float32)
    nbytes = 2 * key_cache.size * 2
    return call(
        attend_kernel,
        jax.ShapeDtypeStruct((row_count, width + gain.shape[0] // 2), jnp.bfloat16),
        [SMEM_SPEC] + [HBM_SPEC] * 6,
        [
            pltpu.VMEM(queries.shape, jnp.bfloat16),
            pltpu.VMEM(key_cache.shape, jnp.bfloat16),
            pltpu.VMEM(value_cache.shape, jnp.bfloat16),
            pltpu.VMEM(new_key.shape, jnp.bfloat16),
            pltpu.VMEM(new_value.shape, jnp.bfloat16),
            pltpu.VMEM(gain.shape, jnp.float32),
            pltpu.VMEM((total_rows, new_key.shape[1]), jnp.float32),
            pltpu.VMEM((8, new_key.shape[1]), jnp.float32),
            table, table,
            pltpu.SemaphoreType.DMA((row_count,)),
            pltpu.SemaphoreType.DMA((row_count,)),
            pltpu.SemaphoreType.DMA((4,)),
        ],
        4 * key_cache.size * 6, nbytes, ATTEND_MIB,
    )(cache_length, queries, key_cache, value_cache, new_key, new_value, gain)


def pair_kernel(place_ref, mine_ref, other_ref, out_ref):
    low = lax.rem(place_ref[0], 2)
    out_ref[low] = mine_ref[...]
    out_ref[1 - low] = other_ref[...]


def pair_up(place, mine, other):
    return call(
        pair_kernel,
        jax.ShapeDtypeStruct((2,) + mine.shape, mine.dtype),
        [SMEM_SPEC] + [VMEM_SPEC] * 2,
        [],
        EXCHANGE_FLOPS, mine.size * 8, 4,
    )(place, mine, other)


def project_kernel(place_ref, *refs):
    quarters, (weight_ref, out_ref, gain_ref, stack) = refs[:-4], refs[-4:]
    _, rows, _ = quarters[0].shape
    width = weight_ref.shape[0]
    half = gain_ref.shape[2] // 2
    high = place_ref[0] // 2
    for k, quarter in enumerate(quarters):
        source = high ^ k
        both = jnp.concatenate(
            [quarter[0, :, :width].astype(jnp.float32), quarter[1, :, :width].astype(jnp.float32)],
            axis=0,
        )
        stack[pl.ds(pl.multiple_of(source * 2 * rows, 2 * rows), 2 * rows), :] = both
        for low in range(2):
            parts = quarter[low, :, width:].astype(jnp.float32)
            gain_ref[source * 2 + low, :, :half] = parts[0:1] + parts[2:3]
            gain_ref[source * 2 + low, :, half:] = parts[1:2] + parts[3:4]
    out_ref[...] = jnp.dot(
        stack[...].astype(jnp.bfloat16), weight_ref[...], preferred_element_type=jnp.float32
    )


def project(place, quarters, out_weight):
    _, rows, _ = quarters[0].shape
    count = 2 * len(quarters)
    depth, cols = out_weight.shape
    return call(
        project_kernel,
        [
            jax.ShapeDtypeStruct((rows * count, cols), jnp.float32),
            jax.ShapeDtypeStruct((count, 1, cols), jnp.float32),
        ],
        [SMEM_SPEC] + [VMEM_SPEC] * (len(quarters) + 1),
        [pltpu.VMEM((rows * count, depth), jnp.float32)],
        2 * rows * count * out_weight.size, out_weight.size * 2, 10,
    )(place, *quarters, out_weight)


def expert_rows(routes, expert, capacity):
    row_count = routes.shape[1]
    hit = jnp.max((routes == expert).astype(jnp.float32), axis=0, keepdims=True)
    earlier = lax.broadcasted_iota(jnp.int32, (row_count, row_count), 0) < lax.broadcasted_iota(
        jnp.int32, (row_count, row_count), 1
    )
    slot = jnp.dot(
        jnp.broadcast_to(hit, (8, row_count)).astype(jnp.bfloat16),
        earlier.astype(jnp.bfloat16),
        preferred_element_type=jnp.float32,
    )[:1]
    place = lax.broadcasted_iota(jnp.int32, (capacity, row_count), 0).astype(jnp.float32)
    return jnp.where((slot == place) & (hit > 0.5), 1.0, 0.0)


def pick_kernel(cores, place_ref, mine_ref, other_ref, residual_ref, routes_ref, weight_ref,
                stream_ref, out_ref, slot_ref):
    count, capacity, _ = out_ref.shape
    stream = (
        residual_ref[...].astype(jnp.float32) + (mine_ref[...] + other_ref[...])
    ).astype(jnp.bfloat16)
    stream_ref[...] = stream
    routes = routes_ref[...]
    sharers = count * cores // HELD
    taken = [expert_rows(routes, e, capacity) for e in range(HELD)]
    chosen = [
        jnp.dot(
            taken[e].astype(jnp.bfloat16), stream, preferred_element_type=jnp.float32
        ).astype(jnp.bfloat16)
        for e in range(HELD)
    ]
    for k in range(count):
        out_ref[k] = chosen[k * cores // sharers]
    first = place_ref[0] * cores < sharers
    expert = jnp.where(first, 0, 1)
    row_weight = jnp.sum(
        jnp.where(routes == expert, weight_ref[...], 0.0), axis=0, keepdims=True
    )
    mine = jnp.where(first, taken[0], taken[1])
    slot_ref[...] = jnp.broadcast_to(
        jnp.sum(mine * row_weight, axis=1, keepdims=True), slot_ref.shape
    )


def pick(place, cores, count, capacity, mine, other, residual, routes, route_weight):
    rows, cols = mine.shape
    return call(
        functools.partial(pick_kernel, cores),
        [
            jax.ShapeDtypeStruct((rows, cols), jnp.bfloat16),
            jax.ShapeDtypeStruct((count, capacity, cols), jnp.bfloat16),
            jax.ShapeDtypeStruct((capacity, 128), jnp.float32),
        ],
        [SMEM_SPEC] + [VMEM_SPEC] * 5,
        [],
        EXCHANGE_FLOPS, rows * cols * 12, 4,
    )(place, mine, other, residual, routes, route_weight)


def expert_kernel(place_ref, slot_ref, pieces, gains, gate_ref, up_ref, down_ref, keep_ref,
                  give_ref):
    count, capacity, cols = pieces.shape
    first = second = 0.0
    for k in range(count):
        wide = pieces[k].astype(jnp.float32)
        first = first + wide
        second = second + wide * wide
    row_mean = jnp.sum(first, axis=1, keepdims=True) / D
    row_var = jnp.sum(second, axis=1, keepdims=True) / D - row_mean * row_mean
    inverse = lax.rsqrt(row_var + EPSILON)
    contract = (((1,), (1,)), ((), ()))
    gate_val = up_val = 0.0
    for k in range(count):
        block = slice(k * cols, (k + 1) * cols)
        wide = pieces[k].astype(jnp.float32)
        normed = ((wide - row_mean) * inverse * gains[k]).astype(jnp.bfloat16)
        gate_val = gate_val + lax.dot_general(
            gate_ref[:, block], normed, contract, preferred_element_type=jnp.float32
        )
        up_val = up_val + lax.dot_general(
            up_ref[:, block], normed, contract, preferred_element_type=jnp.float32
        )
    hidden = (gate_val / (1.0 + jnp.exp(-gate_val)) * up_val).T.astype(jnp.bfloat16)
    slot_weight = slot_ref[:, :1]
    low = lax.rem(place_ref[0], 2)
    for k in range(count // 2):
        block = slice(2 * k * cols, 2 * (k + 1) * cols)
        both = (
            jnp.dot(hidden, down_ref[:, block], preferred_element_type=jnp.float32) * slot_weight
        ).astype(jnp.bfloat16)
        keep_ref[k] = jnp.where(low == 0, both[:, :cols], both[:, cols:])
        give_ref[k] = jnp.where(low == 0, both[:, cols:], both[:, :cols])


def run_experts(place, slots, pieces, gains, gate, up, down):
    count, capacity, cols = pieces.shape
    return call(
        expert_kernel,
        [jax.ShapeDtypeStruct((count // 2, capacity, cols), jnp.bfloat16)] * 2,
        [SMEM_SPEC] + [VMEM_SPEC] * 6,
        [],
        6 * capacity * gate.size, gate.size * 6, 14,
    )(place, slots, pieces, gains, gate, up, down)


def add_kernel(keep_ref, given_ref, out_ref):
    out_ref[...] = (
        keep_ref[...].astype(jnp.float32) + given_ref[...].astype(jnp.float32)
    ).astype(jnp.bfloat16)


def add(keep, given):
    return call(
        add_kernel,
        jax.ShapeDtypeStruct(keep.shape, jnp.bfloat16),
        [VMEM_SPEC] * 2,
        [],
        keep.size, keep.size * 6, 4,
    )(keep, given)


def combine_kernel(sharers, routes_ref, pieces, out_ref):
    count, capacity, cols = pieces.shape
    routes = routes_ref[...]
    taken = [expert_rows(routes, e, capacity) for e in range(HELD)]
    spread = [taken[k // sharers] for k in range(count)]
    out_ref[...] = lax.dot_general(
        jnp.concatenate(spread, axis=0).astype(jnp.bfloat16),
        pieces[...].reshape(count * capacity, cols),
        (((0,), (0,)), ((), ())),
        preferred_element_type=jnp.float32,
    )


def combine(sharers, routes, pieces):
    count, capacity, cols = pieces.shape
    rows = routes.shape[1]
    return call(
        functools.partial(combine_kernel, sharers),
        jax.ShapeDtypeStruct((rows, cols), jnp.float32),
        [VMEM_SPEC] * 2,
        [],
        2 * rows * capacity * count * cols, (count * capacity * 2 + rows * 4) * cols, 4,
    )(routes, pieces)


def exchange(blocks):
    return lax.all_to_all(blocks, "attn", split_axis=0, concat_axis=0, tiled=True)


def exchange_high(blocks, count):
    groups = [list(range(low, count, 2)) for low in range(2)]
    return lax.all_to_all(
        blocks, "attn", split_axis=0, concat_axis=0, axis_index_groups=groups, tiled=True
    )


def crossed(block, count, mask):
    return lax.ppermute(block, "attn", [(index, index ^ mask) for index in range(count)])


def swap(block):
    return lax.ppermute(block, "expert", [(0, 1), (1, 0)])


def shards(
    queries,
    key_cache,
    value_cache,
    new_key,
    new_value,
    cache_length,
    residual,
    out_weight,
    ln_gain,
    gate_weight,
    up_weight,
    down_weight,
    routes,
    route_weight,
):
    count = lax.axis_size("attn")
    cores = lax.axis_size("expert")
    capacity = routes.shape[0] * TOP // EXPERTS * 2
    place = lax.axis_index("attn").astype(jnp.int32).reshape(1)
    routes = routes.T
    route_weight = route_weight.T

    attended = attend(queries, key_cache, value_cache, new_key, new_value, cache_length, ln_gain)
    both = pair_up(place, attended, crossed(attended, count, 1))
    quarters = [both] + [crossed(both, count, 2 * k) for k in range(1, count // 2)]
    mine, gains = project(place, quarters, out_weight)
    attn_stream, chosen, slots = pick(
        place, cores, count, capacity, mine, swap(mine), residual, routes, route_weight
    )
    keep, give = run_experts(
        place, slots, exchange(chosen), gains, gate_weight.T, up_weight.T, down_weight
    )
    summed = exchange_high(add(keep, crossed(give, count, 1)), count)
    combined = combine(count // 2 // HELD, routes, summed)
    expert_out = (combined + swap(combined)).astype(jnp.bfloat16)
    return (attn_stream, expert_out)


def solution(mesh):
    count = mesh.shape["attn"]
    fits = D // count % 256 == 0 and count >= 4 and count & (count - 1) == 0
    return jax.shard_map(
        shards if fits else shards_plain,
        mesh=mesh,
        in_specs=(
            P(("group", "attn"), "expert"),
            P(("group", "attn"), None, "expert"),
            P(("group", "attn"), None, "expert"),
            P(("group", "attn"), "expert"),
            P(("group", "attn"), "expert"),
            P(("group", "attn")),
            P("group", "attn"),
            P("expert", "attn"),
            P("attn"),
            P(None, ("attn", "expert")),
            P(None, ("attn", "expert")),
            P(("attn", "expert"), None),
            P("group", None),
            P("group", None),
        ),
        out_specs=(P("group", "attn"), P("group", "attn")),
        check_vma=False,
    )
```

```python
import functools
import math

import jax
import jax.numpy as jnp
from jax import lax
from jax.experimental import pallas as pl
from jax.experimental.pallas import tpu as pltpu
from jax.sharding import PartitionSpec as P

D = 6144
HEADS = 48
KV_HEADS = 8
HEAD_DIM = 128
EXPERTS = 16
TOP = 4
HELD = 2


NEG_FILL = -1e30
EPSILON = 1e-05


def attend_local(queries, key_cache, value_cache, new_key, new_value, cache_length):
    row_count = queries.shape[0]
    kv_local = new_key.shape[1] // HEAD_DIM
    group = HEADS // KV_HEADS
    length_max = key_cache.shape[1]
    query_heads = queries.reshape(row_count, kv_local, group, HEAD_DIM)
    key_heads = key_cache.reshape(row_count, length_max, kv_local, HEAD_DIM)
    value_heads = value_cache.reshape(row_count, length_max, kv_local, HEAD_DIM)
    own_keys = new_key.reshape(row_count, kv_local, HEAD_DIM)
    own_values = new_value.reshape(row_count, kv_local, HEAD_DIM)
    scale = 1.0 / math.sqrt(HEAD_DIM)
    past = (
        jnp.einsum("rkgd,rlkd->rkgl", query_heads, key_heads, preferred_element_type=jnp.float32)
        * scale
    )
    valid = jnp.arange(length_max, dtype=jnp.int32)[None, :] < cache_length[:, None]
    past = jnp.where(valid[:, None, None, :], past, NEG_FILL)
    own = (
        jnp.einsum("rkgd,rkd->rkg", query_heads, own_keys, preferred_element_type=jnp.float32)
        * scale
    )
    largest = jnp.maximum(jnp.max(past, axis=3), own)
    past_weight = jnp.exp(past - largest[..., None])
    own_weight = jnp.exp(own - largest)
    total = jnp.sum(past_weight, axis=3) + own_weight
    past_prob = (past_weight / total[..., None]).astype(jnp.bfloat16)
    own_prob = (own_weight / total).astype(jnp.bfloat16)
    result = jnp.einsum(
        "rkgl,rlkd->rkgd", past_prob, value_heads, preferred_element_type=jnp.float32
    )
    result = (
        result
        + own_prob.astype(jnp.float32)[..., None] * own_values.astype(jnp.float32)[:, :, None, :]
    )
    return result.reshape(row_count, kv_local * group * HEAD_DIM).astype(jnp.bfloat16)


def selection(routes, route_weight, capacity):
    row_count = routes.shape[0]
    experts = jnp.arange(HELD, dtype=jnp.int32)
    match = routes[None, :, :] == experts[:, None, None]
    hit = jnp.any(match, axis=2)
    row_weight = jnp.sum(jnp.where(match, route_weight[None], 0.0), axis=2)
    earlier = jnp.arange(row_count)[:, None] < jnp.arange(row_count)[None, :]
    slot = jnp.sum(jnp.where(earlier[None] & hit[:, :, None], 1, 0), axis=1)
    taken = hit[:, None, :] & (slot[:, None, :] == jnp.arange(capacity, dtype=jnp.int32)[None, :, None])
    slot_weight = jnp.sum(jnp.where(taken, row_weight[:, None, :], 0.0), axis=2)
    return taken, slot_weight


def gather_attn(block):
    count = lax.axis_size("attn")
    copies = jnp.broadcast_to(block[None], (count,) + block.shape)
    return lax.all_to_all(copies, "attn", split_axis=0, concat_axis=0, tiled=True)


def pair_sum(block):
    return block + lax.ppermute(block, "expert", [(0, 1), (1, 0)])


def shards_plain(
    queries,
    key_cache,
    value_cache,
    new_key,
    new_value,
    cache_length,
    residual,
    out_weight,
    ln_gain,
    gate_weight,
    up_weight,
    down_weight,
    routes,
    route_weight,
):
    attn_count = lax.axis_size("attn")
    core_count = lax.axis_size("expert")
    sharers = attn_count * core_count // HELD
    my_expert = (lax.axis_index("attn") * core_count + lax.axis_index("expert")) // sharers
    dest_expert = [index * core_count // sharers for index in range(attn_count)]
    row_count = routes.shape[0]
    capacity = row_count * TOP // EXPERTS * 2
    cols = residual.shape[1]

    taken, slot_weight = selection(routes, route_weight, capacity)
    pick = taken.astype(jnp.bfloat16)

    gains = gather_attn(ln_gain)

    attended = attend_local(queries, key_cache, value_cache, new_key, new_value, cache_length)
    whole = gather_attn(attended).reshape(row_count, -1)
    partial_proj = jnp.dot(whole, out_weight, preferred_element_type=jnp.float32)
    head_total = pair_sum(partial_proj)
    attn_stream = (residual.astype(jnp.float32) + head_total).astype(jnp.bfloat16)

    chosen = jnp.einsum(
        "esr,rd->esd", pick, attn_stream, preferred_element_type=jnp.float32
    ).astype(jnp.bfloat16)
    outgoing = jnp.stack([chosen[index] for index in dest_expert])
    rows = lax.all_to_all(outgoing, "attn", split_axis=0, concat_axis=0, tiled=True)
    wide = rows.astype(jnp.float32)
    row_mean = jnp.sum(wide, axis=(0, 2)) / D
    row_var = jnp.sum(wide * wide, axis=(0, 2)) / D - row_mean * row_mean
    normed = (
        (wide - row_mean[None, :, None])
        * lax.rsqrt(row_var + EPSILON)[None, :, None]
        * gains.reshape(attn_count, 1, cols)
    ).astype(jnp.bfloat16)
    gate_val = jnp.einsum(
        "asd,adf->sf", normed, gate_weight.reshape(attn_count, cols, -1),
        preferred_element_type=jnp.float32,
    )
    up_val = jnp.einsum(
        "asd,adf->sf", normed, up_weight.reshape(attn_count, cols, -1),
        preferred_element_type=jnp.float32,
    )
    hidden = (jax.nn.silu(gate_val) * up_val).astype(jnp.bfloat16)
    piece = jnp.dot(hidden, down_weight, preferred_element_type=jnp.float32)
    mine = jnp.take(slot_weight, my_expert, axis=0)
    piece = (piece * mine[:, None]).astype(jnp.bfloat16)
    returned = lax.all_to_all(
        piece.reshape(capacity, attn_count, cols).swapaxes(0, 1),
        "attn", split_axis=0, concat_axis=0, tiled=True,
    )
    spread = jnp.stack([pick[index] for index in dest_expert])
    combined = jnp.einsum(
        "asr,asd->rd", spread, returned, preferred_element_type=jnp.float32
    )
    expert_out = pair_sum(combined).astype(jnp.bfloat16)
    return (attn_stream, expert_out)


MIB = 1024 * 1024
ATTEND_MIB = 58_000_000 / MIB
EXCHANGE_FLOPS = 10**10
VMEM_SPEC = pl.BlockSpec(memory_space=pltpu.VMEM)
SMEM_SPEC = pl.BlockSpec(memory_space=pltpu.SMEM)
HBM_SPEC = pl.BlockSpec(memory_space=pltpu.HBM)


def call(kernel, outs, in_specs, scratch, flops, nbytes, vmem_mib):
    single = not isinstance(outs, (list, tuple))
    return pl.pallas_call(
        kernel,
        out_shape=outs,
        in_specs=in_specs,
        out_specs=VMEM_SPEC if single else [VMEM_SPEC] * len(outs),
        scratch_shapes=scratch,
        cost_estimate=pl.CostEstimate(flops=flops, bytes_accessed=nbytes, transcendentals=0),
        compiler_params=pltpu.CompilerParams(vmem_limit_bytes=int(vmem_mib * MIB)),
    )


def attend_kernel(
    length_ref, query_hbm, key_hbm, value_hbm, own_key_hbm, own_value_hbm, gain_hbm, out_ref,
    query_ref, key_buf, value_buf, own_key_ref, own_value_ref, gain_ref,
    query_rows, key_rows, value_rows, result_rows, key_sem, value_sem, small_sem,
):
    row_count, length_max = key_hbm.shape[0], key_hbm.shape[1]
    kv_local = own_key_ref.shape[1] // HEAD_DIM
    group = HEADS // KV_HEADS
    block = group * row_count
    key_copies = [
        pltpu.make_async_copy(key_hbm.at[r], key_buf.at[r], key_sem.at[r]) for r in range(row_count)
    ]
    value_copies = [
        pltpu.make_async_copy(value_hbm.at[r], value_buf.at[r], value_sem.at[r])
        for r in range(row_count)
    ]
    small_copies = [
        pltpu.make_async_copy(source, target, small_sem.at[index])
        for index, (source, target) in enumerate(
            (
                (query_hbm, query_ref),
                (own_key_hbm, own_key_ref),
                (own_value_hbm, own_value_ref),
                (gain_hbm, gain_ref),
            )
        )
    ]
    for copy in small_copies + key_copies + value_copies:
        copy.start()
    for copy in small_copies:
        copy.wait()
    for g in range(kv_local):
        lanes = slice(g * HEAD_DIM, (g + 1) * HEAD_DIM)
        own_key = own_key_ref[:, lanes].astype(jnp.float32)
        own_value = own_value_ref[:, lanes].astype(jnp.float32)
        for i in range(group):
            head = g * group + i
            rows = pl.ds(g * block + i * row_count, row_count)
            query_rows[rows, :] = query_ref[
                :, head * HEAD_DIM : (head + 1) * HEAD_DIM
            ].astype(jnp.float32)
            key_rows[rows, :] = own_key
            value_rows[rows, :] = own_value
    scale = 1.0 / math.sqrt(HEAD_DIM)
    pair_rows = 2 * block
    request = lax.broadcasted_iota(jnp.int32, (pair_rows, 1), 0) % row_count
    lengths = jnp.zeros((pair_rows, 1), jnp.int32)
    for r in range(row_count):
        lengths = jnp.where(request == r, length_ref[r], lengths)
    position = lax.broadcasted_iota(jnp.int32, (pair_rows, length_max), 1)
    valid = position < lengths
    pairs = kv_local // 2
    past = [jnp.zeros((pair_rows, length_max), jnp.float32) for _ in range(pairs)]
    packed = []
    for p in range(pairs):
        rows = query_rows[pl.ds(p * pair_rows, pair_rows), :]
        lower = rows[:block].astype(jnp.bfloat16)
        upper = rows[block:].astype(jnp.bfloat16)
        zero = jnp.zeros_like(lower)
        packed.append(
            jnp.concatenate(
                [
                    jnp.concatenate([lower, zero], axis=1),
                    jnp.concatenate([zero, upper], axis=1),
                ],
                axis=0,
            )
        )
    for r in range(row_count):
        key_copies[r].wait()
        for p in range(pairs):
            keys = key_buf[r, :, p * 2 * HEAD_DIM : (p + 1) * 2 * HEAD_DIM]
            scores = lax.dot_general(
                packed[p], keys, (((1,), (1,)), ((), ())), preferred_element_type=jnp.float32
            )
            past[p] = jnp.where(request == r, scores, past[p])
    probs, own_probs = [], []
    for p in range(pairs):
        rows = pl.ds(p * pair_rows, pair_rows)
        scores = jnp.where(valid, past[p] * scale, NEG_FILL)
        own = jnp.sum(query_rows[rows, :] * key_rows[rows, :], axis=1, keepdims=True) * scale
        largest = jnp.maximum(jnp.max(scores, axis=1, keepdims=True), own)
        weight = jnp.exp(scores - largest)
        own_weight = jnp.exp(own - largest)
        total = jnp.sum(weight, axis=1, keepdims=True) + own_weight
        probs.append((weight / total).astype(jnp.bfloat16))
        own_probs.append((own_weight / total).astype(jnp.bfloat16).astype(jnp.float32))
    sums = [jnp.zeros((pair_rows, 2 * HEAD_DIM), jnp.float32) for _ in range(pairs)]
    for r in range(row_count):
        value_copies[r].wait()
        for p in range(pairs):
            values = value_buf[r, :, p * 2 * HEAD_DIM : (p + 1) * 2 * HEAD_DIM]
            product = jnp.dot(probs[p], values, preferred_element_type=jnp.float32)
            sums[p] = jnp.where(request == r, product, sums[p])
    for p in range(pairs):
        rows = pl.ds(p * pair_rows, pair_rows)
        own_part = own_probs[p] * value_rows[rows, :]
        lower = sums[p][:block, :HEAD_DIM] + own_part[:block]
        upper = sums[p][block:, HEAD_DIM:] + own_part[block:]
        result_rows[pl.ds(p * pair_rows, block), :] = lower
        result_rows[pl.ds(p * pair_rows + block, block), :] = upper
    width = query_hbm.shape[1]
    for head in range(kv_local * group):
        rows = result_rows[pl.ds(head * row_count, row_count), :].astype(jnp.bfloat16)
        out_ref[:, head * HEAD_DIM : (head + 1) * HEAD_DIM] = rows
    gain_row = gain_ref[...].reshape(1, -1)
    half = gain_row.shape[1] // 2
    row = lax.broadcasted_iota(jnp.int32, (row_count, half), 0)
    left = jnp.broadcast_to(gain_row[:, :half], (row_count, half))
    right = jnp.broadcast_to(gain_row[:, half:], (row_count, half))
    gain = jnp.where(row % 2 == 0, left, right)
    upper = gain.astype(jnp.bfloat16).astype(jnp.float32)
    parts = jnp.where(row < 2, upper, gain - upper).astype(jnp.bfloat16)
    out_ref[:, width:] = parts


def attend(queries, key_cache, value_cache, new_key, new_value, cache_length, gain):
    row_count, width = queries.shape
    heads = width // HEAD_DIM
    table = pltpu.VMEM((heads * row_count, HEAD_DIM), jnp.float32)
    nbytes = 2 * key_cache.size * 2
    return call(
        attend_kernel,
        jax.ShapeDtypeStruct((row_count, width + gain.shape[0] // 2), jnp.bfloat16),
        [SMEM_SPEC] + [HBM_SPEC] * 6,
        [
            pltpu.VMEM(queries.shape, jnp.bfloat16),
            pltpu.VMEM(key_cache.shape, jnp.bfloat16),
            pltpu.VMEM(value_cache.shape, jnp.bfloat16),
            pltpu.VMEM(new_key.shape, jnp.bfloat16),
            pltpu.VMEM(new_value.shape, jnp.bfloat16),
            pltpu.VMEM(gain.shape, jnp.float32),
            table, table, table, table,
            pltpu.SemaphoreType.DMA((row_count,)),
            pltpu.SemaphoreType.DMA((row_count,)),
            pltpu.SemaphoreType.DMA((4,)),
        ],
        4 * key_cache.size * 6, nbytes, ATTEND_MIB,
    )(cache_length, queries, key_cache, value_cache, new_key, new_value, gain)


def stack_kernel(count, place_ref, *refs):
    out_ref = refs[-1]
    high = place_ref[0] // 2
    for k, block in enumerate(refs[:count]):
        out_ref[high ^ k] = block[...]


def stack(place, blocks, *earlier):
    shape = (len(blocks),) + blocks[0].shape
    return call(
        functools.partial(stack_kernel, len(blocks)),
        jax.ShapeDtypeStruct(shape, blocks[0].dtype),
        [SMEM_SPEC] + [VMEM_SPEC] * (len(blocks) + len(earlier)),
        [],
        0, 4 * len(blocks) * blocks[0].size, 4,
    )(place, *blocks, *earlier)


def ordered(low, mine, other):
    return jnp.where(low == 0, mine, other), jnp.where(low == 0, other, mine)


def project_kernel(place_ref, mine_ref, other_ref, weight_ref, out_ref, gain_ref, rows_ref):
    highs, rows, _ = mine_ref.shape
    width = weight_ref.shape[0]
    half = gain_ref.shape[2] // 2
    low = lax.rem(place_ref[0], 2)
    for k in range(highs):
        both = ordered(
            low, mine_ref[k].astype(jnp.float32), other_ref[k].astype(jnp.float32)
        )
        for index, block in enumerate(both):
            source = 2 * k + index
            rows_ref[pl.ds(source * rows, rows), :] = block[:, :width]
            gain_ref[source, :, :half] = block[0:1, width:] + block[2:3, width:]
            gain_ref[source, :, half:] = block[1:2, width:] + block[3:4, width:]
    out_ref[...] = jnp.dot(
        rows_ref[...].astype(jnp.bfloat16), weight_ref[...], preferred_element_type=jnp.float32
    )


def project(place, mine, other, out_weight):
    highs, rows, _ = mine.shape
    count = 2 * highs
    depth, cols = out_weight.shape
    return call(
        project_kernel,
        [
            jax.ShapeDtypeStruct((rows * count, cols), jnp.float32),
            jax.ShapeDtypeStruct((count, 1, cols), jnp.float32),
        ],
        [SMEM_SPEC] + [VMEM_SPEC] * 3,
        [pltpu.VMEM((rows * count, depth), jnp.float32)],
        2 * rows * count * out_weight.size, out_weight.size * 2, 10,
    )(place, mine, other, out_weight)


def expert_rows(routes, expert, capacity):
    row_count = routes.shape[1]
    hit = jnp.max((routes == expert).astype(jnp.float32), axis=0, keepdims=True)
    earlier = lax.broadcasted_iota(jnp.int32, (row_count, row_count), 0) < lax.broadcasted_iota(
        jnp.int32, (row_count, row_count), 1
    )
    slot = jnp.dot(
        jnp.broadcast_to(hit, (8, row_count)).astype(jnp.bfloat16),
        earlier.astype(jnp.bfloat16),
        preferred_element_type=jnp.float32,
    )[:1]
    place = lax.broadcasted_iota(jnp.int32, (capacity, row_count), 0).astype(jnp.float32)
    return jnp.where((slot == place) & (hit > 0.5), 1.0, 0.0)


def route_kernel(sharers, place_ref, routes_ref, weight_ref, taken_ref, slot_ref):
    routes = routes_ref[...]
    capacity = slot_ref.shape[0]
    taken = [expert_rows(routes, e, capacity) for e in range(HELD)]
    for e in range(HELD):
        taken_ref[e] = taken[e]
    first = place_ref[0] // 2 < sharers
    expert = jnp.where(first, 0, 1)
    row_weight = jnp.sum(
        jnp.where(routes == expert, weight_ref[...], 0.0), axis=0, keepdims=True
    )
    mine = jnp.where(first, taken[0], taken[1])
    slot_ref[...] = jnp.broadcast_to(
        jnp.sum(mine * row_weight, axis=1, keepdims=True), slot_ref.shape
    )


def route(place, sharers, capacity, routes, route_weight):
    rows = routes.shape[1]
    return call(
        functools.partial(route_kernel, sharers),
        [
            jax.ShapeDtypeStruct((HELD, capacity, rows), jnp.float32),
            jax.ShapeDtypeStruct((capacity, 128), jnp.float32),
        ],
        [SMEM_SPEC] + [VMEM_SPEC] * 2,
        [],
        EXCHANGE_FLOPS, rows * capacity * 16, 4,
    )(place, routes, route_weight)


def pick_kernel(sharers, place_ref, mine_ref, other_ref, residual_ref, taken_ref, stream_ref,
                *out_refs):
    stream = (
        residual_ref[...].astype(jnp.float32) + (mine_ref[...] + other_ref[...])
    ).astype(jnp.bfloat16)
    stream_ref[...] = stream
    chosen = [
        jnp.dot(
            taken_ref[e].astype(jnp.bfloat16), stream, preferred_element_type=jnp.float32
        )
        for e in range(HELD)
    ]
    high = place_ref[0] // 2
    for k, out_ref in enumerate(out_refs):
        out_ref[...] = jnp.where((high ^ k) < sharers, chosen[0], chosen[1]).astype(jnp.bfloat16)


def pick(place, sharers, highs, mine, other, residual, taken):
    rows, cols = mine.shape
    capacity = taken.shape[1]
    return call(
        functools.partial(pick_kernel, sharers),
        [jax.ShapeDtypeStruct((rows, cols), jnp.bfloat16)]
        + [jax.ShapeDtypeStruct((capacity, cols), jnp.bfloat16)] * highs,
        [SMEM_SPEC] + [VMEM_SPEC] * 4,
        [],
        EXCHANGE_FLOPS, rows * cols * 12, 4,
    )(place, mine, other, residual, taken)


def expert_kernel(place_ref, slot_ref, mine_ref, other_ref, gains, gate_ref, up_ref, down_ref,
                  keep_ref, give_ref):
    highs, capacity, cols = mine_ref.shape
    low = lax.rem(place_ref[0], 2)
    blocks = []
    for k in range(highs):
        blocks.extend(
            ordered(low, mine_ref[k].astype(jnp.float32), other_ref[k].astype(jnp.float32))
        )
    first = second = 0.0
    for wide in blocks:
        first = first + wide
        second = second + wide * wide
    row_mean = jnp.sum(first, axis=1, keepdims=True) / D
    row_var = jnp.sum(second, axis=1, keepdims=True) / D - row_mean * row_mean
    inverse = lax.rsqrt(row_var + EPSILON)
    contract = (((1,), (1,)), ((), ()))
    gate_val = up_val = 0.0
    for k, wide in enumerate(blocks):
        columns = slice(k * cols, (k + 1) * cols)
        normed = ((wide - row_mean) * inverse * gains[k]).astype(jnp.bfloat16)
        gate_val = gate_val + lax.dot_general(
            gate_ref[:, columns], normed, contract, preferred_element_type=jnp.float32
        )
        up_val = up_val + lax.dot_general(
            up_ref[:, columns], normed, contract, preferred_element_type=jnp.float32
        )
    hidden = (gate_val / (1.0 + jnp.exp(-gate_val)) * up_val).T.astype(jnp.bfloat16)
    slot_weight = slot_ref[:, :1]
    for k in range(highs):
        columns = slice(2 * k * cols, 2 * (k + 1) * cols)
        both = (
            jnp.dot(hidden, down_ref[:, columns], preferred_element_type=jnp.float32)
            * slot_weight
        ).astype(jnp.bfloat16)
        keep_ref[k], give_ref[k] = ordered(low, both[:, :cols], both[:, cols:])


def run_experts(place, slots, mine, other, gains, gate, up, down):
    return call(
        expert_kernel,
        [jax.ShapeDtypeStruct(mine.shape, jnp.bfloat16)] * 2,
        [SMEM_SPEC] + [VMEM_SPEC] * 7,
        [],
        6 * mine.shape[1] * gate.size, gate.size * 6, 14,
    )(place, slots, mine, other, gains, gate, up, down)


def add_kernel(place_ref, keep_ref, given_ref, *out_refs):
    high = place_ref[0] // 2
    for k, out_ref in enumerate(out_refs):
        out_ref[...] = (
            keep_ref[high ^ k].astype(jnp.float32) + given_ref[high ^ k].astype(jnp.float32)
        ).astype(jnp.bfloat16)


def add(place, keep, given):
    highs, capacity, cols = keep.shape
    return call(
        add_kernel,
        [jax.ShapeDtypeStruct((capacity, cols), jnp.bfloat16)] * highs,
        [SMEM_SPEC] + [VMEM_SPEC] * 2,
        [],
        keep.size, keep.size * 6, 4,
    )(place, keep, given)


def combine_kernel(sharers, place_ref, taken_ref, *refs):
    pieces, out_ref = refs[:-1], refs[-1]
    high = place_ref[0] // 2
    spread = [
        jnp.where((high ^ k) < sharers, taken_ref[0], taken_ref[1]) for k in range(len(pieces))
    ]
    out_ref[...] = lax.dot_general(
        jnp.concatenate(spread, axis=0).astype(jnp.bfloat16),
        jnp.concatenate([piece[...] for piece in pieces], axis=0),
        (((0,), (0,)), ((), ())),
        preferred_element_type=jnp.float32,
    )


def combine(place, sharers, taken, pieces):
    capacity, cols = pieces[0].shape
    rows = taken.shape[2]
    return call(
        functools.partial(combine_kernel, sharers),
        jax.ShapeDtypeStruct((rows, cols), jnp.float32),
        [SMEM_SPEC] + [VMEM_SPEC] * (1 + len(pieces)),
        [],
        2 * rows * capacity * len(pieces) * cols, (len(pieces) * capacity + 2 * rows) * 2 * cols, 4,
    )(place, taken, *pieces)


def crossed(block, count, mask):
    return lax.ppermute(block, "attn", [(index, index ^ mask) for index in range(count)])


def spread_high(blocks, count):
    return [blocks[0]] + [crossed(blocks[k], count, 2 * k) for k in range(1, count // 2)]


def swap(block):
    return lax.ppermute(block, "expert", [(0, 1), (1, 0)])


def shards(
    queries,
    key_cache,
    value_cache,
    new_key,
    new_value,
    cache_length,
    residual,
    out_weight,
    ln_gain,
    gate_weight,
    up_weight,
    down_weight,
    routes,
    route_weight,
):
    count = lax.axis_size("attn")
    capacity = routes.shape[0] * TOP // EXPERTS * 2
    highs = count // 2
    sharers = count // HELD // 2
    place = lax.axis_index("attn").astype(jnp.int32).reshape(1)

    attended = attend(queries, key_cache, value_cache, new_key, new_value, cache_length, ln_gain)
    taken, slots = route(place, sharers, capacity, routes.T, route_weight.T)
    block = stack(place, spread_high([attended] * highs, count), slots)
    mine, gains = project(place, block, crossed(block, count, 1), out_weight)
    attn_stream, *chosen = pick(place, sharers, highs, mine, swap(mine), residual, taken)
    block = stack(place, spread_high(chosen, count))
    keep, give = run_experts(
        place, slots, block, crossed(block, count, 1), gains,
        gate_weight.T, up_weight.T, down_weight,
    )
    summed = add(place, keep, crossed(give, count, 1))
    combined = combine(place, sharers, taken, spread_high(summed, count))
    expert_out = (combined + swap(combined)).astype(jnp.bfloat16)
    return (attn_stream, expert_out)


def solution(mesh):
    count = mesh.shape["attn"]
    fits = D // count % 256 == 0 and count >= 4 and count & (count - 1) == 0
    return jax.shard_map(
        shards if fits else shards_plain,
        mesh=mesh,
        in_specs=(
            P(("group", "attn"), "expert"),
            P(("group", "attn"), None, "expert"),
            P(("group", "attn"), None, "expert"),
            P(("group", "attn"), "expert"),
            P(("group", "attn"), "expert"),
            P(("group", "attn")),
            P("group", "attn"),
            P("expert", "attn"),
            P("attn"),
            P(None, ("attn", "expert")),
            P(None, ("attn", "expert")),
            P(("attn", "expert"), None),
            P("group", None),
            P("group", None),
        ),
        out_specs=(P("group", "attn"), P("group", "attn")),
        check_vma=False,
    )
```

```python
import functools
import math

import jax
import jax.numpy as jnp
from jax import lax
from jax.experimental import pallas as pl
from jax.experimental.pallas import tpu as pltpu
from jax.sharding import PartitionSpec as P

D = 6144
HEADS = 48
KV_HEADS = 8
HEAD_DIM = 128
EXPERTS = 16
TOP = 4
HELD = 2


NEG_FILL = -1e30
EPSILON = 1e-05


def attend_local(queries, key_cache, value_cache, new_key, new_value, cache_length):
    row_count = queries.shape[0]
    kv_local = new_key.shape[1] // HEAD_DIM
    group = HEADS // KV_HEADS
    length_max = key_cache.shape[1]
    query_heads = queries.reshape(row_count, kv_local, group, HEAD_DIM)
    key_heads = key_cache.reshape(row_count, length_max, kv_local, HEAD_DIM)
    value_heads = value_cache.reshape(row_count, length_max, kv_local, HEAD_DIM)
    own_keys = new_key.reshape(row_count, kv_local, HEAD_DIM)
    own_values = new_value.reshape(row_count, kv_local, HEAD_DIM)
    scale = 1.0 / math.sqrt(HEAD_DIM)
    past = (
        jnp.einsum("rkgd,rlkd->rkgl", query_heads, key_heads, preferred_element_type=jnp.float32)
        * scale
    )
    valid = jnp.arange(length_max, dtype=jnp.int32)[None, :] < cache_length[:, None]
    past = jnp.where(valid[:, None, None, :], past, NEG_FILL)
    own = (
        jnp.einsum("rkgd,rkd->rkg", query_heads, own_keys, preferred_element_type=jnp.float32)
        * scale
    )
    largest = jnp.maximum(jnp.max(past, axis=3), own)
    past_weight = jnp.exp(past - largest[..., None])
    own_weight = jnp.exp(own - largest)
    total = jnp.sum(past_weight, axis=3) + own_weight
    past_prob = (past_weight / total[..., None]).astype(jnp.bfloat16)
    own_prob = (own_weight / total).astype(jnp.bfloat16)
    result = jnp.einsum(
        "rkgl,rlkd->rkgd", past_prob, value_heads, preferred_element_type=jnp.float32
    )
    result = (
        result
        + own_prob.astype(jnp.float32)[..., None] * own_values.astype(jnp.float32)[:, :, None, :]
    )
    return result.reshape(row_count, kv_local * group * HEAD_DIM).astype(jnp.bfloat16)


def selection(routes, route_weight, capacity):
    row_count = routes.shape[0]
    experts = jnp.arange(HELD, dtype=jnp.int32)
    match = routes[None, :, :] == experts[:, None, None]
    hit = jnp.any(match, axis=2)
    row_weight = jnp.sum(jnp.where(match, route_weight[None], 0.0), axis=2)
    earlier = jnp.arange(row_count)[:, None] < jnp.arange(row_count)[None, :]
    slot = jnp.sum(jnp.where(earlier[None] & hit[:, :, None], 1, 0), axis=1)
    taken = hit[:, None, :] & (slot[:, None, :] == jnp.arange(capacity, dtype=jnp.int32)[None, :, None])
    slot_weight = jnp.sum(jnp.where(taken, row_weight[:, None, :], 0.0), axis=2)
    return taken, slot_weight


def gather_attn(block):
    count = lax.axis_size("attn")
    copies = jnp.broadcast_to(block[None], (count,) + block.shape)
    return lax.all_to_all(copies, "attn", split_axis=0, concat_axis=0, tiled=True)


def pair_sum(block):
    return block + lax.ppermute(block, "expert", [(0, 1), (1, 0)])


def shards_plain(
    queries,
    key_cache,
    value_cache,
    new_key,
    new_value,
    cache_length,
    residual,
    out_weight,
    ln_gain,
    gate_weight,
    up_weight,
    down_weight,
    routes,
    route_weight,
):
    attn_count = lax.axis_size("attn")
    core_count = lax.axis_size("expert")
    sharers = attn_count * core_count // HELD
    my_expert = (lax.axis_index("attn") * core_count + lax.axis_index("expert")) // sharers
    dest_expert = [index * core_count // sharers for index in range(attn_count)]
    row_count = routes.shape[0]
    capacity = row_count * TOP // EXPERTS * 2
    cols = residual.shape[1]

    taken, slot_weight = selection(routes, route_weight, capacity)
    pick = taken.astype(jnp.bfloat16)

    gains = gather_attn(ln_gain)

    attended = attend_local(queries, key_cache, value_cache, new_key, new_value, cache_length)
    whole = gather_attn(attended).reshape(row_count, -1)
    partial_proj = jnp.dot(whole, out_weight, preferred_element_type=jnp.float32)
    head_total = pair_sum(partial_proj)
    attn_stream = (residual.astype(jnp.float32) + head_total).astype(jnp.bfloat16)

    chosen = jnp.einsum(
        "esr,rd->esd", pick, attn_stream, preferred_element_type=jnp.float32
    ).astype(jnp.bfloat16)
    outgoing = jnp.stack([chosen[index] for index in dest_expert])
    rows = lax.all_to_all(outgoing, "attn", split_axis=0, concat_axis=0, tiled=True)
    wide = rows.astype(jnp.float32)
    row_mean = jnp.sum(wide, axis=(0, 2)) / D
    row_var = jnp.sum(wide * wide, axis=(0, 2)) / D - row_mean * row_mean
    normed = (
        (wide - row_mean[None, :, None])
        * lax.rsqrt(row_var + EPSILON)[None, :, None]
        * gains.reshape(attn_count, 1, cols)
    ).astype(jnp.bfloat16)
    gate_val = jnp.einsum(
        "asd,adf->sf", normed, gate_weight.reshape(attn_count, cols, -1),
        preferred_element_type=jnp.float32,
    )
    up_val = jnp.einsum(
        "asd,adf->sf", normed, up_weight.reshape(attn_count, cols, -1),
        preferred_element_type=jnp.float32,
    )
    hidden = (jax.nn.silu(gate_val) * up_val).astype(jnp.bfloat16)
    piece = jnp.dot(hidden, down_weight, preferred_element_type=jnp.float32)
    mine = jnp.take(slot_weight, my_expert, axis=0)
    piece = (piece * mine[:, None]).astype(jnp.bfloat16)
    returned = lax.all_to_all(
        piece.reshape(capacity, attn_count, cols).swapaxes(0, 1),
        "attn", split_axis=0, concat_axis=0, tiled=True,
    )
    spread = jnp.stack([pick[index] for index in dest_expert])
    combined = jnp.einsum(
        "asr,asd->rd", spread, returned, preferred_element_type=jnp.float32
    )
    expert_out = pair_sum(combined).astype(jnp.bfloat16)
    return (attn_stream, expert_out)


MIB = 1024 * 1024
ATTEND_MIB = 58_000_000 / MIB
EXCHANGE_FLOPS = 10**10
VMEM_SPEC = pl.BlockSpec(memory_space=pltpu.VMEM)
SMEM_SPEC = pl.BlockSpec(memory_space=pltpu.SMEM)
HBM_SPEC = pl.BlockSpec(memory_space=pltpu.HBM)


def call(kernel, outs, in_specs, scratch, flops, nbytes, vmem_mib):
    single = not isinstance(outs, (list, tuple))
    return pl.pallas_call(
        kernel,
        out_shape=outs,
        in_specs=in_specs,
        out_specs=VMEM_SPEC if single else [VMEM_SPEC] * len(outs),
        scratch_shapes=scratch,
        cost_estimate=pl.CostEstimate(flops=flops, bytes_accessed=nbytes, transcendentals=0),
        compiler_params=pltpu.CompilerParams(vmem_limit_bytes=int(vmem_mib * MIB)),
    )


def attend_kernel(
    length_ref, query_hbm, key_hbm, value_hbm, own_key_hbm, own_value_hbm, gain_hbm, out_ref,
    query_ref, key_buf, value_buf, own_key_ref, own_value_ref, gain_ref,
    query_rows, key_rows, value_rows, result_rows, key_sem, value_sem, small_sem,
):
    row_count, length_max = key_hbm.shape[0], key_hbm.shape[1]
    kv_local = own_key_hbm.shape[1] // HEAD_DIM
    group = HEADS // KV_HEADS
    heads = kv_local * group
    small_copies = [
        pltpu.make_async_copy(source, target, small_sem.at[index])
        for index, (source, target) in enumerate(
            (
                (query_hbm, query_ref),
                (own_key_hbm, own_key_ref),
                (own_value_hbm, own_value_ref),
                (gain_hbm, gain_ref),
            )
        )
    ]
    key_copies = [
        pltpu.make_async_copy(key_hbm.at[r], key_buf.at[r], key_sem.at[r]) for r in range(row_count)
    ]
    value_copies = [
        pltpu.make_async_copy(value_hbm.at[r], value_buf.at[r], value_sem.at[r])
        for r in range(row_count)
    ]
    batches = [range(first, min(first + 2, row_count)) for first in range(0, row_count, 2)]
    for copy in small_copies:
        copy.start()
    for batch in batches:
        for r in batch:
            key_copies[r].start()
        for r in batch:
            value_copies[r].start()
    head = lax.broadcasted_iota(jnp.int32, (heads, 1), 0) // group
    position = lax.broadcasted_iota(jnp.int32, (heads, length_max), 1)
    for copy in small_copies:
        copy.wait()
    for g in range(kv_local):
        lanes = slice(g * HEAD_DIM, (g + 1) * HEAD_DIM)
        own_key = own_key_ref[:, lanes].astype(jnp.float32)
        own_value = own_value_ref[:, lanes].astype(jnp.float32)
        for i in range(group):
            index = g * group + i
            rows = pl.ds(index * row_count, row_count)
            query_rows[rows, :] = query_ref[
                :, index * HEAD_DIM : (index + 1) * HEAD_DIM
            ].astype(jnp.float32)
            key_rows[rows, :] = own_key
            value_rows[rows, :] = own_value
    scale = 1.0 / math.sqrt(HEAD_DIM)
    contract = (((1,), (1,)), ((), ()))
    for batch in batches:
        spread, own = {}, {}
        for r in batch:
            strided = pl.ds(r, heads, stride=row_count)
            query = query_rows[strided, :]
            own[r] = jnp.sum(query * key_rows[strided, :], axis=1, keepdims=True) * scale
            spread[r] = jnp.concatenate(
                [jnp.where(head == g, query, 0.0) for g in range(kv_local)], axis=1
            ).astype(jnp.bfloat16)
        scores = {}
        for r in batch:
            key_copies[r].wait()
            scores[r] = lax.dot_general(
                spread[r], key_buf[r], contract, preferred_element_type=jnp.float32
            )
        probs, own_probs = {}, {}
        for r in batch:
            past = jnp.where(position < length_ref[r], scores[r] * scale, NEG_FILL)
            largest = jnp.maximum(jnp.max(past, axis=1, keepdims=True), own[r])
            weight = jnp.exp(past - largest)
            own_weight = jnp.exp(own[r] - largest)
            inverse = 1.0 / (jnp.sum(weight, axis=1, keepdims=True) + own_weight)
            probs[r] = (weight * inverse).astype(jnp.bfloat16)
            own_probs[r] = (own_weight * inverse).astype(jnp.bfloat16).astype(jnp.float32)
        products = {}
        for r in batch:
            value_copies[r].wait()
            products[r] = jnp.dot(probs[r], value_buf[r], preferred_element_type=jnp.float32)
        for r in batch:
            strided = pl.ds(r, heads, stride=row_count)
            total = own_probs[r] * value_rows[strided, :]
            for g in range(kv_local):
                lanes = slice(g * HEAD_DIM, (g + 1) * HEAD_DIM)
                total = total + jnp.where(head == g, products[r][:, lanes], 0.0)
            result_rows[strided, :] = total
    width = query_hbm.shape[1]
    for index in range(heads):
        rows = result_rows[pl.ds(index * row_count, row_count), :].astype(jnp.bfloat16)
        for copy in range(out_ref.shape[0]):
            out_ref[copy, :, index * HEAD_DIM : (index + 1) * HEAD_DIM] = rows
    gain_row = gain_ref[...].reshape(1, -1)
    half = gain_row.shape[1] // 2
    row = lax.broadcasted_iota(jnp.int32, (row_count, half), 0)
    left = jnp.broadcast_to(gain_row[:, :half], (row_count, half))
    right = jnp.broadcast_to(gain_row[:, half:], (row_count, half))
    gain = jnp.where(row % 2 == 0, left, right)
    upper = gain.astype(jnp.bfloat16).astype(jnp.float32)
    parts = jnp.where(row < 2, upper, gain - upper).astype(jnp.bfloat16)
    for copy in range(out_ref.shape[0]):
        out_ref[copy, :, width:] = parts


def attend(count, queries, key_cache, value_cache, new_key, new_value, cache_length, gain):
    row_count, width = queries.shape
    heads = width // HEAD_DIM
    table = pltpu.VMEM((heads * row_count, HEAD_DIM), jnp.float32)
    nbytes = 2 * key_cache.size * 2
    return call(
        attend_kernel,
        jax.ShapeDtypeStruct((count, row_count, width + gain.shape[0] // 2), jnp.bfloat16),
        [SMEM_SPEC] + [HBM_SPEC] * 6,
        [
            pltpu.VMEM(queries.shape, jnp.bfloat16),
            pltpu.VMEM(key_cache.shape, jnp.bfloat16),
            pltpu.VMEM(value_cache.shape, jnp.bfloat16),
            pltpu.VMEM(new_key.shape, jnp.bfloat16),
            pltpu.VMEM(new_value.shape, jnp.bfloat16),
            pltpu.VMEM(gain.shape, jnp.float32),
            table, table, table, table,
            pltpu.SemaphoreType.DMA((row_count,)),
            pltpu.SemaphoreType.DMA((row_count,)),
            pltpu.SemaphoreType.DMA((4,)),
        ],
        4 * key_cache.size * 6, nbytes, ATTEND_MIB,
    )(cache_length, queries, key_cache, value_cache, new_key, new_value, gain)


def project_kernel(pieces, weight_ref, out_ref, gain_ref, stack):
    count, rows, _ = pieces.shape
    width = weight_ref.shape[0]
    half = gain_ref.shape[1] // 2
    for k in range(count):
        stack[pl.ds(k * rows, rows), :] = pieces[k, :, :width].astype(jnp.float32)
        parts = pieces[k, :, width:].astype(jnp.float32)
        gain_ref[pl.ds(k, 1), :half] = parts[0:1] + parts[2:3]
        gain_ref[pl.ds(k, 1), half:] = parts[1:2] + parts[3:4]
    out_ref[...] = jnp.dot(
        stack[...].astype(jnp.bfloat16), weight_ref[...], preferred_element_type=jnp.float32
    )


def project(pieces, out_weight):
    count, rows, _ = pieces.shape
    depth, cols = out_weight.shape
    return call(
        project_kernel,
        [
            jax.ShapeDtypeStruct((rows * count, cols), jnp.float32),
            jax.ShapeDtypeStruct((count, cols), jnp.float32),
        ],
        [VMEM_SPEC, VMEM_SPEC],
        [pltpu.VMEM((rows * count, depth), jnp.float32)],
        2 * rows * count * out_weight.size, out_weight.size * 2, 10,
    )(pieces, out_weight)


def expert_rows(routes, expert, capacity):
    row_count = routes.shape[1]
    hit = jnp.max((routes == expert).astype(jnp.float32), axis=0, keepdims=True)
    earlier = lax.broadcasted_iota(jnp.int32, (row_count, row_count), 0) < lax.broadcasted_iota(
        jnp.int32, (row_count, row_count), 1
    )
    slot = jnp.dot(
        jnp.broadcast_to(hit, (8, row_count)).astype(jnp.bfloat16),
        earlier.astype(jnp.bfloat16),
        preferred_element_type=jnp.float32,
    )[:1]
    place = lax.broadcasted_iota(jnp.int32, (capacity, row_count), 0).astype(jnp.float32)
    return jnp.where((slot == place) & (hit > 0.5), 1.0, 0.0)


def walk(count):
    return list(range(0, count, 2)) + list(range(count - 1, 0, -2))


def pick_kernel(cores, place_ref, mine_ref, other_ref, residual_ref, routes_ref, weight_ref,
                stream_ref, out_ref, slot_ref):
    count, capacity, _ = out_ref.shape
    stream = (
        residual_ref[...].astype(jnp.float32) + (mine_ref[...] + other_ref[...])
    ).astype(jnp.bfloat16)
    stream_ref[...] = stream
    routes = routes_ref[...]
    sharers = count * cores // HELD
    taken = [expert_rows(routes, e, capacity) for e in range(HELD)]
    chosen = [
        jnp.dot(
            taken[e].astype(jnp.bfloat16), stream, preferred_element_type=jnp.float32
        ).astype(jnp.bfloat16)
        for e in range(HELD)
    ]
    for slot, k in enumerate(walk(count)):
        out_ref[slot] = chosen[k * cores // sharers]
    first = place_ref[0] * cores < sharers
    expert = jnp.where(first, 0, 1)
    row_weight = jnp.sum(
        jnp.where(routes == expert, weight_ref[...], 0.0), axis=0, keepdims=True
    )
    mine = jnp.where(first, taken[0], taken[1])
    slot_ref[...] = jnp.broadcast_to(
        jnp.sum(mine * row_weight, axis=1, keepdims=True), slot_ref.shape
    )


def pick(place, cores, count, capacity, mine, other, residual, routes, route_weight):
    rows, cols = mine.shape
    return call(
        functools.partial(pick_kernel, cores),
        [
            jax.ShapeDtypeStruct((rows, cols), jnp.bfloat16),
            jax.ShapeDtypeStruct((count, capacity, cols), jnp.bfloat16),
            jax.ShapeDtypeStruct((capacity, 128), jnp.float32),
        ],
        [SMEM_SPEC] + [VMEM_SPEC] * 5,
        [],
        EXCHANGE_FLOPS, rows * cols * 12, 4,
    )(place, mine, other, residual, routes, route_weight)


def expert_kernel(slot_ref, pieces, gains, gate_ref, up_ref, down_ref, out_ref):
    count, capacity, cols = pieces.shape
    first = second = 0.0
    for k in range(count):
        wide = pieces[k].astype(jnp.float32)
        first = first + wide
        second = second + wide * wide
    row_mean = jnp.sum(first, axis=1, keepdims=True) / D
    row_var = jnp.sum(second, axis=1, keepdims=True) / D - row_mean * row_mean
    inverse = lax.rsqrt(row_var + EPSILON)
    contract = (((1,), (1,)), ((), ()))
    gate_val = up_val = 0.0
    for slot, k in enumerate(walk(count)):
        block = slice(k * cols, (k + 1) * cols)
        wide = pieces[slot].astype(jnp.float32)
        normed = ((wide - row_mean) * inverse * gains[pl.ds(k, 1), :]).astype(jnp.bfloat16)
        gate_val = gate_val + lax.dot_general(
            gate_ref[:, block], normed, contract, preferred_element_type=jnp.float32
        )
        up_val = up_val + lax.dot_general(
            up_ref[:, block], normed, contract, preferred_element_type=jnp.float32
        )
    hidden = (gate_val / (1.0 + jnp.exp(-gate_val)) * up_val).T.astype(jnp.bfloat16)
    slot_weight = slot_ref[:, :1]
    for slot, k in enumerate(walk(count)):
        block = slice(k * cols, (k + 1) * cols)
        out_ref[slot] = (
            jnp.dot(hidden, down_ref[:, block], preferred_element_type=jnp.float32) * slot_weight
        ).astype(jnp.bfloat16)


def run_experts(slots, pieces, gains, gate, up, down):
    return call(
        expert_kernel,
        jax.ShapeDtypeStruct(pieces.shape, jnp.bfloat16),
        [VMEM_SPEC] * 6,
        [],
        6 * pieces.shape[1] * gate.size, gate.size * 6, 14,
    )(slots, pieces, gains, gate, up, down)


def combine_kernel(cores, routes_ref, pieces, out_ref):
    count, capacity, cols = pieces.shape
    sharers = count * cores // HELD
    routes = routes_ref[...]
    taken = [expert_rows(routes, e, capacity) for e in range(HELD)]
    spread = [taken[k * cores // sharers] for k in walk(count)]
    out_ref[...] = lax.dot_general(
        jnp.concatenate(spread, axis=0).astype(jnp.bfloat16),
        pieces[...].reshape(count * capacity, cols),
        (((0,), (0,)), ((), ())),
        preferred_element_type=jnp.float32,
    )


def combine(cores, routes, pieces):
    count, capacity, cols = pieces.shape
    rows = routes.shape[1]
    return call(
        functools.partial(combine_kernel, cores),
        jax.ShapeDtypeStruct((rows, cols), jnp.float32),
        [VMEM_SPEC] * 2,
        [],
        2 * rows * capacity * count * cols, (count * capacity * 2 + rows * 4) * cols, 4,
    )(routes, pieces)


def exchange(blocks, members=None):
    return lax.all_to_all(
        blocks, "attn", split_axis=0, concat_axis=0, axis_index_groups=members, tiled=True
    )


def swap(block):
    return lax.ppermute(block, "expert", [(0, 1), (1, 0)])


def shards(
    queries,
    key_cache,
    value_cache,
    new_key,
    new_value,
    cache_length,
    residual,
    out_weight,
    ln_gain,
    gate_weight,
    up_weight,
    down_weight,
    routes,
    route_weight,
):
    count = lax.axis_size("attn")
    cores = lax.axis_size("expert")
    capacity = routes.shape[0] * TOP // EXPERTS * 2
    place = lax.axis_index("attn").astype(jnp.int32).reshape(1)
    routes = routes.T
    route_weight = route_weight.T

    attended = exchange(
        attend(
            count, queries, key_cache, value_cache, new_key, new_value, cache_length,
            ln_gain,
        )
    )
    mine, gains = project(attended, out_weight)
    attn_stream, chosen, slots = pick(
        place, cores, count, capacity, mine, swap(mine), residual, routes, route_weight
    )
    outgoing = run_experts(
        slots, exchange(chosen, [walk(count)]), gains, gate_weight.T, up_weight.T, down_weight
    )
    combined = combine(cores, routes, exchange(outgoing, [walk(count)]))
    expert_out = (combined + swap(combined)).astype(jnp.bfloat16)
    return (attn_stream, expert_out)


def solution(mesh):
    cols = D // mesh.shape["attn"]
    return jax.shard_map(
        shards if cols % 256 == 0 else shards_plain,
        mesh=mesh,
        in_specs=(
            P(("group", "attn"), "expert"),
            P(("group", "attn"), None, "expert"),
            P(("group", "attn"), None, "expert"),
            P(("group", "attn"), "expert"),
            P(("group", "attn"), "expert"),
            P(("group", "attn")),
            P("group", "attn"),
            P("expert", "attn"),
            P("attn"),
            P(None, ("attn", "expert")),
            P(None, ("attn", "expert")),
            P(("attn", "expert"), None),
            P("group", None),
            P("group", None),
        ),
        out_specs=(P("group", "attn"), P("group", "attn")),
        check_vma=False,
    )
```

```python
import functools
import math

import jax
import jax.numpy as jnp
from jax import lax
from jax.experimental import pallas as pl
from jax.experimental.pallas import tpu as pltpu
from jax.sharding import PartitionSpec as P

D = 6144
HEADS = 48
KV_HEADS = 8
HEAD_DIM = 128
EXPERTS = 16
TOP = 4
HELD = 2


NEG_FILL = -1e30
EPSILON = 1e-05


def attend_local(queries, key_cache, value_cache, new_key, new_value, cache_length):
    row_count = queries.shape[0]
    kv_local = new_key.shape[1] // HEAD_DIM
    group = HEADS // KV_HEADS
    length_max = key_cache.shape[1]
    query_heads = queries.reshape(row_count, kv_local, group, HEAD_DIM)
    key_heads = key_cache.reshape(row_count, length_max, kv_local, HEAD_DIM)
    value_heads = value_cache.reshape(row_count, length_max, kv_local, HEAD_DIM)
    own_keys = new_key.reshape(row_count, kv_local, HEAD_DIM)
    own_values = new_value.reshape(row_count, kv_local, HEAD_DIM)
    scale = 1.0 / math.sqrt(HEAD_DIM)
    past = (
        jnp.einsum("rkgd,rlkd->rkgl", query_heads, key_heads, preferred_element_type=jnp.float32)
        * scale
    )
    valid = jnp.arange(length_max, dtype=jnp.int32)[None, :] < cache_length[:, None]
    past = jnp.where(valid[:, None, None, :], past, NEG_FILL)
    own = (
        jnp.einsum("rkgd,rkd->rkg", query_heads, own_keys, preferred_element_type=jnp.float32)
        * scale
    )
    largest = jnp.maximum(jnp.max(past, axis=3), own)
    past_weight = jnp.exp(past - largest[..., None])
    own_weight = jnp.exp(own - largest)
    total = jnp.sum(past_weight, axis=3) + own_weight
    past_prob = (past_weight / total[..., None]).astype(jnp.bfloat16)
    own_prob = (own_weight / total).astype(jnp.bfloat16)
    result = jnp.einsum(
        "rkgl,rlkd->rkgd", past_prob, value_heads, preferred_element_type=jnp.float32
    )
    result = (
        result
        + own_prob.astype(jnp.float32)[..., None] * own_values.astype(jnp.float32)[:, :, None, :]
    )
    return result.reshape(row_count, kv_local * group * HEAD_DIM).astype(jnp.bfloat16)


def selection(routes, route_weight, capacity):
    row_count = routes.shape[0]
    experts = jnp.arange(HELD, dtype=jnp.int32)
    match = routes[None, :, :] == experts[:, None, None]
    hit = jnp.any(match, axis=2)
    row_weight = jnp.sum(jnp.where(match, route_weight[None], 0.0), axis=2)
    earlier = jnp.arange(row_count)[:, None] < jnp.arange(row_count)[None, :]
    slot = jnp.sum(jnp.where(earlier[None] & hit[:, :, None], 1, 0), axis=1)
    taken = hit[:, None, :] & (slot[:, None, :] == jnp.arange(capacity, dtype=jnp.int32)[None, :, None])
    slot_weight = jnp.sum(jnp.where(taken, row_weight[:, None, :], 0.0), axis=2)
    return taken, slot_weight


def gather_attn(block):
    count = lax.axis_size("attn")
    copies = jnp.broadcast_to(block[None], (count,) + block.shape)
    return lax.all_to_all(copies, "attn", split_axis=0, concat_axis=0, tiled=True)


def pair_sum(block):
    return block + lax.ppermute(block, "expert", [(0, 1), (1, 0)])


def shards_plain(
    queries,
    key_cache,
    value_cache,
    new_key,
    new_value,
    cache_length,
    residual,
    out_weight,
    ln_gain,
    gate_weight,
    up_weight,
    down_weight,
    routes,
    route_weight,
):
    attn_count = lax.axis_size("attn")
    core_count = lax.axis_size("expert")
    sharers = attn_count * core_count // HELD
    my_expert = (lax.axis_index("attn") * core_count + lax.axis_index("expert")) // sharers
    dest_expert = [index * core_count // sharers for index in range(attn_count)]
    row_count = routes.shape[0]
    capacity = row_count * TOP // EXPERTS * 2
    cols = residual.shape[1]

    taken, slot_weight = selection(routes, route_weight, capacity)
    pick = taken.astype(jnp.bfloat16)

    gains = gather_attn(ln_gain)

    attended = attend_local(queries, key_cache, value_cache, new_key, new_value, cache_length)
    whole = gather_attn(attended).reshape(row_count, -1)
    partial_proj = jnp.dot(whole, out_weight, preferred_element_type=jnp.float32)
    head_total = pair_sum(partial_proj)
    attn_stream = (residual.astype(jnp.float32) + head_total).astype(jnp.bfloat16)

    chosen = jnp.einsum(
        "esr,rd->esd", pick, attn_stream, preferred_element_type=jnp.float32
    ).astype(jnp.bfloat16)
    outgoing = jnp.stack([chosen[index] for index in dest_expert])
    rows = lax.all_to_all(outgoing, "attn", split_axis=0, concat_axis=0, tiled=True)
    wide = rows.astype(jnp.float32)
    row_mean = jnp.sum(wide, axis=(0, 2)) / D
    row_var = jnp.sum(wide * wide, axis=(0, 2)) / D - row_mean * row_mean
    normed = (
        (wide - row_mean[None, :, None])
        * lax.rsqrt(row_var + EPSILON)[None, :, None]
        * gains.reshape(attn_count, 1, cols)
    ).astype(jnp.bfloat16)
    gate_val = jnp.einsum(
        "asd,adf->sf", normed, gate_weight.reshape(attn_count, cols, -1),
        preferred_element_type=jnp.float32,
    )
    up_val = jnp.einsum(
        "asd,adf->sf", normed, up_weight.reshape(attn_count, cols, -1),
        preferred_element_type=jnp.float32,
    )
    hidden = (jax.nn.silu(gate_val) * up_val).astype(jnp.bfloat16)
    piece = jnp.dot(hidden, down_weight, preferred_element_type=jnp.float32)
    mine = jnp.take(slot_weight, my_expert, axis=0)
    piece = (piece * mine[:, None]).astype(jnp.bfloat16)
    returned = lax.all_to_all(
        piece.reshape(capacity, attn_count, cols).swapaxes(0, 1),
        "attn", split_axis=0, concat_axis=0, tiled=True,
    )
    spread = jnp.stack([pick[index] for index in dest_expert])
    combined = jnp.einsum(
        "asr,asd->rd", spread, returned, preferred_element_type=jnp.float32
    )
    expert_out = pair_sum(combined).astype(jnp.bfloat16)
    return (attn_stream, expert_out)


MIB = 1024 * 1024
EXCHANGE_FLOPS = 10**10
VMEM_SPEC = pl.BlockSpec(memory_space=pltpu.VMEM)
SMEM_SPEC = pl.BlockSpec(memory_space=pltpu.SMEM)
HBM_SPEC = pl.BlockSpec(memory_space=pltpu.HBM)


def call(kernel, outs, in_specs, scratch, flops, nbytes, vmem_mib):
    single = not isinstance(outs, (list, tuple))
    return pl.pallas_call(
        kernel,
        out_shape=outs,
        in_specs=in_specs,
        out_specs=VMEM_SPEC if single else [VMEM_SPEC] * len(outs),
        scratch_shapes=scratch,
        cost_estimate=pl.CostEstimate(flops=flops, bytes_accessed=nbytes, transcendentals=0),
        compiler_params=pltpu.CompilerParams(vmem_limit_bytes=vmem_mib * MIB),
    )


def order_kernel(place_ref, out_ref):
    rows = out_ref.shape[0]
    before = lax.broadcasted_iota(jnp.int32, (rows, rows), 0) < lax.broadcasted_iota(
        jnp.int32, (rows, rows), 1
    )
    out_ref[...] = jnp.where(before & (place_ref[0] >= 0), 1.0, 0.0).astype(jnp.bfloat16)


def order(place, rows):
    return call(
        order_kernel,
        jax.ShapeDtypeStruct((rows, rows), jnp.bfloat16),
        [SMEM_SPEC],
        [],
        EXCHANGE_FLOPS, rows * rows * 2, 2,
    )(place)


def score_kernel(length_ref, query_ref, key_ref, own_key_ref, earlier_ref, probs_ref, own_ref,
                 query_rows, key_rows):
    row_count, length_max, width = key_ref.shape
    kv_local = width // HEAD_DIM
    group = HEADS // KV_HEADS
    heads = kv_local * group
    for g in range(kv_local):
        own_key = own_key_ref[:, g * HEAD_DIM : (g + 1) * HEAD_DIM].astype(jnp.float32)
        for i in range(group):
            index = g * group + i
            rows = pl.ds(index * row_count, row_count)
            query_rows[rows, :] = query_ref[
                :, index * HEAD_DIM : (index + 1) * HEAD_DIM
            ].astype(jnp.float32)
            key_rows[rows, :] = own_key
    scale = 1.0 / math.sqrt(HEAD_DIM)
    contract = (((1,), (1,)), ((), ()))
    head = lax.broadcasted_iota(jnp.int32, (heads, 1), 0) // group
    position = lax.broadcasted_iota(jnp.int32, (heads, length_max), 1)
    for r in range(row_count):
        strided = pl.ds(r, heads, stride=row_count)
        query = query_rows[strided, :]
        own = jnp.sum(query * key_rows[strided, :], axis=1, keepdims=True) * scale
        spread = jnp.concatenate(
            [jnp.where(head == g, query, 0.0) for g in range(kv_local)], axis=1
        ).astype(jnp.bfloat16)
        scores = lax.dot_general(
            spread, key_ref[r], contract, preferred_element_type=jnp.float32
        )
        past = jnp.where(position < length_ref[r], scores * scale, NEG_FILL)
        largest = jnp.maximum(jnp.max(past, axis=1, keepdims=True), own)
        weight = jnp.exp(past - largest)
        own_weight = jnp.exp(own - largest)
        inverse = 1.0 / (jnp.sum(weight, axis=1, keepdims=True) + own_weight)
        probs_ref[r] = (weight * inverse).astype(jnp.bfloat16)
        own_prob = (own_weight * inverse).astype(jnp.bfloat16).astype(jnp.float32)
        own_ref[r] = jnp.broadcast_to(own_prob, (heads, HEAD_DIM))


def value_kernel(probs_ref, own_ref, value_ref, own_value_ref, gain_ref, out_ref, value_rows,
                 result_rows):
    row_count, length_max, width = value_ref.shape
    kv_local = width // HEAD_DIM
    group = HEADS // KV_HEADS
    heads = kv_local * group
    for g in range(kv_local):
        own_value = own_value_ref[:, g * HEAD_DIM : (g + 1) * HEAD_DIM].astype(jnp.float32)
        for i in range(group):
            value_rows[pl.ds((g * group + i) * row_count, row_count), :] = own_value
    head = lax.broadcasted_iota(jnp.int32, (heads, 1), 0) // group
    for r in range(row_count):
        strided = pl.ds(r, heads, stride=row_count)
        product = jnp.dot(probs_ref[r], value_ref[r], preferred_element_type=jnp.float32)
        total = own_ref[r] * value_rows[strided, :]
        for g in range(kv_local):
            lanes = slice(g * HEAD_DIM, (g + 1) * HEAD_DIM)
            total = total + jnp.where(head == g, product[:, lanes], 0.0)
        result_rows[strided, :] = total
    for index in range(heads):
        rows = result_rows[pl.ds(index * row_count, row_count), :].astype(jnp.bfloat16)
        for copy in range(out_ref.shape[0]):
            out_ref[copy, :, index * HEAD_DIM : (index + 1) * HEAD_DIM] = rows
    gain_row = gain_ref[...].reshape(1, -1)
    half = gain_row.shape[1] // 2
    row = lax.broadcasted_iota(jnp.int32, (row_count, half), 0)
    left = jnp.broadcast_to(gain_row[:, :half], (row_count, half))
    right = jnp.broadcast_to(gain_row[:, half:], (row_count, half))
    gain = jnp.where(row % 2 == 0, left, right)
    upper = gain.astype(jnp.bfloat16).astype(jnp.float32)
    parts = jnp.where(row < 2, upper, gain - upper).astype(jnp.bfloat16)
    for copy in range(out_ref.shape[0]):
        out_ref[copy, :, heads * HEAD_DIM :] = parts


def attend(
    count, queries, key_cache, value_cache, new_key, new_value, cache_length, gain, earlier
):
    row_count, width = queries.shape
    heads = width // HEAD_DIM
    length_max = key_cache.shape[1]
    table = pltpu.VMEM((heads * row_count, HEAD_DIM), jnp.float32)
    probs, own = call(
        score_kernel,
        [
            jax.ShapeDtypeStruct((row_count, heads, length_max), jnp.bfloat16),
            jax.ShapeDtypeStruct((row_count, heads, HEAD_DIM), jnp.float32),
        ],
        [SMEM_SPEC] + [VMEM_SPEC] * 4,
        [table, table],
        2 * key_cache.size * heads, key_cache.size * 2, 8,
    )(cache_length, queries, key_cache, new_key, earlier)
    return call(
        value_kernel,
        jax.ShapeDtypeStruct((count, row_count, width + gain.shape[0] // 2), jnp.bfloat16),
        [VMEM_SPEC] * 5,
        [table, table],
        EXCHANGE_FLOPS, value_cache.size * 2, 8,
    )(probs, own, value_cache, new_value, gain)


def project_kernel(pieces, weight_ref, out_ref, gain_ref, stack):
    count, rows, _ = pieces.shape
    width = weight_ref.shape[0]
    half = gain_ref.shape[1] // 2
    for k in range(count):
        stack[pl.ds(k * rows, rows), :] = pieces[k, :, :width].astype(jnp.float32)
        parts = pieces[k, :, width:].astype(jnp.float32)
        gain_ref[pl.ds(k, 1), :half] = parts[0:1] + parts[2:3]
        gain_ref[pl.ds(k, 1), half:] = parts[1:2] + parts[3:4]
    out_ref[...] = jnp.dot(
        stack[...].astype(jnp.bfloat16), weight_ref[...], preferred_element_type=jnp.float32
    )


def project(pieces, out_weight):
    count, rows, _ = pieces.shape
    depth, cols = out_weight.shape
    return call(
        project_kernel,
        [
            jax.ShapeDtypeStruct((rows * count, cols), jnp.float32),
            jax.ShapeDtypeStruct((count, cols), jnp.float32),
        ],
        [VMEM_SPEC, VMEM_SPEC],
        [pltpu.VMEM((rows * count, depth), jnp.float32)],
        2 * rows * count * out_weight.size, out_weight.size * 2, 10,
    )(pieces, out_weight)


def expert_rows(routes, earlier, expert, capacity):
    row_count = routes.shape[1]
    hit = jnp.max((routes == expert).astype(jnp.float32), axis=0, keepdims=True)
    slot = jnp.dot(
        jnp.broadcast_to(hit, (8, row_count)).astype(jnp.bfloat16),
        earlier,
        preferred_element_type=jnp.float32,
    )[:1]
    place = lax.broadcasted_iota(jnp.int32, (capacity, row_count), 0).astype(jnp.float32)
    return jnp.where((slot == place) & (hit > 0.5), 1.0, 0.0)


def walk(count):
    return list(range(0, count, 2)) + list(range(count - 1, 0, -2))


def pick_kernel(cores, place_ref, mine_ref, other_ref, residual_ref, routes_ref, weight_ref, earlier_ref,
                stream_ref, out_ref, slot_ref):
    count, capacity, _ = out_ref.shape
    stream = (
        residual_ref[...].astype(jnp.float32) + (mine_ref[...] + other_ref[...])
    ).astype(jnp.bfloat16)
    stream_ref[...] = stream
    routes = routes_ref[...]
    sharers = count * cores // HELD
    taken = [expert_rows(routes, earlier_ref[...], e, capacity) for e in range(HELD)]
    chosen = [
        jnp.dot(
            taken[e].astype(jnp.bfloat16), stream, preferred_element_type=jnp.float32
        ).astype(jnp.bfloat16)
        for e in range(HELD)
    ]
    for k in range(count):
        out_ref[k] = chosen[k * cores // sharers]
    first = place_ref[0] * cores < sharers
    expert = jnp.where(first, 0, 1)
    row_weight = jnp.sum(
        jnp.where(routes == expert, weight_ref[...], 0.0), axis=0, keepdims=True
    )
    mine = jnp.where(first, taken[0], taken[1])
    slot_ref[...] = jnp.broadcast_to(
        jnp.sum(mine * row_weight, axis=1, keepdims=True), slot_ref.shape
    )


def pick(place, cores, count, capacity, mine, other, residual, routes, route_weight, earlier):
    rows, cols = mine.shape
    return call(
        functools.partial(pick_kernel, cores),
        [
            jax.ShapeDtypeStruct((rows, cols), jnp.bfloat16),
            jax.ShapeDtypeStruct((count, capacity, cols), jnp.bfloat16),
            jax.ShapeDtypeStruct((capacity, 128), jnp.float32),
        ],
        [SMEM_SPEC] + [VMEM_SPEC] * 6,
        [],
        EXCHANGE_FLOPS, rows * cols * 12, 4,
    )(place, mine, other, residual, routes, route_weight, earlier)


def expert_kernel(slot_ref, pieces, gains, gate_ref, up_ref, down_ref, out_ref):
    count, capacity, cols = pieces.shape
    first = second = 0.0
    for k in range(count):
        wide = pieces[k].astype(jnp.float32)
        first = first + wide
        second = second + wide * wide
    row_mean = jnp.sum(first, axis=1, keepdims=True) / D
    row_var = jnp.sum(second, axis=1, keepdims=True) / D - row_mean * row_mean
    inverse = lax.rsqrt(row_var + EPSILON)
    contract = (((1,), (1,)), ((), ()))
    gate_val = up_val = 0.0
    for k in range(count):
        block = slice(k * cols, (k + 1) * cols)
        wide = pieces[k].astype(jnp.float32)
        normed = ((wide - row_mean) * inverse * gains[pl.ds(k, 1), :]).astype(jnp.bfloat16)
        gate_val = gate_val + lax.dot_general(
            gate_ref[:, block], normed, contract, preferred_element_type=jnp.float32
        )
        up_val = up_val + lax.dot_general(
            up_ref[:, block], normed, contract, preferred_element_type=jnp.float32
        )
    hidden = (gate_val / (1.0 + jnp.exp(-gate_val)) * up_val).T.astype(jnp.bfloat16)
    slot_weight = slot_ref[:, :1]
    for slot, k in enumerate(walk(count)):
        block = slice(k * cols, (k + 1) * cols)
        out_ref[slot] = (
            jnp.dot(hidden, down_ref[:, block], preferred_element_type=jnp.float32) * slot_weight
        ).astype(jnp.bfloat16)


def run_experts(slots, pieces, gains, gate, up, down):
    return call(
        expert_kernel,
        jax.ShapeDtypeStruct(pieces.shape, jnp.bfloat16),
        [VMEM_SPEC] * 6,
        [],
        6 * pieces.shape[1] * gate.size, gate.size * 6, 14,
    )(slots, pieces, gains, gate, up, down)


def combine_kernel(cores, routes_ref, earlier_ref, pieces, out_ref):
    count, capacity, cols = pieces.shape
    sharers = count * cores // HELD
    routes = routes_ref[...]
    taken = [expert_rows(routes, earlier_ref[...], e, capacity) for e in range(HELD)]
    spread = [taken[k * cores // sharers] for k in walk(count)]
    out_ref[...] = lax.dot_general(
        jnp.concatenate(spread, axis=0).astype(jnp.bfloat16),
        pieces[...].reshape(count * capacity, cols),
        (((0,), (0,)), ((), ())),
        preferred_element_type=jnp.float32,
    )


def combine(cores, routes, earlier, pieces):
    count, capacity, cols = pieces.shape
    rows = routes.shape[1]
    return call(
        functools.partial(combine_kernel, cores),
        jax.ShapeDtypeStruct((rows, cols), jnp.float32),
        [VMEM_SPEC] * 3,
        [],
        2 * rows * capacity * count * cols, (count * capacity * 2 + rows * 4) * cols, 4,
    )(routes, earlier, pieces)


def exchange(blocks, members=None):
    return lax.all_to_all(
        blocks, "attn", split_axis=0, concat_axis=0, axis_index_groups=members, tiled=True
    )


def swap(block):
    return lax.ppermute(block, "expert", [(0, 1), (1, 0)])


def shards(
    queries,
    key_cache,
    value_cache,
    new_key,
    new_value,
    cache_length,
    residual,
    out_weight,
    ln_gain,
    gate_weight,
    up_weight,
    down_weight,
    routes,
    route_weight,
):
    count = lax.axis_size("attn")
    cores = lax.axis_size("expert")
    capacity = routes.shape[0] * TOP // EXPERTS * 2
    place = lax.axis_index("attn").astype(jnp.int32).reshape(1)
    routes = routes.T
    route_weight = route_weight.T

    earlier = order(place, routes.shape[1])
    attended = exchange(
        attend(
            count, queries, key_cache, value_cache, new_key, new_value, cache_length,
            ln_gain, earlier,
        )
    )
    mine, gains = project(attended, out_weight)
    attn_stream, chosen, slots = pick(
        place, cores, count, capacity, mine, swap(mine), residual, routes, route_weight, earlier
    )
    outgoing = run_experts(
        slots, exchange(chosen), gains, gate_weight.T, up_weight.T, down_weight
    )
    combined = combine(cores, routes, earlier, exchange(outgoing, [walk(count)]))
    expert_out = (combined + swap(combined)).astype(jnp.bfloat16)
    return (attn_stream, expert_out)


def solution(mesh):
    cols = D // mesh.shape["attn"]
    return jax.shard_map(
        shards if cols % 256 == 0 else shards_plain,
        mesh=mesh,
        in_specs=(
            P(("group", "attn"), "expert"),
            P(("group", "attn"), None, "expert"),
            P(("group", "attn"), None, "expert"),
            P(("group", "attn"), "expert"),
            P(("group", "attn"), "expert"),
            P(("group", "attn")),
            P("group", "attn"),
            P("expert", "attn"),
            P("attn"),
            P(None, ("attn", "expert")),
            P(None, ("attn", "expert")),
            P(("attn", "expert"), None),
            P("group", None),
            P("group", None),
        ),
        out_specs=(P("group", "attn"), P("group", "attn")),
        check_vma=False,
    )
```

```python
import functools
import math

import jax
import jax.numpy as jnp
from jax import lax
from jax.experimental import pallas as pl
from jax.experimental.pallas import tpu as pltpu
from jax.sharding import PartitionSpec as P

D = 6144
HEADS = 48
KV_HEADS = 8
HEAD_DIM = 128
EXPERTS = 16
TOP = 4
HELD = 2


NEG_FILL = -1e30
EPSILON = 1e-05


def attend_local(queries, key_cache, value_cache, new_key, new_value, cache_length):
    row_count = queries.shape[0]
    kv_local = new_key.shape[1] // HEAD_DIM
    group = HEADS // KV_HEADS
    length_max = key_cache.shape[1]
    query_heads = queries.reshape(row_count, kv_local, group, HEAD_DIM)
    key_heads = key_cache.reshape(row_count, length_max, kv_local, HEAD_DIM)
    value_heads = value_cache.reshape(row_count, length_max, kv_local, HEAD_DIM)
    own_keys = new_key.reshape(row_count, kv_local, HEAD_DIM)
    own_values = new_value.reshape(row_count, kv_local, HEAD_DIM)
    scale = 1.0 / math.sqrt(HEAD_DIM)
    past = (
        jnp.einsum("rkgd,rlkd->rkgl", query_heads, key_heads, preferred_element_type=jnp.float32)
        * scale
    )
    valid = jnp.arange(length_max, dtype=jnp.int32)[None, :] < cache_length[:, None]
    past = jnp.where(valid[:, None, None, :], past, NEG_FILL)
    own = (
        jnp.einsum("rkgd,rkd->rkg", query_heads, own_keys, preferred_element_type=jnp.float32)
        * scale
    )
    largest = jnp.maximum(jnp.max(past, axis=3), own)
    past_weight = jnp.exp(past - largest[..., None])
    own_weight = jnp.exp(own - largest)
    total = jnp.sum(past_weight, axis=3) + own_weight
    past_prob = (past_weight / total[..., None]).astype(jnp.bfloat16)
    own_prob = (own_weight / total).astype(jnp.bfloat16)
    result = jnp.einsum(
        "rkgl,rlkd->rkgd", past_prob, value_heads, preferred_element_type=jnp.float32
    )
    result = (
        result
        + own_prob.astype(jnp.float32)[..., None] * own_values.astype(jnp.float32)[:, :, None, :]
    )
    return result.reshape(row_count, kv_local * group * HEAD_DIM).astype(jnp.bfloat16)


def selection(routes, route_weight, capacity):
    row_count = routes.shape[0]
    experts = jnp.arange(HELD, dtype=jnp.int32)
    match = routes[None, :, :] == experts[:, None, None]
    hit = jnp.any(match, axis=2)
    row_weight = jnp.sum(jnp.where(match, route_weight[None], 0.0), axis=2)
    earlier = jnp.arange(row_count)[:, None] < jnp.arange(row_count)[None, :]
    slot = jnp.sum(jnp.where(earlier[None] & hit[:, :, None], 1, 0), axis=1)
    taken = hit[:, None, :] & (slot[:, None, :] == jnp.arange(capacity, dtype=jnp.int32)[None, :, None])
    slot_weight = jnp.sum(jnp.where(taken, row_weight[:, None, :], 0.0), axis=2)
    return taken, slot_weight


def gather_attn(block):
    count = lax.axis_size("attn")
    copies = jnp.broadcast_to(block[None], (count,) + block.shape)
    return lax.all_to_all(copies, "attn", split_axis=0, concat_axis=0, tiled=True)


def pair_sum(block):
    return block + lax.ppermute(block, "expert", [(0, 1), (1, 0)])


def shards_plain(
    queries,
    key_cache,
    value_cache,
    new_key,
    new_value,
    cache_length,
    residual,
    out_weight,
    ln_gain,
    gate_weight,
    up_weight,
    down_weight,
    routes,
    route_weight,
):
    attn_count = lax.axis_size("attn")
    core_count = lax.axis_size("expert")
    sharers = attn_count * core_count // HELD
    my_expert = (lax.axis_index("attn") * core_count + lax.axis_index("expert")) // sharers
    dest_expert = [index * core_count // sharers for index in range(attn_count)]
    row_count = routes.shape[0]
    capacity = row_count * TOP // EXPERTS * 2
    cols = residual.shape[1]

    taken, slot_weight = selection(routes, route_weight, capacity)
    pick = taken.astype(jnp.bfloat16)

    gains = gather_attn(ln_gain)

    attended = attend_local(queries, key_cache, value_cache, new_key, new_value, cache_length)
    whole = gather_attn(attended).reshape(row_count, -1)
    partial_proj = jnp.dot(whole, out_weight, preferred_element_type=jnp.float32)
    head_total = pair_sum(partial_proj)
    attn_stream = (residual.astype(jnp.float32) + head_total).astype(jnp.bfloat16)

    chosen = jnp.einsum(
        "esr,rd->esd", pick, attn_stream, preferred_element_type=jnp.float32
    ).astype(jnp.bfloat16)
    outgoing = jnp.stack([chosen[index] for index in dest_expert])
    rows = lax.all_to_all(outgoing, "attn", split_axis=0, concat_axis=0, tiled=True)
    wide = rows.astype(jnp.float32)
    row_mean = jnp.sum(wide, axis=(0, 2)) / D
    row_var = jnp.sum(wide * wide, axis=(0, 2)) / D - row_mean * row_mean
    normed = (
        (wide - row_mean[None, :, None])
        * lax.rsqrt(row_var + EPSILON)[None, :, None]
        * gains.reshape(attn_count, 1, cols)
    ).astype(jnp.bfloat16)
    gate_val = jnp.einsum(
        "asd,adf->sf", normed, gate_weight.reshape(attn_count, cols, -1),
        preferred_element_type=jnp.float32,
    )
    up_val = jnp.einsum(
        "asd,adf->sf", normed, up_weight.reshape(attn_count, cols, -1),
        preferred_element_type=jnp.float32,
    )
    hidden = (jax.nn.silu(gate_val) * up_val).astype(jnp.bfloat16)
    piece = jnp.dot(hidden, down_weight, preferred_element_type=jnp.float32)
    mine = jnp.take(slot_weight, my_expert, axis=0)
    piece = (piece * mine[:, None]).astype(jnp.bfloat16)
    returned = lax.all_to_all(
        piece.reshape(capacity, attn_count, cols).swapaxes(0, 1),
        "attn", split_axis=0, concat_axis=0, tiled=True,
    )
    spread = jnp.stack([pick[index] for index in dest_expert])
    combined = jnp.einsum(
        "asr,asd->rd", spread, returned, preferred_element_type=jnp.float32
    )
    expert_out = pair_sum(combined).astype(jnp.bfloat16)
    return (attn_stream, expert_out)


MIB = 1024 * 1024
EXCHANGE_FLOPS = 10**10
VMEM_SPEC = pl.BlockSpec(memory_space=pltpu.VMEM)
SMEM_SPEC = pl.BlockSpec(memory_space=pltpu.SMEM)
HBM_SPEC = pl.BlockSpec(memory_space=pltpu.HBM)


def call(kernel, outs, in_specs, scratch, flops, nbytes, vmem_mib):
    single = not isinstance(outs, (list, tuple))
    return pl.pallas_call(
        kernel,
        out_shape=outs,
        in_specs=in_specs,
        out_specs=VMEM_SPEC if single else [VMEM_SPEC] * len(outs),
        scratch_shapes=scratch,
        cost_estimate=pl.CostEstimate(flops=flops, bytes_accessed=nbytes, transcendentals=0),
        compiler_params=pltpu.CompilerParams(vmem_limit_bytes=vmem_mib * MIB),
    )


def order_kernel(place_ref, out_ref):
    rows = out_ref.shape[0]
    before = lax.broadcasted_iota(jnp.int32, (rows, rows), 0) < lax.broadcasted_iota(
        jnp.int32, (rows, rows), 1
    )
    out_ref[...] = jnp.where(before & (place_ref[0] >= 0), 1.0, 0.0).astype(jnp.bfloat16)


def order(place, rows):
    return call(
        order_kernel,
        jax.ShapeDtypeStruct((rows, rows), jnp.bfloat16),
        [SMEM_SPEC],
        [],
        EXCHANGE_FLOPS, rows * rows * 2, 2,
    )(place)


def expert_rows(routes, earlier, expert, capacity):
    row_count = routes.shape[1]
    hit = jnp.max((routes == expert).astype(jnp.float32), axis=0, keepdims=True)
    slot = jnp.dot(
        jnp.broadcast_to(hit, (8, row_count)).astype(jnp.bfloat16),
        earlier,
        preferred_element_type=jnp.float32,
    )[:1]
    place = lax.broadcasted_iota(jnp.int32, (capacity, row_count), 0).astype(jnp.float32)
    return jnp.where((slot == place) & (hit > 0.5), 1.0, 0.0)


def prepare_kernel(sharers, place_ref, earlier_ref, routes_ref, weight_ref, query_ref, own_key_ref,
                   spread_ref, own_ref, taken_ref, slot_ref, query_rows, key_rows):
    row_count = query_ref.shape[0]
    kv_local = own_key_ref.shape[1] // HEAD_DIM
    group = HEADS // KV_HEADS
    heads = kv_local * group
    for g in range(kv_local):
        own_key = own_key_ref[:, g * HEAD_DIM : (g + 1) * HEAD_DIM].astype(jnp.float32)
        for i in range(group):
            index = g * group + i
            rows = pl.ds(index * row_count, row_count)
            query_rows[rows, :] = query_ref[
                :, index * HEAD_DIM : (index + 1) * HEAD_DIM
            ].astype(jnp.float32)
            key_rows[rows, :] = own_key
    scale = 1.0 / math.sqrt(HEAD_DIM)
    head = lax.broadcasted_iota(jnp.int32, (heads, 1), 0) // group
    for r in range(row_count):
        strided = pl.ds(r, heads, stride=row_count)
        query = query_rows[strided, :]
        own = jnp.sum(query * key_rows[strided, :], axis=1, keepdims=True) * scale
        own_ref[r] = jnp.broadcast_to(own, (heads, HEAD_DIM))
        spread_ref[r] = jnp.concatenate(
            [jnp.where(head == g, query, 0.0) for g in range(kv_local)], axis=1
        ).astype(jnp.bfloat16)
    routes = routes_ref[...]
    capacity = slot_ref.shape[0]
    taken = [expert_rows(routes, earlier_ref[...], e, capacity) for e in range(HELD)]
    for e in range(HELD):
        taken_ref[e] = taken[e]
    first = place_ref[0] < sharers
    expert = jnp.where(first, 0, 1)
    row_weight = jnp.sum(
        jnp.where(routes == expert, weight_ref[...], 0.0), axis=0, keepdims=True
    )
    mine = jnp.where(first, taken[0], taken[1])
    slot_ref[...] = jnp.broadcast_to(
        jnp.sum(mine * row_weight, axis=1, keepdims=True), slot_ref.shape
    )


def prepare(place, sharers, capacity, earlier, routes, route_weight, queries, new_key):
    row_count, width = queries.shape
    heads = width // HEAD_DIM
    table = pltpu.VMEM((heads * row_count, HEAD_DIM), jnp.float32)
    return call(
        functools.partial(prepare_kernel, sharers),
        [
            jax.ShapeDtypeStruct((row_count, heads, new_key.shape[1]), jnp.bfloat16),
            jax.ShapeDtypeStruct((row_count, heads, HEAD_DIM), jnp.float32),
            jax.ShapeDtypeStruct((HELD, capacity, routes.shape[1]), jnp.float32),
            jax.ShapeDtypeStruct((capacity, HEAD_DIM), jnp.float32),
        ],
        [SMEM_SPEC] + [VMEM_SPEC] * 5,
        [table, table],
        queries.size * 8, queries.size * 16, 4,
    )(place, earlier, routes, route_weight, queries, new_key)


def score_kernel(length_ref, spread_ref, own_ref, key_ref, probs_ref, own_probs_ref):
    row_count, heads, length_max = probs_ref.shape
    scale = 1.0 / math.sqrt(HEAD_DIM)
    contract = (((1,), (1,)), ((), ()))
    position = lax.broadcasted_iota(jnp.int32, (heads, length_max), 1)
    for r in range(row_count):
        scores = lax.dot_general(
            spread_ref[r], key_ref[r], contract, preferred_element_type=jnp.float32
        )
        past = jnp.where(position < length_ref[r], scores * scale, NEG_FILL)
        own = own_ref[r, :, :1]
        largest = jnp.maximum(jnp.max(past, axis=1, keepdims=True), own)
        weight = jnp.exp(past - largest)
        own_weight = jnp.exp(own - largest)
        inverse = 1.0 / (jnp.sum(weight, axis=1, keepdims=True) + own_weight)
        probs_ref[r] = (weight * inverse).astype(jnp.bfloat16)
        own_prob = (own_weight * inverse).astype(jnp.bfloat16).astype(jnp.float32)
        own_probs_ref[r] = jnp.broadcast_to(own_prob, own_probs_ref.shape[1:])


def value_kernel(probs_ref, own_ref, value_ref, own_value_ref, gain_ref, out_ref, value_rows,
                 result_rows):
    row_count, length_max, width = value_ref.shape
    kv_local = width // HEAD_DIM
    group = HEADS // KV_HEADS
    heads = kv_local * group
    for g in range(kv_local):
        own_value = own_value_ref[:, g * HEAD_DIM : (g + 1) * HEAD_DIM].astype(jnp.float32)
        for i in range(group):
            value_rows[pl.ds((g * group + i) * row_count, row_count), :] = own_value
    head = lax.broadcasted_iota(jnp.int32, (heads, 1), 0) // group
    for r in range(row_count):
        strided = pl.ds(r, heads, stride=row_count)
        product = jnp.dot(probs_ref[r], value_ref[r], preferred_element_type=jnp.float32)
        total = own_ref[r] * value_rows[strided, :]
        for g in range(kv_local):
            lanes = slice(g * HEAD_DIM, (g + 1) * HEAD_DIM)
            total = total + jnp.where(head == g, product[:, lanes], 0.0)
        result_rows[strided, :] = total
    for index in range(heads):
        rows = result_rows[pl.ds(index * row_count, row_count), :].astype(jnp.bfloat16)
        for copy in range(out_ref.shape[0]):
            out_ref[copy, :, index * HEAD_DIM : (index + 1) * HEAD_DIM] = rows
    gain_row = gain_ref[...].reshape(1, -1)
    half = gain_row.shape[1] // 2
    row = lax.broadcasted_iota(jnp.int32, (row_count, half), 0)
    left = jnp.broadcast_to(gain_row[:, :half], (row_count, half))
    right = jnp.broadcast_to(gain_row[:, half:], (row_count, half))
    gain = jnp.where(row % 2 == 0, left, right)
    upper = gain.astype(jnp.bfloat16).astype(jnp.float32)
    parts = jnp.where(row < 2, upper, gain - upper).astype(jnp.bfloat16)
    for copy in range(out_ref.shape[0]):
        out_ref[copy, :, heads * HEAD_DIM :] = parts


def attend(count, spread, own, key_cache, value_cache, new_value, cache_length, gain):
    row_count, heads, _ = spread.shape
    length_max = key_cache.shape[1]
    table = pltpu.VMEM((heads * row_count, HEAD_DIM), jnp.float32)
    probs, own_probs = call(
        score_kernel,
        [
            jax.ShapeDtypeStruct((row_count, heads, length_max), jnp.bfloat16),
            jax.ShapeDtypeStruct((row_count, heads, HEAD_DIM), jnp.float32),
        ],
        [SMEM_SPEC] + [VMEM_SPEC] * 3,
        [],
        2 * key_cache.size * heads, key_cache.size * 2, 8,
    )(cache_length, spread, own, key_cache)
    width = heads * HEAD_DIM + gain.shape[0] // 2
    return call(
        value_kernel,
        jax.ShapeDtypeStruct((count, row_count, width), jnp.bfloat16),
        [VMEM_SPEC] * 5,
        [table, table],
        EXCHANGE_FLOPS, value_cache.size * 2, 8,
    )(probs, own_probs, value_cache, new_value, gain)


def project_kernel(pieces, weight_ref, out_ref, gain_ref, stack):
    count, rows, _ = pieces.shape
    width = weight_ref.shape[0]
    half = gain_ref.shape[1] // 2
    for k in range(count):
        stack[pl.ds(k * rows, rows), :] = pieces[k, :, :width].astype(jnp.float32)
        parts = pieces[k, :, width:].astype(jnp.float32)
        gain_ref[pl.ds(k, 1), :half] = parts[0:1] + parts[2:3]
        gain_ref[pl.ds(k, 1), half:] = parts[1:2] + parts[3:4]
    out_ref[...] = jnp.dot(
        stack[...].astype(jnp.bfloat16), weight_ref[...], preferred_element_type=jnp.float32
    )


def project(pieces, out_weight):
    count, rows, _ = pieces.shape
    depth, cols = out_weight.shape
    return call(
        project_kernel,
        [
            jax.ShapeDtypeStruct((rows * count, cols), jnp.float32),
            jax.ShapeDtypeStruct((count, cols), jnp.float32),
        ],
        [VMEM_SPEC, VMEM_SPEC],
        [pltpu.VMEM((rows * count, depth), jnp.float32)],
        2 * rows * count * out_weight.size, out_weight.size * 2, 10,
    )(pieces, out_weight)


def pick_kernel(sharers, mine_ref, other_ref, residual_ref, taken_ref, stream_ref, out_ref):
    stream = (
        residual_ref[...].astype(jnp.float32) + (mine_ref[...] + other_ref[...])
    ).astype(jnp.bfloat16)
    stream_ref[...] = stream
    chosen = [
        jnp.dot(
            taken_ref[e].astype(jnp.bfloat16), stream, preferred_element_type=jnp.float32
        ).astype(jnp.bfloat16)
        for e in range(HELD)
    ]
    for k in range(out_ref.shape[0]):
        out_ref[k] = chosen[k // sharers]


def pick(sharers, count, mine, other, residual, taken):
    rows, cols = mine.shape
    return call(
        functools.partial(pick_kernel, sharers),
        [
            jax.ShapeDtypeStruct((rows, cols), jnp.bfloat16),
            jax.ShapeDtypeStruct((count, taken.shape[1], cols), jnp.bfloat16),
        ],
        [VMEM_SPEC] * 4,
        [],
        EXCHANGE_FLOPS, rows * cols * 12, 4,
    )(mine, other, residual, taken)


def expert_kernel(slot_ref, pieces, gains, gate_ref, up_ref, down_ref, out_ref):
    count, capacity, cols = pieces.shape
    first = second = 0.0
    for k in range(count):
        wide = pieces[k].astype(jnp.float32)
        first = first + wide
        second = second + wide * wide
    row_mean = jnp.sum(first, axis=1, keepdims=True) / D
    row_var = jnp.sum(second, axis=1, keepdims=True) / D - row_mean * row_mean
    inverse = lax.rsqrt(row_var + EPSILON)
    contract = (((1,), (1,)), ((), ()))
    gate_val = up_val = 0.0
    for k in range(count):
        block = slice(k * cols, (k + 1) * cols)
        wide = pieces[k].astype(jnp.float32)
        normed = ((wide - row_mean) * inverse * gains[pl.ds(k, 1), :]).astype(jnp.bfloat16)
        gate_val = gate_val + lax.dot_general(
            gate_ref[:, block], normed, contract, preferred_element_type=jnp.float32
        )
        up_val = up_val + lax.dot_general(
            up_ref[:, block], normed, contract, preferred_element_type=jnp.float32
        )
    hidden = (gate_val / (1.0 + jnp.exp(-gate_val)) * up_val).T.astype(jnp.bfloat16)
    slot_weight = slot_ref[:, :1]
    for k in range(count):
        block = slice(k * cols, (k + 1) * cols)
        out_ref[k] = (
            jnp.dot(hidden, down_ref[:, block], preferred_element_type=jnp.float32) * slot_weight
        ).astype(jnp.bfloat16)


def run_experts(slots, pieces, gains, gate, up, down):
    return call(
        expert_kernel,
        jax.ShapeDtypeStruct(pieces.shape, jnp.bfloat16),
        [VMEM_SPEC] * 6,
        [],
        6 * pieces.shape[1] * gate.size, gate.size * 6, 14,
    )(slots, pieces, gains, gate, up, down)


def combine_kernel(sharers, taken_ref, pieces, out_ref):
    count, capacity, cols = pieces.shape
    spread = [taken_ref[k // sharers] for k in range(count)]
    out_ref[...] = lax.dot_general(
        jnp.concatenate(spread, axis=0).astype(jnp.bfloat16),
        pieces[...].reshape(count * capacity, cols),
        (((0,), (0,)), ((), ())),
        preferred_element_type=jnp.float32,
    )


def combine(sharers, taken, pieces):
    count, capacity, cols = pieces.shape
    rows = taken.shape[2]
    return call(
        functools.partial(combine_kernel, sharers),
        jax.ShapeDtypeStruct((rows, cols), jnp.float32),
        [VMEM_SPEC] * 2,
        [],
        2 * rows * capacity * count * cols, (count * capacity * 2 + rows * 4) * cols, 4,
    )(taken, pieces)


def finish_kernel(stream_ref, mine_ref, other_ref, stream_out_ref, out_ref):
    stream_out_ref[...] = stream_ref[...]
    out_ref[...] = (mine_ref[...] + other_ref[...]).astype(jnp.bfloat16)


def finish(stream, mine, other):
    return call(
        finish_kernel,
        [jax.ShapeDtypeStruct(stream.shape, jnp.bfloat16)] * 2,
        [VMEM_SPEC] * 3,
        [],
        mine.size, mine.size * 14, 4,
    )(stream, mine, other)


def exchange(blocks):
    return lax.all_to_all(blocks, "attn", split_axis=0, concat_axis=0, tiled=True)


def swap(block):
    return lax.ppermute(block, "expert", [(0, 1), (1, 0)])


def shards(
    queries,
    key_cache,
    value_cache,
    new_key,
    new_value,
    cache_length,
    residual,
    out_weight,
    ln_gain,
    gate_weight,
    up_weight,
    down_weight,
    routes,
    route_weight,
):
    count = lax.axis_size("attn")
    sharers = count // HELD
    capacity = routes.shape[0] * TOP // EXPERTS * 2
    place = lax.axis_index("attn").astype(jnp.int32).reshape(1)

    earlier = order(place, routes.shape[0])
    spread, own, taken, slots = prepare(
        place, sharers, capacity, earlier, routes.T, route_weight.T, queries, new_key
    )
    attended = exchange(
        attend(count, spread, own, key_cache, value_cache, new_value, cache_length, ln_gain)
    )
    mine, gains = project(attended, out_weight)
    stream, chosen = pick(sharers, count, mine, swap(mine), residual, taken)
    outgoing = run_experts(
        slots, exchange(chosen), gains, gate_weight.T, up_weight.T, down_weight
    )
    combined = combine(sharers, taken, exchange(outgoing))
    attn_stream, expert_out = finish(stream, combined, swap(combined))
    return (attn_stream, expert_out)


def solution(mesh):
    count = mesh.shape["attn"]
    fits = D // count % 256 == 0 and count % HELD == 0 and mesh.shape["expert"] == 2
    return jax.shard_map(
        shards if fits else shards_plain,
        mesh=mesh,
        in_specs=(
            P(("group", "attn"), "expert"),
            P(("group", "attn"), None, "expert"),
            P(("group", "attn"), None, "expert"),
            P(("group", "attn"), "expert"),
            P(("group", "attn"), "expert"),
            P(("group", "attn")),
            P("group", "attn"),
            P("expert", "attn"),
            P("attn"),
            P(None, ("attn", "expert")),
            P(None, ("attn", "expert")),
            P(("attn", "expert"), None),
            P("group", None),
            P("group", None),
        ),
        out_specs=(P("group", "attn"), P("group", "attn")),
        check_vma=False,
    )
```

```python
import functools
import math

import jax
import jax.numpy as jnp
from jax import lax
from jax.experimental import pallas as pl
from jax.experimental.pallas import tpu as pltpu
from jax.sharding import PartitionSpec as P

D = 6144
HEADS = 48
KV_HEADS = 8
HEAD_DIM = 128
EXPERTS = 16
TOP = 4
HELD = 2


NEG_FILL = -1e30
EPSILON = 1e-05


def attend_local(queries, key_cache, value_cache, new_key, new_value, cache_length):
    row_count = queries.shape[0]
    kv_local = new_key.shape[1] // HEAD_DIM
    group = HEADS // KV_HEADS
    length_max = key_cache.shape[1]
    query_heads = queries.reshape(row_count, kv_local, group, HEAD_DIM)
    key_heads = key_cache.reshape(row_count, length_max, kv_local, HEAD_DIM)
    value_heads = value_cache.reshape(row_count, length_max, kv_local, HEAD_DIM)
    own_keys = new_key.reshape(row_count, kv_local, HEAD_DIM)
    own_values = new_value.reshape(row_count, kv_local, HEAD_DIM)
    scale = 1.0 / math.sqrt(HEAD_DIM)
    past = (
        jnp.einsum("rkgd,rlkd->rkgl", query_heads, key_heads, preferred_element_type=jnp.float32)
        * scale
    )
    valid = jnp.arange(length_max, dtype=jnp.int32)[None, :] < cache_length[:, None]
    past = jnp.where(valid[:, None, None, :], past, NEG_FILL)
    own = (
        jnp.einsum("rkgd,rkd->rkg", query_heads, own_keys, preferred_element_type=jnp.float32)
        * scale
    )
    largest = jnp.maximum(jnp.max(past, axis=3), own)
    past_weight = jnp.exp(past - largest[..., None])
    own_weight = jnp.exp(own - largest)
    total = jnp.sum(past_weight, axis=3) + own_weight
    past_prob = (past_weight / total[..., None]).astype(jnp.bfloat16)
    own_prob = (own_weight / total).astype(jnp.bfloat16)
    result = jnp.einsum(
        "rkgl,rlkd->rkgd", past_prob, value_heads, preferred_element_type=jnp.float32
    )
    result = (
        result
        + own_prob.astype(jnp.float32)[..., None] * own_values.astype(jnp.float32)[:, :, None, :]
    )
    return result.reshape(row_count, kv_local * group * HEAD_DIM).astype(jnp.bfloat16)


def selection(routes, route_weight, capacity):
    row_count = routes.shape[0]
    experts = jnp.arange(HELD, dtype=jnp.int32)
    match = routes[None, :, :] == experts[:, None, None]
    hit = jnp.any(match, axis=2)
    row_weight = jnp.sum(jnp.where(match, route_weight[None], 0.0), axis=2)
    earlier = jnp.arange(row_count)[:, None] < jnp.arange(row_count)[None, :]
    slot = jnp.sum(jnp.where(earlier[None] & hit[:, :, None], 1, 0), axis=1)
    taken = hit[:, None, :] & (slot[:, None, :] == jnp.arange(capacity, dtype=jnp.int32)[None, :, None])
    slot_weight = jnp.sum(jnp.where(taken, row_weight[:, None, :], 0.0), axis=2)
    return taken, slot_weight


def gather_attn(block):
    count = lax.axis_size("attn")
    copies = jnp.broadcast_to(block[None], (count,) + block.shape)
    return lax.all_to_all(copies, "attn", split_axis=0, concat_axis=0, tiled=True)


def pair_sum(block):
    return block + lax.ppermute(block, "expert", [(0, 1), (1, 0)])


def shards_plain(
    queries,
    key_cache,
    value_cache,
    new_key,
    new_value,
    cache_length,
    residual,
    out_weight,
    ln_gain,
    gate_weight,
    up_weight,
    down_weight,
    routes,
    route_weight,
):
    attn_count = lax.axis_size("attn")
    core_count = lax.axis_size("expert")
    sharers = attn_count * core_count // HELD
    my_expert = (lax.axis_index("attn") * core_count + lax.axis_index("expert")) // sharers
    dest_expert = [index * core_count // sharers for index in range(attn_count)]
    row_count = routes.shape[0]
    capacity = row_count * TOP // EXPERTS * 2
    cols = residual.shape[1]

    taken, slot_weight = selection(routes, route_weight, capacity)
    pick = taken.astype(jnp.bfloat16)

    gains = gather_attn(ln_gain)

    attended = attend_local(queries, key_cache, value_cache, new_key, new_value, cache_length)
    whole = gather_attn(attended).reshape(row_count, -1)
    partial_proj = jnp.dot(whole, out_weight, preferred_element_type=jnp.float32)
    head_total = pair_sum(partial_proj)
    attn_stream = (residual.astype(jnp.float32) + head_total).astype(jnp.bfloat16)

    chosen = jnp.einsum(
        "esr,rd->esd", pick, attn_stream, preferred_element_type=jnp.float32
    ).astype(jnp.bfloat16)
    outgoing = jnp.stack([chosen[index] for index in dest_expert])
    rows = lax.all_to_all(outgoing, "attn", split_axis=0, concat_axis=0, tiled=True)
    wide = rows.astype(jnp.float32)
    row_mean = jnp.sum(wide, axis=(0, 2)) / D
    row_var = jnp.sum(wide * wide, axis=(0, 2)) / D - row_mean * row_mean
    normed = (
        (wide - row_mean[None, :, None])
        * lax.rsqrt(row_var + EPSILON)[None, :, None]
        * gains.reshape(attn_count, 1, cols)
    ).astype(jnp.bfloat16)
    gate_val = jnp.einsum(
        "asd,adf->sf", normed, gate_weight.reshape(attn_count, cols, -1),
        preferred_element_type=jnp.float32,
    )
    up_val = jnp.einsum(
        "asd,adf->sf", normed, up_weight.reshape(attn_count, cols, -1),
        preferred_element_type=jnp.float32,
    )
    hidden = (jax.nn.silu(gate_val) * up_val).astype(jnp.bfloat16)
    piece = jnp.dot(hidden, down_weight, preferred_element_type=jnp.float32)
    mine = jnp.take(slot_weight, my_expert, axis=0)
    piece = (piece * mine[:, None]).astype(jnp.bfloat16)
    returned = lax.all_to_all(
        piece.reshape(capacity, attn_count, cols).swapaxes(0, 1),
        "attn", split_axis=0, concat_axis=0, tiled=True,
    )
    spread = jnp.stack([pick[index] for index in dest_expert])
    combined = jnp.einsum(
        "asr,asd->rd", spread, returned, preferred_element_type=jnp.float32
    )
    expert_out = pair_sum(combined).astype(jnp.bfloat16)
    return (attn_stream, expert_out)


MIB = 1024 * 1024
EXCHANGE_FLOPS = 10**10
VMEM_SPEC = pl.BlockSpec(memory_space=pltpu.VMEM)
SMEM_SPEC = pl.BlockSpec(memory_space=pltpu.SMEM)
HBM_SPEC = pl.BlockSpec(memory_space=pltpu.HBM)


def call(kernel, outs, in_specs, scratch, flops, nbytes, vmem_mib):
    single = not isinstance(outs, (list, tuple))
    return pl.pallas_call(
        kernel,
        out_shape=outs,
        in_specs=in_specs,
        out_specs=VMEM_SPEC if single else [VMEM_SPEC] * len(outs),
        scratch_shapes=scratch,
        cost_estimate=pl.CostEstimate(flops=flops, bytes_accessed=nbytes, transcendentals=0),
        compiler_params=pltpu.CompilerParams(vmem_limit_bytes=vmem_mib * MIB),
    )


def order_kernel(place_ref, out_ref):
    rows = out_ref.shape[0]
    before = lax.broadcasted_iota(jnp.int32, (rows, rows), 0) < lax.broadcasted_iota(
        jnp.int32, (rows, rows), 1
    )
    out_ref[...] = jnp.where(before & (place_ref[0] >= 0), 1.0, 0.0).astype(jnp.bfloat16)


def order(place, rows):
    return call(
        order_kernel,
        jax.ShapeDtypeStruct((rows, rows), jnp.bfloat16),
        [SMEM_SPEC],
        [],
        EXCHANGE_FLOPS, rows * rows * 2, 2,
    )(place)


def expert_rows(routes, earlier, expert, capacity):
    row_count = routes.shape[1]
    hit = jnp.max((routes == expert).astype(jnp.float32), axis=0, keepdims=True)
    slot = jnp.dot(
        jnp.broadcast_to(hit, (8, row_count)).astype(jnp.bfloat16),
        earlier,
        preferred_element_type=jnp.float32,
    )[:1]
    place = lax.broadcasted_iota(jnp.int32, (capacity, row_count), 0).astype(jnp.float32)
    return jnp.where((slot == place) & (hit > 0.5), 1.0, 0.0)


def prepare_kernel(sharers, place_ref, length_ref, earlier_ref, routes_ref, weight_ref, query_ref,
                   own_key_ref, spread_ref, own_ref, limit_ref, taken_ref, slot_ref, query_rows,
                   key_rows):
    row_count = query_ref.shape[0]
    kv_local = own_key_ref.shape[1] // HEAD_DIM
    group = HEADS // KV_HEADS
    heads = kv_local * group
    for g in range(kv_local):
        own_key = own_key_ref[:, g * HEAD_DIM : (g + 1) * HEAD_DIM].astype(jnp.float32)
        for i in range(group):
            index = g * group + i
            rows = pl.ds(index * row_count, row_count)
            query_rows[rows, :] = query_ref[
                :, index * HEAD_DIM : (index + 1) * HEAD_DIM
            ].astype(jnp.float32)
            key_rows[rows, :] = own_key
    scale = 1.0 / math.sqrt(HEAD_DIM)
    head = lax.broadcasted_iota(jnp.int32, (heads, 1), 0) // group
    for r in range(row_count):
        strided = pl.ds(r, heads, stride=row_count)
        query = query_rows[strided, :]
        own = jnp.sum(query * key_rows[strided, :], axis=1, keepdims=True) * scale
        own_ref[r] = jnp.broadcast_to(own, (heads, HEAD_DIM))
        limit_ref[r] = jnp.full((heads, HEAD_DIM), length_ref[r], jnp.int32)
        spread_ref[r] = jnp.concatenate(
            [jnp.where(head == g, query, 0.0) for g in range(kv_local)], axis=1
        ).astype(jnp.bfloat16)
    routes = routes_ref[...]
    capacity = slot_ref.shape[0]
    taken = [expert_rows(routes, earlier_ref[...], e, capacity) for e in range(HELD)]
    for e in range(HELD):
        taken_ref[e] = taken[e]
    first = place_ref[0] // 4 < sharers
    expert = jnp.where(first, 0, 1)
    row_weight = jnp.sum(
        jnp.where(routes == expert, weight_ref[...], 0.0), axis=0, keepdims=True
    )
    mine = jnp.where(first, taken[0], taken[1])
    slot_ref[...] = jnp.broadcast_to(
        jnp.sum(mine * row_weight, axis=1, keepdims=True), slot_ref.shape
    )


def prepare(
    place, sharers, capacity, cache_length, earlier, routes, route_weight, queries, new_key
):
    row_count, width = queries.shape
    heads = width // HEAD_DIM
    table = pltpu.VMEM((heads * row_count, HEAD_DIM), jnp.float32)
    return call(
        functools.partial(prepare_kernel, sharers),
        [
            jax.ShapeDtypeStruct((row_count, heads, new_key.shape[1]), jnp.bfloat16),
            jax.ShapeDtypeStruct((row_count, heads, HEAD_DIM), jnp.float32),
            jax.ShapeDtypeStruct((row_count, heads, HEAD_DIM), jnp.int32),
            jax.ShapeDtypeStruct((HELD, capacity, routes.shape[1]), jnp.float32),
            jax.ShapeDtypeStruct((capacity, HEAD_DIM), jnp.float32),
        ],
        [SMEM_SPEC] * 2 + [VMEM_SPEC] * 5,
        [table, table],
        queries.size * 8, queries.size * 16, 4,
    )(place, cache_length, earlier, routes, route_weight, queries, new_key)


def score_kernel(spread_ref, own_ref, limit_ref, key_ref, probs_ref, own_probs_ref):
    row_count, heads, length_max = probs_ref.shape
    scale = 1.0 / math.sqrt(HEAD_DIM)
    contract = (((1,), (1,)), ((), ()))
    position = lax.broadcasted_iota(jnp.int32, (heads, length_max), 1)
    for r in range(row_count):
        scores = lax.dot_general(
            spread_ref[r], key_ref[r], contract, preferred_element_type=jnp.float32
        )
        past = jnp.where(position < limit_ref[r, :, :1], scores * scale, NEG_FILL)
        own = own_ref[r, :, :1]
        largest = jnp.maximum(jnp.max(past, axis=1, keepdims=True), own)
        weight = jnp.exp(past - largest)
        own_weight = jnp.exp(own - largest)
        inverse = 1.0 / (jnp.sum(weight, axis=1, keepdims=True) + own_weight)
        probs_ref[r] = (weight * inverse).astype(jnp.bfloat16)
        own_prob = (own_weight * inverse).astype(jnp.bfloat16).astype(jnp.float32)
        own_probs_ref[r] = jnp.broadcast_to(own_prob, own_probs_ref.shape[1:])


def value_kernel(probs_ref, own_ref, value_ref, own_value_ref, gain_ref, out_ref, value_rows,
                 result_rows):
    row_count, length_max, width = value_ref.shape
    kv_local = width // HEAD_DIM
    group = HEADS // KV_HEADS
    heads = kv_local * group
    for g in range(kv_local):
        own_value = own_value_ref[:, g * HEAD_DIM : (g + 1) * HEAD_DIM].astype(jnp.float32)
        for i in range(group):
            value_rows[pl.ds((g * group + i) * row_count, row_count), :] = own_value
    head = lax.broadcasted_iota(jnp.int32, (heads, 1), 0) // group
    for r in range(row_count):
        strided = pl.ds(r, heads, stride=row_count)
        product = jnp.dot(probs_ref[r], value_ref[r], preferred_element_type=jnp.float32)
        total = own_ref[r] * value_rows[strided, :]
        for g in range(kv_local):
            lanes = slice(g * HEAD_DIM, (g + 1) * HEAD_DIM)
            total = total + jnp.where(head == g, product[:, lanes], 0.0)
        result_rows[strided, :] = total
    for index in range(heads):
        rows = result_rows[pl.ds(index * row_count, row_count), :].astype(jnp.bfloat16)
        for copy in range(out_ref.shape[0]):
            out_ref[copy, :, index * HEAD_DIM : (index + 1) * HEAD_DIM] = rows
    gain_row = gain_ref[...].reshape(1, -1)
    half = gain_row.shape[1] // 2
    row = lax.broadcasted_iota(jnp.int32, (row_count, half), 0)
    left = jnp.broadcast_to(gain_row[:, :half], (row_count, half))
    right = jnp.broadcast_to(gain_row[:, half:], (row_count, half))
    gain = jnp.where(row % 2 == 0, left, right)
    upper = gain.astype(jnp.bfloat16).astype(jnp.float32)
    parts = jnp.where(row < 2, upper, gain - upper).astype(jnp.bfloat16)
    for copy in range(out_ref.shape[0]):
        out_ref[copy, :, heads * HEAD_DIM :] = parts


def attend(count, spread, own, limit, key_cache, value_cache, new_value, gain):
    row_count, heads, _ = spread.shape
    length_max = key_cache.shape[1]
    table = pltpu.VMEM((heads * row_count, HEAD_DIM), jnp.float32)
    probs, own_probs = call(
        score_kernel,
        [
            jax.ShapeDtypeStruct((row_count, heads, length_max), jnp.bfloat16),
            jax.ShapeDtypeStruct((row_count, heads, HEAD_DIM), jnp.float32),
        ],
        [VMEM_SPEC] * 4,
        [],
        2 * key_cache.size * heads, key_cache.size * 2, 8,
    )(spread, own, limit, key_cache)
    width = heads * HEAD_DIM + gain.shape[0] // 2
    return call(
        value_kernel,
        jax.ShapeDtypeStruct((count, row_count, width), jnp.bfloat16),
        [VMEM_SPEC] * 5,
        [table, table],
        EXCHANGE_FLOPS, value_cache.size * 2, 8,
    )(probs, own_probs, value_cache, new_value, gain)


def project_kernel(pieces, weight_ref, out_ref, gain_ref, stack):
    count, rows, _ = pieces.shape
    width = weight_ref.shape[0]
    half = gain_ref.shape[1] // 2
    for k in range(count):
        stack[pl.ds(k * rows, rows), :] = pieces[k, :, :width].astype(jnp.float32)
        parts = pieces[k, :, width:].astype(jnp.float32)
        gain_ref[pl.ds(k, 1), :half] = parts[0:1] + parts[2:3]
        gain_ref[pl.ds(k, 1), half:] = parts[1:2] + parts[3:4]
    out_ref[...] = jnp.dot(
        stack[...].astype(jnp.bfloat16), weight_ref[...], preferred_element_type=jnp.float32
    )


def project(pieces, out_weight):
    count, rows, _ = pieces.shape
    depth, cols = out_weight.shape
    return call(
        project_kernel,
        [
            jax.ShapeDtypeStruct((rows * count, cols), jnp.float32),
            jax.ShapeDtypeStruct((count, cols), jnp.float32),
        ],
        [VMEM_SPEC, VMEM_SPEC],
        [pltpu.VMEM((rows * count, depth), jnp.float32)],
        EXCHANGE_FLOPS, out_weight.size * 2, 10,
    )(pieces, out_weight)


def pick_kernel(sharers, place_ref, mine_ref, other_ref, residual_ref, taken_ref, stream_ref,
                *out_refs):
    stream = (
        residual_ref[...].astype(jnp.float32) + (mine_ref[...] + other_ref[...])
    ).astype(jnp.bfloat16)
    stream_ref[...] = stream
    chosen = [
        jnp.dot(
            taken_ref[e].astype(jnp.bfloat16), stream, preferred_element_type=jnp.float32
        )
        for e in range(HELD)
    ]
    high = place_ref[0] // 4
    for k, out_ref in enumerate(out_refs):
        out_ref[...] = jnp.where((high ^ k) < sharers, chosen[0], chosen[1]).astype(jnp.bfloat16)


def pick(place, sharers, highs, mine, other, residual, taken):
    rows, cols = mine.shape
    return call(
        functools.partial(pick_kernel, sharers),
        [jax.ShapeDtypeStruct((rows, cols), jnp.bfloat16)]
        + [jax.ShapeDtypeStruct((taken.shape[1], cols), jnp.bfloat16)] * highs,
        [SMEM_SPEC] + [VMEM_SPEC] * 4,
        [],
        2 * HELD * taken.shape[1] * rows * cols, rows * cols * 12, 4,
    )(place, mine, other, residual, taken)


def stack_kernel(place_ref, *refs):
    out_ref = refs[-1]
    high = place_ref[0] // 4
    for k, block in enumerate(refs[:-1]):
        out_ref[high ^ k] = block[...]


def stack(place, blocks):
    return call(
        stack_kernel,
        jax.ShapeDtypeStruct((len(blocks),) + blocks[0].shape, blocks[0].dtype),
        [SMEM_SPEC] + [VMEM_SPEC] * len(blocks),
        [],
        0, 4 * len(blocks) * blocks[0].size, 4,
    )(place, *blocks)


def ordered(low, mine, other):
    return jnp.where(low == 0, mine, other), jnp.where(low == 0, other, mine)


def expert_kernel(place_ref, slot_ref, mine_ref, other_ref, mine_given_ref, other_given_ref, gains,
                  gate_ref, up_ref, down_ref, keep_ref, give_ref):
    highs, capacity, cols = mine_ref.shape
    core = place_ref[0] % 2
    low = place_ref[0] // 2 % 2
    blocks = []
    for k in range(highs):
        mine = jnp.where(core == 1, mine_ref[k], mine_given_ref[k])
        other = jnp.where(core == 1, other_ref[k], other_given_ref[k])
        blocks.extend(ordered(low, mine.astype(jnp.float32), other.astype(jnp.float32)))
    first = second = 0.0
    for wide in blocks:
        first = first + wide
        second = second + wide * wide
    row_mean = jnp.sum(first, axis=1, keepdims=True) / D
    row_var = jnp.sum(second, axis=1, keepdims=True) / D - row_mean * row_mean
    inverse = lax.rsqrt(row_var + EPSILON)
    contract = (((1,), (1,)), ((), ()))
    gate_val = up_val = 0.0
    for k, wide in enumerate(blocks):
        columns = slice(k * cols, (k + 1) * cols)
        normed = ((wide - row_mean) * inverse * gains[pl.ds(k, 1), :]).astype(jnp.bfloat16)
        gate_val = gate_val + lax.dot_general(
            gate_ref[:, columns], normed, contract, preferred_element_type=jnp.float32
        )
        up_val = up_val + lax.dot_general(
            up_ref[:, columns], normed, contract, preferred_element_type=jnp.float32
        )
    hidden = (gate_val / (1.0 + jnp.exp(-gate_val)) * up_val).T.astype(jnp.bfloat16)
    slot_weight = slot_ref[:, :1]
    for k in range(highs):
        columns = slice(2 * k * cols, 2 * (k + 1) * cols)
        both = (
            jnp.dot(hidden, down_ref[:, columns], preferred_element_type=jnp.float32)
            * slot_weight
        ).astype(jnp.bfloat16)
        keep_ref[k], give_ref[k] = ordered(low, both[:, :cols], both[:, cols:])


def run_experts(place, slots, blocks, gains, gate, up, down):
    return call(
        expert_kernel,
        [jax.ShapeDtypeStruct(blocks[0].shape, jnp.bfloat16)] * 2,
        [SMEM_SPEC] + [VMEM_SPEC] * (5 + len(blocks)),
        [],
        6 * blocks[0].shape[1] * gate.size, gate.size * 6, 14,
    )(place, slots, *blocks, gains, gate, up, down)


def add_kernel(mine_ref, given_ref, out_ref):
    out_ref[...] = (
        mine_ref[...].astype(jnp.float32) + given_ref[...].astype(jnp.float32)
    ).astype(jnp.bfloat16)


def add(mine, given):
    return call(
        add_kernel,
        jax.ShapeDtypeStruct(mine.shape, jnp.bfloat16),
        [VMEM_SPEC] * 2,
        [],
        mine.size, mine.size * 6, 4,
    )(mine, given)


def send_kernel(place_ref, *refs):
    highs = refs[0].shape[0]
    terms, out_refs = refs[:-highs], refs[-highs:]
    high = place_ref[0] // 4
    for k, out_ref in enumerate(out_refs):
        total = 0.0
        for term in terms:
            total = total + term[high ^ k].astype(jnp.float32)
        out_ref[...] = total.astype(jnp.bfloat16)


def send_blocks(place, *terms):
    highs, capacity, cols = terms[0].shape
    return call(
        send_kernel,
        [jax.ShapeDtypeStruct((capacity, cols), jnp.bfloat16)] * highs,
        [SMEM_SPEC] + [VMEM_SPEC] * len(terms),
        [],
        terms[0].size, terms[0].size * 8, 4,
    )(place, *terms)


def combine_kernel(sharers, place_ref, taken_ref, *refs):
    pieces, out_ref = refs[:-1], refs[-1]
    high = place_ref[0] // 4
    spread = [
        jnp.where((high ^ k) < sharers, taken_ref[0], taken_ref[1]) for k in range(len(pieces))
    ]
    out_ref[...] = lax.dot_general(
        jnp.concatenate(spread, axis=0).astype(jnp.bfloat16),
        jnp.concatenate([piece[...] for piece in pieces], axis=0),
        (((0,), (0,)), ((), ())),
        preferred_element_type=jnp.float32,
    ).astype(jnp.bfloat16)


def combine(place, sharers, taken, pieces):
    capacity, cols = pieces[0].shape
    rows = taken.shape[2]
    return call(
        functools.partial(combine_kernel, sharers),
        jax.ShapeDtypeStruct((rows, cols), jnp.bfloat16),
        [SMEM_SPEC] + [VMEM_SPEC] * (1 + len(pieces)),
        [],
        2 * rows * capacity * len(pieces) * cols, (len(pieces) * capacity + rows) * 2 * cols, 4,
    )(place, taken, *pieces)


def finish_kernel(place_ref, stream_ref, mine_ref, given_ref, stream_out_ref, out_ref):
    stream_out_ref[...] = stream_ref[...]
    out_ref[...] = jnp.where(place_ref[0] % 2 == 1, mine_ref[...], given_ref[...])


def finish(place, stream, mine, given):
    return call(
        finish_kernel,
        [jax.ShapeDtypeStruct(stream.shape, jnp.bfloat16)] * 2,
        [SMEM_SPEC] + [VMEM_SPEC] * 3,
        [],
        mine.size, mine.size * 10, 4,
    )(place, stream, mine, given)


def exchange(blocks):
    return lax.all_to_all(blocks, "attn", split_axis=0, concat_axis=0, tiled=True)


def crossed(block, count, mask):
    pairs = [(2 * index + 1, 2 * (index ^ mask) + 1) for index in range(count)]
    return lax.ppermute(block, ("attn", "expert"), pairs)


def spread_high(blocks, count):
    return [blocks[0]] + [crossed(blocks[k], count, 2 * k) for k in range(1, count // 2)]


def hand(block, source):
    return lax.ppermute(block, "expert", [(source, 1 - source)])


def swap(block):
    return lax.ppermute(block, "expert", [(0, 1), (1, 0)])


def shards(
    queries,
    key_cache,
    value_cache,
    new_key,
    new_value,
    cache_length,
    residual,
    out_weight,
    ln_gain,
    gate_weight,
    up_weight,
    down_weight,
    routes,
    route_weight,
):
    count = lax.axis_size("attn")
    highs = count // 2
    sharers = highs // HELD
    capacity = routes.shape[0] * TOP // EXPERTS * 2
    place = lax.axis_index(("attn", "expert")).astype(jnp.int32).reshape(1)

    earlier = order(place, routes.shape[0])
    spread, own, limit, taken, slots = prepare(
        place, sharers, capacity, cache_length, earlier, routes.T, route_weight.T, queries, new_key
    )
    attended = exchange(
        attend(count, spread, own, limit, key_cache, value_cache, new_value, ln_gain)
    )
    mine, gains = project(attended, out_weight)
    stream, *chosen = pick(place, sharers, highs, mine, swap(mine), residual, taken)
    block = stack(place, spread_high(chosen, count))
    other = crossed(block, count, 1)
    keep, give = run_experts(
        place, slots, (block, other, hand(block, 1), hand(other, 1)), gains,
        gate_weight.T, up_weight.T, down_weight,
    )
    keep_given = hand(keep, 0)
    arrived = crossed(add(give, hand(give, 0)), count, 1)
    outgoing = send_blocks(place, keep, keep_given, arrived)
    combined = combine(place, sharers, taken, spread_high(outgoing, count))
    attn_stream, expert_out = finish(place, stream, combined, hand(combined, 1))
    return (attn_stream, expert_out)


def solution(mesh):
    count = mesh.shape["attn"]
    fits = D // count % 256 == 0 and count % (2 * HELD) == 0 and count & (count - 1) == 0
    fits = fits and mesh.shape["expert"] == 2
    return jax.shard_map(
        shards if fits else shards_plain,
        mesh=mesh,
        in_specs=(
            P(("group", "attn"), "expert"),
            P(("group", "attn"), None, "expert"),
            P(("group", "attn"), None, "expert"),
            P(("group", "attn"), "expert"),
            P(("group", "attn"), "expert"),
            P(("group", "attn")),
            P("group", "attn"),
            P("expert", "attn"),
            P("attn"),
            P(None, ("attn", "expert")),
            P(None, ("attn", "expert")),
            P(("attn", "expert"), None),
            P("group", None),
            P("group", None),
        ),
        out_specs=(P("group", "attn"), P("group", "attn")),
        check_vma=False,
    )
```

```python
import functools
import math

import jax
import jax.numpy as jnp
from jax import lax
from jax.experimental import pallas as pl
from jax.experimental.pallas import tpu as pltpu
from jax.sharding import PartitionSpec as P

D = 6144
HEADS = 48
KV_HEADS = 8
HEAD_DIM = 128
EXPERTS = 16
TOP = 4
HELD = 2


NEG_FILL = -1e30
EPSILON = 1e-05


def attend_local(queries, key_cache, value_cache, new_key, new_value, cache_length):
    row_count = queries.shape[0]
    kv_local = new_key.shape[1] // HEAD_DIM
    group = HEADS // KV_HEADS
    length_max = key_cache.shape[1]
    query_heads = queries.reshape(row_count, kv_local, group, HEAD_DIM)
    key_heads = key_cache.reshape(row_count, length_max, kv_local, HEAD_DIM)
    value_heads = value_cache.reshape(row_count, length_max, kv_local, HEAD_DIM)
    own_keys = new_key.reshape(row_count, kv_local, HEAD_DIM)
    own_values = new_value.reshape(row_count, kv_local, HEAD_DIM)
    scale = 1.0 / math.sqrt(HEAD_DIM)
    past = (
        jnp.einsum("rkgd,rlkd->rkgl", query_heads, key_heads, preferred_element_type=jnp.float32)
        * scale
    )
    valid = jnp.arange(length_max, dtype=jnp.int32)[None, :] < cache_length[:, None]
    past = jnp.where(valid[:, None, None, :], past, NEG_FILL)
    own = (
        jnp.einsum("rkgd,rkd->rkg", query_heads, own_keys, preferred_element_type=jnp.float32)
        * scale
    )
    largest = jnp.maximum(jnp.max(past, axis=3), own)
    past_weight = jnp.exp(past - largest[..., None])
    own_weight = jnp.exp(own - largest)
    total = jnp.sum(past_weight, axis=3) + own_weight
    past_prob = (past_weight / total[..., None]).astype(jnp.bfloat16)
    own_prob = (own_weight / total).astype(jnp.bfloat16)
    result = jnp.einsum(
        "rkgl,rlkd->rkgd", past_prob, value_heads, preferred_element_type=jnp.float32
    )
    result = (
        result
        + own_prob.astype(jnp.float32)[..., None] * own_values.astype(jnp.float32)[:, :, None, :]
    )
    return result.reshape(row_count, kv_local * group * HEAD_DIM).astype(jnp.bfloat16)


def selection(routes, route_weight, capacity):
    row_count = routes.shape[0]
    experts = jnp.arange(HELD, dtype=jnp.int32)
    match = routes[None, :, :] == experts[:, None, None]
    hit = jnp.any(match, axis=2)
    row_weight = jnp.sum(jnp.where(match, route_weight[None], 0.0), axis=2)
    earlier = jnp.arange(row_count)[:, None] < jnp.arange(row_count)[None, :]
    slot = jnp.sum(jnp.where(earlier[None] & hit[:, :, None], 1, 0), axis=1)
    taken = hit[:, None, :] & (slot[:, None, :] == jnp.arange(capacity, dtype=jnp.int32)[None, :, None])
    slot_weight = jnp.sum(jnp.where(taken, row_weight[:, None, :], 0.0), axis=2)
    return taken, slot_weight


def gather_attn(block):
    count = lax.axis_size("attn")
    copies = jnp.broadcast_to(block[None], (count,) + block.shape)
    return lax.all_to_all(copies, "attn", split_axis=0, concat_axis=0, tiled=True)


def pair_sum(block):
    return block + lax.ppermute(block, "expert", [(0, 1), (1, 0)])


def shards_plain(
    queries,
    key_cache,
    value_cache,
    new_key,
    new_value,
    cache_length,
    residual,
    out_weight,
    ln_gain,
    gate_weight,
    up_weight,
    down_weight,
    routes,
    route_weight,
):
    attn_count = lax.axis_size("attn")
    core_count = lax.axis_size("expert")
    sharers = attn_count * core_count // HELD
    my_expert = (lax.axis_index("attn") * core_count + lax.axis_index("expert")) // sharers
    dest_expert = [index * core_count // sharers for index in range(attn_count)]
    row_count = routes.shape[0]
    capacity = row_count * TOP // EXPERTS * 2
    cols = residual.shape[1]

    taken, slot_weight = selection(routes, route_weight, capacity)
    pick = taken.astype(jnp.bfloat16)

    gains = gather_attn(ln_gain)

    attended = attend_local(queries, key_cache, value_cache, new_key, new_value, cache_length)
    whole = gather_attn(attended).reshape(row_count, -1)
    partial_proj = jnp.dot(whole, out_weight, preferred_element_type=jnp.float32)
    head_total = pair_sum(partial_proj)
    attn_stream = (residual.astype(jnp.float32) + head_total).astype(jnp.bfloat16)

    chosen = jnp.einsum(
        "esr,rd->esd", pick, attn_stream, preferred_element_type=jnp.float32
    ).astype(jnp.bfloat16)
    outgoing = jnp.stack([chosen[index] for index in dest_expert])
    rows = lax.all_to_all(outgoing, "attn", split_axis=0, concat_axis=0, tiled=True)
    wide = rows.astype(jnp.float32)
    row_mean = jnp.sum(wide, axis=(0, 2)) / D
    row_var = jnp.sum(wide * wide, axis=(0, 2)) / D - row_mean * row_mean
    normed = (
        (wide - row_mean[None, :, None])
        * lax.rsqrt(row_var + EPSILON)[None, :, None]
        * gains.reshape(attn_count, 1, cols)
    ).astype(jnp.bfloat16)
    gate_val = jnp.einsum(
        "asd,adf->sf", normed, gate_weight.reshape(attn_count, cols, -1),
        preferred_element_type=jnp.float32,
    )
    up_val = jnp.einsum(
        "asd,adf->sf", normed, up_weight.reshape(attn_count, cols, -1),
        preferred_element_type=jnp.float32,
    )
    hidden = (jax.nn.silu(gate_val) * up_val).astype(jnp.bfloat16)
    piece = jnp.dot(hidden, down_weight, preferred_element_type=jnp.float32)
    mine = jnp.take(slot_weight, my_expert, axis=0)
    piece = (piece * mine[:, None]).astype(jnp.bfloat16)
    returned = lax.all_to_all(
        piece.reshape(capacity, attn_count, cols).swapaxes(0, 1),
        "attn", split_axis=0, concat_axis=0, tiled=True,
    )
    spread = jnp.stack([pick[index] for index in dest_expert])
    combined = jnp.einsum(
        "asr,asd->rd", spread, returned, preferred_element_type=jnp.float32
    )
    expert_out = pair_sum(combined).astype(jnp.bfloat16)
    return (attn_stream, expert_out)


MIB = 1024 * 1024
EXCHANGE_FLOPS = 10**10
VMEM_SPEC = pl.BlockSpec(memory_space=pltpu.VMEM)
SMEM_SPEC = pl.BlockSpec(memory_space=pltpu.SMEM)
HBM_SPEC = pl.BlockSpec(memory_space=pltpu.HBM)


def call(kernel, outs, in_specs, scratch, flops, nbytes, vmem_mib):
    single = not isinstance(outs, (list, tuple))
    return pl.pallas_call(
        kernel,
        out_shape=outs,
        in_specs=in_specs,
        out_specs=VMEM_SPEC if single else [VMEM_SPEC] * len(outs),
        scratch_shapes=scratch,
        cost_estimate=pl.CostEstimate(flops=flops, bytes_accessed=nbytes, transcendentals=0),
        compiler_params=pltpu.CompilerParams(vmem_limit_bytes=vmem_mib * MIB),
    )


def order_kernel(place_ref, out_ref):
    rows = out_ref.shape[0]
    before = lax.broadcasted_iota(jnp.int32, (rows, rows), 0) < lax.broadcasted_iota(
        jnp.int32, (rows, rows), 1
    )
    out_ref[...] = jnp.where(before & (place_ref[0] >= 0), 1.0, 0.0).astype(jnp.bfloat16)


def order(place, rows):
    return call(
        order_kernel,
        jax.ShapeDtypeStruct((rows, rows), jnp.bfloat16),
        [SMEM_SPEC],
        [],
        EXCHANGE_FLOPS, rows * rows * 2, 2,
    )(place)


def expert_rows(routes, earlier, expert, capacity):
    row_count = routes.shape[1]
    hit = jnp.max((routes == expert).astype(jnp.float32), axis=0, keepdims=True)
    slot = jnp.dot(
        jnp.broadcast_to(hit, (8, row_count)).astype(jnp.bfloat16),
        earlier,
        preferred_element_type=jnp.float32,
    )[:1]
    place = lax.broadcasted_iota(jnp.int32, (capacity, row_count), 0).astype(jnp.float32)
    return jnp.where((slot == place) & (hit > 0.5), 1.0, 0.0)


def prepare_kernel(sharers, place_ref, length_ref, earlier_ref, routes_ref, weight_ref, query_ref,
                   own_key_ref, spread_ref, own_ref, limit_ref, taken_ref, slot_ref, query_rows,
                   key_rows):
    row_count = query_ref.shape[0]
    kv_local = own_key_ref.shape[1] // HEAD_DIM
    group = HEADS // KV_HEADS
    heads = kv_local * group
    for g in range(kv_local):
        own_key = own_key_ref[:, g * HEAD_DIM : (g + 1) * HEAD_DIM].astype(jnp.float32)
        for i in range(group):
            index = g * group + i
            rows = pl.ds(index * row_count, row_count)
            query_rows[rows, :] = query_ref[
                :, index * HEAD_DIM : (index + 1) * HEAD_DIM
            ].astype(jnp.float32)
            key_rows[rows, :] = own_key
    scale = 1.0 / math.sqrt(HEAD_DIM)
    head = lax.broadcasted_iota(jnp.int32, (heads, 1), 0) // group
    for r in range(row_count):
        strided = pl.ds(r, heads, stride=row_count)
        query = query_rows[strided, :]
        own = jnp.sum(query * key_rows[strided, :], axis=1, keepdims=True) * scale
        own_ref[r] = jnp.broadcast_to(own, (heads, HEAD_DIM))
        limit_ref[r] = jnp.full((heads, HEAD_DIM), length_ref[r], jnp.int32)
        spread_ref[r] = jnp.concatenate(
            [jnp.where(head == g, query, 0.0) for g in range(kv_local)], axis=1
        ).astype(jnp.bfloat16)
    routes = routes_ref[...]
    capacity = slot_ref.shape[0]
    taken = [expert_rows(routes, earlier_ref[...], e, capacity) for e in range(HELD)]
    for e in range(HELD):
        taken_ref[e] = taken[e]
    first = place_ref[0] < sharers
    expert = jnp.where(first, 0, 1)
    row_weight = jnp.sum(
        jnp.where(routes == expert, weight_ref[...], 0.0), axis=0, keepdims=True
    )
    mine = jnp.where(first, taken[0], taken[1])
    slot_ref[...] = jnp.broadcast_to(
        jnp.sum(mine * row_weight, axis=1, keepdims=True), slot_ref.shape
    )


def prepare(
    place, sharers, capacity, cache_length, earlier, routes, route_weight, queries, new_key
):
    row_count, width = queries.shape
    heads = width // HEAD_DIM
    table = pltpu.VMEM((heads * row_count, HEAD_DIM), jnp.float32)
    return call(
        functools.partial(prepare_kernel, sharers),
        [
            jax.ShapeDtypeStruct((row_count, heads, new_key.shape[1]), jnp.bfloat16),
            jax.ShapeDtypeStruct((row_count, heads, HEAD_DIM), jnp.float32),
            jax.ShapeDtypeStruct((row_count, heads, HEAD_DIM), jnp.int32),
            jax.ShapeDtypeStruct((HELD, capacity, routes.shape[1]), jnp.float32),
            jax.ShapeDtypeStruct((capacity, HEAD_DIM), jnp.float32),
        ],
        [SMEM_SPEC] * 2 + [VMEM_SPEC] * 5,
        [table, table],
        queries.size * 8, queries.size * 16, 4,
    )(place, cache_length, earlier, routes, route_weight, queries, new_key)


def score_kernel(spread_ref, own_ref, limit_ref, key_ref, probs_ref, own_probs_ref):
    row_count, heads, length_max = probs_ref.shape
    scale = 1.0 / math.sqrt(HEAD_DIM)
    contract = (((1,), (1,)), ((), ()))
    position = lax.broadcasted_iota(jnp.int32, (heads, length_max), 1)
    for r in range(row_count):
        scores = lax.dot_general(
            spread_ref[r], key_ref[r], contract, preferred_element_type=jnp.float32
        )
        past = jnp.where(position < limit_ref[r, :, :1], scores * scale, NEG_FILL)
        own = own_ref[r, :, :1]
        largest = jnp.maximum(jnp.max(past, axis=1, keepdims=True), own)
        weight = jnp.exp(past - largest)
        own_weight = jnp.exp(own - largest)
        inverse = 1.0 / (jnp.sum(weight, axis=1, keepdims=True) + own_weight)
        probs_ref[r] = (weight * inverse).astype(jnp.bfloat16)
        own_prob = (own_weight * inverse).astype(jnp.bfloat16).astype(jnp.float32)
        own_probs_ref[r] = jnp.broadcast_to(own_prob, own_probs_ref.shape[1:])


def value_kernel(probs_ref, own_ref, value_ref, own_value_ref, gain_ref, out_ref, value_rows,
                 result_rows):
    row_count, length_max, width = value_ref.shape
    kv_local = width // HEAD_DIM
    group = HEADS // KV_HEADS
    heads = kv_local * group
    for g in range(kv_local):
        own_value = own_value_ref[:, g * HEAD_DIM : (g + 1) * HEAD_DIM].astype(jnp.float32)
        for i in range(group):
            value_rows[pl.ds((g * group + i) * row_count, row_count), :] = own_value
    head = lax.broadcasted_iota(jnp.int32, (heads, 1), 0) // group
    for r in range(row_count):
        strided = pl.ds(r, heads, stride=row_count)
        product = jnp.dot(probs_ref[r], value_ref[r], preferred_element_type=jnp.float32)
        total = own_ref[r] * value_rows[strided, :]
        for g in range(kv_local):
            lanes = slice(g * HEAD_DIM, (g + 1) * HEAD_DIM)
            total = total + jnp.where(head == g, product[:, lanes], 0.0)
        result_rows[strided, :] = total
    for index in range(heads):
        rows = result_rows[pl.ds(index * row_count, row_count), :].astype(jnp.bfloat16)
        for copy in range(out_ref.shape[0]):
            out_ref[copy, :, index * HEAD_DIM : (index + 1) * HEAD_DIM] = rows
    gain_row = gain_ref[...].reshape(1, -1)
    half = gain_row.shape[1] // 2
    row = lax.broadcasted_iota(jnp.int32, (row_count, half), 0)
    left = jnp.broadcast_to(gain_row[:, :half], (row_count, half))
    right = jnp.broadcast_to(gain_row[:, half:], (row_count, half))
    gain = jnp.where(row % 2 == 0, left, right)
    upper = gain.astype(jnp.bfloat16).astype(jnp.float32)
    parts = jnp.where(row < 2, upper, gain - upper).astype(jnp.bfloat16)
    for copy in range(out_ref.shape[0]):
        out_ref[copy, :, heads * HEAD_DIM :] = parts


def attend(count, spread, own, limit, key_cache, value_cache, new_value, gain):
    row_count, heads, _ = spread.shape
    length_max = key_cache.shape[1]
    table = pltpu.VMEM((heads * row_count, HEAD_DIM), jnp.float32)
    probs, own_probs = call(
        score_kernel,
        [
            jax.ShapeDtypeStruct((row_count, heads, length_max), jnp.bfloat16),
            jax.ShapeDtypeStruct((row_count, heads, HEAD_DIM), jnp.float32),
        ],
        [VMEM_SPEC] * 4,
        [],
        2 * key_cache.size * heads, key_cache.size * 2, 8,
    )(spread, own, limit, key_cache)
    width = heads * HEAD_DIM + gain.shape[0] // 2
    return call(
        value_kernel,
        jax.ShapeDtypeStruct((count, row_count, width), jnp.bfloat16),
        [VMEM_SPEC] * 5,
        [table, table],
        EXCHANGE_FLOPS, value_cache.size * 2, 8,
    )(probs, own_probs, value_cache, new_value, gain)


def project_kernel(pieces, weight_ref, out_ref, gain_ref, stack):
    count, rows, _ = pieces.shape
    width = weight_ref.shape[0]
    half = gain_ref.shape[1] // 2
    for k in range(count):
        stack[pl.ds(k * rows, rows), :] = pieces[k, :, :width].astype(jnp.float32)
        parts = pieces[k, :, width:].astype(jnp.float32)
        gain_ref[pl.ds(k, 1), :half] = parts[0:1] + parts[2:3]
        gain_ref[pl.ds(k, 1), half:] = parts[1:2] + parts[3:4]
    out_ref[...] = jnp.dot(
        stack[...].astype(jnp.bfloat16), weight_ref[...], preferred_element_type=jnp.float32
    )


def project(pieces, out_weight):
    count, rows, _ = pieces.shape
    depth, cols = out_weight.shape
    return call(
        project_kernel,
        [
            jax.ShapeDtypeStruct((rows * count, cols), jnp.float32),
            jax.ShapeDtypeStruct((count, cols), jnp.float32),
        ],
        [VMEM_SPEC, VMEM_SPEC],
        [pltpu.VMEM((rows * count, depth), jnp.float32)],
        EXCHANGE_FLOPS, out_weight.size * 2, 10,
    )(pieces, out_weight)


def pick_kernel(sharers, mine_ref, other_ref, residual_ref, taken_ref, stream_ref, out_ref):
    stream = (
        residual_ref[...].astype(jnp.float32) + (mine_ref[...] + other_ref[...])
    ).astype(jnp.bfloat16)
    stream_ref[...] = stream
    chosen = [
        jnp.dot(
            taken_ref[e].astype(jnp.bfloat16), stream, preferred_element_type=jnp.float32
        ).astype(jnp.bfloat16)
        for e in range(HELD)
    ]
    for k in range(out_ref.shape[0]):
        out_ref[k] = chosen[k // sharers]


def pick(sharers, count, mine, other, residual, taken):
    rows, cols = mine.shape
    return call(
        functools.partial(pick_kernel, sharers),
        [
            jax.ShapeDtypeStruct((rows, cols), jnp.bfloat16),
            jax.ShapeDtypeStruct((count, taken.shape[1], cols), jnp.bfloat16),
        ],
        [VMEM_SPEC] * 4,
        [],
        2 * HELD * taken.shape[1] * rows * cols, rows * cols * 12, 4,
    )(mine, other, residual, taken)


def expert_kernel(slot_ref, pieces, gains, gate_ref, up_ref, down_ref, out_ref):
    count, capacity, cols = pieces.shape
    first = second = 0.0
    for k in range(count):
        wide = pieces[k].astype(jnp.float32)
        first = first + wide
        second = second + wide * wide
    row_mean = jnp.sum(first, axis=1, keepdims=True) / D
    row_var = jnp.sum(second, axis=1, keepdims=True) / D - row_mean * row_mean
    inverse = lax.rsqrt(row_var + EPSILON)
    contract = (((1,), (1,)), ((), ()))
    gate_val = up_val = 0.0
    for k in range(count):
        block = slice(k * cols, (k + 1) * cols)
        wide = pieces[k].astype(jnp.float32)
        normed = ((wide - row_mean) * inverse * gains[pl.ds(k, 1), :]).astype(jnp.bfloat16)
        gate_val = gate_val + lax.dot_general(
            gate_ref[:, block], normed, contract, preferred_element_type=jnp.float32
        )
        up_val = up_val + lax.dot_general(
            up_ref[:, block], normed, contract, preferred_element_type=jnp.float32
        )
    hidden = (gate_val / (1.0 + jnp.exp(-gate_val)) * up_val).T.astype(jnp.bfloat16)
    slot_weight = slot_ref[:, :1]
    for k in range(count):
        block = slice(k * cols, (k + 1) * cols)
        out_ref[k] = (
            jnp.dot(hidden, down_ref[:, block], preferred_element_type=jnp.float32) * slot_weight
        ).astype(jnp.bfloat16)


def run_experts(slots, pieces, gains, gate, up, down):
    return call(
        expert_kernel,
        jax.ShapeDtypeStruct(pieces.shape, jnp.bfloat16),
        [VMEM_SPEC] * 6,
        [],
        6 * pieces.shape[1] * gate.size, gate.size * 6, 14,
    )(slots, pieces, gains, gate, up, down)


def combine_kernel(sharers, taken_ref, pieces, out_ref):
    count, capacity, cols = pieces.shape
    spread = [taken_ref[k // sharers] for k in range(count)]
    out_ref[...] = lax.dot_general(
        jnp.concatenate(spread, axis=0).astype(jnp.bfloat16),
        pieces[...].reshape(count * capacity, cols),
        (((0,), (0,)), ((), ())),
        preferred_element_type=jnp.float32,
    )


def combine(sharers, taken, pieces):
    count, capacity, cols = pieces.shape
    rows = taken.shape[2]
    return call(
        functools.partial(combine_kernel, sharers),
        jax.ShapeDtypeStruct((rows, cols), jnp.float32),
        [VMEM_SPEC] * 2,
        [],
        2 * rows * capacity * count * cols, (count * capacity * 2 + rows * 4) * cols, 4,
    )(taken, pieces)


def finish_kernel(stream_ref, mine_ref, other_ref, stream_out_ref, out_ref):
    stream_out_ref[...] = stream_ref[...]
    out_ref[...] = (mine_ref[...] + other_ref[...]).astype(jnp.bfloat16)


def finish(stream, mine, other):
    return call(
        finish_kernel,
        [jax.ShapeDtypeStruct(stream.shape, jnp.bfloat16)] * 2,
        [VMEM_SPEC] * 3,
        [],
        mine.size, mine.size * 14, 4,
    )(stream, mine, other)


def exchange(blocks):
    return lax.all_to_all(blocks, "attn", split_axis=0, concat_axis=0, tiled=True)


def swap(block):
    return lax.ppermute(block, "expert", [(0, 1), (1, 0)])


def shards(
    queries,
    key_cache,
    value_cache,
    new_key,
    new_value,
    cache_length,
    residual,
    out_weight,
    ln_gain,
    gate_weight,
    up_weight,
    down_weight,
    routes,
    route_weight,
):
    count = lax.axis_size("attn")
    sharers = count // HELD
    capacity = routes.shape[0] * TOP // EXPERTS * 2
    place = lax.axis_index("attn").astype(jnp.int32).reshape(1)

    earlier = order(place, routes.shape[0])
    spread, own, limit, taken, slots = prepare(
        place, sharers, capacity, cache_length, earlier, routes.T, route_weight.T, queries, new_key
    )
    attended = exchange(
        attend(count, spread, own, limit, key_cache, value_cache, new_value, ln_gain)
    )
    mine, gains = project(attended, out_weight)
    stream, chosen = pick(sharers, count, mine, swap(mine), residual, taken)
    outgoing = run_experts(
        slots, exchange(chosen), gains, gate_weight.T, up_weight.T, down_weight
    )
    combined = combine(sharers, taken, exchange(outgoing))
    attn_stream, expert_out = finish(stream, combined, swap(combined))
    return (attn_stream, expert_out)


def solution(mesh):
    count = mesh.shape["attn"]
    fits = D // count % 256 == 0 and count % HELD == 0 and mesh.shape["expert"] == 2
    return jax.shard_map(
        shards if fits else shards_plain,
        mesh=mesh,
        in_specs=(
            P(("group", "attn"), "expert"),
            P(("group", "attn"), None, "expert"),
            P(("group", "attn"), None, "expert"),
            P(("group", "attn"), "expert"),
            P(("group", "attn"), "expert"),
            P(("group", "attn")),
            P("group", "attn"),
            P("expert", "attn"),
            P("attn"),
            P(None, ("attn", "expert")),
            P(None, ("attn", "expert")),
            P(("attn", "expert"), None),
            P("group", None),
            P("group", None),
        ),
        out_specs=(P("group", "attn"), P("group", "attn")),
        check_vma=False,
    )
```

```python
import functools
import math

import jax
import jax.numpy as jnp
from jax import lax
from jax.experimental import pallas as pl
from jax.experimental.pallas import tpu as pltpu
from jax.sharding import PartitionSpec as P

D = 6144
HEADS = 48
KV_HEADS = 8
HEAD_DIM = 128
EXPERTS = 16
TOP = 4
HELD = 2


NEG_FILL = -1e30
EPSILON = 1e-05


def attend_local(queries, key_cache, value_cache, new_key, new_value, cache_length):
    row_count = queries.shape[0]
    kv_local = new_key.shape[1] // HEAD_DIM
    group = HEADS // KV_HEADS
    length_max = key_cache.shape[1]
    query_heads = queries.reshape(row_count, kv_local, group, HEAD_DIM)
    key_heads = key_cache.reshape(row_count, length_max, kv_local, HEAD_DIM)
    value_heads = value_cache.reshape(row_count, length_max, kv_local, HEAD_DIM)
    own_keys = new_key.reshape(row_count, kv_local, HEAD_DIM)
    own_values = new_value.reshape(row_count, kv_local, HEAD_DIM)
    scale = 1.0 / math.sqrt(HEAD_DIM)
    past = (
        jnp.einsum("rkgd,rlkd->rkgl", query_heads, key_heads, preferred_element_type=jnp.float32)
        * scale
    )
    valid = jnp.arange(length_max, dtype=jnp.int32)[None, :] < cache_length[:, None]
    past = jnp.where(valid[:, None, None, :], past, NEG_FILL)
    own = (
        jnp.einsum("rkgd,rkd->rkg", query_heads, own_keys, preferred_element_type=jnp.float32)
        * scale
    )
    largest = jnp.maximum(jnp.max(past, axis=3), own)
    past_weight = jnp.exp(past - largest[..., None])
    own_weight = jnp.exp(own - largest)
    total = jnp.sum(past_weight, axis=3) + own_weight
    past_prob = (past_weight / total[..., None]).astype(jnp.bfloat16)
    own_prob = (own_weight / total).astype(jnp.bfloat16)
    result = jnp.einsum(
        "rkgl,rlkd->rkgd", past_prob, value_heads, preferred_element_type=jnp.float32
    )
    result = (
        result
        + own_prob.astype(jnp.float32)[..., None] * own_values.astype(jnp.float32)[:, :, None, :]
    )
    return result.reshape(row_count, kv_local * group * HEAD_DIM).astype(jnp.bfloat16)


def selection(routes, route_weight, capacity):
    row_count = routes.shape[0]
    experts = jnp.arange(HELD, dtype=jnp.int32)
    match = routes[None, :, :] == experts[:, None, None]
    hit = jnp.any(match, axis=2)
    row_weight = jnp.sum(jnp.where(match, route_weight[None], 0.0), axis=2)
    earlier = jnp.arange(row_count)[:, None] < jnp.arange(row_count)[None, :]
    slot = jnp.sum(jnp.where(earlier[None] & hit[:, :, None], 1, 0), axis=1)
    taken = hit[:, None, :] & (slot[:, None, :] == jnp.arange(capacity, dtype=jnp.int32)[None, :, None])
    slot_weight = jnp.sum(jnp.where(taken, row_weight[:, None, :], 0.0), axis=2)
    return taken, slot_weight


def gather_attn(block):
    count = lax.axis_size("attn")
    copies = jnp.broadcast_to(block[None], (count,) + block.shape)
    return lax.all_to_all(copies, "attn", split_axis=0, concat_axis=0, tiled=True)


def pair_sum(block):
    return block + lax.ppermute(block, "expert", [(0, 1), (1, 0)])


def shards_plain(
    queries,
    key_cache,
    value_cache,
    new_key,
    new_value,
    cache_length,
    residual,
    out_weight,
    ln_gain,
    gate_weight,
    up_weight,
    down_weight,
    routes,
    route_weight,
):
    attn_count = lax.axis_size("attn")
    core_count = lax.axis_size("expert")
    sharers = attn_count * core_count // HELD
    my_expert = (lax.axis_index("attn") * core_count + lax.axis_index("expert")) // sharers
    dest_expert = [index * core_count // sharers for index in range(attn_count)]
    row_count = routes.shape[0]
    capacity = row_count * TOP // EXPERTS * 2
    cols = residual.shape[1]

    taken, slot_weight = selection(routes, route_weight, capacity)
    pick = taken.astype(jnp.bfloat16)

    gains = gather_attn(ln_gain)

    attended = attend_local(queries, key_cache, value_cache, new_key, new_value, cache_length)
    whole = gather_attn(attended).reshape(row_count, -1)
    partial_proj = jnp.dot(whole, out_weight, preferred_element_type=jnp.float32)
    head_total = pair_sum(partial_proj)
    attn_stream = (residual.astype(jnp.float32) + head_total).astype(jnp.bfloat16)

    chosen = jnp.einsum(
        "esr,rd->esd", pick, attn_stream, preferred_element_type=jnp.float32
    ).astype(jnp.bfloat16)
    outgoing = jnp.stack([chosen[index] for index in dest_expert])
    rows = lax.all_to_all(outgoing, "attn", split_axis=0, concat_axis=0, tiled=True)
    wide = rows.astype(jnp.float32)
    row_mean = jnp.sum(wide, axis=(0, 2)) / D
    row_var = jnp.sum(wide * wide, axis=(0, 2)) / D - row_mean * row_mean
    normed = (
        (wide - row_mean[None, :, None])
        * lax.rsqrt(row_var + EPSILON)[None, :, None]
        * gains.reshape(attn_count, 1, cols)
    ).astype(jnp.bfloat16)
    gate_val = jnp.einsum(
        "asd,adf->sf", normed, gate_weight.reshape(attn_count, cols, -1),
        preferred_element_type=jnp.float32,
    )
    up_val = jnp.einsum(
        "asd,adf->sf", normed, up_weight.reshape(attn_count, cols, -1),
        preferred_element_type=jnp.float32,
    )
    hidden = (jax.nn.silu(gate_val) * up_val).astype(jnp.bfloat16)
    piece = jnp.dot(hidden, down_weight, preferred_element_type=jnp.float32)
    mine = jnp.take(slot_weight, my_expert, axis=0)
    piece = (piece * mine[:, None]).astype(jnp.bfloat16)
    returned = lax.all_to_all(
        piece.reshape(capacity, attn_count, cols).swapaxes(0, 1),
        "attn", split_axis=0, concat_axis=0, tiled=True,
    )
    spread = jnp.stack([pick[index] for index in dest_expert])
    combined = jnp.einsum(
        "asr,asd->rd", spread, returned, preferred_element_type=jnp.float32
    )
    expert_out = pair_sum(combined).astype(jnp.bfloat16)
    return (attn_stream, expert_out)


MIB = 1024 * 1024
EXCHANGE_FLOPS = 10**10
VMEM_SPEC = pl.BlockSpec(memory_space=pltpu.VMEM)
SMEM_SPEC = pl.BlockSpec(memory_space=pltpu.SMEM)
HBM_SPEC = pl.BlockSpec(memory_space=pltpu.HBM)


def call(kernel, outs, in_specs, scratch, flops, nbytes, vmem_mib):
    single = not isinstance(outs, (list, tuple))
    return pl.pallas_call(
        kernel,
        out_shape=outs,
        in_specs=in_specs,
        out_specs=VMEM_SPEC if single else [VMEM_SPEC] * len(outs),
        scratch_shapes=scratch,
        cost_estimate=pl.CostEstimate(flops=flops, bytes_accessed=nbytes, transcendentals=0),
        compiler_params=pltpu.CompilerParams(vmem_limit_bytes=vmem_mib * MIB),
    )


def order_kernel(place_ref, out_ref):
    rows = out_ref.shape[0]
    before = lax.broadcasted_iota(jnp.int32, (rows, rows), 0) < lax.broadcasted_iota(
        jnp.int32, (rows, rows), 1
    )
    out_ref[...] = jnp.where(before & (place_ref[0] >= 0), 1.0, 0.0).astype(jnp.bfloat16)


def order(place, rows):
    return call(
        order_kernel,
        jax.ShapeDtypeStruct((rows, rows), jnp.bfloat16),
        [SMEM_SPEC],
        [],
        EXCHANGE_FLOPS, rows * rows * 2, 2,
    )(place)


def expert_rows(routes, earlier, expert, capacity):
    row_count = routes.shape[1]
    hit = jnp.max((routes == expert).astype(jnp.float32), axis=0, keepdims=True)
    slot = jnp.dot(
        jnp.broadcast_to(hit, (8, row_count)).astype(jnp.bfloat16),
        earlier,
        preferred_element_type=jnp.float32,
    )[:1]
    place = lax.broadcasted_iota(jnp.int32, (capacity, row_count), 0).astype(jnp.float32)
    return jnp.where((slot == place) & (hit > 0.5), 1.0, 0.0)


def prepare_kernel(sharers, place_ref, length_ref, earlier_ref, routes_ref, weight_ref, query_ref,
                   own_key_ref, spread_ref, own_ref, limit_ref, taken_ref, slot_ref, query_rows,
                   key_rows):
    row_count = query_ref.shape[0]
    kv_local = own_key_ref.shape[1] // HEAD_DIM
    group = HEADS // KV_HEADS
    heads = kv_local * group
    for g in range(kv_local):
        own_key = own_key_ref[:, g * HEAD_DIM : (g + 1) * HEAD_DIM].astype(jnp.float32)
        for i in range(group):
            index = g * group + i
            rows = pl.ds(index * row_count, row_count)
            query_rows[rows, :] = query_ref[
                :, index * HEAD_DIM : (index + 1) * HEAD_DIM
            ].astype(jnp.float32)
            key_rows[rows, :] = own_key
    scale = 1.0 / math.sqrt(HEAD_DIM)
    head = lax.broadcasted_iota(jnp.int32, (heads, 1), 0) // group
    for r in range(row_count):
        strided = pl.ds(r, heads, stride=row_count)
        query = query_rows[strided, :]
        own = jnp.sum(query * key_rows[strided, :], axis=1, keepdims=True) * scale
        own_ref[r] = jnp.broadcast_to(own, (heads, HEAD_DIM))
        limit_ref[r] = jnp.full((heads, HEAD_DIM), length_ref[r], jnp.int32)
        spread_ref[r] = jnp.concatenate(
            [jnp.where(head == g, query, 0.0) for g in range(kv_local)], axis=1
        ).astype(jnp.bfloat16)
    routes = routes_ref[...]
    capacity = slot_ref.shape[0]
    taken = [expert_rows(routes, earlier_ref[...], e, capacity) for e in range(HELD)]
    for e in range(HELD):
        taken_ref[e] = taken[e]
    first = place_ref[0] < sharers
    expert = jnp.where(first, 0, 1)
    row_weight = jnp.sum(
        jnp.where(routes == expert, weight_ref[...], 0.0), axis=0, keepdims=True
    )
    mine = jnp.where(first, taken[0], taken[1])
    slot_ref[...] = jnp.broadcast_to(
        jnp.sum(mine * row_weight, axis=1, keepdims=True), slot_ref.shape
    )


def prepare(
    place, sharers, capacity, cache_length, earlier, routes, route_weight, queries, new_key
):
    row_count, width = queries.shape
    heads = width // HEAD_DIM
    table = pltpu.VMEM((heads * row_count, HEAD_DIM), jnp.float32)
    return call(
        functools.partial(prepare_kernel, sharers),
        [
            jax.ShapeDtypeStruct((row_count, heads, new_key.shape[1]), jnp.bfloat16),
            jax.ShapeDtypeStruct((row_count, heads, HEAD_DIM), jnp.float32),
            jax.ShapeDtypeStruct((row_count, heads, HEAD_DIM), jnp.int32),
            jax.ShapeDtypeStruct((HELD, capacity, routes.shape[1]), jnp.float32),
            jax.ShapeDtypeStruct((capacity, HEAD_DIM), jnp.float32),
        ],
        [SMEM_SPEC] * 2 + [VMEM_SPEC] * 5,
        [table, table],
        queries.size * 8, queries.size * 16, 4,
    )(place, cache_length, earlier, routes, route_weight, queries, new_key)


def score_kernel(spread_ref, own_ref, limit_ref, key_ref, probs_ref, own_probs_ref):
    row_count, heads, length_max = probs_ref.shape
    scale = 1.0 / math.sqrt(HEAD_DIM)
    contract = (((1,), (1,)), ((), ()))
    scores = jnp.concatenate(
        [
            lax.dot_general(
                spread_ref[r], key_ref[r], contract, preferred_element_type=jnp.float32
            )
            for r in range(row_count)
        ],
        axis=0,
    )
    position = lax.broadcasted_iota(jnp.int32, scores.shape, 1)
    limit = jnp.concatenate([limit_ref[r, :, :1] for r in range(row_count)], axis=0)
    own = jnp.concatenate([own_ref[r, :, :1] for r in range(row_count)], axis=0)
    past = jnp.where(position < limit, scores * scale, NEG_FILL)
    largest = jnp.maximum(jnp.max(past, axis=1, keepdims=True), own)
    weight = jnp.exp(past - largest)
    own_weight = jnp.exp(own - largest)
    inverse = 1.0 / (jnp.sum(weight, axis=1, keepdims=True) + own_weight)
    probs = weight * inverse
    own_prob = (own_weight * inverse).astype(jnp.bfloat16).astype(jnp.float32)
    for r in range(row_count):
        rows = slice(r * heads, (r + 1) * heads)
        probs_ref[r] = probs[rows].astype(jnp.bfloat16)
        own_probs_ref[r] = jnp.broadcast_to(own_prob[rows], own_probs_ref.shape[1:])


def value_kernel(probs_ref, own_ref, value_ref, own_value_ref, gain_ref, out_ref, value_rows,
                 result_rows):
    row_count, length_max, width = value_ref.shape
    kv_local = width // HEAD_DIM
    group = HEADS // KV_HEADS
    heads = kv_local * group
    for g in range(kv_local):
        own_value = own_value_ref[:, g * HEAD_DIM : (g + 1) * HEAD_DIM].astype(jnp.float32)
        for i in range(group):
            value_rows[pl.ds((g * group + i) * row_count, row_count), :] = own_value
    head = lax.broadcasted_iota(jnp.int32, (heads, 1), 0) // group
    for r in range(row_count):
        strided = pl.ds(r, heads, stride=row_count)
        product = jnp.dot(probs_ref[r], value_ref[r], preferred_element_type=jnp.float32)
        total = own_ref[r] * value_rows[strided, :]
        for g in range(kv_local):
            lanes = slice(g * HEAD_DIM, (g + 1) * HEAD_DIM)
            total = total + jnp.where(head == g, product[:, lanes], 0.0)
        result_rows[strided, :] = total
    for index in range(heads):
        rows = result_rows[pl.ds(index * row_count, row_count), :].astype(jnp.bfloat16)
        for copy in range(out_ref.shape[0]):
            out_ref[copy, :, index * HEAD_DIM : (index + 1) * HEAD_DIM] = rows
    gain_row = gain_ref[...].reshape(1, -1)
    half = gain_row.shape[1] // 2
    row = lax.broadcasted_iota(jnp.int32, (row_count, half), 0)
    left = jnp.broadcast_to(gain_row[:, :half], (row_count, half))
    right = jnp.broadcast_to(gain_row[:, half:], (row_count, half))
    gain = jnp.where(row % 2 == 0, left, right)
    upper = gain.astype(jnp.bfloat16).astype(jnp.float32)
    parts = jnp.where(row < 2, upper, gain - upper).astype(jnp.bfloat16)
    for copy in range(out_ref.shape[0]):
        out_ref[copy, :, heads * HEAD_DIM :] = parts


def attend(count, spread, own, limit, key_cache, value_cache, new_value, gain):
    row_count, heads, _ = spread.shape
    length_max = key_cache.shape[1]
    table = pltpu.VMEM((heads * row_count, HEAD_DIM), jnp.float32)
    probs, own_probs = call(
        score_kernel,
        [
            jax.ShapeDtypeStruct((row_count, heads, length_max), jnp.bfloat16),
            jax.ShapeDtypeStruct((row_count, heads, HEAD_DIM), jnp.float32),
        ],
        [VMEM_SPEC] * 4,
        [],
        2 * key_cache.size * heads, key_cache.size * 2, 8,
    )(spread, own, limit, key_cache)
    width = heads * HEAD_DIM + gain.shape[0] // 2
    return call(
        value_kernel,
        jax.ShapeDtypeStruct((count, row_count, width), jnp.bfloat16),
        [VMEM_SPEC] * 5,
        [table, table],
        EXCHANGE_FLOPS, value_cache.size * 2, 8,
    )(probs, own_probs, value_cache, new_value, gain)


def project_kernel(pieces, weight_ref, out_ref, gain_ref, stack):
    count, rows, _ = pieces.shape
    width = weight_ref.shape[0]
    half = gain_ref.shape[1] // 2
    for k in range(count):
        stack[pl.ds(k * rows, rows), :] = pieces[k, :, :width].astype(jnp.float32)
        parts = pieces[k, :, width:].astype(jnp.float32)
        gain_ref[pl.ds(k, 1), :half] = parts[0:1] + parts[2:3]
        gain_ref[pl.ds(k, 1), half:] = parts[1:2] + parts[3:4]
    out_ref[...] = jnp.dot(
        stack[...].astype(jnp.bfloat16), weight_ref[...], preferred_element_type=jnp.float32
    )


def project(pieces, out_weight):
    count, rows, _ = pieces.shape
    depth, cols = out_weight.shape
    return call(
        project_kernel,
        [
            jax.ShapeDtypeStruct((rows * count, cols), jnp.float32),
            jax.ShapeDtypeStruct((count, cols), jnp.float32),
        ],
        [VMEM_SPEC, VMEM_SPEC],
        [pltpu.VMEM((rows * count, depth), jnp.float32)],
        EXCHANGE_FLOPS, out_weight.size * 2, 10,
    )(pieces, out_weight)


def pick_kernel(sharers, mine_ref, other_ref, residual_ref, taken_ref, stream_ref, out_ref):
    stream = (
        residual_ref[...].astype(jnp.float32) + (mine_ref[...] + other_ref[...])
    ).astype(jnp.bfloat16)
    stream_ref[...] = stream
    chosen = [
        jnp.dot(
            taken_ref[e].astype(jnp.bfloat16), stream, preferred_element_type=jnp.float32
        ).astype(jnp.bfloat16)
        for e in range(HELD)
    ]
    for k in range(out_ref.shape[0]):
        out_ref[k] = chosen[k // sharers]


def pick(sharers, count, mine, other, residual, taken):
    rows, cols = mine.shape
    return call(
        functools.partial(pick_kernel, sharers),
        [
            jax.ShapeDtypeStruct((rows, cols), jnp.bfloat16),
            jax.ShapeDtypeStruct((count, taken.shape[1], cols), jnp.bfloat16),
        ],
        [VMEM_SPEC] * 4,
        [],
        2 * HELD * taken.shape[1] * rows * cols, rows * cols * 12, 4,
    )(mine, other, residual, taken)


def expert_kernel(slot_ref, pieces, gains, gate_ref, up_ref, down_ref, out_ref):
    count, capacity, cols = pieces.shape
    first = second = 0.0
    for k in range(count):
        wide = pieces[k].astype(jnp.float32)
        first = first + wide
        second = second + wide * wide
    row_mean = jnp.sum(first, axis=1, keepdims=True) / D
    row_var = jnp.sum(second, axis=1, keepdims=True) / D - row_mean * row_mean
    inverse = lax.rsqrt(row_var + EPSILON)
    contract = (((1,), (1,)), ((), ()))
    gate_val = up_val = 0.0
    for k in range(count):
        block = slice(k * cols, (k + 1) * cols)
        wide = pieces[k].astype(jnp.float32)
        normed = ((wide - row_mean) * inverse * gains[pl.ds(k, 1), :]).astype(jnp.bfloat16)
        gate_val = gate_val + lax.dot_general(
            normed, gate_ref[:, block], contract, preferred_element_type=jnp.float32
        )
        up_val = up_val + lax.dot_general(
            normed, up_ref[:, block], contract, preferred_element_type=jnp.float32
        )
    hidden = (gate_val / (1.0 + jnp.exp(-gate_val)) * up_val).astype(jnp.bfloat16)
    slot_weight = slot_ref[:, :1]
    for k in range(count):
        block = slice(k * cols, (k + 1) * cols)
        out_ref[k] = (
            jnp.dot(hidden, down_ref[:, block], preferred_element_type=jnp.float32) * slot_weight
        ).astype(jnp.bfloat16)


def run_experts(slots, pieces, gains, gate, up, down):
    return call(
        expert_kernel,
        jax.ShapeDtypeStruct(pieces.shape, jnp.bfloat16),
        [VMEM_SPEC] * 6,
        [],
        6 * pieces.shape[1] * gate.size, gate.size * 6, 14,
    )(slots, pieces, gains, gate, up, down)


def combine_kernel(sharers, taken_ref, pieces, out_ref):
    count, capacity, cols = pieces.shape
    spread = [taken_ref[k // sharers] for k in range(count)]
    out_ref[...] = lax.dot_general(
        jnp.concatenate(spread, axis=0).astype(jnp.bfloat16),
        pieces[...].reshape(count * capacity, cols),
        (((0,), (0,)), ((), ())),
        preferred_element_type=jnp.float32,
    )


def combine(sharers, taken, pieces):
    count, capacity, cols = pieces.shape
    rows = taken.shape[2]
    return call(
        functools.partial(combine_kernel, sharers),
        jax.ShapeDtypeStruct((rows, cols), jnp.float32),
        [VMEM_SPEC] * 2,
        [],
        2 * rows * capacity * count * cols, (count * capacity * 2 + rows * 4) * cols, 4,
    )(taken, pieces)


def finish_kernel(stream_ref, mine_ref, other_ref, stream_out_ref, out_ref):
    stream_out_ref[...] = stream_ref[...]
    out_ref[...] = (mine_ref[...] + other_ref[...]).astype(jnp.bfloat16)


def finish(stream, mine, other):
    return call(
        finish_kernel,
        [jax.ShapeDtypeStruct(stream.shape, jnp.bfloat16)] * 2,
        [VMEM_SPEC] * 3,
        [],
        mine.size, mine.size * 14, 4,
    )(stream, mine, other)


def exchange(blocks):
    return lax.all_to_all(blocks, "attn", split_axis=0, concat_axis=0, tiled=True)


def swap(block):
    return lax.ppermute(block, "expert", [(0, 1), (1, 0)])


def shards(
    queries,
    key_cache,
    value_cache,
    new_key,
    new_value,
    cache_length,
    residual,
    out_weight,
    ln_gain,
    gate_weight,
    up_weight,
    down_weight,
    routes,
    route_weight,
):
    count = lax.axis_size("attn")
    sharers = count // HELD
    capacity = routes.shape[0] * TOP // EXPERTS * 2
    place = lax.axis_index("attn").astype(jnp.int32).reshape(1)

    earlier = order(place, routes.shape[0])
    spread, own, limit, taken, slots = prepare(
        place, sharers, capacity, cache_length, earlier, routes.T, route_weight.T, queries, new_key
    )
    attended = exchange(
        attend(count, spread, own, limit, key_cache, value_cache, new_value, ln_gain)
    )
    mine, gains = project(attended, out_weight)
    stream, chosen = pick(sharers, count, mine, swap(mine), residual, taken)
    outgoing = run_experts(
        slots, exchange(chosen), gains, gate_weight.T, up_weight.T, down_weight
    )
    combined = combine(sharers, taken, exchange(outgoing))
    attn_stream, expert_out = finish(stream, combined, swap(combined))
    return (attn_stream, expert_out)


def solution(mesh):
    count = mesh.shape["attn"]
    fits = D // count % 256 == 0 and count % HELD == 0 and mesh.shape["expert"] == 2
    return jax.shard_map(
        shards if fits else shards_plain,
        mesh=mesh,
        in_specs=(
            P(("group", "attn"), "expert"),
            P(("group", "attn"), None, "expert"),
            P(("group", "attn"), None, "expert"),
            P(("group", "attn"), "expert"),
            P(("group", "attn"), "expert"),
            P(("group", "attn")),
            P("group", "attn"),
            P("expert", "attn"),
            P("attn"),
            P(None, ("attn", "expert")),
            P(None, ("attn", "expert")),
            P(("attn", "expert"), None),
            P("group", None),
            P("group", None),
        ),
        out_specs=(P("group", "attn"), P("group", "attn")),
        check_vma=False,
    )
```

```python
import functools
import math

import jax
import jax.numpy as jnp
from jax import lax
from jax.experimental import pallas as pl
from jax.experimental.pallas import tpu as pltpu
from jax.sharding import PartitionSpec as P

D = 6144
HEADS = 48
KV_HEADS = 8
HEAD_DIM = 128
EXPERTS = 16
TOP = 4
HELD = 2


NEG_FILL = -1e30
EPSILON = 1e-05


def attend_local(queries, key_cache, value_cache, new_key, new_value, cache_length):
    row_count = queries.shape[0]
    kv_local = new_key.shape[1] // HEAD_DIM
    group = HEADS // KV_HEADS
    length_max = key_cache.shape[1]
    query_heads = queries.reshape(row_count, kv_local, group, HEAD_DIM)
    key_heads = key_cache.reshape(row_count, length_max, kv_local, HEAD_DIM)
    value_heads = value_cache.reshape(row_count, length_max, kv_local, HEAD_DIM)
    own_keys = new_key.reshape(row_count, kv_local, HEAD_DIM)
    own_values = new_value.reshape(row_count, kv_local, HEAD_DIM)
    scale = 1.0 / math.sqrt(HEAD_DIM)
    past = (
        jnp.einsum("rkgd,rlkd->rkgl", query_heads, key_heads, preferred_element_type=jnp.float32)
        * scale
    )
    valid = jnp.arange(length_max, dtype=jnp.int32)[None, :] < cache_length[:, None]
    past = jnp.where(valid[:, None, None, :], past, NEG_FILL)
    own = (
        jnp.einsum("rkgd,rkd->rkg", query_heads, own_keys, preferred_element_type=jnp.float32)
        * scale
    )
    largest = jnp.maximum(jnp.max(past, axis=3), own)
    past_weight = jnp.exp(past - largest[..., None])
    own_weight = jnp.exp(own - largest)
    total = jnp.sum(past_weight, axis=3) + own_weight
    past_prob = (past_weight / total[..., None]).astype(jnp.bfloat16)
    own_prob = (own_weight / total).astype(jnp.bfloat16)
    result = jnp.einsum(
        "rkgl,rlkd->rkgd", past_prob, value_heads, preferred_element_type=jnp.float32
    )
    result = (
        result
        + own_prob.astype(jnp.float32)[..., None] * own_values.astype(jnp.float32)[:, :, None, :]
    )
    return result.reshape(row_count, kv_local * group * HEAD_DIM).astype(jnp.bfloat16)


def selection(routes, route_weight, capacity):
    row_count = routes.shape[0]
    experts = jnp.arange(HELD, dtype=jnp.int32)
    match = routes[None, :, :] == experts[:, None, None]
    hit = jnp.any(match, axis=2)
    row_weight = jnp.sum(jnp.where(match, route_weight[None], 0.0), axis=2)
    earlier = jnp.arange(row_count)[:, None] < jnp.arange(row_count)[None, :]
    slot = jnp.sum(jnp.where(earlier[None] & hit[:, :, None], 1, 0), axis=1)
    taken = hit[:, None, :] & (slot[:, None, :] == jnp.arange(capacity, dtype=jnp.int32)[None, :, None])
    slot_weight = jnp.sum(jnp.where(taken, row_weight[:, None, :], 0.0), axis=2)
    return taken, slot_weight


def gather_attn(block):
    count = lax.axis_size("attn")
    copies = jnp.broadcast_to(block[None], (count,) + block.shape)
    return lax.all_to_all(copies, "attn", split_axis=0, concat_axis=0, tiled=True)


def pair_sum(block):
    return block + lax.ppermute(block, "expert", [(0, 1), (1, 0)])


def shards_plain(
    queries,
    key_cache,
    value_cache,
    new_key,
    new_value,
    cache_length,
    residual,
    out_weight,
    ln_gain,
    gate_weight,
    up_weight,
    down_weight,
    routes,
    route_weight,
):
    attn_count = lax.axis_size("attn")
    core_count = lax.axis_size("expert")
    sharers = attn_count * core_count // HELD
    my_expert = (lax.axis_index("attn") * core_count + lax.axis_index("expert")) // sharers
    dest_expert = [index * core_count // sharers for index in range(attn_count)]
    row_count = routes.shape[0]
    capacity = row_count * TOP // EXPERTS * 2
    cols = residual.shape[1]

    taken, slot_weight = selection(routes, route_weight, capacity)
    pick = taken.astype(jnp.bfloat16)

    gains = gather_attn(ln_gain)

    attended = attend_local(queries, key_cache, value_cache, new_key, new_value, cache_length)
    whole = gather_attn(attended).reshape(row_count, -1)
    partial_proj = jnp.dot(whole, out_weight, preferred_element_type=jnp.float32)
    head_total = pair_sum(partial_proj)
    attn_stream = (residual.astype(jnp.float32) + head_total).astype(jnp.bfloat16)

    chosen = jnp.einsum(
        "esr,rd->esd", pick, attn_stream, preferred_element_type=jnp.float32
    ).astype(jnp.bfloat16)
    outgoing = jnp.stack([chosen[index] for index in dest_expert])
    rows = lax.all_to_all(outgoing, "attn", split_axis=0, concat_axis=0, tiled=True)
    wide = rows.astype(jnp.float32)
    row_mean = jnp.sum(wide, axis=(0, 2)) / D
    row_var = jnp.sum(wide * wide, axis=(0, 2)) / D - row_mean * row_mean
    normed = (
        (wide - row_mean[None, :, None])
        * lax.rsqrt(row_var + EPSILON)[None, :, None]
        * gains.reshape(attn_count, 1, cols)
    ).astype(jnp.bfloat16)
    gate_val = jnp.einsum(
        "asd,adf->sf", normed, gate_weight.reshape(attn_count, cols, -1),
        preferred_element_type=jnp.float32,
    )
    up_val = jnp.einsum(
        "asd,adf->sf", normed, up_weight.reshape(attn_count, cols, -1),
        preferred_element_type=jnp.float32,
    )
    hidden = (jax.nn.silu(gate_val) * up_val).astype(jnp.bfloat16)
    piece = jnp.dot(hidden, down_weight, preferred_element_type=jnp.float32)
    mine = jnp.take(slot_weight, my_expert, axis=0)
    piece = (piece * mine[:, None]).astype(jnp.bfloat16)
    returned = lax.all_to_all(
        piece.reshape(capacity, attn_count, cols).swapaxes(0, 1),
        "attn", split_axis=0, concat_axis=0, tiled=True,
    )
    spread = jnp.stack([pick[index] for index in dest_expert])
    combined = jnp.einsum(
        "asr,asd->rd", spread, returned, preferred_element_type=jnp.float32
    )
    expert_out = pair_sum(combined).astype(jnp.bfloat16)
    return (attn_stream, expert_out)


MIB = 1024 * 1024
EXCHANGE_FLOPS = 10**10
VMEM_SPEC = pl.BlockSpec(memory_space=pltpu.VMEM)
SMEM_SPEC = pl.BlockSpec(memory_space=pltpu.SMEM)
HBM_SPEC = pl.BlockSpec(memory_space=pltpu.HBM)


def call(kernel, outs, in_specs, scratch, flops, nbytes, vmem_mib):
    single = not isinstance(outs, (list, tuple))
    return pl.pallas_call(
        kernel,
        out_shape=outs,
        in_specs=in_specs,
        out_specs=VMEM_SPEC if single else [VMEM_SPEC] * len(outs),
        scratch_shapes=scratch,
        cost_estimate=pl.CostEstimate(flops=flops, bytes_accessed=nbytes, transcendentals=0),
        compiler_params=pltpu.CompilerParams(vmem_limit_bytes=vmem_mib * MIB),
    )


def order_kernel(place_ref, out_ref):
    rows = out_ref.shape[0]
    before = lax.broadcasted_iota(jnp.int32, (rows, rows), 0) < lax.broadcasted_iota(
        jnp.int32, (rows, rows), 1
    )
    out_ref[...] = jnp.where(before & (place_ref[0] >= 0), 1.0, 0.0).astype(jnp.bfloat16)


def order(place, rows):
    return call(
        order_kernel,
        jax.ShapeDtypeStruct((rows, rows), jnp.bfloat16),
        [SMEM_SPEC],
        [],
        EXCHANGE_FLOPS, rows * rows * 2, 2,
    )(place)


def expert_rows(routes, earlier, expert, capacity):
    row_count = routes.shape[1]
    hit = jnp.max((routes == expert).astype(jnp.float32), axis=0, keepdims=True)
    slot = jnp.dot(
        jnp.broadcast_to(hit, (8, row_count)).astype(jnp.bfloat16),
        earlier,
        preferred_element_type=jnp.float32,
    )[:1]
    place = lax.broadcasted_iota(jnp.int32, (capacity, row_count), 0).astype(jnp.float32)
    return jnp.where((slot == place) & (hit > 0.5), 1.0, 0.0)


def prepare_kernel(sharers, place_ref, length_ref, earlier_ref, routes_ref, weight_ref, query_ref,
                   own_key_ref, spread_ref, own_ref, limit_ref, taken_ref, slot_ref, query_rows,
                   key_rows):
    row_count = query_ref.shape[0]
    kv_local = own_key_ref.shape[1] // HEAD_DIM
    group = HEADS // KV_HEADS
    heads = kv_local * group
    for g in range(kv_local):
        own_key = own_key_ref[:, g * HEAD_DIM : (g + 1) * HEAD_DIM].astype(jnp.float32)
        for i in range(group):
            index = g * group + i
            rows = pl.ds(index * row_count, row_count)
            query_rows[rows, :] = query_ref[
                :, index * HEAD_DIM : (index + 1) * HEAD_DIM
            ].astype(jnp.float32)
            key_rows[rows, :] = own_key
    scale = 1.0 / math.sqrt(HEAD_DIM)
    head = lax.broadcasted_iota(jnp.int32, (heads, 1), 0) // group
    for r in range(row_count):
        strided = pl.ds(r, heads, stride=row_count)
        query = query_rows[strided, :]
        own = jnp.sum(query * key_rows[strided, :], axis=1, keepdims=True) * scale
        own_ref[r] = jnp.broadcast_to(own, (heads, HEAD_DIM))
        limit_ref[r] = jnp.full((heads, HEAD_DIM), length_ref[r], jnp.int32)
        spread_ref[r] = jnp.concatenate(
            [jnp.where(head == g, query, 0.0) for g in range(kv_local)], axis=1
        ).astype(jnp.bfloat16)
    routes = routes_ref[...]
    capacity = slot_ref.shape[0]
    core = place_ref[0] % 2
    taken = []
    for e in range(HELD):
        both = expert_rows(routes, earlier_ref[...], e, 2 * capacity)
        taken.append(jnp.where(core == 0, both[:capacity], both[capacity:]))
        taken_ref[e] = taken[e]
    first = place_ref[0] // 2 < sharers
    expert = jnp.where(first, 0, 1)
    row_weight = jnp.sum(
        jnp.where(routes == expert, weight_ref[...], 0.0), axis=0, keepdims=True
    )
    mine = jnp.where(first, taken[0], taken[1])
    slot_ref[...] = jnp.broadcast_to(
        jnp.sum(mine * row_weight, axis=1, keepdims=True), slot_ref.shape
    )


def prepare(
    place, sharers, capacity, cache_length, earlier, routes, route_weight, queries, new_key
):
    row_count, width = queries.shape
    heads = width // HEAD_DIM
    table = pltpu.VMEM((heads * row_count, HEAD_DIM), jnp.float32)
    return call(
        functools.partial(prepare_kernel, sharers),
        [
            jax.ShapeDtypeStruct((row_count, heads, new_key.shape[1]), jnp.bfloat16),
            jax.ShapeDtypeStruct((row_count, heads, HEAD_DIM), jnp.float32),
            jax.ShapeDtypeStruct((row_count, heads, HEAD_DIM), jnp.int32),
            jax.ShapeDtypeStruct((HELD, capacity, routes.shape[1]), jnp.float32),
            jax.ShapeDtypeStruct((capacity, HEAD_DIM), jnp.float32),
        ],
        [SMEM_SPEC] * 2 + [VMEM_SPEC] * 5,
        [table, table],
        queries.size * 8, queries.size * 16, 4,
    )(place, cache_length, earlier, routes, route_weight, queries, new_key)


def score_kernel(spread_ref, own_ref, limit_ref, key_ref, probs_ref, own_probs_ref):
    row_count, heads, length_max = probs_ref.shape
    scale = 1.0 / math.sqrt(HEAD_DIM)
    contract = (((1,), (1,)), ((), ()))
    scores = jnp.concatenate(
        [
            lax.dot_general(
                spread_ref[r], key_ref[r], contract, preferred_element_type=jnp.float32
            )
            for r in range(row_count)
        ],
        axis=0,
    )
    position = lax.broadcasted_iota(jnp.int32, scores.shape, 1)
    limit = jnp.concatenate([limit_ref[r, :, :1] for r in range(row_count)], axis=0)
    own = jnp.concatenate([own_ref[r, :, :1] for r in range(row_count)], axis=0)
    past = jnp.where(position < limit, scores * scale, NEG_FILL)
    largest = jnp.maximum(jnp.max(past, axis=1, keepdims=True), own)
    weight = jnp.exp(past - largest)
    own_weight = jnp.exp(own - largest)
    inverse = 1.0 / (jnp.sum(weight, axis=1, keepdims=True) + own_weight)
    probs = weight * inverse
    own_prob = (own_weight * inverse).astype(jnp.bfloat16).astype(jnp.float32)
    for r in range(row_count):
        rows = slice(r * heads, (r + 1) * heads)
        probs_ref[r] = probs[rows].astype(jnp.bfloat16)
        own_probs_ref[r] = jnp.broadcast_to(own_prob[rows], own_probs_ref.shape[1:])


def value_kernel(probs_ref, own_ref, value_ref, own_value_ref, gain_ref, out_ref, value_rows,
                 result_rows):
    row_count, length_max, width = value_ref.shape
    kv_local = width // HEAD_DIM
    group = HEADS // KV_HEADS
    heads = kv_local * group
    for g in range(kv_local):
        own_value = own_value_ref[:, g * HEAD_DIM : (g + 1) * HEAD_DIM].astype(jnp.float32)
        for i in range(group):
            value_rows[pl.ds((g * group + i) * row_count, row_count), :] = own_value
    head = lax.broadcasted_iota(jnp.int32, (heads, 1), 0) // group
    for r in range(row_count):
        strided = pl.ds(r, heads, stride=row_count)
        product = jnp.dot(probs_ref[r], value_ref[r], preferred_element_type=jnp.float32)
        total = own_ref[r] * value_rows[strided, :]
        for g in range(kv_local):
            lanes = slice(g * HEAD_DIM, (g + 1) * HEAD_DIM)
            total = total + jnp.where(head == g, product[:, lanes], 0.0)
        result_rows[strided, :] = total
    for index in range(heads):
        rows = result_rows[pl.ds(index * row_count, row_count), :].astype(jnp.bfloat16)
        for copy in range(out_ref.shape[0]):
            out_ref[copy, :, index * HEAD_DIM : (index + 1) * HEAD_DIM] = rows
    gain_row = gain_ref[...].reshape(1, -1)
    half = gain_row.shape[1] // 2
    row = lax.broadcasted_iota(jnp.int32, (row_count, half), 0)
    left = jnp.broadcast_to(gain_row[:, :half], (row_count, half))
    right = jnp.broadcast_to(gain_row[:, half:], (row_count, half))
    gain = jnp.where(row % 2 == 0, left, right)
    upper = gain.astype(jnp.bfloat16).astype(jnp.float32)
    parts = jnp.where(row < 2, upper, gain - upper).astype(jnp.bfloat16)
    for copy in range(out_ref.shape[0]):
        out_ref[copy, :, heads * HEAD_DIM :] = parts


def attend(count, spread, own, limit, key_cache, value_cache, new_value, gain):
    row_count, heads, _ = spread.shape
    length_max = key_cache.shape[1]
    table = pltpu.VMEM((heads * row_count, HEAD_DIM), jnp.float32)
    probs, own_probs = call(
        score_kernel,
        [
            jax.ShapeDtypeStruct((row_count, heads, length_max), jnp.bfloat16),
            jax.ShapeDtypeStruct((row_count, heads, HEAD_DIM), jnp.float32),
        ],
        [VMEM_SPEC] * 4,
        [],
        2 * key_cache.size * heads, key_cache.size * 2, 8,
    )(spread, own, limit, key_cache)
    width = heads * HEAD_DIM + gain.shape[0] // 2
    return call(
        value_kernel,
        jax.ShapeDtypeStruct((count, row_count, width), jnp.bfloat16),
        [VMEM_SPEC] * 5,
        [table, table],
        EXCHANGE_FLOPS, value_cache.size * 2, 8,
    )(probs, own_probs, value_cache, new_value, gain)


def project_kernel(pieces, weight_ref, out_ref, gain_ref, stack):
    count, rows, _ = pieces.shape
    width = weight_ref.shape[0]
    half = gain_ref.shape[1] // 2
    for k in range(count):
        stack[pl.ds(k * rows, rows), :] = pieces[k, :, :width].astype(jnp.float32)
        parts = pieces[k, :, width:].astype(jnp.float32)
        gain_ref[pl.ds(k, 1), :half] = parts[0:1] + parts[2:3]
        gain_ref[pl.ds(k, 1), half:] = parts[1:2] + parts[3:4]
    out_ref[...] = jnp.dot(
        stack[...].astype(jnp.bfloat16), weight_ref[...], preferred_element_type=jnp.float32
    )


def project(pieces, out_weight):
    count, rows, _ = pieces.shape
    depth, cols = out_weight.shape
    return call(
        project_kernel,
        [
            jax.ShapeDtypeStruct((rows * count, cols), jnp.float32),
            jax.ShapeDtypeStruct((count, cols), jnp.float32),
        ],
        [VMEM_SPEC, VMEM_SPEC],
        [pltpu.VMEM((rows * count, depth), jnp.float32)],
        EXCHANGE_FLOPS, out_weight.size * 2, 10,
    )(pieces, out_weight)


def pick_kernel(sharers, mine_ref, other_ref, residual_ref, taken_ref, stream_ref, out_ref):
    stream = (
        residual_ref[...].astype(jnp.float32) + (mine_ref[...] + other_ref[...])
    ).astype(jnp.bfloat16)
    stream_ref[...] = stream
    chosen = [
        jnp.dot(
            taken_ref[e].astype(jnp.bfloat16), stream, preferred_element_type=jnp.float32
        ).astype(jnp.bfloat16)
        for e in range(HELD)
    ]
    for k in range(out_ref.shape[0]):
        out_ref[k] = chosen[k // sharers]


def pick(sharers, count, mine, other, residual, taken):
    rows, cols = mine.shape
    return call(
        functools.partial(pick_kernel, sharers),
        [
            jax.ShapeDtypeStruct((rows, cols), jnp.bfloat16),
            jax.ShapeDtypeStruct((count, taken.shape[1], cols), jnp.bfloat16),
        ],
        [VMEM_SPEC] * 4,
        [],
        2 * HELD * taken.shape[1] * rows * cols, rows * cols * 12, 4,
    )(mine, other, residual, taken)


def expert_kernel(slot_ref, pieces, gains, *refs):
    weights, out_ref = (refs[:3], refs[3:6]), refs[6]
    count, capacity, cols = pieces.shape
    first = second = 0.0
    for k in range(count):
        wide = pieces[k].astype(jnp.float32)
        first = first + wide
        second = second + wide * wide
    row_mean = jnp.sum(first, axis=1, keepdims=True) / D
    row_var = jnp.sum(second, axis=1, keepdims=True) / D - row_mean * row_mean
    inverse = lax.rsqrt(row_var + EPSILON)
    contract = (((1,), (1,)), ((), ()))
    gate_val, up_val = [0.0, 0.0], [0.0, 0.0]
    for k in range(count):
        block = slice(k * cols, (k + 1) * cols)
        wide = pieces[k].astype(jnp.float32)
        normed = ((wide - row_mean) * inverse * gains[pl.ds(k, 1), :]).astype(jnp.bfloat16)
        for index, (gate_ref, up_ref, _) in enumerate(weights):
            gate_val[index] = gate_val[index] + lax.dot_general(
                normed, gate_ref[:, block], contract, preferred_element_type=jnp.float32
            )
            up_val[index] = up_val[index] + lax.dot_general(
                normed, up_ref[:, block], contract, preferred_element_type=jnp.float32
            )
    hidden = [
        (gate / (1.0 + jnp.exp(-gate)) * up).astype(jnp.bfloat16)
        for gate, up in zip(gate_val, up_val)
    ]
    slot_weight = slot_ref[:, :1]
    for k in range(count):
        block = slice(k * cols, (k + 1) * cols)
        piece = sum(
            jnp.dot(part, refs_of[2][:, block], preferred_element_type=jnp.float32)
            for part, refs_of in zip(hidden, weights)
        )
        out_ref[k] = (piece * slot_weight).astype(jnp.bfloat16)


def run_experts(slots, pieces, gains, own, other):
    return call(
        expert_kernel,
        jax.ShapeDtypeStruct(pieces.shape, jnp.bfloat16),
        [VMEM_SPEC] * 9,
        [],
        12 * pieces.shape[1] * own[0].size, own[0].size * 12, 20,
    )(slots, pieces, gains, *own, *other)


def combine_kernel(sharers, taken_ref, pieces, out_ref):
    count, capacity, cols = pieces.shape
    spread = [taken_ref[k // sharers] for k in range(count)]
    rows = [pieces[k].astype(jnp.float32) for k in range(count)]
    out_ref[...] = lax.dot_general(
        jnp.concatenate(spread, axis=0).astype(jnp.bfloat16),
        jnp.concatenate(rows, axis=0).astype(jnp.bfloat16),
        (((0,), (0,)), ((), ())),
        preferred_element_type=jnp.float32,
    )


def combine(sharers, taken, pieces):
    count, capacity, cols = pieces.shape
    rows = taken.shape[2]
    return call(
        functools.partial(combine_kernel, sharers),
        jax.ShapeDtypeStruct((rows, cols), jnp.float32),
        [VMEM_SPEC] * 2,
        [],
        2 * rows * capacity * count * cols, (count * capacity * 2 + rows * 4) * cols, 4,
    )(taken, pieces)


def finish_kernel(stream_ref, mine_ref, other_ref, stream_out_ref, out_ref):
    stream_out_ref[...] = stream_ref[...]
    out_ref[...] = (mine_ref[...] + other_ref[...]).astype(jnp.bfloat16)


def finish(stream, mine, other):
    return call(
        finish_kernel,
        [jax.ShapeDtypeStruct(stream.shape, jnp.bfloat16)] * 2,
        [VMEM_SPEC] * 3,
        [],
        mine.size, mine.size * 14, 4,
    )(stream, mine, other)


def exchange(blocks):
    return lax.all_to_all(blocks, "attn", split_axis=0, concat_axis=0, tiled=True)


def swap(block):
    return lax.ppermute(block, "expert", [(0, 1), (1, 0)])


def shards(
    queries,
    key_cache,
    value_cache,
    new_key,
    new_value,
    cache_length,
    residual,
    out_weight,
    ln_gain,
    gate_weight,
    up_weight,
    down_weight,
    routes,
    route_weight,
):
    count = lax.axis_size("attn")
    sharers = count // HELD
    capacity = routes.shape[0] * TOP // EXPERTS
    place = lax.axis_index(("attn", "expert")).astype(jnp.int32).reshape(1)

    earlier = order(place, routes.shape[0])
    weights = (gate_weight.T, up_weight.T, down_weight)
    other_weights = [swap(block) for block in weights]
    spread, own, limit, taken, slots = prepare(
        place, sharers, capacity, cache_length, earlier, routes.T, route_weight.T, queries, new_key
    )
    attended = exchange(
        attend(count, spread, own, limit, key_cache, value_cache, new_value, ln_gain)
    )
    mine, gains = project(attended, out_weight)
    stream, chosen = pick(sharers, count, mine, swap(mine), residual, taken)
    outgoing = run_experts(slots, exchange(chosen), gains, weights, other_weights)
    combined = combine(sharers, taken, exchange(outgoing))
    attn_stream, expert_out = finish(stream, combined, swap(combined))
    return (attn_stream, expert_out)


def solution(mesh):
    count = mesh.shape["attn"]
    fits = D // count % 256 == 0 and count % HELD == 0 and mesh.shape["expert"] == 2
    return jax.shard_map(
        shards if fits else shards_plain,
        mesh=mesh,
        in_specs=(
            P(("group", "attn"), "expert"),
            P(("group", "attn"), None, "expert"),
            P(("group", "attn"), None, "expert"),
            P(("group", "attn"), "expert"),
            P(("group", "attn"), "expert"),
            P(("group", "attn")),
            P("group", "attn"),
            P("expert", "attn"),
            P("attn"),
            P(None, ("attn", "expert")),
            P(None, ("attn", "expert")),
            P(("attn", "expert"), None),
            P("group", None),
            P("group", None),
        ),
        out_specs=(P("group", "attn"), P("group", "attn")),
        check_vma=False,
    )
```

```python
import functools
import math

import jax
import jax.numpy as jnp
from jax import lax
from jax.experimental import pallas as pl
from jax.experimental.pallas import tpu as pltpu
from jax.sharding import PartitionSpec as P

D = 6144
HEADS = 48
KV_HEADS = 8
HEAD_DIM = 128
EXPERTS = 16
TOP = 4
HELD = 2


NEG_FILL = -1e30
EPSILON = 1e-05


def attend_local(queries, key_cache, value_cache, new_key, new_value, cache_length):
    row_count = queries.shape[0]
    kv_local = new_key.shape[1] // HEAD_DIM
    group = HEADS // KV_HEADS
    length_max = key_cache.shape[1]
    query_heads = queries.reshape(row_count, kv_local, group, HEAD_DIM)
    key_heads = key_cache.reshape(row_count, length_max, kv_local, HEAD_DIM)
    value_heads = value_cache.reshape(row_count, length_max, kv_local, HEAD_DIM)
    own_keys = new_key.reshape(row_count, kv_local, HEAD_DIM)
    own_values = new_value.reshape(row_count, kv_local, HEAD_DIM)
    scale = 1.0 / math.sqrt(HEAD_DIM)
    past = (
        jnp.einsum("rkgd,rlkd->rkgl", query_heads, key_heads, preferred_element_type=jnp.float32)
        * scale
    )
    valid = jnp.arange(length_max, dtype=jnp.int32)[None, :] < cache_length[:, None]
    past = jnp.where(valid[:, None, None, :], past, NEG_FILL)
    own = (
        jnp.einsum("rkgd,rkd->rkg", query_heads, own_keys, preferred_element_type=jnp.float32)
        * scale
    )
    largest = jnp.maximum(jnp.max(past, axis=3), own)
    past_weight = jnp.exp(past - largest[..., None])
    own_weight = jnp.exp(own - largest)
    total = jnp.sum(past_weight, axis=3) + own_weight
    past_prob = (past_weight / total[..., None]).astype(jnp.bfloat16)
    own_prob = (own_weight / total).astype(jnp.bfloat16)
    result = jnp.einsum(
        "rkgl,rlkd->rkgd", past_prob, value_heads, preferred_element_type=jnp.float32
    )
    result = (
        result
        + own_prob.astype(jnp.float32)[..., None] * own_values.astype(jnp.float32)[:, :, None, :]
    )
    return result.reshape(row_count, kv_local * group * HEAD_DIM).astype(jnp.bfloat16)


def selection(routes, route_weight, capacity):
    row_count = routes.shape[0]
    experts = jnp.arange(HELD, dtype=jnp.int32)
    match = routes[None, :, :] == experts[:, None, None]
    hit = jnp.any(match, axis=2)
    row_weight = jnp.sum(jnp.where(match, route_weight[None], 0.0), axis=2)
    earlier = jnp.arange(row_count)[:, None] < jnp.arange(row_count)[None, :]
    slot = jnp.sum(jnp.where(earlier[None] & hit[:, :, None], 1, 0), axis=1)
    taken = hit[:, None, :] & (slot[:, None, :] == jnp.arange(capacity, dtype=jnp.int32)[None, :, None])
    slot_weight = jnp.sum(jnp.where(taken, row_weight[:, None, :], 0.0), axis=2)
    return taken, slot_weight


def gather_attn(block):
    count = lax.axis_size("attn")
    copies = jnp.broadcast_to(block[None], (count,) + block.shape)
    return lax.all_to_all(copies, "attn", split_axis=0, concat_axis=0, tiled=True)


def pair_sum(block):
    return block + lax.ppermute(block, "expert", [(0, 1), (1, 0)])


def shards_plain(
    queries,
    key_cache,
    value_cache,
    new_key,
    new_value,
    cache_length,
    residual,
    out_weight,
    ln_gain,
    gate_weight,
    up_weight,
    down_weight,
    routes,
    route_weight,
):
    attn_count = lax.axis_size("attn")
    core_count = lax.axis_size("expert")
    sharers = attn_count * core_count // HELD
    my_expert = (lax.axis_index("attn") * core_count + lax.axis_index("expert")) // sharers
    dest_expert = [index * core_count // sharers for index in range(attn_count)]
    row_count = routes.shape[0]
    capacity = row_count * TOP // EXPERTS * 2
    cols = residual.shape[1]

    taken, slot_weight = selection(routes, route_weight, capacity)
    pick = taken.astype(jnp.bfloat16)

    gains = gather_attn(ln_gain)

    attended = attend_local(queries, key_cache, value_cache, new_key, new_value, cache_length)
    whole = gather_attn(attended).reshape(row_count, -1)
    partial_proj = jnp.dot(whole, out_weight, preferred_element_type=jnp.float32)
    head_total = pair_sum(partial_proj)
    attn_stream = (residual.astype(jnp.float32) + head_total).astype(jnp.bfloat16)

    chosen = jnp.einsum(
        "esr,rd->esd", pick, attn_stream, preferred_element_type=jnp.float32
    ).astype(jnp.bfloat16)
    outgoing = jnp.stack([chosen[index] for index in dest_expert])
    rows = lax.all_to_all(outgoing, "attn", split_axis=0, concat_axis=0, tiled=True)
    wide = rows.astype(jnp.float32)
    row_mean = jnp.sum(wide, axis=(0, 2)) / D
    row_var = jnp.sum(wide * wide, axis=(0, 2)) / D - row_mean * row_mean
    normed = (
        (wide - row_mean[None, :, None])
        * lax.rsqrt(row_var + EPSILON)[None, :, None]
        * gains.reshape(attn_count, 1, cols)
    ).astype(jnp.bfloat16)
    gate_val = jnp.einsum(
        "asd,adf->sf", normed, gate_weight.reshape(attn_count, cols, -1),
        preferred_element_type=jnp.float32,
    )
    up_val = jnp.einsum(
        "asd,adf->sf", normed, up_weight.reshape(attn_count, cols, -1),
        preferred_element_type=jnp.float32,
    )
    hidden = (jax.nn.silu(gate_val) * up_val).astype(jnp.bfloat16)
    piece = jnp.dot(hidden, down_weight, preferred_element_type=jnp.float32)
    mine = jnp.take(slot_weight, my_expert, axis=0)
    piece = (piece * mine[:, None]).astype(jnp.bfloat16)
    returned = lax.all_to_all(
        piece.reshape(capacity, attn_count, cols).swapaxes(0, 1),
        "attn", split_axis=0, concat_axis=0, tiled=True,
    )
    spread = jnp.stack([pick[index] for index in dest_expert])
    combined = jnp.einsum(
        "asr,asd->rd", spread, returned, preferred_element_type=jnp.float32
    )
    expert_out = pair_sum(combined).astype(jnp.bfloat16)
    return (attn_stream, expert_out)


MIB = 1024 * 1024
EXCHANGE_FLOPS = 10**10
VMEM_SPEC = pl.BlockSpec(memory_space=pltpu.VMEM)
SMEM_SPEC = pl.BlockSpec(memory_space=pltpu.SMEM)
HBM_SPEC = pl.BlockSpec(memory_space=pltpu.HBM)


def call(kernel, outs, in_specs, scratch, flops, nbytes, vmem_mib):
    single = not isinstance(outs, (list, tuple))
    return pl.pallas_call(
        kernel,
        out_shape=outs,
        in_specs=in_specs,
        out_specs=VMEM_SPEC if single else [VMEM_SPEC] * len(outs),
        scratch_shapes=scratch,
        cost_estimate=pl.CostEstimate(flops=flops, bytes_accessed=nbytes, transcendentals=0),
        compiler_params=pltpu.CompilerParams(vmem_limit_bytes=vmem_mib * MIB),
    )


def order_kernel(out_ref):
    rows = out_ref.shape[0]
    before = lax.broadcasted_iota(jnp.int32, (rows, rows), 0) < lax.broadcasted_iota(
        jnp.int32, (rows, rows), 1
    )
    out_ref[...] = jnp.where(before, 1.0, 0.0).astype(jnp.bfloat16)


def order(rows):
    return call(
        order_kernel,
        jax.ShapeDtypeStruct((rows, rows), jnp.bfloat16),
        [],
        [],
        EXCHANGE_FLOPS, rows * rows * 2, 2,
    )()


def expert_rows(routes, earlier, expert, capacity):
    row_count = routes.shape[1]
    hit = jnp.max((routes == expert).astype(jnp.float32), axis=0, keepdims=True)
    slot = jnp.dot(
        jnp.broadcast_to(hit, (8, row_count)).astype(jnp.bfloat16),
        earlier,
        preferred_element_type=jnp.float32,
    )[:1]
    place = lax.broadcasted_iota(jnp.int32, (capacity, row_count), 0).astype(jnp.float32)
    return jnp.where((slot == place) & (hit > 0.5), 1.0, 0.0)


def prepare_kernel(sharers, length_ref, earlier_ref, routes_ref, weight_ref, query_ref,
                   own_key_ref, spread_ref, own_ref, limit_ref, taken_ref, slot_ref, query_rows,
                   key_rows):
    row_count = query_ref.shape[0]
    kv_local = own_key_ref.shape[1] // HEAD_DIM
    group = HEADS // KV_HEADS
    heads = kv_local * group
    for g in range(kv_local):
        own_key = own_key_ref[:, g * HEAD_DIM : (g + 1) * HEAD_DIM].astype(jnp.float32)
        for i in range(group):
            index = g * group + i
            rows = pl.ds(index * row_count, row_count)
            query_rows[rows, :] = query_ref[
                :, index * HEAD_DIM : (index + 1) * HEAD_DIM
            ].astype(jnp.float32)
            key_rows[rows, :] = own_key
    scale = 1.0 / math.sqrt(HEAD_DIM)
    head = lax.broadcasted_iota(jnp.int32, (heads, 1), 0) // group
    for r in range(row_count):
        strided = pl.ds(r, heads, stride=row_count)
        query = query_rows[strided, :]
        own = jnp.sum(query * key_rows[strided, :], axis=1, keepdims=True) * scale
        own_ref[r] = jnp.broadcast_to(own, (heads, HEAD_DIM))
        limit_ref[r] = jnp.full((heads, HEAD_DIM), length_ref[r], jnp.int32)
        spread_ref[r] = jnp.concatenate(
            [jnp.where(head == g, query, 0.0) for g in range(kv_local)], axis=1
        ).astype(jnp.bfloat16)
    routes = routes_ref[...]
    capacity = slot_ref.shape[0]
    core = lax.axis_index("expert")
    taken = []
    for e in range(HELD):
        both = expert_rows(routes, earlier_ref[...], e, 2 * capacity)
        taken.append(jnp.where(core == 0, both[:capacity], both[capacity:]))
        taken_ref[e] = taken[e]
    first = lax.axis_index("attn") < sharers
    expert = jnp.where(first, 0, 1)
    row_weight = jnp.sum(
        jnp.where(routes == expert, weight_ref[...], 0.0), axis=0, keepdims=True
    )
    mine = jnp.where(first, taken[0], taken[1])
    slot_ref[...] = jnp.broadcast_to(
        jnp.sum(mine * row_weight, axis=1, keepdims=True), slot_ref.shape
    )


def prepare(
    sharers, capacity, cache_length, earlier, routes, route_weight, queries, new_key
):
    row_count, width = queries.shape
    heads = width // HEAD_DIM
    table = pltpu.VMEM((heads * row_count, HEAD_DIM), jnp.float32)
    return call(
        functools.partial(prepare_kernel, sharers),
        [
            jax.ShapeDtypeStruct((row_count, heads, new_key.shape[1]), jnp.bfloat16),
            jax.ShapeDtypeStruct((row_count, heads, HEAD_DIM), jnp.float32),
            jax.ShapeDtypeStruct((row_count, heads, HEAD_DIM), jnp.int32),
            jax.ShapeDtypeStruct((HELD, capacity, routes.shape[1]), jnp.float32),
            jax.ShapeDtypeStruct((capacity, HEAD_DIM), jnp.float32),
        ],
        [SMEM_SPEC] + [VMEM_SPEC] * 5,
        [table, table],
        queries.size * 8, queries.size * 16, 4,
    )(cache_length, earlier, routes, route_weight, queries, new_key)


def score_kernel(spread_ref, own_ref, limit_ref, key_ref, probs_ref, own_probs_ref):
    row_count, heads, length_max = probs_ref.shape
    scale = 1.0 / math.sqrt(HEAD_DIM)
    contract = (((1,), (1,)), ((), ()))
    scores = jnp.concatenate(
        [
            lax.dot_general(
                spread_ref[r], key_ref[r], contract, preferred_element_type=jnp.float32
            )
            for r in range(row_count)
        ],
        axis=0,
    )
    position = lax.broadcasted_iota(jnp.int32, scores.shape, 1)
    limit = jnp.concatenate([limit_ref[r, :, :1] for r in range(row_count)], axis=0)
    own = jnp.concatenate([own_ref[r, :, :1] for r in range(row_count)], axis=0)
    past = jnp.where(position < limit, scores * scale, NEG_FILL)
    largest = jnp.maximum(jnp.max(past, axis=1, keepdims=True), own)
    weight = jnp.exp(past - largest)
    own_weight = jnp.exp(own - largest)
    inverse = 1.0 / (jnp.sum(weight, axis=1, keepdims=True) + own_weight)
    probs = weight * inverse
    own_prob = (own_weight * inverse).astype(jnp.bfloat16).astype(jnp.float32)
    for r in range(row_count):
        rows = slice(r * heads, (r + 1) * heads)
        probs_ref[r] = probs[rows].astype(jnp.bfloat16)
        own_probs_ref[r] = jnp.broadcast_to(own_prob[rows], own_probs_ref.shape[1:])


def value_kernel(probs_ref, own_ref, value_ref, own_value_ref, gain_ref, out_ref, value_rows,
                 result_rows):
    row_count, length_max, width = value_ref.shape
    kv_local = width // HEAD_DIM
    group = HEADS // KV_HEADS
    heads = kv_local * group
    for g in range(kv_local):
        own_value = own_value_ref[:, g * HEAD_DIM : (g + 1) * HEAD_DIM].astype(jnp.float32)
        for i in range(group):
            value_rows[pl.ds((g * group + i) * row_count, row_count), :] = own_value
    head = lax.broadcasted_iota(jnp.int32, (heads, 1), 0) // group
    for r in range(row_count):
        strided = pl.ds(r, heads, stride=row_count)
        product = jnp.dot(probs_ref[r], value_ref[r], preferred_element_type=jnp.float32)
        total = own_ref[r] * value_rows[strided, :]
        for g in range(kv_local):
            lanes = slice(g * HEAD_DIM, (g + 1) * HEAD_DIM)
            total = total + jnp.where(head == g, product[:, lanes], 0.0)
        result_rows[strided, :] = total
    for index in range(heads):
        rows = result_rows[pl.ds(index * row_count, row_count), :].astype(jnp.bfloat16)
        for copy in range(out_ref.shape[0]):
            out_ref[copy, :, index * HEAD_DIM : (index + 1) * HEAD_DIM] = rows
    gain_row = gain_ref[...].reshape(1, -1)
    half = gain_row.shape[1] // 2
    row = lax.broadcasted_iota(jnp.int32, (row_count, half), 0)
    left = jnp.broadcast_to(gain_row[:, :half], (row_count, half))
    right = jnp.broadcast_to(gain_row[:, half:], (row_count, half))
    gain = jnp.where(row % 2 == 0, left, right)
    upper = gain.astype(jnp.bfloat16).astype(jnp.float32)
    parts = jnp.where(row < 2, upper, gain - upper).astype(jnp.bfloat16)
    for copy in range(out_ref.shape[0]):
        out_ref[copy, :, heads * HEAD_DIM :] = parts


def attend(count, spread, own, limit, key_cache, value_cache, new_value, gain):
    row_count, heads, _ = spread.shape
    length_max = key_cache.shape[1]
    table = pltpu.VMEM((heads * row_count, HEAD_DIM), jnp.float32)
    probs, own_probs = call(
        score_kernel,
        [
            jax.ShapeDtypeStruct((row_count, heads, length_max), jnp.bfloat16),
            jax.ShapeDtypeStruct((row_count, heads, HEAD_DIM), jnp.float32),
        ],
        [VMEM_SPEC] * 4,
        [],
        2 * key_cache.size * heads, key_cache.size * 2, 8,
    )(spread, own, limit, key_cache)
    width = heads * HEAD_DIM + gain.shape[0] // 2
    return call(
        value_kernel,
        jax.ShapeDtypeStruct((count, row_count, width), jnp.bfloat16),
        [VMEM_SPEC] * 5,
        [table, table],
        EXCHANGE_FLOPS, value_cache.size * 2, 8,
    )(probs, own_probs, value_cache, new_value, gain)


def project_kernel(pieces, weight_ref, out_ref, gain_ref, stack):
    count, rows, _ = pieces.shape
    width = weight_ref.shape[0]
    half = gain_ref.shape[1] // 2
    for k in range(count):
        stack[pl.ds(k * rows, rows), :] = pieces[k, :, :width].astype(jnp.float32)
        parts = pieces[k, :, width:].astype(jnp.float32)
        gain_ref[pl.ds(k, 1), :half] = parts[0:1] + parts[2:3]
        gain_ref[pl.ds(k, 1), half:] = parts[1:2] + parts[3:4]
    out_ref[...] = jnp.dot(
        stack[...].astype(jnp.bfloat16), weight_ref[...], preferred_element_type=jnp.float32
    )


def project(pieces, out_weight):
    count, rows, _ = pieces.shape
    depth, cols = out_weight.shape
    return call(
        project_kernel,
        [
            jax.ShapeDtypeStruct((rows * count, cols), jnp.float32),
            jax.ShapeDtypeStruct((count, cols), jnp.float32),
        ],
        [VMEM_SPEC, VMEM_SPEC],
        [pltpu.VMEM((rows * count, depth), jnp.float32)],
        EXCHANGE_FLOPS, out_weight.size * 2, 10,
    )(pieces, out_weight)


def pick_kernel(sharers, mine_ref, other_ref, residual_ref, taken_ref, stream_ref, out_ref):
    stream = (
        residual_ref[...].astype(jnp.float32) + (mine_ref[...] + other_ref[...])
    ).astype(jnp.bfloat16)
    stream_ref[...] = stream
    chosen = [
        jnp.dot(
            taken_ref[e].astype(jnp.bfloat16), stream, preferred_element_type=jnp.float32
        ).astype(jnp.bfloat16)
        for e in range(HELD)
    ]
    for k in range(out_ref.shape[0]):
        out_ref[k] = chosen[k // sharers]


def pick(sharers, count, mine, other, residual, taken):
    rows, cols = mine.shape
    return call(
        functools.partial(pick_kernel, sharers),
        [
            jax.ShapeDtypeStruct((rows, cols), jnp.bfloat16),
            jax.ShapeDtypeStruct((count, taken.shape[1], cols), jnp.bfloat16),
        ],
        [VMEM_SPEC] * 4,
        [],
        2 * HELD * taken.shape[1] * rows * cols, rows * cols * 12, 4,
    )(mine, other, residual, taken)


def expert_kernel(slot_ref, pieces, gains, *refs):
    weights, out_ref = (refs[:3], refs[3:6]), refs[6]
    count, capacity, cols = pieces.shape
    first = second = 0.0
    for k in range(count):
        wide = pieces[k].astype(jnp.float32)
        first = first + wide
        second = second + wide * wide
    row_mean = jnp.sum(first, axis=1, keepdims=True) / D
    row_var = jnp.sum(second, axis=1, keepdims=True) / D - row_mean * row_mean
    inverse = lax.rsqrt(row_var + EPSILON)
    contract = (((1,), (1,)), ((), ()))
    gate_val, up_val = [0.0, 0.0], [0.0, 0.0]
    for k in range(count):
        block = slice(k * cols, (k + 1) * cols)
        wide = pieces[k].astype(jnp.float32)
        normed = ((wide - row_mean) * inverse * gains[pl.ds(k, 1), :]).astype(jnp.bfloat16)
        for index, (gate_ref, up_ref, _) in enumerate(weights):
            gate_val[index] = gate_val[index] + lax.dot_general(
                normed, gate_ref[:, block], contract, preferred_element_type=jnp.float32
            )
            up_val[index] = up_val[index] + lax.dot_general(
                normed, up_ref[:, block], contract, preferred_element_type=jnp.float32
            )
    hidden = [
        (gate / (1.0 + jnp.exp(-gate)) * up).astype(jnp.bfloat16)
        for gate, up in zip(gate_val, up_val)
    ]
    slot_weight = slot_ref[:, :1]
    for k in range(count):
        block = slice(k * cols, (k + 1) * cols)
        piece = sum(
            jnp.dot(part, refs_of[2][:, block], preferred_element_type=jnp.float32)
            for part, refs_of in zip(hidden, weights)
        )
        out_ref[k] = (piece * slot_weight).astype(jnp.bfloat16)


def run_experts(slots, pieces, gains, own, other):
    return call(
        expert_kernel,
        jax.ShapeDtypeStruct(pieces.shape, jnp.bfloat16),
        [VMEM_SPEC] * 9,
        [],
        12 * pieces.shape[1] * own[0].size, own[0].size * 12, 20,
    )(slots, pieces, gains, *own, *other)


def combine_kernel(sharers, taken_ref, pieces, out_ref):
    count, capacity, cols = pieces.shape
    spread = [taken_ref[k // sharers] for k in range(count)]
    rows = [pieces[k].astype(jnp.float32) for k in range(count)]
    out_ref[...] = lax.dot_general(
        jnp.concatenate(spread, axis=0).astype(jnp.bfloat16),
        jnp.concatenate(rows, axis=0).astype(jnp.bfloat16),
        (((0,), (0,)), ((), ())),
        preferred_element_type=jnp.float32,
    )


def combine(sharers, taken, pieces):
    count, capacity, cols = pieces.shape
    rows = taken.shape[2]
    return call(
        functools.partial(combine_kernel, sharers),
        jax.ShapeDtypeStruct((rows, cols), jnp.float32),
        [VMEM_SPEC] * 2,
        [],
        2 * rows * capacity * count * cols, (count * capacity * 2 + rows * 4) * cols, 4,
    )(taken, pieces)


def finish_kernel(stream_ref, mine_ref, other_ref, stream_out_ref, out_ref):
    stream_out_ref[...] = stream_ref[...]
    out_ref[...] = (mine_ref[...] + other_ref[...]).astype(jnp.bfloat16)


def finish(stream, mine, other):
    return call(
        finish_kernel,
        [jax.ShapeDtypeStruct(stream.shape, jnp.bfloat16)] * 2,
        [VMEM_SPEC] * 3,
        [],
        mine.size, mine.size * 14, 4,
    )(stream, mine, other)


def exchange(blocks):
    return lax.all_to_all(blocks, "attn", split_axis=0, concat_axis=0, tiled=True)


def swap(block):
    return lax.ppermute(block, "expert", [(0, 1), (1, 0)])


def shards(
    queries,
    key_cache,
    value_cache,
    new_key,
    new_value,
    cache_length,
    residual,
    out_weight,
    ln_gain,
    gate_weight,
    up_weight,
    down_weight,
    routes,
    route_weight,
):
    count = lax.axis_size("attn")
    sharers = count // HELD
    capacity = routes.shape[0] * TOP // EXPERTS

    earlier = order(routes.shape[0])
    weights = (gate_weight.T, up_weight.T, down_weight)
    other_weights = [swap(block) for block in weights]
    spread, own, limit, taken, slots = prepare(
        sharers, capacity, cache_length, earlier, routes.T, route_weight.T, queries, new_key
    )
    attended = exchange(
        attend(count, spread, own, limit, key_cache, value_cache, new_value, ln_gain)
    )
    mine, gains = project(attended, out_weight)
    stream, chosen = pick(sharers, count, mine, swap(mine), residual, taken)
    outgoing = run_experts(slots, exchange(chosen), gains, weights, other_weights)
    combined = combine(sharers, taken, exchange(outgoing))
    attn_stream, expert_out = finish(stream, combined, swap(combined))
    return (attn_stream, expert_out)


def solution(mesh):
    count = mesh.shape["attn"]
    fits = D // count % 256 == 0 and count % HELD == 0 and mesh.shape["expert"] == 2
    return jax.shard_map(
        shards if fits else shards_plain,
        mesh=mesh,
        in_specs=(
            P(("group", "attn"), "expert"),
            P(("group", "attn"), None, "expert"),
            P(("group", "attn"), None, "expert"),
            P(("group", "attn"), "expert"),
            P(("group", "attn"), "expert"),
            P(("group", "attn")),
            P("group", "attn"),
            P("expert", "attn"),
            P("attn"),
            P(None, ("attn", "expert")),
            P(None, ("attn", "expert")),
            P(("attn", "expert"), None),
            P("group", None),
            P("group", None),
        ),
        out_specs=(P("group", "attn"), P("group", "attn")),
        check_vma=False,
    )
```

```python
import functools
import math

import jax
import jax.numpy as jnp
from jax import lax
from jax.experimental import pallas as pl
from jax.experimental.pallas import tpu as pltpu
from jax.sharding import PartitionSpec as P

D = 6144
HEADS = 48
KV_HEADS = 8
HEAD_DIM = 128
EXPERTS = 16
TOP = 4
HELD = 2


NEG_FILL = -1e30
EPSILON = 1e-05


def attend_local(queries, key_cache, value_cache, new_key, new_value, cache_length):
    row_count = queries.shape[0]
    kv_local = new_key.shape[1] // HEAD_DIM
    group = HEADS // KV_HEADS
    length_max = key_cache.shape[1]
    query_heads = queries.reshape(row_count, kv_local, group, HEAD_DIM)
    key_heads = key_cache.reshape(row_count, length_max, kv_local, HEAD_DIM)
    value_heads = value_cache.reshape(row_count, length_max, kv_local, HEAD_DIM)
    own_keys = new_key.reshape(row_count, kv_local, HEAD_DIM)
    own_values = new_value.reshape(row_count, kv_local, HEAD_DIM)
    scale = 1.0 / math.sqrt(HEAD_DIM)
    past = (
        jnp.einsum("rkgd,rlkd->rkgl", query_heads, key_heads, preferred_element_type=jnp.float32)
        * scale
    )
    valid = jnp.arange(length_max, dtype=jnp.int32)[None, :] < cache_length[:, None]
    past = jnp.where(valid[:, None, None, :], past, NEG_FILL)
    own = (
        jnp.einsum("rkgd,rkd->rkg", query_heads, own_keys, preferred_element_type=jnp.float32)
        * scale
    )
    largest = jnp.maximum(jnp.max(past, axis=3), own)
    past_weight = jnp.exp(past - largest[..., None])
    own_weight = jnp.exp(own - largest)
    total = jnp.sum(past_weight, axis=3) + own_weight
    past_prob = (past_weight / total[..., None]).astype(jnp.bfloat16)
    own_prob = (own_weight / total).astype(jnp.bfloat16)
    result = jnp.einsum(
        "rkgl,rlkd->rkgd", past_prob, value_heads, preferred_element_type=jnp.float32
    )
    result = (
        result
        + own_prob.astype(jnp.float32)[..., None] * own_values.astype(jnp.float32)[:, :, None, :]
    )
    return result.reshape(row_count, kv_local * group * HEAD_DIM).astype(jnp.bfloat16)


def selection(routes, route_weight, capacity):
    row_count = routes.shape[0]
    experts = jnp.arange(HELD, dtype=jnp.int32)
    match = routes[None, :, :] == experts[:, None, None]
    hit = jnp.any(match, axis=2)
    row_weight = jnp.sum(jnp.where(match, route_weight[None], 0.0), axis=2)
    earlier = jnp.arange(row_count)[:, None] < jnp.arange(row_count)[None, :]
    slot = jnp.sum(jnp.where(earlier[None] & hit[:, :, None], 1, 0), axis=1)
    taken = hit[:, None, :] & (slot[:, None, :] == jnp.arange(capacity, dtype=jnp.int32)[None, :, None])
    slot_weight = jnp.sum(jnp.where(taken, row_weight[:, None, :], 0.0), axis=2)
    return taken, slot_weight


def gather_attn(block):
    count = lax.axis_size("attn")
    copies = jnp.broadcast_to(block[None], (count,) + block.shape)
    return lax.all_to_all(copies, "attn", split_axis=0, concat_axis=0, tiled=True)


def pair_sum(block):
    return block + lax.ppermute(block, "expert", [(0, 1), (1, 0)])


def shards_plain(
    queries,
    key_cache,
    value_cache,
    new_key,
    new_value,
    cache_length,
    residual,
    out_weight,
    ln_gain,
    gate_weight,
    up_weight,
    down_weight,
    routes,
    route_weight,
):
    attn_count = lax.axis_size("attn")
    core_count = lax.axis_size("expert")
    sharers = attn_count * core_count // HELD
    my_expert = (lax.axis_index("attn") * core_count + lax.axis_index("expert")) // sharers
    dest_expert = [index * core_count // sharers for index in range(attn_count)]
    row_count = routes.shape[0]
    capacity = row_count * TOP // EXPERTS * 2
    cols = residual.shape[1]

    taken, slot_weight = selection(routes, route_weight, capacity)
    pick = taken.astype(jnp.bfloat16)

    gains = gather_attn(ln_gain)

    attended = attend_local(queries, key_cache, value_cache, new_key, new_value, cache_length)
    whole = gather_attn(attended).reshape(row_count, -1)
    partial_proj = jnp.dot(whole, out_weight, preferred_element_type=jnp.float32)
    head_total = pair_sum(partial_proj)
    attn_stream = (residual.astype(jnp.float32) + head_total).astype(jnp.bfloat16)

    chosen = jnp.einsum(
        "esr,rd->esd", pick, attn_stream, preferred_element_type=jnp.float32
    ).astype(jnp.bfloat16)
    outgoing = jnp.stack([chosen[index] for index in dest_expert])
    rows = lax.all_to_all(outgoing, "attn", split_axis=0, concat_axis=0, tiled=True)
    wide = rows.astype(jnp.float32)
    row_mean = jnp.sum(wide, axis=(0, 2)) / D
    row_var = jnp.sum(wide * wide, axis=(0, 2)) / D - row_mean * row_mean
    normed = (
        (wide - row_mean[None, :, None])
        * lax.rsqrt(row_var + EPSILON)[None, :, None]
        * gains.reshape(attn_count, 1, cols)
    ).astype(jnp.bfloat16)
    gate_val = jnp.einsum(
        "asd,adf->sf", normed, gate_weight.reshape(attn_count, cols, -1),
        preferred_element_type=jnp.float32,
    )
    up_val = jnp.einsum(
        "asd,adf->sf", normed, up_weight.reshape(attn_count, cols, -1),
        preferred_element_type=jnp.float32,
    )
    hidden = (jax.nn.silu(gate_val) * up_val).astype(jnp.bfloat16)
    piece = jnp.dot(hidden, down_weight, preferred_element_type=jnp.float32)
    mine = jnp.take(slot_weight, my_expert, axis=0)
    piece = (piece * mine[:, None]).astype(jnp.bfloat16)
    returned = lax.all_to_all(
        piece.reshape(capacity, attn_count, cols).swapaxes(0, 1),
        "attn", split_axis=0, concat_axis=0, tiled=True,
    )
    spread = jnp.stack([pick[index] for index in dest_expert])
    combined = jnp.einsum(
        "asr,asd->rd", spread, returned, preferred_element_type=jnp.float32
    )
    expert_out = pair_sum(combined).astype(jnp.bfloat16)
    return (attn_stream, expert_out)


MIB = 1024 * 1024
EXCHANGE_FLOPS = 10**10
VMEM_SPEC = pl.BlockSpec(memory_space=pltpu.VMEM)
SMEM_SPEC = pl.BlockSpec(memory_space=pltpu.SMEM)
HBM_SPEC = pl.BlockSpec(memory_space=pltpu.HBM)


def call(kernel, outs, in_specs, scratch, flops, nbytes, vmem_mib):
    single = not isinstance(outs, (list, tuple))
    return pl.pallas_call(
        kernel,
        out_shape=outs,
        in_specs=in_specs,
        out_specs=VMEM_SPEC if single else [VMEM_SPEC] * len(outs),
        scratch_shapes=scratch,
        cost_estimate=pl.CostEstimate(flops=flops, bytes_accessed=nbytes, transcendentals=0),
        compiler_params=pltpu.CompilerParams(vmem_limit_bytes=vmem_mib * MIB),
    )


def order_kernel(out_ref):
    rows = out_ref.shape[0]
    before = lax.broadcasted_iota(jnp.int32, (rows, rows), 0) < lax.broadcasted_iota(
        jnp.int32, (rows, rows), 1
    )
    out_ref[...] = jnp.where(before, 1.0, 0.0).astype(jnp.bfloat16)


def order(rows):
    return call(
        order_kernel,
        jax.ShapeDtypeStruct((rows, rows), jnp.bfloat16),
        [],
        [],
        EXCHANGE_FLOPS, rows * rows * 2, 2,
    )()


def expert_rows(routes, earlier, expert, capacity):
    row_count = routes.shape[1]
    hit = jnp.max((routes == expert).astype(jnp.float32), axis=0, keepdims=True)
    slot = jnp.dot(
        jnp.broadcast_to(hit, (8, row_count)).astype(jnp.bfloat16),
        earlier,
        preferred_element_type=jnp.float32,
    )[:1]
    place = lax.broadcasted_iota(jnp.int32, (capacity, row_count), 0).astype(jnp.float32)
    return jnp.where((slot == place) & (hit > 0.5), 1.0, 0.0)


def prepare_kernel(sharers, length_ref, earlier_ref, routes_ref, weight_ref, query_ref,
                   own_key_ref, spread_ref, own_ref, limit_ref, taken_ref, slot_ref, query_rows,
                   key_rows):
    row_count = query_ref.shape[0]
    kv_local = own_key_ref.shape[1] // HEAD_DIM
    group = HEADS // KV_HEADS
    heads = kv_local * group
    for g in range(kv_local):
        own_key = own_key_ref[:, g * HEAD_DIM : (g + 1) * HEAD_DIM].astype(jnp.float32)
        for i in range(group):
            index = g * group + i
            rows = pl.ds(index * row_count, row_count)
            query_rows[rows, :] = query_ref[
                :, index * HEAD_DIM : (index + 1) * HEAD_DIM
            ].astype(jnp.float32)
            key_rows[rows, :] = own_key
    scale = 1.0 / math.sqrt(HEAD_DIM)
    lengths = length_ref[...].reshape(1, -1)
    head = lax.broadcasted_iota(jnp.int32, (heads, 1), 0) // group
    for r in range(row_count):
        strided = pl.ds(r, heads, stride=row_count)
        query = query_rows[strided, :]
        own = jnp.sum(query * key_rows[strided, :], axis=1, keepdims=True) * scale
        own_ref[r] = jnp.broadcast_to(own, (heads, HEAD_DIM))
        limit_ref[r] = jnp.broadcast_to(lengths[:, r : r + 1], (heads, HEAD_DIM))
        spread_ref[r] = jnp.concatenate(
            [jnp.where(head == g, query, 0.0) for g in range(kv_local)], axis=1
        ).astype(jnp.bfloat16)
    routes = routes_ref[...]
    capacity = slot_ref.shape[0]
    core = lax.axis_index("expert")
    taken = []
    for e in range(HELD):
        both = expert_rows(routes, earlier_ref[...], e, 2 * capacity)
        taken.append(jnp.where(core == 0, both[:capacity], both[capacity:]))
        taken_ref[e] = taken[e]
    first = lax.axis_index("attn") < sharers
    expert = jnp.where(first, 0, 1)
    row_weight = jnp.sum(
        jnp.where(routes == expert, weight_ref[...], 0.0), axis=0, keepdims=True
    )
    mine = jnp.where(first, taken[0], taken[1])
    slot_ref[...] = jnp.broadcast_to(
        jnp.sum(mine * row_weight, axis=1, keepdims=True), slot_ref.shape
    )


def prepare(
    sharers, capacity, cache_length, earlier, routes, route_weight, queries, new_key
):
    row_count, width = queries.shape
    heads = width // HEAD_DIM
    table = pltpu.VMEM((heads * row_count, HEAD_DIM), jnp.float32)
    return call(
        functools.partial(prepare_kernel, sharers),
        [
            jax.ShapeDtypeStruct((row_count, heads, new_key.shape[1]), jnp.bfloat16),
            jax.ShapeDtypeStruct((row_count, heads, HEAD_DIM), jnp.float32),
            jax.ShapeDtypeStruct((row_count, heads, HEAD_DIM), jnp.int32),
            jax.ShapeDtypeStruct((HELD, capacity, routes.shape[1]), jnp.float32),
            jax.ShapeDtypeStruct((capacity, HEAD_DIM), jnp.float32),
        ],
        [VMEM_SPEC] * 6,
        [table, table],
        queries.size * 8, queries.size * 16, 4,
    )(cache_length, earlier, routes, route_weight, queries, new_key)


def score_kernel(spread_ref, own_ref, limit_ref, key_ref, probs_ref, own_probs_ref):
    row_count, heads, length_max = probs_ref.shape
    scale = 1.0 / math.sqrt(HEAD_DIM)
    contract = (((1,), (1,)), ((), ()))
    scores = jnp.concatenate(
        [
            lax.dot_general(
                spread_ref[r], key_ref[r], contract, preferred_element_type=jnp.float32
            )
            for r in range(row_count)
        ],
        axis=0,
    )
    position = lax.broadcasted_iota(jnp.int32, scores.shape, 1)
    limit = jnp.concatenate([limit_ref[r, :, :1] for r in range(row_count)], axis=0)
    own = jnp.concatenate([own_ref[r, :, :1] for r in range(row_count)], axis=0)
    past = jnp.where(position < limit, scores * scale, NEG_FILL)
    largest = jnp.maximum(jnp.max(past, axis=1, keepdims=True), own)
    weight = jnp.exp(past - largest)
    own_weight = jnp.exp(own - largest)
    inverse = 1.0 / (jnp.sum(weight, axis=1, keepdims=True) + own_weight)
    probs = weight * inverse
    own_prob = (own_weight * inverse).astype(jnp.bfloat16).astype(jnp.float32)
    for r in range(row_count):
        rows = slice(r * heads, (r + 1) * heads)
        probs_ref[r] = probs[rows].astype(jnp.bfloat16)
        own_probs_ref[r] = jnp.broadcast_to(own_prob[rows], own_probs_ref.shape[1:])


def value_kernel(probs_ref, own_ref, value_ref, own_value_ref, gain_ref, out_ref, value_rows,
                 result_rows):
    row_count, length_max, width = value_ref.shape
    kv_local = width // HEAD_DIM
    group = HEADS // KV_HEADS
    heads = kv_local * group
    for g in range(kv_local):
        own_value = own_value_ref[:, g * HEAD_DIM : (g + 1) * HEAD_DIM].astype(jnp.float32)
        for i in range(group):
            value_rows[pl.ds((g * group + i) * row_count, row_count), :] = own_value
    head = lax.broadcasted_iota(jnp.int32, (heads, 1), 0) // group
    for r in range(row_count):
        strided = pl.ds(r, heads, stride=row_count)
        product = jnp.dot(probs_ref[r], value_ref[r], preferred_element_type=jnp.float32)
        total = own_ref[r] * value_rows[strided, :]
        for g in range(kv_local):
            lanes = slice(g * HEAD_DIM, (g + 1) * HEAD_DIM)
            total = total + jnp.where(head == g, product[:, lanes], 0.0)
        result_rows[strided, :] = total
    for index in range(heads):
        rows = result_rows[pl.ds(index * row_count, row_count), :].astype(jnp.bfloat16)
        for copy in range(out_ref.shape[0]):
            out_ref[copy, :, index * HEAD_DIM : (index + 1) * HEAD_DIM] = rows
    gain_row = gain_ref[...].reshape(1, -1)
    half = gain_row.shape[1] // 2
    row = lax.broadcasted_iota(jnp.int32, (row_count, half), 0)
    left = jnp.broadcast_to(gain_row[:, :half], (row_count, half))
    right = jnp.broadcast_to(gain_row[:, half:], (row_count, half))
    gain = jnp.where(row % 2 == 0, left, right)
    upper = gain.astype(jnp.bfloat16).astype(jnp.float32)
    parts = jnp.where(row < 2, upper, gain - upper).astype(jnp.bfloat16)
    for copy in range(out_ref.shape[0]):
        out_ref[copy, :, heads * HEAD_DIM :] = parts


def attend(count, spread, own, limit, key_cache, value_cache, new_value, gain):
    row_count, heads, _ = spread.shape
    length_max = key_cache.shape[1]
    table = pltpu.VMEM((heads * row_count, HEAD_DIM), jnp.float32)
    probs, own_probs = call(
        score_kernel,
        [
            jax.ShapeDtypeStruct((row_count, heads, length_max), jnp.bfloat16),
            jax.ShapeDtypeStruct((row_count, heads, HEAD_DIM), jnp.float32),
        ],
        [VMEM_SPEC] * 4,
        [],
        2 * key_cache.size * heads, key_cache.size * 2, 8,
    )(spread, own, limit, key_cache)
    width = heads * HEAD_DIM + gain.shape[0] // 2
    return call(
        value_kernel,
        jax.ShapeDtypeStruct((count, row_count, width), jnp.bfloat16),
        [VMEM_SPEC] * 5,
        [table, table],
        EXCHANGE_FLOPS, value_cache.size * 2, 8,
    )(probs, own_probs, value_cache, new_value, gain)


def project_kernel(pieces, weight_ref, out_ref, gain_ref, stack):
    count, rows, _ = pieces.shape
    width = weight_ref.shape[0]
    half = gain_ref.shape[1] // 2
    for k in range(count):
        stack[pl.ds(k * rows, rows), :] = pieces[k, :, :width].astype(jnp.float32)
        parts = pieces[k, :, width:].astype(jnp.float32)
        gain_ref[pl.ds(k, 1), :half] = parts[0:1] + parts[2:3]
        gain_ref[pl.ds(k, 1), half:] = parts[1:2] + parts[3:4]
    out_ref[...] = jnp.dot(
        stack[...].astype(jnp.bfloat16), weight_ref[...], preferred_element_type=jnp.float32
    )


def project(pieces, out_weight):
    count, rows, _ = pieces.shape
    depth, cols = out_weight.shape
    return call(
        project_kernel,
        [
            jax.ShapeDtypeStruct((rows * count, cols), jnp.float32),
            jax.ShapeDtypeStruct((count, cols), jnp.float32),
        ],
        [VMEM_SPEC, VMEM_SPEC],
        [pltpu.VMEM((rows * count, depth), jnp.float32)],
        EXCHANGE_FLOPS, out_weight.size * 2, 10,
    )(pieces, out_weight)


def pick_kernel(sharers, mine_ref, other_ref, residual_ref, taken_ref, stream_ref, out_ref):
    stream = (
        residual_ref[...].astype(jnp.float32) + (mine_ref[...] + other_ref[...])
    ).astype(jnp.bfloat16)
    stream_ref[...] = stream
    chosen = [
        jnp.dot(
            taken_ref[e].astype(jnp.bfloat16), stream, preferred_element_type=jnp.float32
        ).astype(jnp.bfloat16)
        for e in range(HELD)
    ]
    for k in range(out_ref.shape[0]):
        out_ref[k] = chosen[k // sharers]


def pick(sharers, count, mine, other, residual, taken):
    rows, cols = mine.shape
    return call(
        functools.partial(pick_kernel, sharers),
        [
            jax.ShapeDtypeStruct((rows, cols), jnp.bfloat16),
            jax.ShapeDtypeStruct((count, taken.shape[1], cols), jnp.bfloat16),
        ],
        [VMEM_SPEC] * 4,
        [],
        2 * HELD * taken.shape[1] * rows * cols, rows * cols * 12, 4,
    )(mine, other, residual, taken)


def expert_kernel(slot_ref, pieces, gains, *refs):
    weights, out_ref, rows_ref = (refs[:3], refs[3:6]), refs[6], refs[7]
    count, capacity, cols = pieces.shape
    first = second = 0.0
    for k in range(count):
        wide = pieces[k].astype(jnp.float32)
        first = first + wide
        second = second + wide * wide
    row_mean = jnp.sum(first, axis=1, keepdims=True) / D
    row_var = jnp.sum(second, axis=1, keepdims=True) / D - row_mean * row_mean
    inverse = lax.rsqrt(row_var + EPSILON)
    for k in range(count):
        wide = pieces[k].astype(jnp.float32)
        normed = (wide - row_mean) * inverse * gains[pl.ds(k, 1), :]
        rows_ref[:, k * cols : (k + 1) * cols] = normed.astype(jnp.bfloat16)
    rows = rows_ref[...]
    contract = (((1,), (1,)), ((), ()))
    hidden = []
    for gate_ref, up_ref, _ in weights:
        gate = lax.dot_general(rows, gate_ref[...], contract, preferred_element_type=jnp.float32)
        up = lax.dot_general(rows, up_ref[...], contract, preferred_element_type=jnp.float32)
        hidden.append((gate / (1.0 + jnp.exp(-gate)) * up).astype(jnp.bfloat16))
    slot_weight = slot_ref[:, :1]
    for k in range(count):
        block = slice(k * cols, (k + 1) * cols)
        piece = sum(
            jnp.dot(part, refs_of[2][:, block], preferred_element_type=jnp.float32)
            for part, refs_of in zip(hidden, weights)
        )
        out_ref[k] = (piece * slot_weight).astype(jnp.bfloat16)


def run_experts(slots, pieces, gains, own, other):
    count, capacity, cols = pieces.shape
    return call(
        expert_kernel,
        jax.ShapeDtypeStruct(pieces.shape, jnp.bfloat16),
        [VMEM_SPEC] * 9,
        [pltpu.VMEM((capacity, count * cols), jnp.bfloat16)],
        12 * capacity * own[0].size, own[0].size * 12, 20,
    )(slots, pieces, gains, *own, *other)


def combine_kernel(sharers, taken_ref, pieces, out_ref):
    count, capacity, cols = pieces.shape
    spread = [taken_ref[k // sharers] for k in range(count)]
    rows = [pieces[k].astype(jnp.float32) for k in range(count)]
    out_ref[...] = lax.dot_general(
        jnp.concatenate(spread, axis=0).astype(jnp.bfloat16),
        jnp.concatenate(rows, axis=0).astype(jnp.bfloat16),
        (((0,), (0,)), ((), ())),
        preferred_element_type=jnp.float32,
    )


def combine(sharers, taken, pieces):
    count, capacity, cols = pieces.shape
    rows = taken.shape[2]
    return call(
        functools.partial(combine_kernel, sharers),
        jax.ShapeDtypeStruct((rows, cols), jnp.float32),
        [VMEM_SPEC] * 2,
        [],
        2 * rows * capacity * count * cols, (count * capacity * 2 + rows * 4) * cols, 4,
    )(taken, pieces)


def finish_kernel(stream_ref, mine_ref, other_ref, stream_out_ref, out_ref):
    stream_out_ref[...] = stream_ref[...]
    out_ref[...] = (mine_ref[...] + other_ref[...]).astype(jnp.bfloat16)


def finish(stream, mine, other):
    return call(
        finish_kernel,
        [jax.ShapeDtypeStruct(stream.shape, jnp.bfloat16)] * 2,
        [VMEM_SPEC] * 3,
        [],
        mine.size, mine.size * 14, 4,
    )(stream, mine, other)


def exchange(blocks):
    return lax.all_to_all(blocks, "attn", split_axis=0, concat_axis=0, tiled=True)


def swap(block):
    return lax.ppermute(block, "expert", [(0, 1), (1, 0)])


def shards(
    queries,
    key_cache,
    value_cache,
    new_key,
    new_value,
    cache_length,
    residual,
    out_weight,
    ln_gain,
    gate_weight,
    up_weight,
    down_weight,
    routes,
    route_weight,
):
    count = lax.axis_size("attn")
    sharers = count // HELD
    capacity = routes.shape[0] * TOP // EXPERTS

    earlier = order(routes.shape[0])
    weights = (gate_weight.T, up_weight.T, down_weight)
    spread, own, limit, taken, slots = prepare(
        sharers, capacity, cache_length, earlier, routes.T, route_weight.T, queries, new_key
    )
    other_weights = [swap(block) for block in weights]
    attended = exchange(
        attend(count, spread, own, limit, key_cache, value_cache, new_value, ln_gain)
    )
    mine, gains = project(attended, out_weight)
    stream, chosen = pick(sharers, count, mine, swap(mine), residual, taken)
    outgoing = run_experts(slots, exchange(chosen), gains, weights, other_weights)
    combined = combine(sharers, taken, exchange(outgoing))
    attn_stream, expert_out = finish(stream, combined, swap(combined))
    return (attn_stream, expert_out)


def solution(mesh):
    count = mesh.shape["attn"]
    fits = D // count % 256 == 0 and count % HELD == 0 and mesh.shape["expert"] == 2
    return jax.shard_map(
        shards if fits else shards_plain,
        mesh=mesh,
        in_specs=(
            P(("group", "attn"), "expert"),
            P(("group", "attn"), None, "expert"),
            P(("group", "attn"), None, "expert"),
            P(("group", "attn"), "expert"),
            P(("group", "attn"), "expert"),
            P(("group", "attn")),
            P("group", "attn"),
            P("expert", "attn"),
            P("attn"),
            P(None, ("attn", "expert")),
            P(None, ("attn", "expert")),
            P(("attn", "expert"), None),
            P("group", None),
            P("group", None),
        ),
        out_specs=(P("group", "attn"), P("group", "attn")),
        check_vma=False,
    )
```

```python
import functools
import math

import jax
import jax.numpy as jnp
from jax import lax
from jax.experimental import pallas as pl
from jax.experimental.pallas import tpu as pltpu
from jax.sharding import PartitionSpec as P

D = 6144
HEADS = 48
KV_HEADS = 8
HEAD_DIM = 128
EXPERTS = 16
TOP = 4
HELD = 2


NEG_FILL = -1e30
EPSILON = 1e-05


def attend_local(queries, key_cache, value_cache, new_key, new_value, cache_length):
    row_count = queries.shape[0]
    kv_local = new_key.shape[1] // HEAD_DIM
    group = HEADS // KV_HEADS
    length_max = key_cache.shape[1]
    query_heads = queries.reshape(row_count, kv_local, group, HEAD_DIM)
    key_heads = key_cache.reshape(row_count, length_max, kv_local, HEAD_DIM)
    value_heads = value_cache.reshape(row_count, length_max, kv_local, HEAD_DIM)
    own_keys = new_key.reshape(row_count, kv_local, HEAD_DIM)
    own_values = new_value.reshape(row_count, kv_local, HEAD_DIM)
    scale = 1.0 / math.sqrt(HEAD_DIM)
    past = (
        jnp.einsum("rkgd,rlkd->rkgl", query_heads, key_heads, preferred_element_type=jnp.float32)
        * scale
    )
    valid = jnp.arange(length_max, dtype=jnp.int32)[None, :] < cache_length[:, None]
    past = jnp.where(valid[:, None, None, :], past, NEG_FILL)
    own = (
        jnp.einsum("rkgd,rkd->rkg", query_heads, own_keys, preferred_element_type=jnp.float32)
        * scale
    )
    largest = jnp.maximum(jnp.max(past, axis=3), own)
    past_weight = jnp.exp(past - largest[..., None])
    own_weight = jnp.exp(own - largest)
    total = jnp.sum(past_weight, axis=3) + own_weight
    past_prob = (past_weight / total[..., None]).astype(jnp.bfloat16)
    own_prob = (own_weight / total).astype(jnp.bfloat16)
    result = jnp.einsum(
        "rkgl,rlkd->rkgd", past_prob, value_heads, preferred_element_type=jnp.float32
    )
    result = (
        result
        + own_prob.astype(jnp.float32)[..., None] * own_values.astype(jnp.float32)[:, :, None, :]
    )
    return result.reshape(row_count, kv_local * group * HEAD_DIM).astype(jnp.bfloat16)


def selection(routes, route_weight, capacity):
    row_count = routes.shape[0]
    experts = jnp.arange(HELD, dtype=jnp.int32)
    match = routes[None, :, :] == experts[:, None, None]
    hit = jnp.any(match, axis=2)
    row_weight = jnp.sum(jnp.where(match, route_weight[None], 0.0), axis=2)
    earlier = jnp.arange(row_count)[:, None] < jnp.arange(row_count)[None, :]
    slot = jnp.sum(jnp.where(earlier[None] & hit[:, :, None], 1, 0), axis=1)
    taken = hit[:, None, :] & (slot[:, None, :] == jnp.arange(capacity, dtype=jnp.int32)[None, :, None])
    slot_weight = jnp.sum(jnp.where(taken, row_weight[:, None, :], 0.0), axis=2)
    return taken, slot_weight


def gather_attn(block):
    count = lax.axis_size("attn")
    copies = jnp.broadcast_to(block[None], (count,) + block.shape)
    return lax.all_to_all(copies, "attn", split_axis=0, concat_axis=0, tiled=True)


def pair_sum(block):
    return block + lax.ppermute(block, "expert", [(0, 1), (1, 0)])


def shards_plain(
    queries,
    key_cache,
    value_cache,
    new_key,
    new_value,
    cache_length,
    residual,
    out_weight,
    ln_gain,
    gate_weight,
    up_weight,
    down_weight,
    routes,
    route_weight,
):
    attn_count = lax.axis_size("attn")
    core_count = lax.axis_size("expert")
    sharers = attn_count * core_count // HELD
    my_expert = (lax.axis_index("attn") * core_count + lax.axis_index("expert")) // sharers
    dest_expert = [index * core_count // sharers for index in range(attn_count)]
    row_count = routes.shape[0]
    capacity = row_count * TOP // EXPERTS * 2
    cols = residual.shape[1]

    taken, slot_weight = selection(routes, route_weight, capacity)
    pick = taken.astype(jnp.bfloat16)

    gains = gather_attn(ln_gain)

    attended = attend_local(queries, key_cache, value_cache, new_key, new_value, cache_length)
    whole = gather_attn(attended).reshape(row_count, -1)
    partial_proj = jnp.dot(whole, out_weight, preferred_element_type=jnp.float32)
    head_total = pair_sum(partial_proj)
    attn_stream = (residual.astype(jnp.float32) + head_total).astype(jnp.bfloat16)

    chosen = jnp.einsum(
        "esr,rd->esd", pick, attn_stream, preferred_element_type=jnp.float32
    ).astype(jnp.bfloat16)
    outgoing = jnp.stack([chosen[index] for index in dest_expert])
    rows = lax.all_to_all(outgoing, "attn", split_axis=0, concat_axis=0, tiled=True)
    wide = rows.astype(jnp.float32)
    row_mean = jnp.sum(wide, axis=(0, 2)) / D
    row_var = jnp.sum(wide * wide, axis=(0, 2)) / D - row_mean * row_mean
    normed = (
        (wide - row_mean[None, :, None])
        * lax.rsqrt(row_var + EPSILON)[None, :, None]
        * gains.reshape(attn_count, 1, cols)
    ).astype(jnp.bfloat16)
    gate_val = jnp.einsum(
        "asd,adf->sf", normed, gate_weight.reshape(attn_count, cols, -1),
        preferred_element_type=jnp.float32,
    )
    up_val = jnp.einsum(
        "asd,adf->sf", normed, up_weight.reshape(attn_count, cols, -1),
        preferred_element_type=jnp.float32,
    )
    hidden = (jax.nn.silu(gate_val) * up_val).astype(jnp.bfloat16)
    piece = jnp.dot(hidden, down_weight, preferred_element_type=jnp.float32)
    mine = jnp.take(slot_weight, my_expert, axis=0)
    piece = (piece * mine[:, None]).astype(jnp.bfloat16)
    returned = lax.all_to_all(
        piece.reshape(capacity, attn_count, cols).swapaxes(0, 1),
        "attn", split_axis=0, concat_axis=0, tiled=True,
    )
    spread = jnp.stack([pick[index] for index in dest_expert])
    combined = jnp.einsum(
        "asr,asd->rd", spread, returned, preferred_element_type=jnp.float32
    )
    expert_out = pair_sum(combined).astype(jnp.bfloat16)
    return (attn_stream, expert_out)


MIB = 1024 * 1024
EXCHANGE_FLOPS = 10**10
VMEM_SPEC = pl.BlockSpec(memory_space=pltpu.VMEM)
SMEM_SPEC = pl.BlockSpec(memory_space=pltpu.SMEM)
HBM_SPEC = pl.BlockSpec(memory_space=pltpu.HBM)


def call(kernel, outs, in_specs, scratch, flops, nbytes, vmem_mib):
    single = not isinstance(outs, (list, tuple))
    return pl.pallas_call(
        kernel,
        out_shape=outs,
        in_specs=in_specs,
        out_specs=VMEM_SPEC if single else [VMEM_SPEC] * len(outs),
        scratch_shapes=scratch,
        cost_estimate=pl.CostEstimate(flops=flops, bytes_accessed=nbytes, transcendentals=0),
        compiler_params=pltpu.CompilerParams(vmem_limit_bytes=vmem_mib * MIB),
    )


def order_kernel(out_ref):
    rows = out_ref.shape[0]
    before = lax.broadcasted_iota(jnp.int32, (rows, rows), 0) < lax.broadcasted_iota(
        jnp.int32, (rows, rows), 1
    )
    out_ref[...] = jnp.where(before, 1.0, 0.0).astype(jnp.bfloat16)


def order(rows):
    return call(
        order_kernel,
        jax.ShapeDtypeStruct((rows, rows), jnp.bfloat16),
        [],
        [],
        EXCHANGE_FLOPS, rows * rows * 2, 2,
    )()


def expert_rows(routes, earlier, expert, capacity):
    row_count = routes.shape[1]
    hit = jnp.max((routes == expert).astype(jnp.float32), axis=0, keepdims=True)
    slot = jnp.dot(
        jnp.broadcast_to(hit, (8, row_count)).astype(jnp.bfloat16),
        earlier,
        preferred_element_type=jnp.float32,
    )[:1]
    place = lax.broadcasted_iota(jnp.int32, (capacity, row_count), 0).astype(jnp.float32)
    return jnp.where((slot == place) & (hit > 0.5), 1.0, 0.0)


def prepare_kernel(sharers, length_ref, earlier_ref, routes_ref, weight_ref, query_ref,
                   own_key_ref, spread_ref, own_ref, limit_ref, taken_ref, slot_ref, query_rows,
                   key_rows):
    row_count = query_ref.shape[0]
    kv_local = own_key_ref.shape[1] // HEAD_DIM
    group = HEADS // KV_HEADS
    heads = kv_local * group
    for g in range(kv_local):
        own_key = own_key_ref[:, g * HEAD_DIM : (g + 1) * HEAD_DIM].astype(jnp.float32)
        for i in range(group):
            index = g * group + i
            rows = pl.ds(index * row_count, row_count)
            query_rows[rows, :] = query_ref[
                :, index * HEAD_DIM : (index + 1) * HEAD_DIM
            ].astype(jnp.float32)
            key_rows[rows, :] = own_key
    scale = 1.0 / math.sqrt(HEAD_DIM)
    lengths = length_ref[...].reshape(1, -1)
    head = lax.broadcasted_iota(jnp.int32, (heads, 1), 0) // group
    for r in range(row_count):
        strided = pl.ds(r, heads, stride=row_count)
        query = query_rows[strided, :]
        own = jnp.sum(query * key_rows[strided, :], axis=1, keepdims=True) * scale
        own_ref[r] = jnp.broadcast_to(own, (heads, HEAD_DIM))
        limit_ref[r] = jnp.broadcast_to(lengths[:, r : r + 1], (heads, HEAD_DIM))
        spread_ref[r] = jnp.concatenate(
            [jnp.where(head == g, query, 0.0) for g in range(kv_local)], axis=1
        ).astype(jnp.bfloat16)
    routes = routes_ref[...]
    capacity = slot_ref.shape[0]
    core = lax.axis_index("expert")
    taken = []
    for e in range(HELD):
        both = expert_rows(routes, earlier_ref[...], e, 2 * capacity)
        taken.append(jnp.where(core == 0, both[:capacity], both[capacity:]))
        taken_ref[e] = taken[e]
    first = lax.axis_index("attn") < sharers
    expert = jnp.where(first, 0, 1)
    row_weight = jnp.sum(
        jnp.where(routes == expert, weight_ref[...], 0.0), axis=0, keepdims=True
    )
    mine = jnp.where(first, taken[0], taken[1])
    slot_ref[...] = jnp.broadcast_to(
        jnp.sum(mine * row_weight, axis=1, keepdims=True), slot_ref.shape
    )


def prepare(
    sharers, capacity, cache_length, earlier, routes, route_weight, queries, new_key
):
    row_count, width = queries.shape
    heads = width // HEAD_DIM
    table = pltpu.VMEM((heads * row_count, HEAD_DIM), jnp.float32)
    return call(
        functools.partial(prepare_kernel, sharers),
        [
            jax.ShapeDtypeStruct((row_count, heads, new_key.shape[1]), jnp.bfloat16),
            jax.ShapeDtypeStruct((row_count, heads, HEAD_DIM), jnp.float32),
            jax.ShapeDtypeStruct((row_count, heads, HEAD_DIM), jnp.int32),
            jax.ShapeDtypeStruct((HELD, capacity, routes.shape[1]), jnp.float32),
            jax.ShapeDtypeStruct((capacity, HEAD_DIM), jnp.float32),
        ],
        [VMEM_SPEC] * 6,
        [table, table],
        queries.size * 8, queries.size * 16, 4,
    )(cache_length, earlier, routes, route_weight, queries, new_key)


def score_kernel(spread_ref, own_ref, limit_ref, key_ref, probs_ref, own_probs_ref):
    row_count, heads, length_max = probs_ref.shape
    scale = 1.0 / math.sqrt(HEAD_DIM)
    contract = (((1,), (1,)), ((), ()))
    scores = jnp.concatenate(
        [
            lax.dot_general(
                spread_ref[r], key_ref[r], contract, preferred_element_type=jnp.float32
            )
            for r in range(row_count)
        ],
        axis=0,
    )
    position = lax.broadcasted_iota(jnp.int32, scores.shape, 1)
    limit = jnp.concatenate([limit_ref[r, :, :1] for r in range(row_count)], axis=0)
    own = jnp.concatenate([own_ref[r, :, :1] for r in range(row_count)], axis=0)
    past = jnp.where(position < limit, scores * scale, NEG_FILL)
    largest = jnp.maximum(jnp.max(past, axis=1, keepdims=True), own)
    weight = jnp.exp(past - largest)
    own_weight = jnp.exp(own - largest)
    inverse = 1.0 / (jnp.sum(weight, axis=1, keepdims=True) + own_weight)
    probs = weight * inverse
    own_prob = (own_weight * inverse).astype(jnp.bfloat16).astype(jnp.float32)
    for r in range(row_count):
        rows = slice(r * heads, (r + 1) * heads)
        probs_ref[r] = probs[rows].astype(jnp.bfloat16)
        own_probs_ref[r] = jnp.broadcast_to(own_prob[rows], own_probs_ref.shape[1:])


def value_kernel(probs_ref, own_ref, value_ref, own_value_ref, gain_ref, out_ref, value_rows,
                 result_rows):
    row_count, length_max, width = value_ref.shape
    kv_local = width // HEAD_DIM
    group = HEADS // KV_HEADS
    heads = kv_local * group
    for g in range(kv_local):
        own_value = own_value_ref[:, g * HEAD_DIM : (g + 1) * HEAD_DIM].astype(jnp.float32)
        for i in range(group):
            value_rows[pl.ds((g * group + i) * row_count, row_count), :] = own_value
    head = lax.broadcasted_iota(jnp.int32, (heads, 1), 0) // group
    for r in range(row_count):
        strided = pl.ds(r, heads, stride=row_count)
        product = jnp.dot(probs_ref[r], value_ref[r], preferred_element_type=jnp.float32)
        total = own_ref[r] * value_rows[strided, :]
        for g in range(kv_local):
            lanes = slice(g * HEAD_DIM, (g + 1) * HEAD_DIM)
            total = total + jnp.where(head == g, product[:, lanes], 0.0)
        result_rows[strided, :] = total
    for index in range(heads):
        rows = result_rows[pl.ds(index * row_count, row_count), :].astype(jnp.bfloat16)
        for copy in range(out_ref.shape[0]):
            out_ref[copy, :, index * HEAD_DIM : (index + 1) * HEAD_DIM] = rows
    gain_row = gain_ref[...].reshape(1, -1)
    half = gain_row.shape[1] // 2
    row = lax.broadcasted_iota(jnp.int32, (row_count, half), 0)
    left = jnp.broadcast_to(gain_row[:, :half], (row_count, half))
    right = jnp.broadcast_to(gain_row[:, half:], (row_count, half))
    gain = jnp.where(row % 2 == 0, left, right)
    upper = gain.astype(jnp.bfloat16).astype(jnp.float32)
    parts = jnp.where(row < 2, upper, gain - upper).astype(jnp.bfloat16)
    for copy in range(out_ref.shape[0]):
        out_ref[copy, :, heads * HEAD_DIM :] = parts


def attend(count, spread, own, limit, key_cache, value_cache, new_value, gain):
    row_count, heads, _ = spread.shape
    length_max = key_cache.shape[1]
    table = pltpu.VMEM((heads * row_count, HEAD_DIM), jnp.float32)
    probs, own_probs = call(
        score_kernel,
        [
            jax.ShapeDtypeStruct((row_count, heads, length_max), jnp.bfloat16),
            jax.ShapeDtypeStruct((row_count, heads, HEAD_DIM), jnp.float32),
        ],
        [VMEM_SPEC] * 4,
        [],
        2 * key_cache.size * heads, key_cache.size * 2, 8,
    )(spread, own, limit, key_cache)
    width = heads * HEAD_DIM + gain.shape[0] // 2
    return call(
        value_kernel,
        jax.ShapeDtypeStruct((count, row_count, width), jnp.bfloat16),
        [VMEM_SPEC] * 5,
        [table, table],
        EXCHANGE_FLOPS, value_cache.size * 2, 8,
    )(probs, own_probs, value_cache, new_value, gain)


def project_kernel(pieces, weight_ref, out_ref, gain_ref, stack):
    count, rows, _ = pieces.shape
    width = weight_ref.shape[0]
    half = gain_ref.shape[1] // 2
    for k in range(count):
        stack[pl.ds(k * rows, rows), :] = pieces[k, :, :width].astype(jnp.float32)
        parts = pieces[k, :, width:].astype(jnp.float32)
        gain_ref[pl.ds(k, 1), :half] = parts[0:1] + parts[2:3]
        gain_ref[pl.ds(k, 1), half:] = parts[1:2] + parts[3:4]
    out_ref[...] = jnp.dot(
        stack[...].astype(jnp.bfloat16), weight_ref[...], preferred_element_type=jnp.float32
    )


def project(pieces, out_weight):
    count, rows, _ = pieces.shape
    depth, cols = out_weight.shape
    return call(
        project_kernel,
        [
            jax.ShapeDtypeStruct((rows * count, cols), jnp.float32),
            jax.ShapeDtypeStruct((count, cols), jnp.float32),
        ],
        [VMEM_SPEC, VMEM_SPEC],
        [pltpu.VMEM((rows * count, depth), jnp.float32)],
        EXCHANGE_FLOPS, out_weight.size * 2, 10,
    )(pieces, out_weight)


def pick_kernel(sharers, mine_ref, other_ref, residual_ref, taken_ref, stream_ref, out_ref):
    stream = (
        residual_ref[...].astype(jnp.float32) + (mine_ref[...] + other_ref[...])
    ).astype(jnp.bfloat16)
    stream_ref[...] = stream
    chosen = [
        jnp.dot(
            taken_ref[e].astype(jnp.bfloat16), stream, preferred_element_type=jnp.float32
        ).astype(jnp.bfloat16)
        for e in range(HELD)
    ]
    for k in range(out_ref.shape[0]):
        out_ref[k] = chosen[k // sharers]


def pick(sharers, count, mine, other, residual, taken):
    rows, cols = mine.shape
    return call(
        functools.partial(pick_kernel, sharers),
        [
            jax.ShapeDtypeStruct((rows, cols), jnp.bfloat16),
            jax.ShapeDtypeStruct((count, taken.shape[1], cols), jnp.bfloat16),
        ],
        [VMEM_SPEC] * 4,
        [],
        2 * HELD * taken.shape[1] * rows * cols, rows * cols * 12, 4,
    )(mine, other, residual, taken)


def expert_kernel(slot_ref, pieces, gains, *refs):
    weights, out_ref, rows_ref = (refs[:3], refs[3:6]), refs[6], refs[7]
    count, capacity, cols = pieces.shape
    first = second = 0.0
    for k in range(count):
        wide = pieces[k].astype(jnp.float32)
        first = first + wide
        second = second + wide * wide
    row_mean = jnp.sum(first, axis=1, keepdims=True) / D
    row_var = jnp.sum(second, axis=1, keepdims=True) / D - row_mean * row_mean
    inverse = lax.rsqrt(row_var + EPSILON)
    for k in range(count):
        wide = pieces[k].astype(jnp.float32)
        normed = (wide - row_mean) * inverse * gains[pl.ds(k, 1), :]
        rows_ref[:, k * cols : (k + 1) * cols] = normed.astype(jnp.bfloat16)
    rows = rows_ref[...]
    contract = (((1,), (1,)), ((), ()))
    hidden = []
    for gate_ref, up_ref, _ in weights:
        gate = lax.dot_general(rows, gate_ref[...], contract, preferred_element_type=jnp.float32)
        up = lax.dot_general(up_ref[...], rows, contract, preferred_element_type=jnp.float32).T
        hidden.append((gate / (1.0 + jnp.exp(-gate)) * up).astype(jnp.bfloat16))
    slot_weight = slot_ref[:, :1]
    for k in range(count):
        block = slice(k * cols, (k + 1) * cols)
        piece = sum(
            jnp.dot(part, refs_of[2][:, block], preferred_element_type=jnp.float32)
            for part, refs_of in zip(hidden, weights)
        )
        out_ref[k] = (piece * slot_weight).astype(jnp.bfloat16)


def run_experts(slots, pieces, gains, own, other):
    count, capacity, cols = pieces.shape
    return call(
        expert_kernel,
        jax.ShapeDtypeStruct(pieces.shape, jnp.bfloat16),
        [VMEM_SPEC] * 9,
        [pltpu.VMEM((capacity, count * cols), jnp.bfloat16)],
        12 * capacity * own[0].size, own[0].size * 12, 20,
    )(slots, pieces, gains, *own, *other)


def combine_kernel(sharers, taken_ref, pieces, out_ref):
    count, capacity, cols = pieces.shape
    spread = [taken_ref[k // sharers] for k in range(count)]
    rows = [pieces[k].astype(jnp.float32) for k in range(count)]
    out_ref[...] = lax.dot_general(
        jnp.concatenate(spread, axis=0).astype(jnp.bfloat16),
        jnp.concatenate(rows, axis=0).astype(jnp.bfloat16),
        (((0,), (0,)), ((), ())),
        preferred_element_type=jnp.float32,
    )


def combine(sharers, taken, pieces):
    count, capacity, cols = pieces.shape
    rows = taken.shape[2]
    return call(
        functools.partial(combine_kernel, sharers),
        jax.ShapeDtypeStruct((rows, cols), jnp.float32),
        [VMEM_SPEC] * 2,
        [],
        2 * rows * capacity * count * cols, (count * capacity * 2 + rows * 4) * cols, 4,
    )(taken, pieces)


def finish_kernel(stream_ref, mine_ref, other_ref, stream_out_ref, out_ref):
    stream_out_ref[...] = stream_ref[...]
    out_ref[...] = (mine_ref[...] + other_ref[...]).astype(jnp.bfloat16)


def finish(stream, mine, other):
    return call(
        finish_kernel,
        [jax.ShapeDtypeStruct(stream.shape, jnp.bfloat16)] * 2,
        [VMEM_SPEC] * 3,
        [],
        mine.size, mine.size * 14, 4,
    )(stream, mine, other)


def exchange(blocks):
    return lax.all_to_all(blocks, "attn", split_axis=0, concat_axis=0, tiled=True)


def swap(block):
    return lax.ppermute(block, "expert", [(0, 1), (1, 0)])


def shards(
    queries,
    key_cache,
    value_cache,
    new_key,
    new_value,
    cache_length,
    residual,
    out_weight,
    ln_gain,
    gate_weight,
    up_weight,
    down_weight,
    routes,
    route_weight,
):
    count = lax.axis_size("attn")
    sharers = count // HELD
    capacity = routes.shape[0] * TOP // EXPERTS

    earlier = order(routes.shape[0])
    weights = (gate_weight.T, up_weight.T, down_weight)
    spread, own, limit, taken, slots = prepare(
        sharers, capacity, cache_length, earlier, routes.T, route_weight.T, queries, new_key
    )
    other_weights = [swap(block) for block in weights]
    attended = exchange(
        attend(count, spread, own, limit, key_cache, value_cache, new_value, ln_gain)
    )
    mine, gains = project(attended, out_weight)
    stream, chosen = pick(sharers, count, mine, swap(mine), residual, taken)
    outgoing = run_experts(slots, exchange(chosen), gains, weights, other_weights)
    combined = combine(sharers, taken, exchange(outgoing))
    attn_stream, expert_out = finish(stream, combined, swap(combined))
    return (attn_stream, expert_out)


def solution(mesh):
    count = mesh.shape["attn"]
    fits = D // count % 256 == 0 and count % HELD == 0 and mesh.shape["expert"] == 2
    return jax.shard_map(
        shards if fits else shards_plain,
        mesh=mesh,
        in_specs=(
            P(("group", "attn"), "expert"),
            P(("group", "attn"), None, "expert"),
            P(("group", "attn"), None, "expert"),
            P(("group", "attn"), "expert"),
            P(("group", "attn"), "expert"),
            P(("group", "attn")),
            P("group", "attn"),
            P("expert", "attn"),
            P("attn"),
            P(None, ("attn", "expert")),
            P(None, ("attn", "expert")),
            P(("attn", "expert"), None),
            P("group", None),
            P("group", None),
        ),
        out_specs=(P("group", "attn"), P("group", "attn")),
        check_vma=False,
    )
```

```python
import functools
import math

import jax
import jax.numpy as jnp
from jax import lax
from jax.experimental import pallas as pl
from jax.experimental.pallas import tpu as pltpu
from jax.sharding import PartitionSpec as P

D = 6144
HEADS = 48
KV_HEADS = 8
HEAD_DIM = 128
EXPERTS = 16
TOP = 4
HELD = 2


NEG_FILL = -1e30
EPSILON = 1e-05


def attend_local(queries, key_cache, value_cache, new_key, new_value, cache_length):
    row_count = queries.shape[0]
    kv_local = new_key.shape[1] // HEAD_DIM
    group = HEADS // KV_HEADS
    length_max = key_cache.shape[1]
    query_heads = queries.reshape(row_count, kv_local, group, HEAD_DIM)
    key_heads = key_cache.reshape(row_count, length_max, kv_local, HEAD_DIM)
    value_heads = value_cache.reshape(row_count, length_max, kv_local, HEAD_DIM)
    own_keys = new_key.reshape(row_count, kv_local, HEAD_DIM)
    own_values = new_value.reshape(row_count, kv_local, HEAD_DIM)
    scale = 1.0 / math.sqrt(HEAD_DIM)
    past = (
        jnp.einsum("rkgd,rlkd->rkgl", query_heads, key_heads, preferred_element_type=jnp.float32)
        * scale
    )
    valid = jnp.arange(length_max, dtype=jnp.int32)[None, :] < cache_length[:, None]
    past = jnp.where(valid[:, None, None, :], past, NEG_FILL)
    own = (
        jnp.einsum("rkgd,rkd->rkg", query_heads, own_keys, preferred_element_type=jnp.float32)
        * scale
    )
    largest = jnp.maximum(jnp.max(past, axis=3), own)
    past_weight = jnp.exp(past - largest[..., None])
    own_weight = jnp.exp(own - largest)
    total = jnp.sum(past_weight, axis=3) + own_weight
    past_prob = (past_weight / total[..., None]).astype(jnp.bfloat16)
    own_prob = (own_weight / total).astype(jnp.bfloat16)
    result = jnp.einsum(
        "rkgl,rlkd->rkgd", past_prob, value_heads, preferred_element_type=jnp.float32
    )
    result = (
        result
        + own_prob.astype(jnp.float32)[..., None] * own_values.astype(jnp.float32)[:, :, None, :]
    )
    return result.reshape(row_count, kv_local * group * HEAD_DIM).astype(jnp.bfloat16)


def selection(routes, route_weight, capacity):
    row_count = routes.shape[0]
    experts = jnp.arange(HELD, dtype=jnp.int32)
    match = routes[None, :, :] == experts[:, None, None]
    hit = jnp.any(match, axis=2)
    row_weight = jnp.sum(jnp.where(match, route_weight[None], 0.0), axis=2)
    earlier = jnp.arange(row_count)[:, None] < jnp.arange(row_count)[None, :]
    slot = jnp.sum(jnp.where(earlier[None] & hit[:, :, None], 1, 0), axis=1)
    taken = hit[:, None, :] & (slot[:, None, :] == jnp.arange(capacity, dtype=jnp.int32)[None, :, None])
    slot_weight = jnp.sum(jnp.where(taken, row_weight[:, None, :], 0.0), axis=2)
    return taken, slot_weight


def gather_attn(block):
    count = lax.axis_size("attn")
    copies = jnp.broadcast_to(block[None], (count,) + block.shape)
    return lax.all_to_all(copies, "attn", split_axis=0, concat_axis=0, tiled=True)


def pair_sum(block):
    return block + lax.ppermute(block, "expert", [(0, 1), (1, 0)])


def shards_plain(
    queries,
    key_cache,
    value_cache,
    new_key,
    new_value,
    cache_length,
    residual,
    out_weight,
    ln_gain,
    gate_weight,
    up_weight,
    down_weight,
    routes,
    route_weight,
):
    attn_count = lax.axis_size("attn")
    core_count = lax.axis_size("expert")
    sharers = attn_count * core_count // HELD
    my_expert = (lax.axis_index("attn") * core_count + lax.axis_index("expert")) // sharers
    dest_expert = [index * core_count // sharers for index in range(attn_count)]
    row_count = routes.shape[0]
    capacity = row_count * TOP // EXPERTS * 2
    cols = residual.shape[1]

    taken, slot_weight = selection(routes, route_weight, capacity)
    pick = taken.astype(jnp.bfloat16)

    gains = gather_attn(ln_gain)

    attended = attend_local(queries, key_cache, value_cache, new_key, new_value, cache_length)
    whole = gather_attn(attended).reshape(row_count, -1)
    partial_proj = jnp.dot(whole, out_weight, preferred_element_type=jnp.float32)
    head_total = pair_sum(partial_proj)
    attn_stream = (residual.astype(jnp.float32) + head_total).astype(jnp.bfloat16)

    chosen = jnp.einsum(
        "esr,rd->esd", pick, attn_stream, preferred_element_type=jnp.float32
    ).astype(jnp.bfloat16)
    outgoing = jnp.stack([chosen[index] for index in dest_expert])
    rows = lax.all_to_all(outgoing, "attn", split_axis=0, concat_axis=0, tiled=True)
    wide = rows.astype(jnp.float32)
    row_mean = jnp.sum(wide, axis=(0, 2)) / D
    row_var = jnp.sum(wide * wide, axis=(0, 2)) / D - row_mean * row_mean
    normed = (
        (wide - row_mean[None, :, None])
        * lax.rsqrt(row_var + EPSILON)[None, :, None]
        * gains.reshape(attn_count, 1, cols)
    ).astype(jnp.bfloat16)
    gate_val = jnp.einsum(
        "asd,adf->sf", normed, gate_weight.reshape(attn_count, cols, -1),
        preferred_element_type=jnp.float32,
    )
    up_val = jnp.einsum(
        "asd,adf->sf", normed, up_weight.reshape(attn_count, cols, -1),
        preferred_element_type=jnp.float32,
    )
    hidden = (jax.nn.silu(gate_val) * up_val).astype(jnp.bfloat16)
    piece = jnp.dot(hidden, down_weight, preferred_element_type=jnp.float32)
    mine = jnp.take(slot_weight, my_expert, axis=0)
    piece = (piece * mine[:, None]).astype(jnp.bfloat16)
    returned = lax.all_to_all(
        piece.reshape(capacity, attn_count, cols).swapaxes(0, 1),
        "attn", split_axis=0, concat_axis=0, tiled=True,
    )
    spread = jnp.stack([pick[index] for index in dest_expert])
    combined = jnp.einsum(
        "asr,asd->rd", spread, returned, preferred_element_type=jnp.float32
    )
    expert_out = pair_sum(combined).astype(jnp.bfloat16)
    return (attn_stream, expert_out)


MIB = 1024 * 1024
EXCHANGE_FLOPS = 10**10
VMEM_SPEC = pl.BlockSpec(memory_space=pltpu.VMEM)
SMEM_SPEC = pl.BlockSpec(memory_space=pltpu.SMEM)
HBM_SPEC = pl.BlockSpec(memory_space=pltpu.HBM)


def call(kernel, outs, in_specs, scratch, flops, nbytes, vmem_mib):
    single = not isinstance(outs, (list, tuple))
    return pl.pallas_call(
        kernel,
        out_shape=outs,
        in_specs=in_specs,
        out_specs=VMEM_SPEC if single else [VMEM_SPEC] * len(outs),
        scratch_shapes=scratch,
        cost_estimate=pl.CostEstimate(flops=flops, bytes_accessed=nbytes, transcendentals=0),
        compiler_params=pltpu.CompilerParams(vmem_limit_bytes=vmem_mib * MIB),
    )


def order_kernel(out_ref):
    rows = out_ref.shape[0]
    before = lax.broadcasted_iota(jnp.int32, (rows, rows), 0) < lax.broadcasted_iota(
        jnp.int32, (rows, rows), 1
    )
    out_ref[...] = jnp.where(before, 1.0, 0.0).astype(jnp.bfloat16)


def order(rows):
    return call(
        order_kernel,
        jax.ShapeDtypeStruct((rows, rows), jnp.bfloat16),
        [],
        [],
        EXCHANGE_FLOPS, rows * rows * 2, 2,
    )()


def expert_rows(routes, earlier, expert, capacity):
    row_count = routes.shape[1]
    hit = jnp.max((routes == expert).astype(jnp.float32), axis=0, keepdims=True)
    slot = jnp.dot(
        jnp.broadcast_to(hit, (8, row_count)).astype(jnp.bfloat16),
        earlier,
        preferred_element_type=jnp.float32,
    )[:1]
    place = lax.broadcasted_iota(jnp.int32, (capacity, row_count), 0).astype(jnp.float32)
    return jnp.where((slot == place) & (hit > 0.5), 1.0, 0.0)


def prepare_kernel(sharers, length_ref, earlier_ref, routes_ref, weight_ref, query_ref,
                   own_key_ref, spread_ref, own_ref, limit_ref, taken_ref, slot_ref, query_rows,
                   key_rows):
    row_count = query_ref.shape[0]
    kv_local = own_key_ref.shape[1] // HEAD_DIM
    group = HEADS // KV_HEADS
    heads = kv_local * group
    for g in range(kv_local):
        own_key = own_key_ref[:, g * HEAD_DIM : (g + 1) * HEAD_DIM].astype(jnp.float32)
        for i in range(group):
            index = g * group + i
            rows = pl.ds(index * row_count, row_count)
            query_rows[rows, :] = query_ref[
                :, index * HEAD_DIM : (index + 1) * HEAD_DIM
            ].astype(jnp.float32)
            key_rows[rows, :] = own_key
    scale = 1.0 / math.sqrt(HEAD_DIM)
    lengths = length_ref[...].reshape(1, -1)
    head = lax.broadcasted_iota(jnp.int32, (heads, 1), 0) // group
    for r in range(row_count):
        strided = pl.ds(r, heads, stride=row_count)
        query = query_rows[strided, :]
        own = jnp.sum(query * key_rows[strided, :], axis=1, keepdims=True) * scale
        own_ref[r] = jnp.broadcast_to(own, (heads, HEAD_DIM))
        limit_ref[r] = jnp.broadcast_to(lengths[:, r : r + 1], (heads, HEAD_DIM))
        spread_ref[r] = jnp.concatenate(
            [jnp.where(head == g, query, 0.0) for g in range(kv_local)], axis=1
        ).astype(jnp.bfloat16)
    routes = routes_ref[...]
    capacity = slot_ref.shape[0]
    core = lax.axis_index("expert")
    taken = []
    for e in range(HELD):
        both = expert_rows(routes, earlier_ref[...], e, 2 * capacity)
        taken.append(jnp.where(core == 0, both[:capacity], both[capacity:]))
        taken_ref[e] = taken[e]
    first = lax.axis_index("attn") < sharers
    expert = jnp.where(first, 0, 1)
    row_weight = jnp.sum(
        jnp.where(routes == expert, weight_ref[...], 0.0), axis=0, keepdims=True
    )
    mine = jnp.where(first, taken[0], taken[1])
    slot_ref[...] = jnp.broadcast_to(
        jnp.sum(mine * row_weight, axis=1, keepdims=True), slot_ref.shape
    )


def prepare(
    sharers, capacity, cache_length, earlier, routes, route_weight, queries, new_key
):
    row_count, width = queries.shape
    heads = width // HEAD_DIM
    table = pltpu.VMEM((heads * row_count, HEAD_DIM), jnp.float32)
    return call(
        functools.partial(prepare_kernel, sharers),
        [
            jax.ShapeDtypeStruct((row_count, heads, new_key.shape[1]), jnp.bfloat16),
            jax.ShapeDtypeStruct((row_count, heads, HEAD_DIM), jnp.float32),
            jax.ShapeDtypeStruct((row_count, heads, HEAD_DIM), jnp.int32),
            jax.ShapeDtypeStruct((HELD, capacity, routes.shape[1]), jnp.float32),
            jax.ShapeDtypeStruct((capacity, HEAD_DIM), jnp.float32),
        ],
        [VMEM_SPEC] * 6,
        [table, table],
        queries.size * 8, queries.size * 16, 4,
    )(cache_length, earlier, routes, route_weight, queries, new_key)


def score_kernel(spread_ref, own_ref, limit_ref, key_ref, probs_ref, own_probs_ref):
    row_count, heads, length_max = probs_ref.shape
    scale = 1.0 / math.sqrt(HEAD_DIM)
    contract = (((1,), (1,)), ((), ()))
    scores = jnp.concatenate(
        [
            lax.dot_general(
                spread_ref[r], key_ref[r], contract, preferred_element_type=jnp.float32
            )
            for r in range(row_count)
        ],
        axis=0,
    )
    position = lax.broadcasted_iota(jnp.int32, scores.shape, 1)
    limit = jnp.concatenate([limit_ref[r, :, :1] for r in range(row_count)], axis=0)
    own = jnp.concatenate([own_ref[r, :, :1] for r in range(row_count)], axis=0)
    past = jnp.where(position < limit, scores * scale, NEG_FILL)
    largest = jnp.maximum(jnp.max(past, axis=1, keepdims=True), own)
    weight = jnp.exp(past - largest)
    own_weight = jnp.exp(own - largest)
    inverse = 1.0 / (jnp.sum(weight, axis=1, keepdims=True) + own_weight)
    probs = weight * inverse
    own_prob = (own_weight * inverse).astype(jnp.bfloat16).astype(jnp.float32)
    for r in range(row_count):
        rows = slice(r * heads, (r + 1) * heads)
        probs_ref[r] = probs[rows].astype(jnp.bfloat16)
        own_probs_ref[r] = jnp.broadcast_to(own_prob[rows], own_probs_ref.shape[1:])


def value_kernel(probs_ref, own_ref, value_ref, own_value_ref, gain_ref, out_ref, value_rows,
                 result_rows):
    row_count, length_max, width = value_ref.shape
    kv_local = width // HEAD_DIM
    group = HEADS // KV_HEADS
    heads = kv_local * group
    for g in range(kv_local):
        own_value = own_value_ref[:, g * HEAD_DIM : (g + 1) * HEAD_DIM].astype(jnp.float32)
        for i in range(group):
            value_rows[pl.ds((g * group + i) * row_count, row_count), :] = own_value
    head = lax.broadcasted_iota(jnp.int32, (heads, 1), 0) // group
    for r in range(row_count):
        strided = pl.ds(r, heads, stride=row_count)
        product = jnp.dot(probs_ref[r], value_ref[r], preferred_element_type=jnp.float32)
        total = own_ref[r] * value_rows[strided, :]
        for g in range(kv_local):
            lanes = slice(g * HEAD_DIM, (g + 1) * HEAD_DIM)
            total = total + jnp.where(head == g, product[:, lanes], 0.0)
        result_rows[strided, :] = total
    for index in range(heads):
        rows = result_rows[pl.ds(index * row_count, row_count), :].astype(jnp.bfloat16)
        for copy in range(out_ref.shape[0]):
            out_ref[copy, :, index * HEAD_DIM : (index + 1) * HEAD_DIM] = rows
    gain_row = gain_ref[...].reshape(1, -1)
    half = gain_row.shape[1] // 2
    row = lax.broadcasted_iota(jnp.int32, (row_count, half), 0)
    left = jnp.broadcast_to(gain_row[:, :half], (row_count, half))
    right = jnp.broadcast_to(gain_row[:, half:], (row_count, half))
    gain = jnp.where(row % 2 == 0, left, right)
    upper = gain.astype(jnp.bfloat16).astype(jnp.float32)
    parts = jnp.where(row < 2, upper, gain - upper).astype(jnp.bfloat16)
    for copy in range(out_ref.shape[0]):
        out_ref[copy, :, heads * HEAD_DIM :] = parts


def attend(count, spread, own, limit, key_cache, value_cache, new_value, gain):
    row_count, heads, _ = spread.shape
    length_max = key_cache.shape[1]
    table = pltpu.VMEM((heads * row_count, HEAD_DIM), jnp.float32)
    probs, own_probs = call(
        score_kernel,
        [
            jax.ShapeDtypeStruct((row_count, heads, length_max), jnp.bfloat16),
            jax.ShapeDtypeStruct((row_count, heads, HEAD_DIM), jnp.float32),
        ],
        [VMEM_SPEC] * 4,
        [],
        2 * key_cache.size * heads, key_cache.size * 2, 8,
    )(spread, own, limit, key_cache)
    width = heads * HEAD_DIM + gain.shape[0] // 2
    return call(
        value_kernel,
        jax.ShapeDtypeStruct((count, row_count, width), jnp.bfloat16),
        [VMEM_SPEC] * 5,
        [table, table],
        EXCHANGE_FLOPS, value_cache.size * 2, 8,
    )(probs, own_probs, value_cache, new_value, gain)


def project_kernel(pieces, weight_ref, out_ref, gain_ref, stack):
    count, rows, _ = pieces.shape
    width = weight_ref.shape[0]
    half = gain_ref.shape[1] // 2
    for k in range(count):
        stack[pl.ds(k * rows, rows), :] = pieces[k, :, :width].astype(jnp.float32)
        parts = pieces[k, :, width:].astype(jnp.float32)
        gain_ref[pl.ds(k, 1), :half] = parts[0:1] + parts[2:3]
        gain_ref[pl.ds(k, 1), half:] = parts[1:2] + parts[3:4]
    out_ref[...] = jnp.dot(
        stack[...].astype(jnp.bfloat16), weight_ref[...], preferred_element_type=jnp.float32
    )


def project(pieces, out_weight):
    count, rows, _ = pieces.shape
    depth, cols = out_weight.shape
    return call(
        project_kernel,
        [
            jax.ShapeDtypeStruct((rows * count, cols), jnp.float32),
            jax.ShapeDtypeStruct((count, cols), jnp.float32),
        ],
        [VMEM_SPEC, VMEM_SPEC],
        [pltpu.VMEM((rows * count, depth), jnp.float32)],
        EXCHANGE_FLOPS, out_weight.size * 2, 10,
    )(pieces, out_weight)


def pick_kernel(sharers, mine_ref, other_ref, residual_ref, taken_ref, stream_ref, out_ref):
    stream = (
        residual_ref[...].astype(jnp.float32) + (mine_ref[...] + other_ref[...])
    ).astype(jnp.bfloat16)
    stream_ref[...] = stream
    chosen = [
        jnp.dot(
            taken_ref[e].astype(jnp.bfloat16), stream, preferred_element_type=jnp.float32
        ).astype(jnp.bfloat16)
        for e in range(HELD)
    ]
    for k in range(out_ref.shape[0]):
        out_ref[k] = chosen[k // sharers]


def pick(sharers, count, mine, other, residual, taken):
    rows, cols = mine.shape
    return call(
        functools.partial(pick_kernel, sharers),
        [
            jax.ShapeDtypeStruct((rows, cols), jnp.bfloat16),
            jax.ShapeDtypeStruct((count, taken.shape[1], cols), jnp.bfloat16),
        ],
        [VMEM_SPEC] * 4,
        [],
        2 * HELD * taken.shape[1] * rows * cols, rows * cols * 12, 4,
    )(mine, other, residual, taken)


def expert_kernel(slot_ref, pieces, gains, *refs):
    weights, out_ref, rows_ref = (refs[:3], refs[3:6]), refs[6], refs[7]
    count, capacity, cols = pieces.shape
    first = second = 0.0
    for k in range(count):
        wide = pieces[k].astype(jnp.float32)
        first = first + wide
        second = second + wide * wide
    row_mean = jnp.sum(first, axis=1, keepdims=True) / D
    row_var = jnp.sum(second, axis=1, keepdims=True) / D - row_mean * row_mean
    inverse = lax.rsqrt(row_var + EPSILON)
    for k in range(count):
        wide = pieces[k].astype(jnp.float32)
        normed = (wide - row_mean) * inverse * gains[pl.ds(k, 1), :]
        rows_ref[:, k * cols : (k + 1) * cols] = normed.astype(jnp.bfloat16)
    rows = rows_ref[...]
    contract = (((1,), (1,)), ((), ()))
    hidden = []
    for gate_ref, up_ref, _ in weights:
        gate = lax.dot_general(rows, gate_ref[...], contract, preferred_element_type=jnp.float32)
        up = lax.dot_general(rows, up_ref[...], contract, preferred_element_type=jnp.float32)
        hidden.append((gate / (1.0 + jnp.exp(-gate)) * up).astype(jnp.bfloat16))
    slot_weight = slot_ref[:, :1]
    for k in range(count):
        block = slice(k * cols, (k + 1) * cols)
        piece = sum(
            jnp.dot(part, refs_of[2][:, block], preferred_element_type=jnp.float32)
            for part, refs_of in zip(hidden, weights)
        )
        out_ref[k] = (piece * slot_weight).astype(jnp.bfloat16)


def run_experts(slots, pieces, gains, own, other):
    count, capacity, cols = pieces.shape
    return call(
        expert_kernel,
        jax.ShapeDtypeStruct(pieces.shape, jnp.bfloat16),
        [VMEM_SPEC] * 9,
        [pltpu.VMEM((capacity, count * cols), jnp.bfloat16)],
        12 * capacity * own[0].size, own[0].size * 12, 20,
    )(slots, pieces, gains, *own, *other)


def combine_kernel(sharers, taken_ref, pieces, out_ref):
    count, capacity, cols = pieces.shape
    spread = [taken_ref[k // sharers] for k in range(count)]
    rows = [pieces[k].astype(jnp.float32) for k in range(count)]
    out_ref[...] = lax.dot_general(
        jnp.concatenate(spread, axis=0).astype(jnp.bfloat16),
        jnp.concatenate(rows, axis=0).astype(jnp.bfloat16),
        (((0,), (0,)), ((), ())),
        preferred_element_type=jnp.float32,
    )


def combine(sharers, taken, pieces):
    count, capacity, cols = pieces.shape
    rows = taken.shape[2]
    return call(
        functools.partial(combine_kernel, sharers),
        jax.ShapeDtypeStruct((rows, cols), jnp.float32),
        [VMEM_SPEC] * 2,
        [],
        2 * rows * capacity * count * cols, (count * capacity * 2 + rows * 4) * cols, 4,
    )(taken, pieces)


def finish_kernel(stream_ref, mine_ref, other_ref, stream_out_ref, out_ref):
    stream_out_ref[...] = stream_ref[...]
    out_ref[...] = (mine_ref[...] + other_ref[...]).astype(jnp.bfloat16)


def finish(stream, mine, other):
    return call(
        finish_kernel,
        [jax.ShapeDtypeStruct(stream.shape, jnp.bfloat16)] * 2,
        [VMEM_SPEC] * 3,
        [],
        mine.size, mine.size * 14, 4,
    )(stream, mine, other)


def exchange(blocks):
    return lax.all_to_all(blocks, "attn", split_axis=0, concat_axis=0, tiled=True)


def swap(block):
    return lax.ppermute(block, "expert", [(0, 1), (1, 0)])


def shards(
    queries,
    key_cache,
    value_cache,
    new_key,
    new_value,
    cache_length,
    residual,
    out_weight,
    ln_gain,
    gate_weight,
    up_weight,
    down_weight,
    routes,
    route_weight,
):
    count = lax.axis_size("attn")
    sharers = count // HELD
    capacity = routes.shape[0] * TOP // EXPERTS

    earlier = order(routes.shape[0])
    weights = (gate_weight.T, up_weight.T, down_weight)
    spread, own, limit, taken, slots = prepare(
        sharers, capacity, cache_length, earlier, routes.T, route_weight.T, queries, new_key
    )
    other_weights = [swap(block) for block in lax.optimization_barrier(weights)]
    attended = exchange(
        attend(count, spread, own, limit, key_cache, value_cache, new_value, ln_gain)
    )
    mine, gains = project(attended, out_weight)
    stream, chosen = pick(sharers, count, mine, swap(mine), residual, taken)
    outgoing = run_experts(slots, exchange(chosen), gains, weights, other_weights)
    combined = combine(sharers, taken, exchange(outgoing))
    attn_stream, expert_out = finish(stream, combined, swap(combined))
    return (attn_stream, expert_out)


def solution(mesh):
    count = mesh.shape["attn"]
    fits = D // count % 256 == 0 and count % HELD == 0 and mesh.shape["expert"] == 2
    return jax.shard_map(
        shards if fits else shards_plain,
        mesh=mesh,
        in_specs=(
            P(("group", "attn"), "expert"),
            P(("group", "attn"), None, "expert"),
            P(("group", "attn"), None, "expert"),
            P(("group", "attn"), "expert"),
            P(("group", "attn"), "expert"),
            P(("group", "attn")),
            P("group", "attn"),
            P("expert", "attn"),
            P("attn"),
            P(None, ("attn", "expert")),
            P(None, ("attn", "expert")),
            P(("attn", "expert"), None),
            P("group", None),
            P("group", None),
        ),
        out_specs=(P("group", "attn"), P("group", "attn")),
        check_vma=False,
    )
```

```python
import functools
import math

import jax
import jax.numpy as jnp
from jax import lax
from jax.experimental import pallas as pl
from jax.experimental.pallas import tpu as pltpu
from jax.sharding import PartitionSpec as P

D = 6144
HEADS = 48
KV_HEADS = 8
HEAD_DIM = 128
EXPERTS = 16
TOP = 4
HELD = 2


NEG_FILL = -1e30
EPSILON = 1e-05


def attend_local(queries, key_cache, value_cache, new_key, new_value, cache_length):
    row_count = queries.shape[0]
    kv_local = new_key.shape[1] // HEAD_DIM
    group = HEADS // KV_HEADS
    length_max = key_cache.shape[1]
    query_heads = queries.reshape(row_count, kv_local, group, HEAD_DIM)
    key_heads = key_cache.reshape(row_count, length_max, kv_local, HEAD_DIM)
    value_heads = value_cache.reshape(row_count, length_max, kv_local, HEAD_DIM)
    own_keys = new_key.reshape(row_count, kv_local, HEAD_DIM)
    own_values = new_value.reshape(row_count, kv_local, HEAD_DIM)
    scale = 1.0 / math.sqrt(HEAD_DIM)
    past = (
        jnp.einsum("rkgd,rlkd->rkgl", query_heads, key_heads, preferred_element_type=jnp.float32)
        * scale
    )
    valid = jnp.arange(length_max, dtype=jnp.int32)[None, :] < cache_length[:, None]
    past = jnp.where(valid[:, None, None, :], past, NEG_FILL)
    own = (
        jnp.einsum("rkgd,rkd->rkg", query_heads, own_keys, preferred_element_type=jnp.float32)
        * scale
    )
    largest = jnp.maximum(jnp.max(past, axis=3), own)
    past_weight = jnp.exp(past - largest[..., None])
    own_weight = jnp.exp(own - largest)
    total = jnp.sum(past_weight, axis=3) + own_weight
    past_prob = (past_weight / total[..., None]).astype(jnp.bfloat16)
    own_prob = (own_weight / total).astype(jnp.bfloat16)
    result = jnp.einsum(
        "rkgl,rlkd->rkgd", past_prob, value_heads, preferred_element_type=jnp.float32
    )
    result = (
        result
        + own_prob.astype(jnp.float32)[..., None] * own_values.astype(jnp.float32)[:, :, None, :]
    )
    return result.reshape(row_count, kv_local * group * HEAD_DIM).astype(jnp.bfloat16)


def selection(routes, route_weight, capacity):
    row_count = routes.shape[0]
    experts = jnp.arange(HELD, dtype=jnp.int32)
    match = routes[None, :, :] == experts[:, None, None]
    hit = jnp.any(match, axis=2)
    row_weight = jnp.sum(jnp.where(match, route_weight[None], 0.0), axis=2)
    earlier = jnp.arange(row_count)[:, None] < jnp.arange(row_count)[None, :]
    slot = jnp.sum(jnp.where(earlier[None] & hit[:, :, None], 1, 0), axis=1)
    taken = hit[:, None, :] & (slot[:, None, :] == jnp.arange(capacity, dtype=jnp.int32)[None, :, None])
    slot_weight = jnp.sum(jnp.where(taken, row_weight[:, None, :], 0.0), axis=2)
    return taken, slot_weight


def gather_attn(block):
    count = lax.axis_size("attn")
    copies = jnp.broadcast_to(block[None], (count,) + block.shape)
    return lax.all_to_all(copies, "attn", split_axis=0, concat_axis=0, tiled=True)


def pair_sum(block):
    return block + lax.ppermute(block, "expert", [(0, 1), (1, 0)])


def shards_plain(
    queries,
    key_cache,
    value_cache,
    new_key,
    new_value,
    cache_length,
    residual,
    out_weight,
    ln_gain,
    gate_weight,
    up_weight,
    down_weight,
    routes,
    route_weight,
):
    attn_count = lax.axis_size("attn")
    core_count = lax.axis_size("expert")
    sharers = attn_count * core_count // HELD
    my_expert = (lax.axis_index("attn") * core_count + lax.axis_index("expert")) // sharers
    dest_expert = [index * core_count // sharers for index in range(attn_count)]
    row_count = routes.shape[0]
    capacity = row_count * TOP // EXPERTS * 2
    cols = residual.shape[1]

    taken, slot_weight = selection(routes, route_weight, capacity)
    pick = taken.astype(jnp.bfloat16)

    gains = gather_attn(ln_gain)

    attended = attend_local(queries, key_cache, value_cache, new_key, new_value, cache_length)
    whole = gather_attn(attended).reshape(row_count, -1)
    partial_proj = jnp.dot(whole, out_weight, preferred_element_type=jnp.float32)
    head_total = pair_sum(partial_proj)
    attn_stream = (residual.astype(jnp.float32) + head_total).astype(jnp.bfloat16)

    chosen = jnp.einsum(
        "esr,rd->esd", pick, attn_stream, preferred_element_type=jnp.float32
    ).astype(jnp.bfloat16)
    outgoing = jnp.stack([chosen[index] for index in dest_expert])
    rows = lax.all_to_all(outgoing, "attn", split_axis=0, concat_axis=0, tiled=True)
    wide = rows.astype(jnp.float32)
    row_mean = jnp.sum(wide, axis=(0, 2)) / D
    row_var = jnp.sum(wide * wide, axis=(0, 2)) / D - row_mean * row_mean
    normed = (
        (wide - row_mean[None, :, None])
        * lax.rsqrt(row_var + EPSILON)[None, :, None]
        * gains.reshape(attn_count, 1, cols)
    ).astype(jnp.bfloat16)
    gate_val = jnp.einsum(
        "asd,adf->sf", normed, gate_weight.reshape(attn_count, cols, -1),
        preferred_element_type=jnp.float32,
    )
    up_val = jnp.einsum(
        "asd,adf->sf", normed, up_weight.reshape(attn_count, cols, -1),
        preferred_element_type=jnp.float32,
    )
    hidden = (jax.nn.silu(gate_val) * up_val).astype(jnp.bfloat16)
    piece = jnp.dot(hidden, down_weight, preferred_element_type=jnp.float32)
    mine = jnp.take(slot_weight, my_expert, axis=0)
    piece = (piece * mine[:, None]).astype(jnp.bfloat16)
    returned = lax.all_to_all(
        piece.reshape(capacity, attn_count, cols).swapaxes(0, 1),
        "attn", split_axis=0, concat_axis=0, tiled=True,
    )
    spread = jnp.stack([pick[index] for index in dest_expert])
    combined = jnp.einsum(
        "asr,asd->rd", spread, returned, preferred_element_type=jnp.float32
    )
    expert_out = pair_sum(combined).astype(jnp.bfloat16)
    return (attn_stream, expert_out)


MIB = 1024 * 1024
EXCHANGE_FLOPS = 10**10
VMEM_SPEC = pl.BlockSpec(memory_space=pltpu.VMEM)
SMEM_SPEC = pl.BlockSpec(memory_space=pltpu.SMEM)
HBM_SPEC = pl.BlockSpec(memory_space=pltpu.HBM)


def call(kernel, outs, in_specs, scratch, flops, nbytes, vmem_mib):
    single = not isinstance(outs, (list, tuple))
    return pl.pallas_call(
        kernel,
        out_shape=outs,
        in_specs=in_specs,
        out_specs=VMEM_SPEC if single else [VMEM_SPEC] * len(outs),
        scratch_shapes=scratch,
        cost_estimate=pl.CostEstimate(flops=flops, bytes_accessed=nbytes, transcendentals=0),
        compiler_params=pltpu.CompilerParams(vmem_limit_bytes=vmem_mib * MIB),
    )


def order_kernel(out_ref):
    rows = out_ref.shape[0]
    before = lax.broadcasted_iota(jnp.int32, (rows, rows), 0) < lax.broadcasted_iota(
        jnp.int32, (rows, rows), 1
    )
    out_ref[...] = jnp.where(before, 1.0, 0.0).astype(jnp.bfloat16)


def order(rows):
    return call(
        order_kernel,
        jax.ShapeDtypeStruct((rows, rows), jnp.bfloat16),
        [],
        [],
        EXCHANGE_FLOPS, rows * rows * 2, 2,
    )()


def expert_rows(routes, earlier, expert, capacity):
    row_count = routes.shape[1]
    hit = jnp.max((routes == expert).astype(jnp.float32), axis=0, keepdims=True)
    slot = jnp.dot(
        jnp.broadcast_to(hit, (8, row_count)).astype(jnp.bfloat16),
        earlier,
        preferred_element_type=jnp.float32,
    )[:1]
    place = lax.broadcasted_iota(jnp.int32, (capacity, row_count), 0).astype(jnp.float32)
    return jnp.where((slot == place) & (hit > 0.5), 1.0, 0.0)


def prepare_kernel(sharers, length_ref, earlier_ref, routes_ref, weight_ref, query_ref,
                   own_key_ref, spread_ref, own_ref, limit_ref, taken_ref, slot_ref, query_rows,
                   key_rows):
    row_count = query_ref.shape[0]
    kv_local = own_key_ref.shape[1] // HEAD_DIM
    group = HEADS // KV_HEADS
    heads = kv_local * group
    for g in range(kv_local):
        own_key = own_key_ref[:, g * HEAD_DIM : (g + 1) * HEAD_DIM].astype(jnp.float32)
        for i in range(group):
            index = g * group + i
            rows = pl.ds(index * row_count, row_count)
            query_rows[rows, :] = query_ref[
                :, index * HEAD_DIM : (index + 1) * HEAD_DIM
            ].astype(jnp.float32)
            key_rows[rows, :] = own_key
    scale = 1.0 / math.sqrt(HEAD_DIM)
    lengths = length_ref[...].reshape(1, -1)
    head = lax.broadcasted_iota(jnp.int32, (heads, 1), 0) // group
    for r in range(row_count):
        strided = pl.ds(r, heads, stride=row_count)
        query = query_rows[strided, :]
        own = jnp.sum(query * key_rows[strided, :], axis=1, keepdims=True) * scale
        own_ref[r] = jnp.broadcast_to(own, (heads, HEAD_DIM))
        limit_ref[r] = jnp.broadcast_to(lengths[:, r : r + 1], (heads, HEAD_DIM))
        spread_ref[r] = jnp.concatenate(
            [jnp.where(head == g, query, 0.0) for g in range(kv_local)], axis=1
        ).astype(jnp.bfloat16)
    routes = routes_ref[...]
    capacity = slot_ref.shape[0]
    core = lax.axis_index("expert")
    taken = []
    for e in range(HELD):
        both = expert_rows(routes, earlier_ref[...], e, 2 * capacity)
        taken.append(jnp.where(core == 0, both[:capacity], both[capacity:]))
        taken_ref[e] = taken[e]
    first = lax.axis_index("attn") < sharers
    expert = jnp.where(first, 0, 1)
    row_weight = jnp.sum(
        jnp.where(routes == expert, weight_ref[...], 0.0), axis=0, keepdims=True
    )
    mine = jnp.where(first, taken[0], taken[1])
    slot_ref[...] = jnp.broadcast_to(
        jnp.sum(mine * row_weight, axis=1, keepdims=True), slot_ref.shape
    )


def prepare(
    sharers, capacity, cache_length, earlier, routes, route_weight, queries, new_key
):
    row_count, width = queries.shape
    heads = width // HEAD_DIM
    table = pltpu.VMEM((heads * row_count, HEAD_DIM), jnp.float32)
    return call(
        functools.partial(prepare_kernel, sharers),
        [
            jax.ShapeDtypeStruct((row_count, heads, new_key.shape[1]), jnp.bfloat16),
            jax.ShapeDtypeStruct((row_count, heads, HEAD_DIM), jnp.float32),
            jax.ShapeDtypeStruct((row_count, heads, HEAD_DIM), jnp.int32),
            jax.ShapeDtypeStruct((HELD, capacity, routes.shape[1]), jnp.float32),
            jax.ShapeDtypeStruct((capacity, HEAD_DIM), jnp.float32),
        ],
        [VMEM_SPEC] * 6,
        [table, table],
        queries.size * 8, queries.size * 16, 4,
    )(cache_length, earlier, routes, route_weight, queries, new_key)


def score_kernel(spread_ref, own_ref, limit_ref, key_ref, probs_ref, own_probs_ref):
    row_count, heads, length_max = probs_ref.shape
    scale = 1.0 / math.sqrt(HEAD_DIM)
    contract = (((1,), (1,)), ((), ()))
    scores = jnp.concatenate(
        [
            lax.dot_general(
                spread_ref[r], key_ref[r], contract, preferred_element_type=jnp.float32
            )
            for r in range(row_count)
        ],
        axis=0,
    )
    position = lax.broadcasted_iota(jnp.int32, scores.shape, 1)
    limit = jnp.concatenate([limit_ref[r, :, :1] for r in range(row_count)], axis=0)
    own = jnp.concatenate([own_ref[r, :, :1] for r in range(row_count)], axis=0)
    past = jnp.where(position < limit, scores * scale, NEG_FILL)
    largest = jnp.maximum(jnp.max(past, axis=1, keepdims=True), own)
    weight = jnp.exp(past - largest)
    own_weight = jnp.exp(own - largest)
    inverse = 1.0 / (jnp.sum(weight, axis=1, keepdims=True) + own_weight)
    probs = weight * inverse
    own_prob = (own_weight * inverse).astype(jnp.bfloat16).astype(jnp.float32)
    for r in range(row_count):
        rows = slice(r * heads, (r + 1) * heads)
        probs_ref[r] = probs[rows].astype(jnp.bfloat16)
        own_probs_ref[r] = jnp.broadcast_to(own_prob[rows], own_probs_ref.shape[1:])


def value_kernel(probs_ref, own_ref, value_ref, own_value_ref, gain_ref, out_ref, value_rows,
                 result_rows):
    row_count, length_max, width = value_ref.shape
    kv_local = width // HEAD_DIM
    group = HEADS // KV_HEADS
    heads = kv_local * group
    for g in range(kv_local):
        own_value = own_value_ref[:, g * HEAD_DIM : (g + 1) * HEAD_DIM].astype(jnp.float32)
        for i in range(group):
            value_rows[pl.ds((g * group + i) * row_count, row_count), :] = own_value
    head = lax.broadcasted_iota(jnp.int32, (heads, 1), 0) // group
    for r in range(row_count):
        strided = pl.ds(r, heads, stride=row_count)
        product = jnp.dot(probs_ref[r], value_ref[r], preferred_element_type=jnp.float32)
        total = own_ref[r] * value_rows[strided, :]
        for g in range(kv_local):
            lanes = slice(g * HEAD_DIM, (g + 1) * HEAD_DIM)
            total = total + jnp.where(head == g, product[:, lanes], 0.0)
        result_rows[strided, :] = total
    for index in range(heads):
        rows = result_rows[pl.ds(index * row_count, row_count), :].astype(jnp.bfloat16)
        for copy in range(out_ref.shape[0]):
            out_ref[copy, :, index * HEAD_DIM : (index + 1) * HEAD_DIM] = rows
    gain_row = gain_ref[...].reshape(1, -1)
    half = gain_row.shape[1] // 2
    row = lax.broadcasted_iota(jnp.int32, (row_count, half), 0)
    left = jnp.broadcast_to(gain_row[:, :half], (row_count, half))
    right = jnp.broadcast_to(gain_row[:, half:], (row_count, half))
    gain = jnp.where(row % 2 == 0, left, right)
    upper = gain.astype(jnp.bfloat16).astype(jnp.float32)
    parts = jnp.where(row < 2, upper, gain - upper).astype(jnp.bfloat16)
    for copy in range(out_ref.shape[0]):
        out_ref[copy, :, heads * HEAD_DIM :] = parts


def attend(count, spread, own, limit, key_cache, value_cache, new_value, gain):
    row_count, heads, _ = spread.shape
    length_max = key_cache.shape[1]
    table = pltpu.VMEM((heads * row_count, HEAD_DIM), jnp.float32)
    probs, own_probs = call(
        score_kernel,
        [
            jax.ShapeDtypeStruct((row_count, heads, length_max), jnp.bfloat16),
            jax.ShapeDtypeStruct((row_count, heads, HEAD_DIM), jnp.float32),
        ],
        [VMEM_SPEC] * 4,
        [],
        2 * key_cache.size * heads, key_cache.size * 2, 8,
    )(spread, own, limit, key_cache)
    width = heads * HEAD_DIM + gain.shape[0] // 2
    return call(
        value_kernel,
        jax.ShapeDtypeStruct((count, row_count, width), jnp.bfloat16),
        [VMEM_SPEC] * 5,
        [table, table],
        EXCHANGE_FLOPS, value_cache.size * 2, 8,
    )(probs, own_probs, value_cache, new_value, gain)


def project_kernel(pieces, weight_ref, out_ref, gain_ref, stack):
    count, rows, _ = pieces.shape
    width = weight_ref.shape[0]
    half = gain_ref.shape[1] // 2
    for k in range(count):
        stack[pl.ds(k * rows, rows), :] = pieces[k, :, :width].astype(jnp.float32)
        parts = pieces[k, :, width:].astype(jnp.float32)
        gain_ref[pl.ds(k, 1), :half] = parts[0:1] + parts[2:3]
        gain_ref[pl.ds(k, 1), half:] = parts[1:2] + parts[3:4]
    out_ref[...] = jnp.dot(
        stack[...].astype(jnp.bfloat16), weight_ref[...], preferred_element_type=jnp.float32
    )


def project(pieces, out_weight):
    count, rows, _ = pieces.shape
    depth, cols = out_weight.shape
    return call(
        project_kernel,
        [
            jax.ShapeDtypeStruct((rows * count, cols), jnp.float32),
            jax.ShapeDtypeStruct((count, cols), jnp.float32),
        ],
        [VMEM_SPEC, VMEM_SPEC],
        [pltpu.VMEM((rows * count, depth), jnp.float32)],
        EXCHANGE_FLOPS, out_weight.size * 2, 10,
    )(pieces, out_weight)


def pick_kernel(sharers, mine_ref, other_ref, residual_ref, taken_ref, stream_ref, out_ref):
    stream = (
        residual_ref[...].astype(jnp.float32) + (mine_ref[...] + other_ref[...])
    ).astype(jnp.bfloat16)
    stream_ref[...] = stream
    chosen = [
        jnp.dot(
            taken_ref[e].astype(jnp.bfloat16), stream, preferred_element_type=jnp.float32
        ).astype(jnp.bfloat16)
        for e in range(HELD)
    ]
    for k in range(out_ref.shape[0]):
        out_ref[k] = chosen[k // sharers]


def pick(sharers, count, mine, other, residual, taken):
    rows, cols = mine.shape
    return call(
        functools.partial(pick_kernel, sharers),
        [
            jax.ShapeDtypeStruct((rows, cols), jnp.bfloat16),
            jax.ShapeDtypeStruct((count, taken.shape[1], cols), jnp.bfloat16),
        ],
        [VMEM_SPEC] * 4,
        [],
        2 * HELD * taken.shape[1] * rows * cols, rows * cols * 12, 4,
    )(mine, other, residual, taken)


def packed_rows(height, number):
    whole = height // 16 * 16
    ranges, groups, room = [], [[]], 256
    for n in range(number):
        ranges.append((n, 0, whole))
    ranges += [(n, whole, height) for n in range(number) if whole < height]
    for n, low, high in ranges:
        while low < high:
            if room == 0:
                groups.append([])
                room = 256
            step = min(room, high - low)
            groups[-1].append((n, low, low + step))
            low, room = low + step, room - step
    return groups


def expert_kernel(slot_ref, pieces, gains, *refs):
    weights, out_ref, rows_ref = (refs[:3], refs[3:6]), refs[6], refs[7]
    count, capacity, cols = pieces.shape
    first = second = 0.0
    for k in range(count):
        wide = pieces[k].astype(jnp.float32)
        first = first + wide
        second = second + wide * wide
    row_mean = jnp.sum(first, axis=1, keepdims=True) / D
    row_var = jnp.sum(second, axis=1, keepdims=True) / D - row_mean * row_mean
    inverse = lax.rsqrt(row_var + EPSILON)
    for k in range(count):
        wide = pieces[k].astype(jnp.float32)
        normed = (wide - row_mean) * inverse * gains[pl.ds(k, 1), :]
        rows_ref[:, k * cols : (k + 1) * cols] = normed.astype(jnp.bfloat16)
    contract = (((1,), (1,)), ((), ()))
    blocks = [ref for refs_of in weights for ref in refs_of[:2]]
    groups = packed_rows(blocks[0].shape[0], len(blocks))
    sums = [0.0] * len(groups)
    for k in range(count):
        columns = slice(k * cols, (k + 1) * cols)
        rows = rows_ref[:, columns]
        for index, group in enumerate(groups):
            tile = jnp.concatenate([blocks[n][low:high, columns] for n, low, high in group], axis=0)
            sums[index] = sums[index] + lax.dot_general(
                rows, tile, contract, preferred_element_type=jnp.float32
            )
    parts = [[] for _ in blocks]
    for group, total in zip(groups, sums):
        start = 0
        for n, low, high in group:
            parts[n].append((low, total[:, start : start + high - low]))
            start += high - low
    values = [
        jnp.concatenate([part for _, part in sorted(pieces_of, key=lambda item: item[0])], axis=1)
        for pieces_of in parts
    ]
    hidden = [
        (gate / (1.0 + jnp.exp(-gate)) * up).astype(jnp.bfloat16)
        for gate, up in (values[:2], values[2:])
    ]
    slot_weight = slot_ref[:, :1]
    for k in range(count):
        block = slice(k * cols, (k + 1) * cols)
        piece = sum(
            jnp.dot(part, refs_of[2][:, block], preferred_element_type=jnp.float32)
            for part, refs_of in zip(hidden, weights)
        )
        out_ref[k] = (piece * slot_weight).astype(jnp.bfloat16)


def run_experts(slots, pieces, gains, own, other):
    count, capacity, cols = pieces.shape
    return call(
        expert_kernel,
        jax.ShapeDtypeStruct(pieces.shape, jnp.bfloat16),
        [VMEM_SPEC] * 9,
        [pltpu.VMEM((capacity, count * cols), jnp.bfloat16)],
        12 * capacity * own[0].size, own[0].size * 12, 20,
    )(slots, pieces, gains, *own, *other)


def combine_kernel(sharers, taken_ref, pieces, out_ref):
    count, capacity, cols = pieces.shape
    spread = [taken_ref[k // sharers] for k in range(count)]
    rows = [pieces[k].astype(jnp.float32) for k in range(count)]
    out_ref[...] = lax.dot_general(
        jnp.concatenate(spread, axis=0).astype(jnp.bfloat16),
        jnp.concatenate(rows, axis=0).astype(jnp.bfloat16),
        (((0,), (0,)), ((), ())),
        preferred_element_type=jnp.float32,
    )


def combine(sharers, taken, pieces):
    count, capacity, cols = pieces.shape
    rows = taken.shape[2]
    return call(
        functools.partial(combine_kernel, sharers),
        jax.ShapeDtypeStruct((rows, cols), jnp.float32),
        [VMEM_SPEC] * 2,
        [],
        2 * rows * capacity * count * cols, (count * capacity * 2 + rows * 4) * cols, 4,
    )(taken, pieces)


def finish_kernel(stream_ref, mine_ref, other_ref, stream_out_ref, out_ref):
    stream_out_ref[...] = stream_ref[...]
    out_ref[...] = (mine_ref[...] + other_ref[...]).astype(jnp.bfloat16)


def finish(stream, mine, other):
    return call(
        finish_kernel,
        [jax.ShapeDtypeStruct(stream.shape, jnp.bfloat16)] * 2,
        [VMEM_SPEC] * 3,
        [],
        mine.size, mine.size * 14, 4,
    )(stream, mine, other)


def exchange(blocks):
    return lax.all_to_all(blocks, "attn", split_axis=0, concat_axis=0, tiled=True)


def swap(block):
    return lax.ppermute(block, "expert", [(0, 1), (1, 0)])


def shards(
    queries,
    key_cache,
    value_cache,
    new_key,
    new_value,
    cache_length,
    residual,
    out_weight,
    ln_gain,
    gate_weight,
    up_weight,
    down_weight,
    routes,
    route_weight,
):
    count = lax.axis_size("attn")
    sharers = count // HELD
    capacity = routes.shape[0] * TOP // EXPERTS

    earlier = order(routes.shape[0])
    weights = (gate_weight.T, up_weight.T, down_weight)
    spread, own, limit, taken, slots = prepare(
        sharers, capacity, cache_length, earlier, routes.T, route_weight.T, queries, new_key
    )
    other_weights = [swap(block) for block in lax.optimization_barrier(weights)]
    attended = exchange(
        attend(count, spread, own, limit, key_cache, value_cache, new_value, ln_gain)
    )
    mine, gains = project(attended, out_weight)
    stream, chosen = pick(sharers, count, mine, swap(mine), residual, taken)
    outgoing = run_experts(slots, exchange(chosen), gains, weights, other_weights)
    combined = combine(sharers, taken, exchange(outgoing))
    attn_stream, expert_out = finish(stream, combined, swap(combined))
    return (attn_stream, expert_out)


def solution(mesh):
    count = mesh.shape["attn"]
    fits = D // count % 256 == 0 and count % HELD == 0 and mesh.shape["expert"] == 2
    return jax.shard_map(
        shards if fits else shards_plain,
        mesh=mesh,
        in_specs=(
            P(("group", "attn"), "expert"),
            P(("group", "attn"), None, "expert"),
            P(("group", "attn"), None, "expert"),
            P(("group", "attn"), "expert"),
            P(("group", "attn"), "expert"),
            P(("group", "attn")),
            P("group", "attn"),
            P("expert", "attn"),
            P("attn"),
            P(None, ("attn", "expert")),
            P(None, ("attn", "expert")),
            P(("attn", "expert"), None),
            P("group", None),
            P("group", None),
        ),
        out_specs=(P("group", "attn"), P("group", "attn")),
        check_vma=False,
    )
```

```python
import functools
import math

import jax
import jax.numpy as jnp
from jax import lax
from jax.experimental import pallas as pl
from jax.experimental.pallas import tpu as pltpu
from jax.sharding import PartitionSpec as P

D = 6144
HEADS = 48
KV_HEADS = 8
HEAD_DIM = 128
EXPERTS = 16
TOP = 4
HELD = 2


NEG_FILL = -1e30
EPSILON = 1e-05


def attend_local(queries, key_cache, value_cache, new_key, new_value, cache_length):
    row_count = queries.shape[0]
    kv_local = new_key.shape[1] // HEAD_DIM
    group = HEADS // KV_HEADS
    length_max = key_cache.shape[1]
    query_heads = queries.reshape(row_count, kv_local, group, HEAD_DIM)
    key_heads = key_cache.reshape(row_count, length_max, kv_local, HEAD_DIM)
    value_heads = value_cache.reshape(row_count, length_max, kv_local, HEAD_DIM)
    own_keys = new_key.reshape(row_count, kv_local, HEAD_DIM)
    own_values = new_value.reshape(row_count, kv_local, HEAD_DIM)
    scale = 1.0 / math.sqrt(HEAD_DIM)
    past = (
        jnp.einsum("rkgd,rlkd->rkgl", query_heads, key_heads, preferred_element_type=jnp.float32)
        * scale
    )
    valid = jnp.arange(length_max, dtype=jnp.int32)[None, :] < cache_length[:, None]
    past = jnp.where(valid[:, None, None, :], past, NEG_FILL)
    own = (
        jnp.einsum("rkgd,rkd->rkg", query_heads, own_keys, preferred_element_type=jnp.float32)
        * scale
    )
    largest = jnp.maximum(jnp.max(past, axis=3), own)
    past_weight = jnp.exp(past - largest[..., None])
    own_weight = jnp.exp(own - largest)
    total = jnp.sum(past_weight, axis=3) + own_weight
    past_prob = (past_weight / total[..., None]).astype(jnp.bfloat16)
    own_prob = (own_weight / total).astype(jnp.bfloat16)
    result = jnp.einsum(
        "rkgl,rlkd->rkgd", past_prob, value_heads, preferred_element_type=jnp.float32
    )
    result = (
        result
        + own_prob.astype(jnp.float32)[..., None] * own_values.astype(jnp.float32)[:, :, None, :]
    )
    return result.reshape(row_count, kv_local * group * HEAD_DIM).astype(jnp.bfloat16)


def selection(routes, route_weight, capacity):
    row_count = routes.shape[0]
    experts = jnp.arange(HELD, dtype=jnp.int32)
    match = routes[None, :, :] == experts[:, None, None]
    hit = jnp.any(match, axis=2)
    row_weight = jnp.sum(jnp.where(match, route_weight[None], 0.0), axis=2)
    earlier = jnp.arange(row_count)[:, None] < jnp.arange(row_count)[None, :]
    slot = jnp.sum(jnp.where(earlier[None] & hit[:, :, None], 1, 0), axis=1)
    taken = hit[:, None, :] & (slot[:, None, :] == jnp.arange(capacity, dtype=jnp.int32)[None, :, None])
    slot_weight = jnp.sum(jnp.where(taken, row_weight[:, None, :], 0.0), axis=2)
    return taken, slot_weight


def gather_attn(block):
    count = lax.axis_size("attn")
    copies = jnp.broadcast_to(block[None], (count,) + block.shape)
    return lax.all_to_all(copies, "attn", split_axis=0, concat_axis=0, tiled=True)


def pair_sum(block):
    return block + lax.ppermute(block, "expert", [(0, 1), (1, 0)])


def shards_plain(
    queries,
    key_cache,
    value_cache,
    new_key,
    new_value,
    cache_length,
    residual,
    out_weight,
    ln_gain,
    gate_weight,
    up_weight,
    down_weight,
    routes,
    route_weight,
):
    attn_count = lax.axis_size("attn")
    core_count = lax.axis_size("expert")
    sharers = attn_count * core_count // HELD
    my_expert = (lax.axis_index("attn") * core_count + lax.axis_index("expert")) // sharers
    dest_expert = [index * core_count // sharers for index in range(attn_count)]
    row_count = routes.shape[0]
    capacity = row_count * TOP // EXPERTS * 2
    cols = residual.shape[1]

    taken, slot_weight = selection(routes, route_weight, capacity)
    pick = taken.astype(jnp.bfloat16)

    gains = gather_attn(ln_gain)

    attended = attend_local(queries, key_cache, value_cache, new_key, new_value, cache_length)
    whole = gather_attn(attended).reshape(row_count, -1)
    partial_proj = jnp.dot(whole, out_weight, preferred_element_type=jnp.float32)
    head_total = pair_sum(partial_proj)
    attn_stream = (residual.astype(jnp.float32) + head_total).astype(jnp.bfloat16)

    chosen = jnp.einsum(
        "esr,rd->esd", pick, attn_stream, preferred_element_type=jnp.float32
    ).astype(jnp.bfloat16)
    outgoing = jnp.stack([chosen[index] for index in dest_expert])
    rows = lax.all_to_all(outgoing, "attn", split_axis=0, concat_axis=0, tiled=True)
    wide = rows.astype(jnp.float32)
    row_mean = jnp.sum(wide, axis=(0, 2)) / D
    row_var = jnp.sum(wide * wide, axis=(0, 2)) / D - row_mean * row_mean
    normed = (
        (wide - row_mean[None, :, None])
        * lax.rsqrt(row_var + EPSILON)[None, :, None]
        * gains.reshape(attn_count, 1, cols)
    ).astype(jnp.bfloat16)
    gate_val = jnp.einsum(
        "asd,adf->sf", normed, gate_weight.reshape(attn_count, cols, -1),
        preferred_element_type=jnp.float32,
    )
    up_val = jnp.einsum(
        "asd,adf->sf", normed, up_weight.reshape(attn_count, cols, -1),
        preferred_element_type=jnp.float32,
    )
    hidden = (jax.nn.silu(gate_val) * up_val).astype(jnp.bfloat16)
    piece = jnp.dot(hidden, down_weight, preferred_element_type=jnp.float32)
    mine = jnp.take(slot_weight, my_expert, axis=0)
    piece = (piece * mine[:, None]).astype(jnp.bfloat16)
    returned = lax.all_to_all(
        piece.reshape(capacity, attn_count, cols).swapaxes(0, 1),
        "attn", split_axis=0, concat_axis=0, tiled=True,
    )
    spread = jnp.stack([pick[index] for index in dest_expert])
    combined = jnp.einsum(
        "asr,asd->rd", spread, returned, preferred_element_type=jnp.float32
    )
    expert_out = pair_sum(combined).astype(jnp.bfloat16)
    return (attn_stream, expert_out)


MIB = 1024 * 1024
EXCHANGE_FLOPS = 10**10
VMEM_SPEC = pl.BlockSpec(memory_space=pltpu.VMEM)
SMEM_SPEC = pl.BlockSpec(memory_space=pltpu.SMEM)
HBM_SPEC = pl.BlockSpec(memory_space=pltpu.HBM)


def call(kernel, outs, in_specs, scratch, flops, nbytes, vmem_mib):
    single = not isinstance(outs, (list, tuple))
    return pl.pallas_call(
        kernel,
        out_shape=outs,
        in_specs=in_specs,
        out_specs=VMEM_SPEC if single else [VMEM_SPEC] * len(outs),
        scratch_shapes=scratch,
        cost_estimate=pl.CostEstimate(flops=flops, bytes_accessed=nbytes, transcendentals=0),
        compiler_params=pltpu.CompilerParams(vmem_limit_bytes=vmem_mib * MIB),
    )


def order_kernel(out_ref):
    rows = out_ref.shape[0]
    before = lax.broadcasted_iota(jnp.int32, (rows, rows), 0) < lax.broadcasted_iota(
        jnp.int32, (rows, rows), 1
    )
    out_ref[...] = jnp.where(before, 1.0, 0.0).astype(jnp.bfloat16)


def order(rows):
    return call(
        order_kernel,
        jax.ShapeDtypeStruct((rows, rows), jnp.bfloat16),
        [],
        [],
        EXCHANGE_FLOPS, rows * rows * 2, 2,
    )()


def expert_rows(routes, earlier, expert, capacity):
    row_count = routes.shape[1]
    hit = jnp.max((routes == expert).astype(jnp.float32), axis=0, keepdims=True)
    slot = jnp.dot(
        jnp.broadcast_to(hit, (8, row_count)).astype(jnp.bfloat16),
        earlier,
        preferred_element_type=jnp.float32,
    )[:1]
    place = lax.broadcasted_iota(jnp.int32, (capacity, row_count), 0).astype(jnp.float32)
    return jnp.where((slot == place) & (hit > 0.5), 1.0, 0.0)


def prepare_kernel(sharers, length_ref, earlier_ref, routes_ref, weight_ref, query_ref,
                   own_key_ref, spread_ref, own_ref, limit_ref, taken_ref, slot_ref, query_rows,
                   key_rows):
    row_count = query_ref.shape[0]
    kv_local = own_key_ref.shape[1] // HEAD_DIM
    group = HEADS // KV_HEADS
    heads = kv_local * group
    for g in range(kv_local):
        own_key = own_key_ref[:, g * HEAD_DIM : (g + 1) * HEAD_DIM].astype(jnp.float32)
        for i in range(group):
            index = g * group + i
            rows = pl.ds(index * row_count, row_count)
            query_rows[rows, :] = query_ref[
                :, index * HEAD_DIM : (index + 1) * HEAD_DIM
            ].astype(jnp.float32)
            key_rows[rows, :] = own_key
    scale = 1.0 / math.sqrt(HEAD_DIM)
    lengths = length_ref[...].reshape(1, -1)
    head = lax.broadcasted_iota(jnp.int32, (heads, 1), 0) // group
    for r in range(row_count):
        strided = pl.ds(r, heads, stride=row_count)
        query = query_rows[strided, :]
        own = jnp.sum(query * key_rows[strided, :], axis=1, keepdims=True) * scale
        own_ref[r] = jnp.broadcast_to(own, (heads, HEAD_DIM))
        limit_ref[r] = jnp.broadcast_to(lengths[:, r : r + 1], (heads, HEAD_DIM))
        spread_ref[r] = jnp.concatenate(
            [jnp.where(head == g, query, 0.0) for g in range(kv_local)], axis=1
        ).astype(jnp.bfloat16)
    routes = routes_ref[...]
    capacity = slot_ref.shape[0]
    core = lax.axis_index("expert")
    taken = []
    for e in range(HELD):
        both = expert_rows(routes, earlier_ref[...], e, 2 * capacity)
        taken.append(jnp.where(core == 0, both[:capacity], both[capacity:]))
        taken_ref[e] = taken[e]
    first = lax.axis_index("attn") < sharers
    expert = jnp.where(first, 0, 1)
    row_weight = jnp.sum(
        jnp.where(routes == expert, weight_ref[...], 0.0), axis=0, keepdims=True
    )
    mine = jnp.where(first, taken[0], taken[1])
    slot_ref[...] = jnp.broadcast_to(
        jnp.sum(mine * row_weight, axis=1, keepdims=True), slot_ref.shape
    )


def prepare(
    sharers, capacity, cache_length, earlier, routes, route_weight, queries, new_key
):
    row_count, width = queries.shape
    heads = width // HEAD_DIM
    table = pltpu.VMEM((heads * row_count, HEAD_DIM), jnp.float32)
    return call(
        functools.partial(prepare_kernel, sharers),
        [
            jax.ShapeDtypeStruct((row_count, heads, new_key.shape[1]), jnp.bfloat16),
            jax.ShapeDtypeStruct((row_count, heads, HEAD_DIM), jnp.float32),
            jax.ShapeDtypeStruct((row_count, heads, HEAD_DIM), jnp.int32),
            jax.ShapeDtypeStruct((HELD, capacity, routes.shape[1]), jnp.float32),
            jax.ShapeDtypeStruct((capacity, HEAD_DIM), jnp.float32),
        ],
        [VMEM_SPEC] * 6,
        [table, table],
        queries.size * 8, queries.size * 16, 4,
    )(cache_length, earlier, routes, route_weight, queries, new_key)


def score_kernel(spread_ref, own_ref, limit_ref, key_ref, probs_ref, own_probs_ref):
    row_count, heads, length_max = probs_ref.shape
    scale = 1.0 / math.sqrt(HEAD_DIM)
    contract = (((1,), (1,)), ((), ()))
    products = [
        lax.dot_general(spread_ref[r], key_ref[r], contract, preferred_element_type=jnp.float32)
        for r in range(row_count)
    ]
    for first in range(0, row_count, 2):
        batch = range(first, min(first + 2, row_count))
        scores = jnp.concatenate([products[r] for r in batch], axis=0)
        position = lax.broadcasted_iota(jnp.int32, scores.shape, 1)
        limit = jnp.concatenate([limit_ref[r, :, :1] for r in batch], axis=0)
        own = jnp.concatenate([own_ref[r, :, :1] for r in batch], axis=0)
        past = jnp.where(position < limit, scores * scale, NEG_FILL)
        largest = jnp.maximum(jnp.max(past, axis=1, keepdims=True), own)
        weight = jnp.exp(past - largest)
        own_weight = jnp.exp(own - largest)
        inverse = 1.0 / (jnp.sum(weight, axis=1, keepdims=True) + own_weight)
        probs = weight * inverse
        own_prob = (own_weight * inverse).astype(jnp.bfloat16).astype(jnp.float32)
        for index, r in enumerate(batch):
            rows = slice(index * heads, (index + 1) * heads)
            probs_ref[r] = probs[rows].astype(jnp.bfloat16)
            own_probs_ref[r] = jnp.broadcast_to(own_prob[rows], own_probs_ref.shape[1:])


def value_kernel(probs_ref, own_ref, value_ref, own_value_ref, gain_ref, out_ref, value_rows,
                 result_rows):
    row_count, length_max, width = value_ref.shape
    kv_local = width // HEAD_DIM
    group = HEADS // KV_HEADS
    heads = kv_local * group
    for g in range(kv_local):
        own_value = own_value_ref[:, g * HEAD_DIM : (g + 1) * HEAD_DIM].astype(jnp.float32)
        for i in range(group):
            value_rows[pl.ds((g * group + i) * row_count, row_count), :] = own_value
    head = lax.broadcasted_iota(jnp.int32, (heads, 1), 0) // group
    for r in range(row_count):
        strided = pl.ds(r, heads, stride=row_count)
        product = jnp.dot(probs_ref[r], value_ref[r], preferred_element_type=jnp.float32)
        total = own_ref[r] * value_rows[strided, :]
        for g in range(kv_local):
            lanes = slice(g * HEAD_DIM, (g + 1) * HEAD_DIM)
            total = total + jnp.where(head == g, product[:, lanes], 0.0)
        result_rows[strided, :] = total
    for index in range(heads):
        rows = result_rows[pl.ds(index * row_count, row_count), :].astype(jnp.bfloat16)
        for copy in range(out_ref.shape[0]):
            out_ref[copy, :, index * HEAD_DIM : (index + 1) * HEAD_DIM] = rows
    gain_row = gain_ref[...].reshape(1, -1)
    half = gain_row.shape[1] // 2
    row = lax.broadcasted_iota(jnp.int32, (row_count, half), 0)
    left = jnp.broadcast_to(gain_row[:, :half], (row_count, half))
    right = jnp.broadcast_to(gain_row[:, half:], (row_count, half))
    gain = jnp.where(row % 2 == 0, left, right)
    upper = gain.astype(jnp.bfloat16).astype(jnp.float32)
    parts = jnp.where(row < 2, upper, gain - upper).astype(jnp.bfloat16)
    for copy in range(out_ref.shape[0]):
        out_ref[copy, :, heads * HEAD_DIM :] = parts


def attend(count, spread, own, limit, key_cache, value_cache, new_value, gain):
    row_count, heads, _ = spread.shape
    length_max = key_cache.shape[1]
    table = pltpu.VMEM((heads * row_count, HEAD_DIM), jnp.float32)
    probs, own_probs = call(
        score_kernel,
        [
            jax.ShapeDtypeStruct((row_count, heads, length_max), jnp.bfloat16),
            jax.ShapeDtypeStruct((row_count, heads, HEAD_DIM), jnp.float32),
        ],
        [VMEM_SPEC] * 4,
        [],
        2 * key_cache.size * heads, key_cache.size * 2, 8,
    )(spread, own, limit, key_cache)
    width = heads * HEAD_DIM + gain.shape[0] // 2
    return call(
        value_kernel,
        jax.ShapeDtypeStruct((count, row_count, width), jnp.bfloat16),
        [VMEM_SPEC] * 5,
        [table, table],
        EXCHANGE_FLOPS, value_cache.size * 2, 8,
    )(probs, own_probs, value_cache, new_value, gain)


def project_kernel(pieces, weight_ref, out_ref, gain_ref, stack):
    count, rows, _ = pieces.shape
    width = weight_ref.shape[0]
    half = gain_ref.shape[1] // 2
    for k in range(count):
        parts = pieces[k, :, width:].astype(jnp.float32)
        gain_ref[pl.ds(k, 1), :half] = parts[0:1] + parts[2:3]
        gain_ref[pl.ds(k, 1), half:] = parts[1:2] + parts[3:4]
    total = 0.0
    step = width // 4
    for start in range(0, width, step):
        part = slice(start, start + step)
        for k in range(count):
            stack[pl.ds(k * rows, rows), part] = pieces[k, :, part].astype(jnp.float32)
        total = total + jnp.dot(
            stack[:, part].astype(jnp.bfloat16),
            weight_ref[part, :],
            preferred_element_type=jnp.float32,
        )
    out_ref[...] = total


def project(pieces, out_weight):
    count, rows, _ = pieces.shape
    depth, cols = out_weight.shape
    return call(
        project_kernel,
        [
            jax.ShapeDtypeStruct((rows * count, cols), jnp.float32),
            jax.ShapeDtypeStruct((count, cols), jnp.float32),
        ],
        [VMEM_SPEC, VMEM_SPEC],
        [pltpu.VMEM((rows * count, depth), jnp.float32)],
        EXCHANGE_FLOPS, out_weight.size * 2, 10,
    )(pieces, out_weight)


def pick_kernel(sharers, mine_ref, other_ref, residual_ref, taken_ref, stream_ref, out_ref):
    stream = (
        residual_ref[...].astype(jnp.float32) + (mine_ref[...] + other_ref[...])
    ).astype(jnp.bfloat16)
    stream_ref[...] = stream
    chosen = [
        jnp.dot(
            taken_ref[e].astype(jnp.bfloat16), stream, preferred_element_type=jnp.float32
        ).astype(jnp.bfloat16)
        for e in range(HELD)
    ]
    for k in range(out_ref.shape[0]):
        out_ref[k] = chosen[k // sharers]


def pick(sharers, count, mine, other, residual, taken):
    rows, cols = mine.shape
    return call(
        functools.partial(pick_kernel, sharers),
        [
            jax.ShapeDtypeStruct((rows, cols), jnp.bfloat16),
            jax.ShapeDtypeStruct((count, taken.shape[1], cols), jnp.bfloat16),
        ],
        [VMEM_SPEC] * 4,
        [],
        2 * HELD * taken.shape[1] * rows * cols, rows * cols * 12, 4,
    )(mine, other, residual, taken)


def expert_kernel(slot_ref, pieces, gains, *refs):
    weights, out_ref, rows_ref = (refs[:3], refs[3:6]), refs[6], refs[7]
    count, capacity, cols = pieces.shape
    first = second = 0.0
    for k in range(count):
        wide = pieces[k].astype(jnp.float32)
        first = first + wide
        second = second + wide * wide
    row_mean = jnp.sum(first, axis=1, keepdims=True) / D
    row_var = jnp.sum(second, axis=1, keepdims=True) / D - row_mean * row_mean
    inverse = lax.rsqrt(row_var + EPSILON)
    for k in range(count):
        wide = pieces[k].astype(jnp.float32)
        normed = (wide - row_mean) * inverse * gains[pl.ds(k, 1), :]
        rows_ref[:, k * cols : (k + 1) * cols] = normed.astype(jnp.bfloat16)
    rows = rows_ref[...]
    contract = (((1,), (1,)), ((), ()))
    hidden = []
    for gate_ref, up_ref, _ in weights:
        gate = lax.dot_general(rows, gate_ref[...], contract, preferred_element_type=jnp.float32)
        up = lax.dot_general(rows, up_ref[...], contract, preferred_element_type=jnp.float32)
        hidden.append((gate / (1.0 + jnp.exp(-gate)) * up).astype(jnp.bfloat16))
    slot_weight = slot_ref[:, :1]
    for k in range(count):
        block = slice(k * cols, (k + 1) * cols)
        piece = sum(
            jnp.dot(part, refs_of[2][:, block], preferred_element_type=jnp.float32)
            for part, refs_of in zip(hidden, weights)
        )
        out_ref[k] = (piece * slot_weight).astype(jnp.bfloat16)


def run_experts(slots, pieces, gains, own, other):
    count, capacity, cols = pieces.shape
    return call(
        expert_kernel,
        jax.ShapeDtypeStruct(pieces.shape, jnp.bfloat16),
        [VMEM_SPEC] * 9,
        [pltpu.VMEM((capacity, count * cols), jnp.bfloat16)],
        12 * capacity * own[0].size, own[0].size * 12, 20,
    )(slots, pieces, gains, *own, *other)


def combine_kernel(sharers, taken_ref, pieces, out_ref):
    count, capacity, cols = pieces.shape
    spread = [taken_ref[k // sharers] for k in range(count)]
    rows = [pieces[k].astype(jnp.float32) for k in range(count)]
    out_ref[...] = lax.dot_general(
        jnp.concatenate(spread, axis=0).astype(jnp.bfloat16),
        jnp.concatenate(rows, axis=0).astype(jnp.bfloat16),
        (((0,), (0,)), ((), ())),
        preferred_element_type=jnp.float32,
    )


def combine(sharers, taken, pieces):
    count, capacity, cols = pieces.shape
    rows = taken.shape[2]
    return call(
        functools.partial(combine_kernel, sharers),
        jax.ShapeDtypeStruct((rows, cols), jnp.float32),
        [VMEM_SPEC] * 2,
        [],
        2 * rows * capacity * count * cols, (count * capacity * 2 + rows * 4) * cols, 4,
    )(taken, pieces)


def finish_kernel(stream_ref, mine_ref, other_ref, stream_out_ref, out_ref):
    stream_out_ref[...] = stream_ref[...]
    out_ref[...] = (mine_ref[...] + other_ref[...]).astype(jnp.bfloat16)


def finish(stream, mine, other):
    return call(
        finish_kernel,
        [jax.ShapeDtypeStruct(stream.shape, jnp.bfloat16)] * 2,
        [VMEM_SPEC] * 3,
        [],
        mine.size, mine.size * 14, 4,
    )(stream, mine, other)


def exchange(blocks):
    return lax.all_to_all(blocks, "attn", split_axis=0, concat_axis=0, tiled=True)


def swap(block):
    return lax.ppermute(block, "expert", [(0, 1), (1, 0)])


def shards(
    queries,
    key_cache,
    value_cache,
    new_key,
    new_value,
    cache_length,
    residual,
    out_weight,
    ln_gain,
    gate_weight,
    up_weight,
    down_weight,
    routes,
    route_weight,
):
    count = lax.axis_size("attn")
    sharers = count // HELD
    capacity = routes.shape[0] * TOP // EXPERTS

    earlier = order(routes.shape[0])
    weights = (gate_weight.T, up_weight.T, down_weight)
    spread, own, limit, taken, slots = prepare(
        sharers, capacity, cache_length, earlier, routes.T, route_weight.T, queries, new_key
    )
    other_weights = [swap(block) for block in lax.optimization_barrier(weights)]
    attended = exchange(
        attend(count, spread, own, limit, key_cache, value_cache, new_value, ln_gain)
    )
    mine, gains = project(attended, out_weight)
    stream, chosen = pick(sharers, count, mine, swap(mine), residual, taken)
    outgoing = run_experts(slots, exchange(chosen), gains, weights, other_weights)
    combined = combine(sharers, taken, exchange(outgoing))
    attn_stream, expert_out = finish(stream, combined, swap(combined))
    return (attn_stream, expert_out)


def solution(mesh):
    count = mesh.shape["attn"]
    fits = D // count % 256 == 0 and count % HELD == 0 and mesh.shape["expert"] == 2
    return jax.shard_map(
        shards if fits else shards_plain,
        mesh=mesh,
        in_specs=(
            P(("group", "attn"), "expert"),
            P(("group", "attn"), None, "expert"),
            P(("group", "attn"), None, "expert"),
            P(("group", "attn"), "expert"),
            P(("group", "attn"), "expert"),
            P(("group", "attn")),
            P("group", "attn"),
            P("expert", "attn"),
            P("attn"),
            P(None, ("attn", "expert")),
            P(None, ("attn", "expert")),
            P(("attn", "expert"), None),
            P("group", None),
            P("group", None),
        ),
        out_specs=(P("group", "attn"), P("group", "attn")),
        check_vma=False,
    )
```

```python
import functools
import math

import jax
import jax.numpy as jnp
from jax import lax
from jax.experimental import pallas as pl
from jax.experimental.pallas import tpu as pltpu
from jax.sharding import PartitionSpec as P

D = 6144
HEADS = 48
KV_HEADS = 8
HEAD_DIM = 128
EXPERTS = 16
TOP = 4
HELD = 2


NEG_FILL = -1e30
EPSILON = 1e-05


def attend_local(queries, key_cache, value_cache, new_key, new_value, cache_length):
    row_count = queries.shape[0]
    kv_local = new_key.shape[1] // HEAD_DIM
    group = HEADS // KV_HEADS
    length_max = key_cache.shape[1]
    query_heads = queries.reshape(row_count, kv_local, group, HEAD_DIM)
    key_heads = key_cache.reshape(row_count, length_max, kv_local, HEAD_DIM)
    value_heads = value_cache.reshape(row_count, length_max, kv_local, HEAD_DIM)
    own_keys = new_key.reshape(row_count, kv_local, HEAD_DIM)
    own_values = new_value.reshape(row_count, kv_local, HEAD_DIM)
    scale = 1.0 / math.sqrt(HEAD_DIM)
    past = (
        jnp.einsum("rkgd,rlkd->rkgl", query_heads, key_heads, preferred_element_type=jnp.float32)
        * scale
    )
    valid = jnp.arange(length_max, dtype=jnp.int32)[None, :] < cache_length[:, None]
    past = jnp.where(valid[:, None, None, :], past, NEG_FILL)
    own = (
        jnp.einsum("rkgd,rkd->rkg", query_heads, own_keys, preferred_element_type=jnp.float32)
        * scale
    )
    largest = jnp.maximum(jnp.max(past, axis=3), own)
    past_weight = jnp.exp(past - largest[..., None])
    own_weight = jnp.exp(own - largest)
    total = jnp.sum(past_weight, axis=3) + own_weight
    past_prob = (past_weight / total[..., None]).astype(jnp.bfloat16)
    own_prob = (own_weight / total).astype(jnp.bfloat16)
    result = jnp.einsum(
        "rkgl,rlkd->rkgd", past_prob, value_heads, preferred_element_type=jnp.float32
    )
    result = (
        result
        + own_prob.astype(jnp.float32)[..., None] * own_values.astype(jnp.float32)[:, :, None, :]
    )
    return result.reshape(row_count, kv_local * group * HEAD_DIM).astype(jnp.bfloat16)


def selection(routes, route_weight, capacity):
    row_count = routes.shape[0]
    experts = jnp.arange(HELD, dtype=jnp.int32)
    match = routes[None, :, :] == experts[:, None, None]
    hit = jnp.any(match, axis=2)
    row_weight = jnp.sum(jnp.where(match, route_weight[None], 0.0), axis=2)
    earlier = jnp.arange(row_count)[:, None] < jnp.arange(row_count)[None, :]
    slot = jnp.sum(jnp.where(earlier[None] & hit[:, :, None], 1, 0), axis=1)
    taken = hit[:, None, :] & (slot[:, None, :] == jnp.arange(capacity, dtype=jnp.int32)[None, :, None])
    slot_weight = jnp.sum(jnp.where(taken, row_weight[:, None, :], 0.0), axis=2)
    return taken, slot_weight


def gather_attn(block):
    count = lax.axis_size("attn")
    copies = jnp.broadcast_to(block[None], (count,) + block.shape)
    return lax.all_to_all(copies, "attn", split_axis=0, concat_axis=0, tiled=True)


def pair_sum(block):
    return block + lax.ppermute(block, "expert", [(0, 1), (1, 0)])


def shards_plain(
    queries,
    key_cache,
    value_cache,
    new_key,
    new_value,
    cache_length,
    residual,
    out_weight,
    ln_gain,
    gate_weight,
    up_weight,
    down_weight,
    routes,
    route_weight,
):
    attn_count = lax.axis_size("attn")
    core_count = lax.axis_size("expert")
    sharers = attn_count * core_count // HELD
    my_expert = (lax.axis_index("attn") * core_count + lax.axis_index("expert")) // sharers
    dest_expert = [index * core_count // sharers for index in range(attn_count)]
    row_count = routes.shape[0]
    capacity = row_count * TOP // EXPERTS * 2
    cols = residual.shape[1]

    taken, slot_weight = selection(routes, route_weight, capacity)
    pick = taken.astype(jnp.bfloat16)

    gains = gather_attn(ln_gain)

    attended = attend_local(queries, key_cache, value_cache, new_key, new_value, cache_length)
    whole = gather_attn(attended).reshape(row_count, -1)
    partial_proj = jnp.dot(whole, out_weight, preferred_element_type=jnp.float32)
    head_total = pair_sum(partial_proj)
    attn_stream = (residual.astype(jnp.float32) + head_total).astype(jnp.bfloat16)

    chosen = jnp.einsum(
        "esr,rd->esd", pick, attn_stream, preferred_element_type=jnp.float32
    ).astype(jnp.bfloat16)
    outgoing = jnp.stack([chosen[index] for index in dest_expert])
    rows = lax.all_to_all(outgoing, "attn", split_axis=0, concat_axis=0, tiled=True)
    wide = rows.astype(jnp.float32)
    row_mean = jnp.sum(wide, axis=(0, 2)) / D
    row_var = jnp.sum(wide * wide, axis=(0, 2)) / D - row_mean * row_mean
    normed = (
        (wide - row_mean[None, :, None])
        * lax.rsqrt(row_var + EPSILON)[None, :, None]
        * gains.reshape(attn_count, 1, cols)
    ).astype(jnp.bfloat16)
    gate_val = jnp.einsum(
        "asd,adf->sf", normed, gate_weight.reshape(attn_count, cols, -1),
        preferred_element_type=jnp.float32,
    )
    up_val = jnp.einsum(
        "asd,adf->sf", normed, up_weight.reshape(attn_count, cols, -1),
        preferred_element_type=jnp.float32,
    )
    hidden = (jax.nn.silu(gate_val) * up_val).astype(jnp.bfloat16)
    piece = jnp.dot(hidden, down_weight, preferred_element_type=jnp.float32)
    mine = jnp.take(slot_weight, my_expert, axis=0)
    piece = (piece * mine[:, None]).astype(jnp.bfloat16)
    returned = lax.all_to_all(
        piece.reshape(capacity, attn_count, cols).swapaxes(0, 1),
        "attn", split_axis=0, concat_axis=0, tiled=True,
    )
    spread = jnp.stack([pick[index] for index in dest_expert])
    combined = jnp.einsum(
        "asr,asd->rd", spread, returned, preferred_element_type=jnp.float32
    )
    expert_out = pair_sum(combined).astype(jnp.bfloat16)
    return (attn_stream, expert_out)


MIB = 1024 * 1024
EXCHANGE_FLOPS = 10**10
VMEM_SPEC = pl.BlockSpec(memory_space=pltpu.VMEM)
SMEM_SPEC = pl.BlockSpec(memory_space=pltpu.SMEM)
HBM_SPEC = pl.BlockSpec(memory_space=pltpu.HBM)


def call(kernel, outs, in_specs, scratch, flops, nbytes, vmem_mib):
    single = not isinstance(outs, (list, tuple))
    return pl.pallas_call(
        kernel,
        out_shape=outs,
        in_specs=in_specs,
        out_specs=VMEM_SPEC if single else [VMEM_SPEC] * len(outs),
        scratch_shapes=scratch,
        cost_estimate=pl.CostEstimate(flops=flops, bytes_accessed=nbytes, transcendentals=0),
        compiler_params=pltpu.CompilerParams(vmem_limit_bytes=vmem_mib * MIB),
    )


def order_kernel(out_ref):
    rows = out_ref.shape[0]
    before = lax.broadcasted_iota(jnp.int32, (rows, rows), 0) < lax.broadcasted_iota(
        jnp.int32, (rows, rows), 1
    )
    out_ref[...] = jnp.where(before, 1.0, 0.0).astype(jnp.bfloat16)


def order(rows):
    return call(
        order_kernel,
        jax.ShapeDtypeStruct((rows, rows), jnp.bfloat16),
        [],
        [],
        EXCHANGE_FLOPS, rows * rows * 2, 2,
    )()


def expert_rows(routes, earlier, expert, capacity):
    row_count = routes.shape[1]
    hit = jnp.max((routes == expert).astype(jnp.float32), axis=0, keepdims=True)
    slot = jnp.dot(
        jnp.broadcast_to(hit, (8, row_count)).astype(jnp.bfloat16),
        earlier,
        preferred_element_type=jnp.float32,
    )[:1]
    place = lax.broadcasted_iota(jnp.int32, (capacity, row_count), 0).astype(jnp.float32)
    return jnp.where((slot == place) & (hit > 0.5), 1.0, 0.0)


def prepare_kernel(sharers, length_ref, earlier_ref, routes_ref, weight_ref, query_ref,
                   own_key_ref, spread_ref, own_ref, limit_ref, taken_ref, slot_ref, query_rows,
                   key_rows):
    row_count = query_ref.shape[0]
    kv_local = own_key_ref.shape[1] // HEAD_DIM
    group = HEADS // KV_HEADS
    heads = kv_local * group
    for g in range(kv_local):
        own_key = own_key_ref[:, g * HEAD_DIM : (g + 1) * HEAD_DIM].astype(jnp.float32)
        for i in range(group):
            index = g * group + i
            rows = pl.ds(index * row_count, row_count)
            query_rows[rows, :] = query_ref[
                :, index * HEAD_DIM : (index + 1) * HEAD_DIM
            ].astype(jnp.float32)
            key_rows[rows, :] = own_key
    scale = 1.0 / math.sqrt(HEAD_DIM)
    lengths = length_ref[...].reshape(1, -1)
    head = lax.broadcasted_iota(jnp.int32, (heads, 1), 0) // group
    for r in range(row_count):
        strided = pl.ds(r, heads, stride=row_count)
        query = query_rows[strided, :]
        own = jnp.sum(query * key_rows[strided, :], axis=1, keepdims=True) * scale
        own_ref[r] = jnp.broadcast_to(own, (heads, HEAD_DIM))
        limit_ref[r] = jnp.broadcast_to(lengths[:, r : r + 1], (heads, HEAD_DIM))
        spread_ref[r] = jnp.concatenate(
            [jnp.where(head == g, query, 0.0) for g in range(kv_local)], axis=1
        ).astype(jnp.bfloat16)
    routes = routes_ref[...]
    capacity = slot_ref.shape[0]
    core = lax.axis_index("expert")
    taken = []
    for e in range(HELD):
        both = expert_rows(routes, earlier_ref[...], e, 2 * capacity)
        taken.append(jnp.where(core == 0, both[:capacity], both[capacity:]))
        taken_ref[e] = taken[e]
    first = lax.axis_index("attn") < sharers
    expert = jnp.where(first, 0, 1)
    row_weight = jnp.sum(
        jnp.where(routes == expert, weight_ref[...], 0.0), axis=0, keepdims=True
    )
    mine = jnp.where(first, taken[0], taken[1])
    slot_ref[...] = jnp.broadcast_to(
        jnp.sum(mine * row_weight, axis=1, keepdims=True), slot_ref.shape
    )


def prepare(
    sharers, capacity, cache_length, earlier, routes, route_weight, queries, new_key
):
    row_count, width = queries.shape
    heads = width // HEAD_DIM
    table = pltpu.VMEM((heads * row_count, HEAD_DIM), jnp.float32)
    return call(
        functools.partial(prepare_kernel, sharers),
        [
            jax.ShapeDtypeStruct((row_count, heads, new_key.shape[1]), jnp.bfloat16),
            jax.ShapeDtypeStruct((row_count, heads, HEAD_DIM), jnp.float32),
            jax.ShapeDtypeStruct((row_count, heads, HEAD_DIM), jnp.int32),
            jax.ShapeDtypeStruct((HELD, capacity, routes.shape[1]), jnp.float32),
            jax.ShapeDtypeStruct((capacity, HEAD_DIM), jnp.float32),
        ],
        [VMEM_SPEC] * 6,
        [table, table],
        queries.size * 8, queries.size * 16, 4,
    )(cache_length, earlier, routes, route_weight, queries, new_key)


def score_kernel(spread_ref, own_ref, limit_ref, key_ref, probs_ref, own_probs_ref):
    row_count, heads, length_max = probs_ref.shape
    scale = 1.0 / math.sqrt(HEAD_DIM)
    contract = (((1,), (1,)), ((), ()))
    products = [
        lax.dot_general(spread_ref[r], key_ref[r], contract, preferred_element_type=jnp.float32)
        for r in range(row_count)
    ]
    for first in range(0, row_count, 2):
        batch = range(first, min(first + 2, row_count))
        scores = jnp.concatenate([products[r] for r in batch], axis=0)
        position = lax.broadcasted_iota(jnp.int32, scores.shape, 1)
        limit = jnp.concatenate([limit_ref[r, :, :1] for r in batch], axis=0)
        own = jnp.concatenate([own_ref[r, :, :1] for r in batch], axis=0)
        past = jnp.where(position < limit, scores * scale, NEG_FILL)
        largest = jnp.maximum(jnp.max(past, axis=1, keepdims=True), own)
        weight = jnp.exp(past - largest)
        own_weight = jnp.exp(own - largest)
        inverse = 1.0 / (jnp.sum(weight, axis=1, keepdims=True) + own_weight)
        probs = weight * inverse
        own_prob = (own_weight * inverse).astype(jnp.bfloat16).astype(jnp.float32)
        for index, r in enumerate(batch):
            rows = slice(index * heads, (index + 1) * heads)
            probs_ref[r] = probs[rows].astype(jnp.bfloat16)
            own_probs_ref[r] = jnp.broadcast_to(own_prob[rows], own_probs_ref.shape[1:])


def value_kernel(probs_ref, own_ref, value_ref, own_value_ref, gain_ref, out_ref, value_rows,
                 result_rows):
    row_count, length_max, width = value_ref.shape
    kv_local = width // HEAD_DIM
    group = HEADS // KV_HEADS
    heads = kv_local * group
    for g in range(kv_local):
        own_value = own_value_ref[:, g * HEAD_DIM : (g + 1) * HEAD_DIM].astype(jnp.float32)
        for i in range(group):
            value_rows[pl.ds((g * group + i) * row_count, row_count), :] = own_value
    head = lax.broadcasted_iota(jnp.int32, (heads, 1), 0) // group
    for r in range(row_count):
        strided = pl.ds(r, heads, stride=row_count)
        product = jnp.dot(probs_ref[r], value_ref[r], preferred_element_type=jnp.float32)
        total = own_ref[r] * value_rows[strided, :]
        for g in range(kv_local):
            lanes = slice(g * HEAD_DIM, (g + 1) * HEAD_DIM)
            total = total + jnp.where(head == g, product[:, lanes], 0.0)
        result_rows[strided, :] = total
    for index in range(heads):
        rows = result_rows[pl.ds(index * row_count, row_count), :].astype(jnp.bfloat16)
        for copy in range(out_ref.shape[0]):
            out_ref[copy, :, index * HEAD_DIM : (index + 1) * HEAD_DIM] = rows
    gain_row = gain_ref[...].reshape(1, -1)
    half = gain_row.shape[1] // 2
    row = lax.broadcasted_iota(jnp.int32, (row_count, half), 0)
    left = jnp.broadcast_to(gain_row[:, :half], (row_count, half))
    right = jnp.broadcast_to(gain_row[:, half:], (row_count, half))
    gain = jnp.where(row % 2 == 0, left, right)
    upper = gain.astype(jnp.bfloat16).astype(jnp.float32)
    parts = jnp.where(row < 2, upper, gain - upper).astype(jnp.bfloat16)
    for copy in range(out_ref.shape[0]):
        out_ref[copy, :, heads * HEAD_DIM :] = parts


def attend(count, spread, own, limit, key_cache, value_cache, new_value, gain):
    row_count, heads, _ = spread.shape
    length_max = key_cache.shape[1]
    table = pltpu.VMEM((heads * row_count, HEAD_DIM), jnp.float32)
    probs, own_probs = call(
        score_kernel,
        [
            jax.ShapeDtypeStruct((row_count, heads, length_max), jnp.bfloat16),
            jax.ShapeDtypeStruct((row_count, heads, HEAD_DIM), jnp.float32),
        ],
        [VMEM_SPEC] * 4,
        [],
        2 * key_cache.size * heads, key_cache.size * 2, 8,
    )(spread, own, limit, key_cache)
    width = heads * HEAD_DIM + gain.shape[0] // 2
    return call(
        value_kernel,
        jax.ShapeDtypeStruct((count, row_count, width), jnp.bfloat16),
        [VMEM_SPEC] * 5,
        [table, table],
        EXCHANGE_FLOPS, value_cache.size * 2, 8,
    )(probs, own_probs, value_cache, new_value, gain)


def project_kernel(pieces, weight_ref, out_ref, gain_ref, stack):
    count, rows, _ = pieces.shape
    width = weight_ref.shape[0]
    half = gain_ref.shape[1] // 2
    for k in range(count):
        parts = pieces[k, :, width:].astype(jnp.float32)
        gain_ref[pl.ds(k, 1), :half] = parts[0:1] + parts[2:3]
        gain_ref[pl.ds(k, 1), half:] = parts[1:2] + parts[3:4]
    total = 0.0
    step = width // 4
    for start in range(0, width, step):
        part = slice(start, start + step)
        for k in range(count):
            stack[pl.ds(k * rows, rows), part] = pieces[k, :, part].astype(jnp.float32)
        total = total + jnp.dot(
            stack[:, part].astype(jnp.bfloat16),
            weight_ref[part, :],
            preferred_element_type=jnp.float32,
        )
    out_ref[...] = total


def project(pieces, out_weight):
    count, rows, _ = pieces.shape
    depth, cols = out_weight.shape
    return call(
        project_kernel,
        [
            jax.ShapeDtypeStruct((rows * count, cols), jnp.float32),
            jax.ShapeDtypeStruct((count, cols), jnp.float32),
        ],
        [VMEM_SPEC, VMEM_SPEC],
        [pltpu.VMEM((rows * count, depth), jnp.float32)],
        2 * rows * count * out_weight.size, out_weight.size * 2, 10,
    )(pieces, out_weight)


def pick_kernel(sharers, mine_ref, other_ref, residual_ref, taken_ref, stream_ref, out_ref):
    stream = (
        residual_ref[...].astype(jnp.float32) + (mine_ref[...] + other_ref[...])
    ).astype(jnp.bfloat16)
    stream_ref[...] = stream
    chosen = [
        jnp.dot(
            taken_ref[e].astype(jnp.bfloat16), stream, preferred_element_type=jnp.float32
        ).astype(jnp.bfloat16)
        for e in range(HELD)
    ]
    for k in range(out_ref.shape[0]):
        out_ref[k] = chosen[k // sharers]


def pick(sharers, count, mine, other, residual, taken):
    rows, cols = mine.shape
    return call(
        functools.partial(pick_kernel, sharers),
        [
            jax.ShapeDtypeStruct((rows, cols), jnp.bfloat16),
            jax.ShapeDtypeStruct((count, taken.shape[1], cols), jnp.bfloat16),
        ],
        [VMEM_SPEC] * 4,
        [],
        2 * HELD * taken.shape[1] * rows * cols, rows * cols * 12, 4,
    )(mine, other, residual, taken)


def expert_kernel(slot_ref, pieces, gains, *refs):
    weights, out_ref, rows_ref = (refs[:3], refs[3:6]), refs[6], refs[7]
    count, capacity, cols = pieces.shape
    first = second = 0.0
    for k in range(count):
        wide = pieces[k].astype(jnp.float32)
        first = first + wide
        second = second + wide * wide
    row_mean = jnp.sum(first, axis=1, keepdims=True) / D
    row_var = jnp.sum(second, axis=1, keepdims=True) / D - row_mean * row_mean
    inverse = lax.rsqrt(row_var + EPSILON)
    for k in range(count):
        wide = pieces[k].astype(jnp.float32)
        normed = (wide - row_mean) * inverse * gains[pl.ds(k, 1), :]
        rows_ref[:, k * cols : (k + 1) * cols] = normed.astype(jnp.bfloat16)
    rows = rows_ref[...]
    contract = (((1,), (1,)), ((), ()))
    hidden = []
    for gate_ref, up_ref, _ in weights:
        gate = lax.dot_general(rows, gate_ref[...], contract, preferred_element_type=jnp.float32)
        up = lax.dot_general(rows, up_ref[...], contract, preferred_element_type=jnp.float32)
        hidden.append((gate / (1.0 + jnp.exp(-gate)) * up).astype(jnp.bfloat16))
    slot_weight = slot_ref[:, :1]
    for k in range(count):
        block = slice(k * cols, (k + 1) * cols)
        piece = sum(
            jnp.dot(part, refs_of[2][:, block], preferred_element_type=jnp.float32)
            for part, refs_of in zip(hidden, weights)
        )
        out_ref[k] = (piece * slot_weight).astype(jnp.bfloat16)


def run_experts(slots, pieces, gains, own, other):
    count, capacity, cols = pieces.shape
    return call(
        expert_kernel,
        jax.ShapeDtypeStruct(pieces.shape, jnp.bfloat16),
        [VMEM_SPEC] * 9,
        [pltpu.VMEM((capacity, count * cols), jnp.bfloat16)],
        12 * capacity * own[0].size, own[0].size * 12, 20,
    )(slots, pieces, gains, *own, *other)


def combine_kernel(sharers, taken_ref, pieces, out_ref):
    count, capacity, cols = pieces.shape
    spread = [taken_ref[k // sharers] for k in range(count)]
    rows = [pieces[k].astype(jnp.float32) for k in range(count)]
    out_ref[...] = lax.dot_general(
        jnp.concatenate(spread, axis=0).astype(jnp.bfloat16),
        jnp.concatenate(rows, axis=0).astype(jnp.bfloat16),
        (((0,), (0,)), ((), ())),
        preferred_element_type=jnp.float32,
    )


def combine(sharers, taken, pieces):
    count, capacity, cols = pieces.shape
    rows = taken.shape[2]
    return call(
        functools.partial(combine_kernel, sharers),
        jax.ShapeDtypeStruct((rows, cols), jnp.float32),
        [VMEM_SPEC] * 2,
        [],
        2 * rows * capacity * count * cols, (count * capacity * 2 + rows * 4) * cols, 4,
    )(taken, pieces)


def finish_kernel(stream_ref, mine_ref, other_ref, stream_out_ref, out_ref):
    stream_out_ref[...] = stream_ref[...]
    out_ref[...] = (mine_ref[...] + other_ref[...]).astype(jnp.bfloat16)


def finish(stream, mine, other):
    return call(
        finish_kernel,
        [jax.ShapeDtypeStruct(stream.shape, jnp.bfloat16)] * 2,
        [VMEM_SPEC] * 3,
        [],
        mine.size, mine.size * 14, 4,
    )(stream, mine, other)


def exchange(blocks):
    return lax.all_to_all(blocks, "attn", split_axis=0, concat_axis=0, tiled=True)


def swap(block):
    return lax.ppermute(block, "expert", [(0, 1), (1, 0)])


def shards(
    queries,
    key_cache,
    value_cache,
    new_key,
    new_value,
    cache_length,
    residual,
    out_weight,
    ln_gain,
    gate_weight,
    up_weight,
    down_weight,
    routes,
    route_weight,
):
    count = lax.axis_size("attn")
    sharers = count // HELD
    capacity = routes.shape[0] * TOP // EXPERTS

    earlier = order(routes.shape[0])
    weights = (gate_weight.T, up_weight.T, down_weight)
    spread, own, limit, taken, slots = prepare(
        sharers, capacity, cache_length, earlier, routes.T, route_weight.T, queries, new_key
    )
    other_weights = [swap(block) for block in lax.optimization_barrier(weights)]
    attended = exchange(
        attend(count, spread, own, limit, key_cache, value_cache, new_value, ln_gain)
    )
    mine, gains = project(attended, out_weight)
    stream, chosen = pick(sharers, count, mine, swap(mine), residual, taken)
    outgoing = run_experts(slots, exchange(chosen), gains, weights, other_weights)
    combined = combine(sharers, taken, exchange(outgoing))
    attn_stream, expert_out = finish(stream, combined, swap(combined))
    return (attn_stream, expert_out)


def solution(mesh):
    count = mesh.shape["attn"]
    fits = D // count % 256 == 0 and count % HELD == 0 and mesh.shape["expert"] == 2
    return jax.shard_map(
        shards if fits else shards_plain,
        mesh=mesh,
        in_specs=(
            P(("group", "attn"), "expert"),
            P(("group", "attn"), None, "expert"),
            P(("group", "attn"), None, "expert"),
            P(("group", "attn"), "expert"),
            P(("group", "attn"), "expert"),
            P(("group", "attn")),
            P("group", "attn"),
            P("expert", "attn"),
            P("attn"),
            P(None, ("attn", "expert")),
            P(None, ("attn", "expert")),
            P(("attn", "expert"), None),
            P("group", None),
            P("group", None),
        ),
        out_specs=(P("group", "attn"), P("group", "attn")),
        check_vma=False,
    )
```

```python
import functools
import math

import jax
import jax.numpy as jnp
from jax import lax
from jax.experimental import pallas as pl
from jax.experimental.pallas import tpu as pltpu
from jax.sharding import PartitionSpec as P

D = 6144
HEADS = 48
KV_HEADS = 8
HEAD_DIM = 128
EXPERTS = 16
TOP = 4
HELD = 2


NEG_FILL = -1e30
EPSILON = 1e-05


def attend_local(queries, key_cache, value_cache, new_key, new_value, cache_length):
    row_count = queries.shape[0]
    kv_local = new_key.shape[1] // HEAD_DIM
    group = HEADS // KV_HEADS
    length_max = key_cache.shape[1]
    query_heads = queries.reshape(row_count, kv_local, group, HEAD_DIM)
    key_heads = key_cache.reshape(row_count, length_max, kv_local, HEAD_DIM)
    value_heads = value_cache.reshape(row_count, length_max, kv_local, HEAD_DIM)
    own_keys = new_key.reshape(row_count, kv_local, HEAD_DIM)
    own_values = new_value.reshape(row_count, kv_local, HEAD_DIM)
    scale = 1.0 / math.sqrt(HEAD_DIM)
    past = (
        jnp.einsum("rkgd,rlkd->rkgl", query_heads, key_heads, preferred_element_type=jnp.float32)
        * scale
    )
    valid = jnp.arange(length_max, dtype=jnp.int32)[None, :] < cache_length[:, None]
    past = jnp.where(valid[:, None, None, :], past, NEG_FILL)
    own = (
        jnp.einsum("rkgd,rkd->rkg", query_heads, own_keys, preferred_element_type=jnp.float32)
        * scale
    )
    largest = jnp.maximum(jnp.max(past, axis=3), own)
    past_weight = jnp.exp(past - largest[..., None])
    own_weight = jnp.exp(own - largest)
    total = jnp.sum(past_weight, axis=3) + own_weight
    past_prob = (past_weight / total[..., None]).astype(jnp.bfloat16)
    own_prob = (own_weight / total).astype(jnp.bfloat16)
    result = jnp.einsum(
        "rkgl,rlkd->rkgd", past_prob, value_heads, preferred_element_type=jnp.float32
    )
    result = (
        result
        + own_prob.astype(jnp.float32)[..., None] * own_values.astype(jnp.float32)[:, :, None, :]
    )
    return result.reshape(row_count, kv_local * group * HEAD_DIM).astype(jnp.bfloat16)


def selection(routes, route_weight, capacity):
    row_count = routes.shape[0]
    experts = jnp.arange(HELD, dtype=jnp.int32)
    match = routes[None, :, :] == experts[:, None, None]
    hit = jnp.any(match, axis=2)
    row_weight = jnp.sum(jnp.where(match, route_weight[None], 0.0), axis=2)
    earlier = jnp.arange(row_count)[:, None] < jnp.arange(row_count)[None, :]
    slot = jnp.sum(jnp.where(earlier[None] & hit[:, :, None], 1, 0), axis=1)
    taken = hit[:, None, :] & (slot[:, None, :] == jnp.arange(capacity, dtype=jnp.int32)[None, :, None])
    slot_weight = jnp.sum(jnp.where(taken, row_weight[:, None, :], 0.0), axis=2)
    return taken, slot_weight


def gather_attn(block):
    count = lax.axis_size("attn")
    copies = jnp.broadcast_to(block[None], (count,) + block.shape)
    return lax.all_to_all(copies, "attn", split_axis=0, concat_axis=0, tiled=True)


def pair_sum(block):
    return block + lax.ppermute(block, "expert", [(0, 1), (1, 0)])


def shards_plain(
    queries,
    key_cache,
    value_cache,
    new_key,
    new_value,
    cache_length,
    residual,
    out_weight,
    ln_gain,
    gate_weight,
    up_weight,
    down_weight,
    routes,
    route_weight,
):
    attn_count = lax.axis_size("attn")
    core_count = lax.axis_size("expert")
    sharers = attn_count * core_count // HELD
    my_expert = (lax.axis_index("attn") * core_count + lax.axis_index("expert")) // sharers
    dest_expert = [index * core_count // sharers for index in range(attn_count)]
    row_count = routes.shape[0]
    capacity = row_count * TOP // EXPERTS * 2
    cols = residual.shape[1]

    taken, slot_weight = selection(routes, route_weight, capacity)
    pick = taken.astype(jnp.bfloat16)

    gains = gather_attn(ln_gain)

    attended = attend_local(queries, key_cache, value_cache, new_key, new_value, cache_length)
    whole = gather_attn(attended).reshape(row_count, -1)
    partial_proj = jnp.dot(whole, out_weight, preferred_element_type=jnp.float32)
    head_total = pair_sum(partial_proj)
    attn_stream = (residual.astype(jnp.float32) + head_total).astype(jnp.bfloat16)

    chosen = jnp.einsum(
        "esr,rd->esd", pick, attn_stream, preferred_element_type=jnp.float32
    ).astype(jnp.bfloat16)
    outgoing = jnp.stack([chosen[index] for index in dest_expert])
    rows = lax.all_to_all(outgoing, "attn", split_axis=0, concat_axis=0, tiled=True)
    wide = rows.astype(jnp.float32)
    row_mean = jnp.sum(wide, axis=(0, 2)) / D
    row_var = jnp.sum(wide * wide, axis=(0, 2)) / D - row_mean * row_mean
    normed = (
        (wide - row_mean[None, :, None])
        * lax.rsqrt(row_var + EPSILON)[None, :, None]
        * gains.reshape(attn_count, 1, cols)
    ).astype(jnp.bfloat16)
    gate_val = jnp.einsum(
        "asd,adf->sf", normed, gate_weight.reshape(attn_count, cols, -1),
        preferred_element_type=jnp.float32,
    )
    up_val = jnp.einsum(
        "asd,adf->sf", normed, up_weight.reshape(attn_count, cols, -1),
        preferred_element_type=jnp.float32,
    )
    hidden = (jax.nn.silu(gate_val) * up_val).astype(jnp.bfloat16)
    piece = jnp.dot(hidden, down_weight, preferred_element_type=jnp.float32)
    mine = jnp.take(slot_weight, my_expert, axis=0)
    piece = (piece * mine[:, None]).astype(jnp.bfloat16)
    returned = lax.all_to_all(
        piece.reshape(capacity, attn_count, cols).swapaxes(0, 1),
        "attn", split_axis=0, concat_axis=0, tiled=True,
    )
    spread = jnp.stack([pick[index] for index in dest_expert])
    combined = jnp.einsum(
        "asr,asd->rd", spread, returned, preferred_element_type=jnp.float32
    )
    expert_out = pair_sum(combined).astype(jnp.bfloat16)
    return (attn_stream, expert_out)


MIB = 1024 * 1024
EXCHANGE_FLOPS = 10**10
VMEM_SPEC = pl.BlockSpec(memory_space=pltpu.VMEM)
SMEM_SPEC = pl.BlockSpec(memory_space=pltpu.SMEM)
HBM_SPEC = pl.BlockSpec(memory_space=pltpu.HBM)


def call(kernel, outs, in_specs, scratch, flops, nbytes, vmem_mib):
    single = not isinstance(outs, (list, tuple))
    return pl.pallas_call(
        kernel,
        out_shape=outs,
        in_specs=in_specs,
        out_specs=VMEM_SPEC if single else [VMEM_SPEC] * len(outs),
        scratch_shapes=scratch,
        cost_estimate=pl.CostEstimate(flops=flops, bytes_accessed=nbytes, transcendentals=0),
        compiler_params=pltpu.CompilerParams(vmem_limit_bytes=vmem_mib * MIB),
    )


def order_kernel(out_ref):
    rows = out_ref.shape[0]
    before = lax.broadcasted_iota(jnp.int32, (rows, rows), 0) < lax.broadcasted_iota(
        jnp.int32, (rows, rows), 1
    )
    out_ref[...] = jnp.where(before, 1.0, 0.0).astype(jnp.bfloat16)


def order(rows):
    return call(
        order_kernel,
        jax.ShapeDtypeStruct((rows, rows), jnp.bfloat16),
        [],
        [],
        EXCHANGE_FLOPS, rows * rows * 2, 2,
    )()


def expert_rows(routes, earlier, expert, capacity):
    row_count = routes.shape[1]
    hit = jnp.max((routes == expert).astype(jnp.float32), axis=0, keepdims=True)
    slot = jnp.dot(
        jnp.broadcast_to(hit, (8, row_count)).astype(jnp.bfloat16),
        earlier,
        preferred_element_type=jnp.float32,
    )[:1]
    place = lax.broadcasted_iota(jnp.int32, (capacity, row_count), 0).astype(jnp.float32)
    return jnp.where((slot == place) & (hit > 0.5), 1.0, 0.0)


def prepare_kernel(sharers, length_ref, earlier_ref, routes_ref, weight_ref, query_ref,
                   own_key_ref, spread_ref, own_ref, limit_ref, taken_ref, slot_ref, query_rows,
                   key_rows):
    row_count = query_ref.shape[0]
    kv_local = own_key_ref.shape[1] // HEAD_DIM
    group = HEADS // KV_HEADS
    heads = kv_local * group
    for g in range(kv_local):
        own_key = own_key_ref[:, g * HEAD_DIM : (g + 1) * HEAD_DIM].astype(jnp.float32)
        for i in range(group):
            index = g * group + i
            rows = pl.ds(index * row_count, row_count)
            query_rows[rows, :] = query_ref[
                :, index * HEAD_DIM : (index + 1) * HEAD_DIM
            ].astype(jnp.float32)
            key_rows[rows, :] = own_key
    scale = 1.0 / math.sqrt(HEAD_DIM)
    lengths = length_ref[...].reshape(1, -1)
    head = lax.broadcasted_iota(jnp.int32, (heads, 1), 0) // group
    for r in range(row_count):
        strided = pl.ds(r, heads, stride=row_count)
        query = query_rows[strided, :]
        own = jnp.sum(query * key_rows[strided, :], axis=1, keepdims=True) * scale
        own_ref[r] = jnp.broadcast_to(own, (heads, HEAD_DIM))
        limit_ref[r] = jnp.broadcast_to(lengths[:, r : r + 1], (heads, HEAD_DIM))
        spread_ref[r] = jnp.concatenate(
            [jnp.where(head == g, query, 0.0) for g in range(kv_local)], axis=1
        ).astype(jnp.bfloat16)
    routes = routes_ref[...]
    capacity = slot_ref.shape[0]
    core = lax.axis_index("expert")
    taken = []
    for e in range(HELD):
        both = expert_rows(routes, earlier_ref[...], e, 2 * capacity)
        taken.append(jnp.where(core == 0, both[:capacity], both[capacity:]))
        taken_ref[e] = taken[e]
    first = lax.axis_index("attn") < sharers
    expert = jnp.where(first, 0, 1)
    row_weight = jnp.sum(
        jnp.where(routes == expert, weight_ref[...], 0.0), axis=0, keepdims=True
    )
    mine = jnp.where(first, taken[0], taken[1])
    slot_ref[...] = jnp.broadcast_to(
        jnp.sum(mine * row_weight, axis=1, keepdims=True), slot_ref.shape
    )


def prepare(
    sharers, capacity, cache_length, earlier, routes, route_weight, queries, new_key
):
    row_count, width = queries.shape
    heads = width // HEAD_DIM
    table = pltpu.VMEM((heads * row_count, HEAD_DIM), jnp.float32)
    return call(
        functools.partial(prepare_kernel, sharers),
        [
            jax.ShapeDtypeStruct((row_count, heads, new_key.shape[1]), jnp.bfloat16),
            jax.ShapeDtypeStruct((row_count, heads, HEAD_DIM), jnp.float32),
            jax.ShapeDtypeStruct((row_count, heads, HEAD_DIM), jnp.int32),
            jax.ShapeDtypeStruct((HELD, capacity, routes.shape[1]), jnp.float32),
            jax.ShapeDtypeStruct((capacity, HEAD_DIM), jnp.float32),
        ],
        [VMEM_SPEC] * 6,
        [table, table],
        queries.size * 8, queries.size * 16, 4,
    )(cache_length, earlier, routes, route_weight, queries, new_key)


def score_kernel(spread_ref, own_ref, limit_ref, key_ref, probs_ref, own_probs_ref):
    row_count, heads, length_max = probs_ref.shape
    scale = 1.0 / math.sqrt(HEAD_DIM)
    contract = (((1,), (1,)), ((), ()))
    products = [
        lax.dot_general(spread_ref[r], key_ref[r], contract, preferred_element_type=jnp.float32)
        for r in range(row_count)
    ]
    for first in range(0, row_count, 2):
        batch = range(first, min(first + 2, row_count))
        scores = jnp.concatenate([products[r] for r in batch], axis=0)
        position = lax.broadcasted_iota(jnp.int32, scores.shape, 1)
        limit = jnp.concatenate([limit_ref[r, :, :1] for r in batch], axis=0)
        own = jnp.concatenate([own_ref[r, :, :1] for r in batch], axis=0)
        past = jnp.where(position < limit, scores * scale, NEG_FILL)
        largest = jnp.maximum(jnp.max(past, axis=1, keepdims=True), own)
        weight = jnp.exp(past - largest)
        own_weight = jnp.exp(own - largest)
        inverse = 1.0 / (jnp.sum(weight, axis=1, keepdims=True) + own_weight)
        probs = weight * inverse
        own_prob = (own_weight * inverse).astype(jnp.bfloat16).astype(jnp.float32)
        for index, r in enumerate(batch):
            rows = slice(index * heads, (index + 1) * heads)
            probs_ref[r] = probs[rows].astype(jnp.bfloat16)
            own_probs_ref[r] = jnp.broadcast_to(own_prob[rows], own_probs_ref.shape[1:])


def value_kernel(probs_ref, own_ref, value_ref, own_value_ref, gain_ref, out_ref, value_rows,
                 result_rows):
    row_count, length_max, width = value_ref.shape
    kv_local = width // HEAD_DIM
    group = HEADS // KV_HEADS
    heads = kv_local * group
    for g in range(kv_local):
        own_value = own_value_ref[:, g * HEAD_DIM : (g + 1) * HEAD_DIM].astype(jnp.float32)
        for i in range(group):
            value_rows[pl.ds((g * group + i) * row_count, row_count), :] = own_value
    head = lax.broadcasted_iota(jnp.int32, (heads, 1), 0) // group
    for r in range(row_count):
        strided = pl.ds(r, heads, stride=row_count)
        product = jnp.dot(probs_ref[r], value_ref[r], preferred_element_type=jnp.float32)
        total = own_ref[r] * value_rows[strided, :]
        for g in range(kv_local):
            lanes = slice(g * HEAD_DIM, (g + 1) * HEAD_DIM)
            total = total + jnp.where(head == g, product[:, lanes], 0.0)
        result_rows[strided, :] = total
    for index in range(heads):
        rows = result_rows[pl.ds(index * row_count, row_count), :].astype(jnp.bfloat16)
        for copy in range(out_ref.shape[0]):
            out_ref[copy, :, index * HEAD_DIM : (index + 1) * HEAD_DIM] = rows
    gain_row = gain_ref[...].reshape(1, -1)
    half = gain_row.shape[1] // 2
    row = lax.broadcasted_iota(jnp.int32, (row_count, half), 0)
    left = jnp.broadcast_to(gain_row[:, :half], (row_count, half))
    right = jnp.broadcast_to(gain_row[:, half:], (row_count, half))
    gain = jnp.where(row % 2 == 0, left, right)
    upper = gain.astype(jnp.bfloat16).astype(jnp.float32)
    parts = jnp.where(row < 2, upper, gain - upper).astype(jnp.bfloat16)
    for copy in range(out_ref.shape[0]):
        out_ref[copy, :, heads * HEAD_DIM :] = parts


def attend(count, spread, own, limit, key_cache, value_cache, new_value, gain):
    row_count, heads, _ = spread.shape
    length_max = key_cache.shape[1]
    table = pltpu.VMEM((heads * row_count, HEAD_DIM), jnp.float32)
    probs, own_probs = call(
        score_kernel,
        [
            jax.ShapeDtypeStruct((row_count, heads, length_max), jnp.bfloat16),
            jax.ShapeDtypeStruct((row_count, heads, HEAD_DIM), jnp.float32),
        ],
        [VMEM_SPEC] * 4,
        [],
        2 * key_cache.size * heads, key_cache.size * 2, 8,
    )(spread, own, limit, key_cache)
    width = heads * HEAD_DIM + gain.shape[0] // 2
    return call(
        value_kernel,
        jax.ShapeDtypeStruct((count, row_count, width), jnp.bfloat16),
        [VMEM_SPEC] * 5,
        [table, table],
        EXCHANGE_FLOPS, value_cache.size * 2, 8,
    )(probs, own_probs, value_cache, new_value, gain)


def project_kernel(pieces, weight_ref, out_ref, gain_ref, stack):
    count, rows, _ = pieces.shape
    width = weight_ref.shape[0]
    half = gain_ref.shape[1] // 2
    for k in range(count):
        parts = pieces[k, :, width:].astype(jnp.float32)
        gain_ref[pl.ds(k, 1), :half] = parts[0:1] + parts[2:3]
        gain_ref[pl.ds(k, 1), half:] = parts[1:2] + parts[3:4]
    total = 0.0
    step = width // 4
    for start in range(0, width, step):
        part = slice(start, start + step)
        for k in range(count):
            stack[pl.ds(k * rows, rows), part] = pieces[k, :, part].astype(jnp.float32)
        total = total + jnp.dot(
            stack[:, part].astype(jnp.bfloat16),
            weight_ref[part, :],
            preferred_element_type=jnp.float32,
        )
    out_ref[...] = total.astype(jnp.bfloat16)


def project(pieces, out_weight):
    count, rows, _ = pieces.shape
    depth, cols = out_weight.shape
    return call(
        project_kernel,
        [
            jax.ShapeDtypeStruct((rows * count, cols), jnp.bfloat16),
            jax.ShapeDtypeStruct((count, cols), jnp.float32),
        ],
        [VMEM_SPEC, VMEM_SPEC],
        [pltpu.VMEM((rows * count, depth), jnp.float32)],
        2 * rows * count * out_weight.size, out_weight.size * 2, 10,
    )(pieces, out_weight)


def pick_kernel(sharers, mine_ref, other_ref, residual_ref, taken_ref, stream_ref, out_ref):
    stream = (
        residual_ref[...].astype(jnp.float32)
        + (mine_ref[...].astype(jnp.float32) + other_ref[...].astype(jnp.float32))
    ).astype(jnp.bfloat16)
    stream_ref[...] = stream
    chosen = [
        jnp.dot(
            taken_ref[e].astype(jnp.bfloat16), stream, preferred_element_type=jnp.float32
        ).astype(jnp.bfloat16)
        for e in range(HELD)
    ]
    for k in range(out_ref.shape[0]):
        out_ref[k] = chosen[k // sharers]


def pick(sharers, count, mine, other, residual, taken):
    rows, cols = mine.shape
    return call(
        functools.partial(pick_kernel, sharers),
        [
            jax.ShapeDtypeStruct((rows, cols), jnp.bfloat16),
            jax.ShapeDtypeStruct((count, taken.shape[1], cols), jnp.bfloat16),
        ],
        [VMEM_SPEC] * 4,
        [],
        2 * HELD * taken.shape[1] * rows * cols, rows * cols * 12, 4,
    )(mine, other, residual, taken)


def expert_kernel(slot_ref, pieces, gains, *refs):
    weights, out_ref, rows_ref = (refs[:3], refs[3:6]), refs[6], refs[7]
    count, capacity, cols = pieces.shape
    first = second = 0.0
    for k in range(count):
        wide = pieces[k].astype(jnp.float32)
        first = first + wide
        second = second + wide * wide
    row_mean = jnp.sum(first, axis=1, keepdims=True) / D
    row_var = jnp.sum(second, axis=1, keepdims=True) / D - row_mean * row_mean
    inverse = lax.rsqrt(row_var + EPSILON)
    for k in range(count):
        wide = pieces[k].astype(jnp.float32)
        normed = (wide - row_mean) * inverse * gains[pl.ds(k, 1), :]
        rows_ref[:, k * cols : (k + 1) * cols] = normed.astype(jnp.bfloat16)
    rows = rows_ref[...]
    contract = (((1,), (1,)), ((), ()))
    hidden = []
    for gate_ref, up_ref, _ in weights:
        gate = lax.dot_general(rows, gate_ref[...], contract, preferred_element_type=jnp.float32)
        up = lax.dot_general(rows, up_ref[...], contract, preferred_element_type=jnp.float32)
        hidden.append((gate / (1.0 + jnp.exp(-gate)) * up).astype(jnp.bfloat16))
    slot_weight = slot_ref[:, :1]
    for k in range(count):
        block = slice(k * cols, (k + 1) * cols)
        piece = sum(
            jnp.dot(part, refs_of[2][:, block], preferred_element_type=jnp.float32)
            for part, refs_of in zip(hidden, weights)
        )
        out_ref[k] = (piece * slot_weight).astype(jnp.bfloat16)


def run_experts(slots, pieces, gains, own, other):
    count, capacity, cols = pieces.shape
    return call(
        expert_kernel,
        jax.ShapeDtypeStruct(pieces.shape, jnp.bfloat16),
        [VMEM_SPEC] * 9,
        [pltpu.VMEM((capacity, count * cols), jnp.bfloat16)],
        12 * capacity * own[0].size, own[0].size * 12, 20,
    )(slots, pieces, gains, *own, *other)


def combine_kernel(sharers, taken_ref, pieces, out_ref):
    count, capacity, cols = pieces.shape
    spread = [taken_ref[k // sharers] for k in range(count)]
    rows = [pieces[k].astype(jnp.float32) for k in range(count)]
    out_ref[...] = lax.dot_general(
        jnp.concatenate(spread, axis=0).astype(jnp.bfloat16),
        jnp.concatenate(rows, axis=0).astype(jnp.bfloat16),
        (((0,), (0,)), ((), ())),
        preferred_element_type=jnp.float32,
    ).astype(jnp.bfloat16)


def combine(sharers, taken, pieces):
    count, capacity, cols = pieces.shape
    rows = taken.shape[2]
    return call(
        functools.partial(combine_kernel, sharers),
        jax.ShapeDtypeStruct((rows, cols), jnp.bfloat16),
        [VMEM_SPEC] * 2,
        [],
        2 * rows * capacity * count * cols, (count * capacity * 2 + rows * 4) * cols, 4,
    )(taken, pieces)


def finish_kernel(stream_ref, mine_ref, other_ref, stream_out_ref, out_ref):
    stream_out_ref[...] = stream_ref[...]
    out_ref[...] = (
        mine_ref[...].astype(jnp.float32) + other_ref[...].astype(jnp.float32)
    ).astype(jnp.bfloat16)


def finish(stream, mine, other):
    return call(
        finish_kernel,
        [jax.ShapeDtypeStruct(stream.shape, jnp.bfloat16)] * 2,
        [VMEM_SPEC] * 3,
        [],
        mine.size, mine.size * 14, 4,
    )(stream, mine, other)


def exchange(blocks):
    return lax.all_to_all(blocks, "attn", split_axis=0, concat_axis=0, tiled=True)


def swap(block):
    return lax.ppermute(block, "expert", [(0, 1), (1, 0)])


def shards(
    queries,
    key_cache,
    value_cache,
    new_key,
    new_value,
    cache_length,
    residual,
    out_weight,
    ln_gain,
    gate_weight,
    up_weight,
    down_weight,
    routes,
    route_weight,
):
    count = lax.axis_size("attn")
    sharers = count // HELD
    capacity = routes.shape[0] * TOP // EXPERTS

    earlier = order(routes.shape[0])
    weights = (gate_weight.T, up_weight.T, down_weight)
    spread, own, limit, taken, slots = prepare(
        sharers, capacity, cache_length, earlier, routes.T, route_weight.T, queries, new_key
    )
    other_weights = [swap(block) for block in lax.optimization_barrier(weights)]
    attended = exchange(
        attend(count, spread, own, limit, key_cache, value_cache, new_value, ln_gain)
    )
    mine, gains = project(attended, out_weight)
    stream, chosen = pick(sharers, count, mine, swap(mine), residual, taken)
    outgoing = run_experts(slots, exchange(chosen), gains, weights, other_weights)
    combined = combine(sharers, taken, exchange(outgoing))
    attn_stream, expert_out = finish(stream, combined, swap(combined))
    return (attn_stream, expert_out)


def solution(mesh):
    count = mesh.shape["attn"]
    fits = D // count % 256 == 0 and count % HELD == 0 and mesh.shape["expert"] == 2
    return jax.shard_map(
        shards if fits else shards_plain,
        mesh=mesh,
        in_specs=(
            P(("group", "attn"), "expert"),
            P(("group", "attn"), None, "expert"),
            P(("group", "attn"), None, "expert"),
            P(("group", "attn"), "expert"),
            P(("group", "attn"), "expert"),
            P(("group", "attn")),
            P("group", "attn"),
            P("expert", "attn"),
            P("attn"),
            P(None, ("attn", "expert")),
            P(None, ("attn", "expert")),
            P(("attn", "expert"), None),
            P("group", None),
            P("group", None),
        ),
        out_specs=(P("group", "attn"), P("group", "attn")),
        check_vma=False,
    )
```

```python
import functools
import math

import jax
import jax.numpy as jnp
from jax import lax
from jax.experimental import pallas as pl
from jax.experimental.pallas import tpu as pltpu
from jax.sharding import PartitionSpec as P

D = 6144
HEADS = 48
KV_HEADS = 8
HEAD_DIM = 128
EXPERTS = 16
TOP = 4
HELD = 2


NEG_FILL = -1e30
EPSILON = 1e-05


def attend_local(queries, key_cache, value_cache, new_key, new_value, cache_length):
    row_count = queries.shape[0]
    kv_local = new_key.shape[1] // HEAD_DIM
    group = HEADS // KV_HEADS
    length_max = key_cache.shape[1]
    query_heads = queries.reshape(row_count, kv_local, group, HEAD_DIM)
    key_heads = key_cache.reshape(row_count, length_max, kv_local, HEAD_DIM)
    value_heads = value_cache.reshape(row_count, length_max, kv_local, HEAD_DIM)
    own_keys = new_key.reshape(row_count, kv_local, HEAD_DIM)
    own_values = new_value.reshape(row_count, kv_local, HEAD_DIM)
    scale = 1.0 / math.sqrt(HEAD_DIM)
    past = (
        jnp.einsum("rkgd,rlkd->rkgl", query_heads, key_heads, preferred_element_type=jnp.float32)
        * scale
    )
    valid = jnp.arange(length_max, dtype=jnp.int32)[None, :] < cache_length[:, None]
    past = jnp.where(valid[:, None, None, :], past, NEG_FILL)
    own = (
        jnp.einsum("rkgd,rkd->rkg", query_heads, own_keys, preferred_element_type=jnp.float32)
        * scale
    )
    largest = jnp.maximum(jnp.max(past, axis=3), own)
    past_weight = jnp.exp(past - largest[..., None])
    own_weight = jnp.exp(own - largest)
    total = jnp.sum(past_weight, axis=3) + own_weight
    past_prob = (past_weight / total[..., None]).astype(jnp.bfloat16)
    own_prob = (own_weight / total).astype(jnp.bfloat16)
    result = jnp.einsum(
        "rkgl,rlkd->rkgd", past_prob, value_heads, preferred_element_type=jnp.float32
    )
    result = (
        result
        + own_prob.astype(jnp.float32)[..., None] * own_values.astype(jnp.float32)[:, :, None, :]
    )
    return result.reshape(row_count, kv_local * group * HEAD_DIM).astype(jnp.bfloat16)


def selection(routes, route_weight, capacity):
    row_count = routes.shape[0]
    experts = jnp.arange(HELD, dtype=jnp.int32)
    match = routes[None, :, :] == experts[:, None, None]
    hit = jnp.any(match, axis=2)
    row_weight = jnp.sum(jnp.where(match, route_weight[None], 0.0), axis=2)
    earlier = jnp.arange(row_count)[:, None] < jnp.arange(row_count)[None, :]
    slot = jnp.sum(jnp.where(earlier[None] & hit[:, :, None], 1, 0), axis=1)
    taken = hit[:, None, :] & (slot[:, None, :] == jnp.arange(capacity, dtype=jnp.int32)[None, :, None])
    slot_weight = jnp.sum(jnp.where(taken, row_weight[:, None, :], 0.0), axis=2)
    return taken, slot_weight


def gather_attn(block):
    count = lax.axis_size("attn")
    copies = jnp.broadcast_to(block[None], (count,) + block.shape)
    return lax.all_to_all(copies, "attn", split_axis=0, concat_axis=0, tiled=True)


def pair_sum(block):
    return block + lax.ppermute(block, "expert", [(0, 1), (1, 0)])


def shards_plain(
    queries,
    key_cache,
    value_cache,
    new_key,
    new_value,
    cache_length,
    residual,
    out_weight,
    ln_gain,
    gate_weight,
    up_weight,
    down_weight,
    routes,
    route_weight,
):
    attn_count = lax.axis_size("attn")
    core_count = lax.axis_size("expert")
    sharers = attn_count * core_count // HELD
    my_expert = (lax.axis_index("attn") * core_count + lax.axis_index("expert")) // sharers
    dest_expert = [index * core_count // sharers for index in range(attn_count)]
    row_count = routes.shape[0]
    capacity = row_count * TOP // EXPERTS * 2
    cols = residual.shape[1]

    taken, slot_weight = selection(routes, route_weight, capacity)
    pick = taken.astype(jnp.bfloat16)

    gains = gather_attn(ln_gain)

    attended = attend_local(queries, key_cache, value_cache, new_key, new_value, cache_length)
    whole = gather_attn(attended).reshape(row_count, -1)
    partial_proj = jnp.dot(whole, out_weight, preferred_element_type=jnp.float32)
    head_total = pair_sum(partial_proj)
    attn_stream = (residual.astype(jnp.float32) + head_total).astype(jnp.bfloat16)

    chosen = jnp.einsum(
        "esr,rd->esd", pick, attn_stream, preferred_element_type=jnp.float32
    ).astype(jnp.bfloat16)
    outgoing = jnp.stack([chosen[index] for index in dest_expert])
    rows = lax.all_to_all(outgoing, "attn", split_axis=0, concat_axis=0, tiled=True)
    wide = rows.astype(jnp.float32)
    row_mean = jnp.sum(wide, axis=(0, 2)) / D
    row_var = jnp.sum(wide * wide, axis=(0, 2)) / D - row_mean * row_mean
    normed = (
        (wide - row_mean[None, :, None])
        * lax.rsqrt(row_var + EPSILON)[None, :, None]
        * gains.reshape(attn_count, 1, cols)
    ).astype(jnp.bfloat16)
    gate_val = jnp.einsum(
        "asd,adf->sf", normed, gate_weight.reshape(attn_count, cols, -1),
        preferred_element_type=jnp.float32,
    )
    up_val = jnp.einsum(
        "asd,adf->sf", normed, up_weight.reshape(attn_count, cols, -1),
        preferred_element_type=jnp.float32,
    )
    hidden = (jax.nn.silu(gate_val) * up_val).astype(jnp.bfloat16)
    piece = jnp.dot(hidden, down_weight, preferred_element_type=jnp.float32)
    mine = jnp.take(slot_weight, my_expert, axis=0)
    piece = (piece * mine[:, None]).astype(jnp.bfloat16)
    returned = lax.all_to_all(
        piece.reshape(capacity, attn_count, cols).swapaxes(0, 1),
        "attn", split_axis=0, concat_axis=0, tiled=True,
    )
    spread = jnp.stack([pick[index] for index in dest_expert])
    combined = jnp.einsum(
        "asr,asd->rd", spread, returned, preferred_element_type=jnp.float32
    )
    expert_out = pair_sum(combined).astype(jnp.bfloat16)
    return (attn_stream, expert_out)


MIB = 1024 * 1024
EXCHANGE_FLOPS = 10**10
VMEM_SPEC = pl.BlockSpec(memory_space=pltpu.VMEM)
SMEM_SPEC = pl.BlockSpec(memory_space=pltpu.SMEM)
HBM_SPEC = pl.BlockSpec(memory_space=pltpu.HBM)


def call(kernel, outs, in_specs, scratch, flops, nbytes, vmem_mib):
    single = not isinstance(outs, (list, tuple))
    return pl.pallas_call(
        kernel,
        out_shape=outs,
        in_specs=in_specs,
        out_specs=VMEM_SPEC if single else [VMEM_SPEC] * len(outs),
        scratch_shapes=scratch,
        cost_estimate=pl.CostEstimate(flops=flops, bytes_accessed=nbytes, transcendentals=0),
        compiler_params=pltpu.CompilerParams(vmem_limit_bytes=vmem_mib * MIB),
    )


def order_kernel(out_ref):
    rows = out_ref.shape[0]
    before = lax.broadcasted_iota(jnp.int32, (rows, rows), 0) < lax.broadcasted_iota(
        jnp.int32, (rows, rows), 1
    )
    out_ref[...] = jnp.where(before, 1.0, 0.0).astype(jnp.bfloat16)


def order(rows):
    return call(
        order_kernel,
        jax.ShapeDtypeStruct((rows, rows), jnp.bfloat16),
        [],
        [],
        EXCHANGE_FLOPS, rows * rows * 2, 2,
    )()


def expert_rows(routes, earlier, expert, capacity):
    row_count = routes.shape[1]
    hit = jnp.max((routes == expert).astype(jnp.float32), axis=0, keepdims=True)
    slot = jnp.dot(
        jnp.broadcast_to(hit, (8, row_count)).astype(jnp.bfloat16),
        earlier,
        preferred_element_type=jnp.float32,
    )[:1]
    place = lax.broadcasted_iota(jnp.int32, (capacity, row_count), 0).astype(jnp.float32)
    return jnp.where((slot == place) & (hit > 0.5), 1.0, 0.0)


def prepare_kernel(sharers, length_ref, earlier_ref, routes_ref, weight_ref, query_ref,
                   own_key_ref, own_value_ref, gain_ref, spread_ref, own_ref, limit_ref, taken_ref,
                   slot_ref, value_rows, part_ref, query_rows, key_rows):
    row_count = query_ref.shape[0]
    kv_local = own_key_ref.shape[1] // HEAD_DIM
    group = HEADS // KV_HEADS
    heads = kv_local * group
    for g in range(kv_local):
        own_key = own_key_ref[:, g * HEAD_DIM : (g + 1) * HEAD_DIM].astype(jnp.float32)
        for i in range(group):
            index = g * group + i
            rows = pl.ds(index * row_count, row_count)
            query_rows[rows, :] = query_ref[
                :, index * HEAD_DIM : (index + 1) * HEAD_DIM
            ].astype(jnp.float32)
            key_rows[rows, :] = own_key
            value_rows[rows, :] = own_value_ref[
                :, g * HEAD_DIM : (g + 1) * HEAD_DIM
            ].astype(jnp.float32)
    gain_row = gain_ref[...].reshape(1, -1)
    half = gain_row.shape[1] // 2
    row = lax.broadcasted_iota(jnp.int32, (row_count, half), 0)
    left = jnp.broadcast_to(gain_row[:, :half], (row_count, half))
    right = jnp.broadcast_to(gain_row[:, half:], (row_count, half))
    gain = jnp.where(row % 2 == 0, left, right)
    upper = gain.astype(jnp.bfloat16).astype(jnp.float32)
    part_ref[...] = jnp.where(row < 2, upper, gain - upper).astype(jnp.bfloat16)
    scale = 1.0 / math.sqrt(HEAD_DIM)
    lengths = length_ref[...].reshape(1, -1)
    head = lax.broadcasted_iota(jnp.int32, (heads, 1), 0) // group
    for r in range(row_count):
        strided = pl.ds(r, heads, stride=row_count)
        query = query_rows[strided, :]
        own = jnp.sum(query * key_rows[strided, :], axis=1, keepdims=True) * scale
        own_ref[r] = jnp.broadcast_to(own, (heads, HEAD_DIM))
        limit_ref[r] = jnp.broadcast_to(lengths[:, r : r + 1], (heads, HEAD_DIM))
        spread_ref[r] = jnp.concatenate(
            [jnp.where(head == g, query, 0.0) for g in range(kv_local)], axis=1
        ).astype(jnp.bfloat16)
    routes = routes_ref[...]
    capacity = slot_ref.shape[0]
    core = lax.axis_index("expert")
    taken = []
    for e in range(HELD):
        both = expert_rows(routes, earlier_ref[...], e, 2 * capacity)
        taken.append(jnp.where(core == 0, both[:capacity], both[capacity:]))
        taken_ref[e] = taken[e]
    first = lax.axis_index("attn") < sharers
    expert = jnp.where(first, 0, 1)
    row_weight = jnp.sum(
        jnp.where(routes == expert, weight_ref[...], 0.0), axis=0, keepdims=True
    )
    mine = jnp.where(first, taken[0], taken[1])
    slot_ref[...] = jnp.broadcast_to(
        jnp.sum(mine * row_weight, axis=1, keepdims=True), slot_ref.shape
    )


def prepare(
    sharers, capacity, cache_length, earlier, routes, route_weight, queries, new_key, new_value,
    gain,
):
    row_count, width = queries.shape
    heads = width // HEAD_DIM
    table = pltpu.VMEM((heads * row_count, HEAD_DIM), jnp.float32)
    return call(
        functools.partial(prepare_kernel, sharers),
        [
            jax.ShapeDtypeStruct((row_count, heads, new_key.shape[1]), jnp.bfloat16),
            jax.ShapeDtypeStruct((row_count, heads, HEAD_DIM), jnp.float32),
            jax.ShapeDtypeStruct((row_count, heads, HEAD_DIM), jnp.int32),
            jax.ShapeDtypeStruct((HELD, capacity, routes.shape[1]), jnp.float32),
            jax.ShapeDtypeStruct((capacity, HEAD_DIM), jnp.float32),
            jax.ShapeDtypeStruct((heads * row_count, HEAD_DIM), jnp.float32),
            jax.ShapeDtypeStruct((row_count, gain.shape[0] // 2), jnp.bfloat16),
        ],
        [VMEM_SPEC] * 8,
        [table, table],
        queries.size * 8, queries.size * 16, 4,
    )(cache_length, earlier, routes, route_weight, queries, new_key, new_value, gain)


def score_kernel(spread_ref, own_ref, limit_ref, key_ref, probs_ref, own_probs_ref):
    row_count, heads, length_max = probs_ref.shape
    scale = 1.0 / math.sqrt(HEAD_DIM)
    contract = (((1,), (1,)), ((), ()))
    products = [
        lax.dot_general(spread_ref[r], key_ref[r], contract, preferred_element_type=jnp.float32)
        for r in range(row_count)
    ]
    for first in range(0, row_count, 2):
        batch = range(first, min(first + 2, row_count))
        scores = jnp.concatenate([products[r] for r in batch], axis=0)
        position = lax.broadcasted_iota(jnp.int32, scores.shape, 1)
        limit = jnp.concatenate([limit_ref[r, :, :1] for r in batch], axis=0)
        own = jnp.concatenate([own_ref[r, :, :1] for r in batch], axis=0)
        past = jnp.where(position < limit, scores * scale, NEG_FILL)
        largest = jnp.maximum(jnp.max(past, axis=1, keepdims=True), own)
        weight = jnp.exp(past - largest)
        own_weight = jnp.exp(own - largest)
        inverse = 1.0 / (jnp.sum(weight, axis=1, keepdims=True) + own_weight)
        probs = weight * inverse
        own_prob = (own_weight * inverse).astype(jnp.bfloat16).astype(jnp.float32)
        for index, r in enumerate(batch):
            rows = slice(index * heads, (index + 1) * heads)
            probs_ref[r] = probs[rows].astype(jnp.bfloat16)
            own_probs_ref[r] = jnp.broadcast_to(own_prob[rows], own_probs_ref.shape[1:])


def value_kernel(probs_ref, own_ref, value_ref, value_rows, part_ref, out_ref, result_rows):
    row_count, length_max, width = value_ref.shape
    kv_local = width // HEAD_DIM
    group = HEADS // KV_HEADS
    heads = kv_local * group
    head = lax.broadcasted_iota(jnp.int32, (heads, 1), 0) // group
    for r in range(row_count):
        strided = pl.ds(r, heads, stride=row_count)
        product = jnp.dot(probs_ref[r], value_ref[r], preferred_element_type=jnp.float32)
        total = own_ref[r] * value_rows[strided, :]
        for g in range(kv_local):
            lanes = slice(g * HEAD_DIM, (g + 1) * HEAD_DIM)
            total = total + jnp.where(head == g, product[:, lanes], 0.0)
        result_rows[strided, :] = total
    for index in range(heads):
        rows = result_rows[pl.ds(index * row_count, row_count), :].astype(jnp.bfloat16)
        for copy in range(out_ref.shape[0]):
            out_ref[copy, :, index * HEAD_DIM : (index + 1) * HEAD_DIM] = rows
    parts = part_ref[...]
    for copy in range(out_ref.shape[0]):
        out_ref[copy, :, heads * HEAD_DIM :] = parts


def attend(count, spread, own, limit, key_cache, value_cache, value_rows, parts):
    row_count, heads, _ = spread.shape
    length_max = key_cache.shape[1]
    table = pltpu.VMEM((heads * row_count, HEAD_DIM), jnp.float32)
    probs, own_probs = call(
        score_kernel,
        [
            jax.ShapeDtypeStruct((row_count, heads, length_max), jnp.bfloat16),
            jax.ShapeDtypeStruct((row_count, heads, HEAD_DIM), jnp.float32),
        ],
        [VMEM_SPEC] * 4,
        [],
        2 * key_cache.size * heads, key_cache.size * 2, 8,
    )(spread, own, limit, key_cache)
    width = heads * HEAD_DIM + parts.shape[1]
    return call(
        value_kernel,
        jax.ShapeDtypeStruct((count, row_count, width), jnp.bfloat16),
        [VMEM_SPEC] * 5,
        [table],
        EXCHANGE_FLOPS, value_cache.size * 2, 8,
    )(probs, own_probs, value_cache, value_rows, parts)


def project_kernel(pieces, weight_ref, out_ref, gain_ref, stack):
    count, rows, _ = pieces.shape
    width = weight_ref.shape[0]
    half = gain_ref.shape[1] // 2
    for k in range(count):
        parts = pieces[k, :, width:].astype(jnp.float32)
        gain_ref[pl.ds(k, 1), :half] = parts[0:1] + parts[2:3]
        gain_ref[pl.ds(k, 1), half:] = parts[1:2] + parts[3:4]
    total = 0.0
    step = width // 4
    for start in range(0, width, step):
        part = slice(start, start + step)
        for k in range(count):
            stack[pl.ds(k * rows, rows), part] = pieces[k, :, part].astype(jnp.float32)
        total = total + jnp.dot(
            stack[:, part].astype(jnp.bfloat16),
            weight_ref[part, :],
            preferred_element_type=jnp.float32,
        )
    out_ref[...] = total


def project(pieces, out_weight):
    count, rows, _ = pieces.shape
    depth, cols = out_weight.shape
    return call(
        project_kernel,
        [
            jax.ShapeDtypeStruct((rows * count, cols), jnp.float32),
            jax.ShapeDtypeStruct((count, cols), jnp.float32),
        ],
        [VMEM_SPEC, VMEM_SPEC],
        [pltpu.VMEM((rows * count, depth), jnp.float32)],
        2 * rows * count * out_weight.size, out_weight.size * 2, 10,
    )(pieces, out_weight)


def pick_kernel(sharers, mine_ref, other_ref, residual_ref, taken_ref, stream_ref, out_ref):
    stream = (
        residual_ref[...].astype(jnp.float32) + (mine_ref[...] + other_ref[...])
    ).astype(jnp.bfloat16)
    stream_ref[...] = stream
    chosen = [
        jnp.dot(
            taken_ref[e].astype(jnp.bfloat16), stream, preferred_element_type=jnp.float32
        ).astype(jnp.bfloat16)
        for e in range(HELD)
    ]
    for k in range(out_ref.shape[0]):
        out_ref[k] = chosen[k // sharers]


def pick(sharers, count, mine, other, residual, taken):
    rows, cols = mine.shape
    return call(
        functools.partial(pick_kernel, sharers),
        [
            jax.ShapeDtypeStruct((rows, cols), jnp.bfloat16),
            jax.ShapeDtypeStruct((count, taken.shape[1], cols), jnp.bfloat16),
        ],
        [VMEM_SPEC] * 4,
        [],
        2 * HELD * taken.shape[1] * rows * cols, rows * cols * 12, 4,
    )(mine, other, residual, taken)


def expert_kernel(slot_ref, pieces, gains, *refs):
    weights, out_ref, rows_ref = (refs[:3], refs[3:6]), refs[6], refs[7]
    count, capacity, cols = pieces.shape
    first = second = 0.0
    for k in range(count):
        wide = pieces[k].astype(jnp.float32)
        first = first + wide
        second = second + wide * wide
    row_mean = jnp.sum(first, axis=1, keepdims=True) / D
    row_var = jnp.sum(second, axis=1, keepdims=True) / D - row_mean * row_mean
    inverse = lax.rsqrt(row_var + EPSILON)
    for k in range(count):
        wide = pieces[k].astype(jnp.float32)
        normed = (wide - row_mean) * inverse * gains[pl.ds(k, 1), :]
        rows_ref[:, k * cols : (k + 1) * cols] = normed.astype(jnp.bfloat16)
    rows = rows_ref[...]
    contract = (((1,), (1,)), ((), ()))
    hidden = []
    for gate_ref, up_ref, _ in weights:
        gate = lax.dot_general(rows, gate_ref[...], contract, preferred_element_type=jnp.float32)
        up = lax.dot_general(rows, up_ref[...], contract, preferred_element_type=jnp.float32)
        hidden.append((gate / (1.0 + jnp.exp(-gate)) * up).astype(jnp.bfloat16))
    slot_weight = slot_ref[:, :1]
    for k in range(count):
        block = slice(k * cols, (k + 1) * cols)
        piece = sum(
            jnp.dot(part, refs_of[2][:, block], preferred_element_type=jnp.float32)
            for part, refs_of in zip(hidden, weights)
        )
        out_ref[k] = (piece * slot_weight).astype(jnp.bfloat16)


def run_experts(slots, pieces, gains, own, other):
    count, capacity, cols = pieces.shape
    return call(
        expert_kernel,
        jax.ShapeDtypeStruct(pieces.shape, jnp.bfloat16),
        [VMEM_SPEC] * 9,
        [pltpu.VMEM((capacity, count * cols), jnp.bfloat16)],
        12 * capacity * own[0].size, own[0].size * 12, 20,
    )(slots, pieces, gains, *own, *other)


def combine_kernel(sharers, taken_ref, pieces, out_ref):
    count, capacity, cols = pieces.shape
    spread = [taken_ref[k // sharers] for k in range(count)]
    rows = [pieces[k].astype(jnp.float32) for k in range(count)]
    out_ref[...] = lax.dot_general(
        jnp.concatenate(spread, axis=0).astype(jnp.bfloat16),
        jnp.concatenate(rows, axis=0).astype(jnp.bfloat16),
        (((0,), (0,)), ((), ())),
        preferred_element_type=jnp.float32,
    )


def combine(sharers, taken, pieces):
    count, capacity, cols = pieces.shape
    rows = taken.shape[2]
    return call(
        functools.partial(combine_kernel, sharers),
        jax.ShapeDtypeStruct((rows, cols), jnp.float32),
        [VMEM_SPEC] * 2,
        [],
        2 * rows * capacity * count * cols, (count * capacity * 2 + rows * 4) * cols, 4,
    )(taken, pieces)


def finish_kernel(stream_ref, mine_ref, other_ref, stream_out_ref, out_ref):
    stream_out_ref[...] = stream_ref[...]
    out_ref[...] = (mine_ref[...] + other_ref[...]).astype(jnp.bfloat16)


def finish(stream, mine, other):
    return call(
        finish_kernel,
        [jax.ShapeDtypeStruct(stream.shape, jnp.bfloat16)] * 2,
        [VMEM_SPEC] * 3,
        [],
        mine.size, mine.size * 14, 4,
    )(stream, mine, other)


def exchange(blocks):
    return lax.all_to_all(blocks, "attn", split_axis=0, concat_axis=0, tiled=True)


def swap(block):
    return lax.ppermute(block, "expert", [(0, 1), (1, 0)])


def shards(
    queries,
    key_cache,
    value_cache,
    new_key,
    new_value,
    cache_length,
    residual,
    out_weight,
    ln_gain,
    gate_weight,
    up_weight,
    down_weight,
    routes,
    route_weight,
):
    count = lax.axis_size("attn")
    sharers = count // HELD
    capacity = routes.shape[0] * TOP // EXPERTS

    earlier = order(routes.shape[0])
    weights = (gate_weight.T, up_weight.T, down_weight)
    spread, own, limit, taken, slots, value_rows, parts = prepare(
        sharers, capacity, cache_length, earlier, routes.T, route_weight.T, queries, new_key,
        new_value, ln_gain,
    )
    other_weights = [swap(block) for block in lax.optimization_barrier(weights)]
    attended = exchange(
        attend(count, spread, own, limit, key_cache, value_cache, value_rows, parts)
    )
    mine, gains = project(attended, out_weight)
    stream, chosen = pick(sharers, count, mine, swap(mine), residual, taken)
    outgoing = run_experts(slots, exchange(chosen), gains, weights, other_weights)
    combined = combine(sharers, taken, exchange(outgoing))
    attn_stream, expert_out = finish(stream, combined, swap(combined))
    return (attn_stream, expert_out)


def solution(mesh):
    count = mesh.shape["attn"]
    fits = D // count % 256 == 0 and count % HELD == 0 and mesh.shape["expert"] == 2
    return jax.shard_map(
        shards if fits else shards_plain,
        mesh=mesh,
        in_specs=(
            P(("group", "attn"), "expert"),
            P(("group", "attn"), None, "expert"),
            P(("group", "attn"), None, "expert"),
            P(("group", "attn"), "expert"),
            P(("group", "attn"), "expert"),
            P(("group", "attn")),
            P("group", "attn"),
            P("expert", "attn"),
            P("attn"),
            P(None, ("attn", "expert")),
            P(None, ("attn", "expert")),
            P(("attn", "expert"), None),
            P("group", None),
            P("group", None),
        ),
        out_specs=(P("group", "attn"), P("group", "attn")),
        check_vma=False,
    )
```

```python
import functools
import math

import jax
import jax.numpy as jnp
from jax import lax
from jax.experimental import pallas as pl
from jax.experimental.pallas import tpu as pltpu
from jax.sharding import PartitionSpec as P

D = 6144
HEADS = 48
KV_HEADS = 8
HEAD_DIM = 128
EXPERTS = 16
TOP = 4
HELD = 2


NEG_FILL = -1e30
EPSILON = 1e-05


def attend_local(queries, key_cache, value_cache, new_key, new_value, cache_length):
    row_count = queries.shape[0]
    kv_local = new_key.shape[1] // HEAD_DIM
    group = HEADS // KV_HEADS
    length_max = key_cache.shape[1]
    query_heads = queries.reshape(row_count, kv_local, group, HEAD_DIM)
    key_heads = key_cache.reshape(row_count, length_max, kv_local, HEAD_DIM)
    value_heads = value_cache.reshape(row_count, length_max, kv_local, HEAD_DIM)
    own_keys = new_key.reshape(row_count, kv_local, HEAD_DIM)
    own_values = new_value.reshape(row_count, kv_local, HEAD_DIM)
    scale = 1.0 / math.sqrt(HEAD_DIM)
    past = (
        jnp.einsum("rkgd,rlkd->rkgl", query_heads, key_heads, preferred_element_type=jnp.float32)
        * scale
    )
    valid = jnp.arange(length_max, dtype=jnp.int32)[None, :] < cache_length[:, None]
    past = jnp.where(valid[:, None, None, :], past, NEG_FILL)
    own = (
        jnp.einsum("rkgd,rkd->rkg", query_heads, own_keys, preferred_element_type=jnp.float32)
        * scale
    )
    largest = jnp.maximum(jnp.max(past, axis=3), own)
    past_weight = jnp.exp(past - largest[..., None])
    own_weight = jnp.exp(own - largest)
    total = jnp.sum(past_weight, axis=3) + own_weight
    past_prob = (past_weight / total[..., None]).astype(jnp.bfloat16)
    own_prob = (own_weight / total).astype(jnp.bfloat16)
    result = jnp.einsum(
        "rkgl,rlkd->rkgd", past_prob, value_heads, preferred_element_type=jnp.float32
    )
    result = (
        result
        + own_prob.astype(jnp.float32)[..., None] * own_values.astype(jnp.float32)[:, :, None, :]
    )
    return result.reshape(row_count, kv_local * group * HEAD_DIM).astype(jnp.bfloat16)


def selection(routes, route_weight, capacity):
    row_count = routes.shape[0]
    experts = jnp.arange(HELD, dtype=jnp.int32)
    match = routes[None, :, :] == experts[:, None, None]
    hit = jnp.any(match, axis=2)
    row_weight = jnp.sum(jnp.where(match, route_weight[None], 0.0), axis=2)
    earlier = jnp.arange(row_count)[:, None] < jnp.arange(row_count)[None, :]
    slot = jnp.sum(jnp.where(earlier[None] & hit[:, :, None], 1, 0), axis=1)
    taken = hit[:, None, :] & (slot[:, None, :] == jnp.arange(capacity, dtype=jnp.int32)[None, :, None])
    slot_weight = jnp.sum(jnp.where(taken, row_weight[:, None, :], 0.0), axis=2)
    return taken, slot_weight


def gather_attn(block):
    count = lax.axis_size("attn")
    copies = jnp.broadcast_to(block[None], (count,) + block.shape)
    return lax.all_to_all(copies, "attn", split_axis=0, concat_axis=0, tiled=True)


def pair_sum(block):
    return block + lax.ppermute(block, "expert", [(0, 1), (1, 0)])


def shards_plain(
    queries,
    key_cache,
    value_cache,
    new_key,
    new_value,
    cache_length,
    residual,
    out_weight,
    ln_gain,
    gate_weight,
    up_weight,
    down_weight,
    routes,
    route_weight,
):
    attn_count = lax.axis_size("attn")
    core_count = lax.axis_size("expert")
    sharers = attn_count * core_count // HELD
    my_expert = (lax.axis_index("attn") * core_count + lax.axis_index("expert")) // sharers
    dest_expert = [index * core_count // sharers for index in range(attn_count)]
    row_count = routes.shape[0]
    capacity = row_count * TOP // EXPERTS * 2
    cols = residual.shape[1]

    taken, slot_weight = selection(routes, route_weight, capacity)
    pick = taken.astype(jnp.bfloat16)

    gains = gather_attn(ln_gain)

    attended = attend_local(queries, key_cache, value_cache, new_key, new_value, cache_length)
    whole = gather_attn(attended).reshape(row_count, -1)
    partial_proj = jnp.dot(whole, out_weight, preferred_element_type=jnp.float32)
    head_total = pair_sum(partial_proj)
    attn_stream = (residual.astype(jnp.float32) + head_total).astype(jnp.bfloat16)

    chosen = jnp.einsum(
        "esr,rd->esd", pick, attn_stream, preferred_element_type=jnp.float32
    ).astype(jnp.bfloat16)
    outgoing = jnp.stack([chosen[index] for index in dest_expert])
    rows = lax.all_to_all(outgoing, "attn", split_axis=0, concat_axis=0, tiled=True)
    wide = rows.astype(jnp.float32)
    row_mean = jnp.sum(wide, axis=(0, 2)) / D
    row_var = jnp.sum(wide * wide, axis=(0, 2)) / D - row_mean * row_mean
    normed = (
        (wide - row_mean[None, :, None])
        * lax.rsqrt(row_var + EPSILON)[None, :, None]
        * gains.reshape(attn_count, 1, cols)
    ).astype(jnp.bfloat16)
    gate_val = jnp.einsum(
        "asd,adf->sf", normed, gate_weight.reshape(attn_count, cols, -1),
        preferred_element_type=jnp.float32,
    )
    up_val = jnp.einsum(
        "asd,adf->sf", normed, up_weight.reshape(attn_count, cols, -1),
        preferred_element_type=jnp.float32,
    )
    hidden = (jax.nn.silu(gate_val) * up_val).astype(jnp.bfloat16)
    piece = jnp.dot(hidden, down_weight, preferred_element_type=jnp.float32)
    mine = jnp.take(slot_weight, my_expert, axis=0)
    piece = (piece * mine[:, None]).astype(jnp.bfloat16)
    returned = lax.all_to_all(
        piece.reshape(capacity, attn_count, cols).swapaxes(0, 1),
        "attn", split_axis=0, concat_axis=0, tiled=True,
    )
    spread = jnp.stack([pick[index] for index in dest_expert])
    combined = jnp.einsum(
        "asr,asd->rd", spread, returned, preferred_element_type=jnp.float32
    )
    expert_out = pair_sum(combined).astype(jnp.bfloat16)
    return (attn_stream, expert_out)


MIB = 1024 * 1024
EXCHANGE_FLOPS = 10**10
VMEM_SPEC = pl.BlockSpec(memory_space=pltpu.VMEM)
SMEM_SPEC = pl.BlockSpec(memory_space=pltpu.SMEM)
HBM_SPEC = pl.BlockSpec(memory_space=pltpu.HBM)


def call(kernel, outs, in_specs, scratch, flops, nbytes, vmem_mib):
    single = not isinstance(outs, (list, tuple))
    return pl.pallas_call(
        kernel,
        out_shape=outs,
        in_specs=in_specs,
        out_specs=VMEM_SPEC if single else [VMEM_SPEC] * len(outs),
        scratch_shapes=scratch,
        cost_estimate=pl.CostEstimate(flops=flops, bytes_accessed=nbytes, transcendentals=0),
        compiler_params=pltpu.CompilerParams(vmem_limit_bytes=vmem_mib * MIB),
    )


def order_kernel(out_ref):
    rows = out_ref.shape[0]
    before = lax.broadcasted_iota(jnp.int32, (rows, rows), 0) < lax.broadcasted_iota(
        jnp.int32, (rows, rows), 1
    )
    out_ref[...] = jnp.where(before, 1.0, 0.0).astype(jnp.bfloat16)


def order(rows):
    return call(
        order_kernel,
        jax.ShapeDtypeStruct((rows, rows), jnp.bfloat16),
        [],
        [],
        EXCHANGE_FLOPS, rows * rows * 2, 2,
    )()


def expert_rows(routes, earlier, expert, capacity):
    row_count = routes.shape[1]
    hit = jnp.max((routes == expert).astype(jnp.float32), axis=0, keepdims=True)
    slot = jnp.dot(
        jnp.broadcast_to(hit, (8, row_count)).astype(jnp.bfloat16),
        earlier,
        preferred_element_type=jnp.float32,
    )[:1]
    place = lax.broadcasted_iota(jnp.int32, (capacity, row_count), 0).astype(jnp.float32)
    return jnp.where((slot == place) & (hit > 0.5), 1.0, 0.0)


def prepare_kernel(sharers, length_ref, earlier_ref, routes_ref, weight_ref, query_ref,
                   own_key_ref, own_value_ref, gain_ref, spread_ref, own_ref, limit_ref, taken_ref,
                   slot_ref, value_rows, part_ref, query_rows, key_rows):
    row_count = query_ref.shape[0]
    kv_local = own_key_ref.shape[1] // HEAD_DIM
    group = HEADS // KV_HEADS
    heads = kv_local * group
    for g in range(kv_local):
        own_key = own_key_ref[:, g * HEAD_DIM : (g + 1) * HEAD_DIM].astype(jnp.float32)
        for i in range(group):
            index = g * group + i
            rows = pl.ds(index * row_count, row_count)
            query_rows[rows, :] = query_ref[
                :, index * HEAD_DIM : (index + 1) * HEAD_DIM
            ].astype(jnp.float32)
            key_rows[rows, :] = own_key
            value_rows[rows, :] = own_value_ref[
                :, g * HEAD_DIM : (g + 1) * HEAD_DIM
            ].astype(jnp.float32)
    gain_row = gain_ref[...].reshape(1, -1)
    half = gain_row.shape[1] // 2
    row = lax.broadcasted_iota(jnp.int32, (row_count, half), 0)
    left = jnp.broadcast_to(gain_row[:, :half], (row_count, half))
    right = jnp.broadcast_to(gain_row[:, half:], (row_count, half))
    gain = jnp.where(row % 2 == 0, left, right)
    upper = gain.astype(jnp.bfloat16).astype(jnp.float32)
    part_ref[...] = jnp.where(row < 2, upper, gain - upper).astype(jnp.bfloat16)
    scale = 1.0 / math.sqrt(HEAD_DIM)
    lengths = length_ref[...].reshape(1, -1)
    head = lax.broadcasted_iota(jnp.int32, (heads, 1), 0) // group
    for r in range(row_count):
        strided = pl.ds(r, heads, stride=row_count)
        query = query_rows[strided, :]
        own = jnp.sum(query * key_rows[strided, :], axis=1, keepdims=True) * scale
        own_ref[r] = jnp.broadcast_to(own, (heads, HEAD_DIM))
        limit_ref[r] = jnp.broadcast_to(lengths[:, r : r + 1], (heads, HEAD_DIM))
        spread_ref[r] = jnp.concatenate(
            [jnp.where(head == g, query, 0.0) for g in range(kv_local)], axis=1
        ).astype(jnp.bfloat16)
    routes = routes_ref[...]
    capacity = slot_ref.shape[0]
    core = lax.axis_index("expert")
    taken = []
    for e in range(HELD):
        both = expert_rows(routes, earlier_ref[...], e, 2 * capacity)
        taken.append(jnp.where(core == 0, both[:capacity], both[capacity:]))
        taken_ref[e] = taken[e]
    first = lax.axis_index("attn") < sharers
    expert = jnp.where(first, 0, 1)
    row_weight = jnp.sum(
        jnp.where(routes == expert, weight_ref[...], 0.0), axis=0, keepdims=True
    )
    mine = jnp.where(first, taken[0], taken[1])
    slot_ref[...] = jnp.broadcast_to(
        jnp.sum(mine * row_weight, axis=1, keepdims=True), slot_ref.shape
    )


def prepare(
    sharers, capacity, cache_length, earlier, routes, route_weight, queries, new_key, new_value,
    gain,
):
    row_count, width = queries.shape
    heads = width // HEAD_DIM
    table = pltpu.VMEM((heads * row_count, HEAD_DIM), jnp.float32)
    return call(
        functools.partial(prepare_kernel, sharers),
        [
            jax.ShapeDtypeStruct((row_count, heads, new_key.shape[1]), jnp.bfloat16),
            jax.ShapeDtypeStruct((row_count, heads, HEAD_DIM), jnp.float32),
            jax.ShapeDtypeStruct((row_count, heads, HEAD_DIM), jnp.int32),
            jax.ShapeDtypeStruct((HELD, capacity, routes.shape[1]), jnp.float32),
            jax.ShapeDtypeStruct((capacity, HEAD_DIM), jnp.float32),
            jax.ShapeDtypeStruct((heads * row_count, HEAD_DIM), jnp.float32),
            jax.ShapeDtypeStruct((row_count, gain.shape[0] // 2), jnp.bfloat16),
        ],
        [VMEM_SPEC] * 8,
        [table, table],
        queries.size * 8, queries.size * 16, 4,
    )(cache_length, earlier, routes, route_weight, queries, new_key, new_value, gain)


def score_kernel(spread_ref, own_ref, limit_ref, key_ref, probs_ref, own_probs_ref):
    row_count, heads, length_max = probs_ref.shape
    scale = 1.0 / math.sqrt(HEAD_DIM)
    contract = (((1,), (1,)), ((), ()))
    products = [
        lax.dot_general(spread_ref[r], key_ref[r], contract, preferred_element_type=jnp.float32)
        for r in range(row_count)
    ]
    for first in range(0, row_count, 2):
        batch = range(first, min(first + 2, row_count))
        scores = jnp.concatenate([products[r] for r in batch], axis=0)
        position = lax.broadcasted_iota(jnp.int32, scores.shape, 1)
        limit = jnp.concatenate([limit_ref[r, :, :1] for r in batch], axis=0)
        own = jnp.concatenate([own_ref[r, :, :1] for r in batch], axis=0)
        past = jnp.where(position < limit, scores * scale, NEG_FILL)
        largest = jnp.maximum(jnp.max(past, axis=1, keepdims=True), own)
        weight = jnp.exp(past - largest)
        own_weight = jnp.exp(own - largest)
        inverse = 1.0 / (jnp.sum(weight, axis=1, keepdims=True) + own_weight)
        probs = weight * inverse
        own_prob = (own_weight * inverse).astype(jnp.bfloat16).astype(jnp.float32)
        for index, r in enumerate(batch):
            rows = slice(index * heads, (index + 1) * heads)
            probs_ref[r] = probs[rows].astype(jnp.bfloat16)
            own_probs_ref[r] = jnp.broadcast_to(own_prob[rows], own_probs_ref.shape[1:])


def value_kernel(probs_ref, own_ref, value_ref, value_rows, part_ref, out_ref, result_rows):
    row_count, length_max, width = value_ref.shape
    kv_local = width // HEAD_DIM
    group = HEADS // KV_HEADS
    heads = kv_local * group
    head = lax.broadcasted_iota(jnp.int32, (heads, 1), 0) // group
    for r in range(row_count):
        strided = pl.ds(r, heads, stride=row_count)
        product = jnp.dot(probs_ref[r], value_ref[r], preferred_element_type=jnp.float32)
        total = own_ref[r] * value_rows[strided, :]
        for g in range(kv_local):
            lanes = slice(g * HEAD_DIM, (g + 1) * HEAD_DIM)
            total = total + jnp.where(head == g, product[:, lanes], 0.0)
        result_rows[strided, :] = total
    for index in range(heads):
        rows = result_rows[pl.ds(index * row_count, row_count), :].astype(jnp.bfloat16)
        for copy in range(out_ref.shape[0]):
            out_ref[copy, :, index * HEAD_DIM : (index + 1) * HEAD_DIM] = rows
    parts = part_ref[...]
    for copy in range(out_ref.shape[0]):
        out_ref[copy, :, heads * HEAD_DIM :] = parts


def attend(count, spread, own, limit, key_cache, value_cache, value_rows, parts):
    row_count, heads, _ = spread.shape
    length_max = key_cache.shape[1]
    table = pltpu.VMEM((heads * row_count, HEAD_DIM), jnp.float32)
    probs, own_probs = call(
        score_kernel,
        [
            jax.ShapeDtypeStruct((row_count, heads, length_max), jnp.bfloat16),
            jax.ShapeDtypeStruct((row_count, heads, HEAD_DIM), jnp.float32),
        ],
        [VMEM_SPEC] * 4,
        [],
        2 * key_cache.size * heads, key_cache.size * 2, 8,
    )(spread, own, limit, key_cache)
    width = heads * HEAD_DIM + parts.shape[1]
    return call(
        value_kernel,
        jax.ShapeDtypeStruct((count, row_count, width), jnp.bfloat16),
        [VMEM_SPEC] * 5,
        [table],
        EXCHANGE_FLOPS, value_cache.size * 2, 8,
    )(probs, own_probs, value_cache, value_rows, parts)


def project_kernel(pieces, weight_ref, out_ref, gain_ref, stack):
    count, rows, _ = pieces.shape
    width = weight_ref.shape[0]
    half = gain_ref.shape[1] // 2
    for k in range(count):
        parts = pieces[k, :, width:].astype(jnp.float32)
        gain_ref[pl.ds(k, 1), :half] = parts[0:1] + parts[2:3]
        gain_ref[pl.ds(k, 1), half:] = parts[1:2] + parts[3:4]
    total = 0.0
    step = width // 4
    for start in range(0, width, step):
        part = slice(start, start + step)
        for k in range(count):
            stack[pl.ds(k * rows, rows), part] = pieces[k, :, part].astype(jnp.float32)
        total = total + jnp.dot(
            stack[:, part].astype(jnp.bfloat16),
            weight_ref[part, :],
            preferred_element_type=jnp.float32,
        )
    out_ref[...] = total


def project(pieces, out_weight):
    count, rows, _ = pieces.shape
    depth, cols = out_weight.shape
    return call(
        project_kernel,
        [
            jax.ShapeDtypeStruct((rows * count, cols), jnp.float32),
            jax.ShapeDtypeStruct((count, cols), jnp.float32),
        ],
        [VMEM_SPEC, VMEM_SPEC],
        [pltpu.VMEM((rows * count, depth), jnp.float32)],
        2 * rows * count * out_weight.size, out_weight.size * 2, 10,
    )(pieces, out_weight)


def pick_kernel(sharers, mine_ref, other_ref, residual_ref, taken_ref, stream_ref, out_ref):
    stream = (
        residual_ref[...].astype(jnp.float32) + (mine_ref[...] + other_ref[...])
    ).astype(jnp.bfloat16)
    stream_ref[...] = stream
    chosen = [
        jnp.dot(
            taken_ref[e].astype(jnp.bfloat16), stream, preferred_element_type=jnp.float32
        ).astype(jnp.bfloat16)
        for e in range(HELD)
    ]
    for k in range(out_ref.shape[0]):
        out_ref[k] = chosen[k // sharers]


def pick(sharers, count, mine, other, residual, taken):
    rows, cols = mine.shape
    return call(
        functools.partial(pick_kernel, sharers),
        [
            jax.ShapeDtypeStruct((rows, cols), jnp.bfloat16),
            jax.ShapeDtypeStruct((count, taken.shape[1], cols), jnp.bfloat16),
        ],
        [VMEM_SPEC] * 4,
        [],
        2 * HELD * taken.shape[1] * rows * cols, rows * cols * 12, 4,
    )(mine, other, residual, taken)


def expert_kernel(slot_ref, pieces, gains, *refs):
    weights, out_ref, rows_ref = (refs[:3], refs[3:6]), refs[6], refs[7]
    count, capacity, cols = pieces.shape
    first = second = 0.0
    for k in range(count):
        wide = pieces[k].astype(jnp.float32)
        first = first + wide
        second = second + wide * wide
    row_mean = jnp.sum(first, axis=1, keepdims=True) / D
    row_var = jnp.sum(second, axis=1, keepdims=True) / D - row_mean * row_mean
    inverse = lax.rsqrt(row_var + EPSILON)
    for k in range(count):
        wide = pieces[k].astype(jnp.float32)
        normed = (wide - row_mean) * inverse * gains[pl.ds(k, 1), :]
        rows_ref[:, k * cols : (k + 1) * cols] = normed.astype(jnp.bfloat16)
    rows = rows_ref[...]
    contract = (((1,), (1,)), ((), ()))
    hidden = []
    for gate_ref, up_ref, _ in weights:
        gate = lax.dot_general(rows, gate_ref[...], contract, preferred_element_type=jnp.float32)
        up = lax.dot_general(rows, up_ref[...], contract, preferred_element_type=jnp.float32)
        hidden.append((gate / (1.0 + jnp.exp(-gate)) * up).astype(jnp.bfloat16))
    slot_weight = slot_ref[:, :1]
    for k in range(count):
        block = slice(k * cols, (k + 1) * cols)
        piece = sum(
            jnp.dot(part, refs_of[2][:, block], preferred_element_type=jnp.float32)
            for part, refs_of in zip(hidden, weights)
        )
        out_ref[k] = (piece * slot_weight).astype(jnp.bfloat16)


def run_experts(slots, pieces, gains, own, other):
    count, capacity, cols = pieces.shape
    return call(
        expert_kernel,
        jax.ShapeDtypeStruct(pieces.shape, jnp.bfloat16),
        [VMEM_SPEC] * 9,
        [pltpu.VMEM((capacity, count * cols), jnp.bfloat16)],
        12 * capacity * own[0].size, own[0].size * 12, 20,
    )(slots, pieces, gains, *own, *other)


def combine_kernel(sharers, taken_ref, pieces, out_ref):
    count, capacity, cols = pieces.shape
    spread = [taken_ref[k // sharers] for k in range(count)]
    rows = [pieces[k].astype(jnp.float32) for k in range(count)]
    out_ref[...] = lax.dot_general(
        jnp.concatenate(spread, axis=0).astype(jnp.bfloat16),
        jnp.concatenate(rows, axis=0).astype(jnp.bfloat16),
        (((0,), (0,)), ((), ())),
        preferred_element_type=jnp.float32,
    )


def combine(sharers, taken, pieces):
    count, capacity, cols = pieces.shape
    rows = taken.shape[2]
    return call(
        functools.partial(combine_kernel, sharers),
        jax.ShapeDtypeStruct((rows, cols), jnp.float32),
        [VMEM_SPEC] * 2,
        [],
        2 * rows * capacity * count * cols, (count * capacity * 2 + rows * 4) * cols, 4,
    )(taken, pieces)


def finish_kernel(stream_ref, mine_ref, other_ref, stream_out_ref, out_ref):
    stream_out_ref[...] = stream_ref[...]
    out_ref[...] = (mine_ref[...] + other_ref[...]).astype(jnp.bfloat16)


def finish(stream, mine, other):
    return call(
        finish_kernel,
        [jax.ShapeDtypeStruct(stream.shape, jnp.bfloat16)] * 2,
        [VMEM_SPEC] * 3,
        [],
        mine.size, mine.size * 14, 4,
    )(stream, mine, other)


def exchange(blocks):
    return lax.all_to_all(blocks, "attn", split_axis=0, concat_axis=0, tiled=True)


def swap(block):
    return lax.ppermute(block, "expert", [(0, 1), (1, 0)])


def shards(
    queries,
    key_cache,
    value_cache,
    new_key,
    new_value,
    cache_length,
    residual,
    out_weight,
    ln_gain,
    gate_weight,
    up_weight,
    down_weight,
    routes,
    route_weight,
):
    count = lax.axis_size("attn")
    sharers = count // HELD
    capacity = routes.shape[0] * TOP // EXPERTS

    earlier = order(routes.shape[0])
    weights = (gate_weight.T, up_weight.T, down_weight)
    spread, own, limit, taken, slots, value_rows, parts = prepare(
        sharers, capacity, cache_length, earlier, routes.T, route_weight.T, queries, new_key,
        new_value, ln_gain,
    )
    other_weights = [swap(block) for block in lax.optimization_barrier(weights[:2])]
    attended = exchange(
        attend(count, spread, own, limit, key_cache, value_cache, value_rows, parts)
    )
    mine, gains = project(attended, out_weight)
    stream, chosen = pick(sharers, count, mine, swap(mine), residual, taken)
    late_down, chosen = lax.optimization_barrier((weights[2], chosen))
    other_weights.append(swap(late_down))
    outgoing = run_experts(slots, exchange(chosen), gains, weights, other_weights)
    combined = combine(sharers, taken, exchange(outgoing))
    attn_stream, expert_out = finish(stream, combined, swap(combined))
    return (attn_stream, expert_out)


def solution(mesh):
    count = mesh.shape["attn"]
    fits = D // count % 256 == 0 and count % HELD == 0 and mesh.shape["expert"] == 2
    return jax.shard_map(
        shards if fits else shards_plain,
        mesh=mesh,
        in_specs=(
            P(("group", "attn"), "expert"),
            P(("group", "attn"), None, "expert"),
            P(("group", "attn"), None, "expert"),
            P(("group", "attn"), "expert"),
            P(("group", "attn"), "expert"),
            P(("group", "attn")),
            P("group", "attn"),
            P("expert", "attn"),
            P("attn"),
            P(None, ("attn", "expert")),
            P(None, ("attn", "expert")),
            P(("attn", "expert"), None),
            P("group", None),
            P("group", None),
        ),
        out_specs=(P("group", "attn"), P("group", "attn")),
        check_vma=False,
    )
```

```python
import functools
import math

import jax
import jax.numpy as jnp
from jax import lax
from jax.experimental import pallas as pl
from jax.experimental.pallas import tpu as pltpu
from jax.sharding import PartitionSpec as P

D = 6144
HEADS = 48
KV_HEADS = 8
HEAD_DIM = 128
EXPERTS = 16
TOP = 4
HELD = 2


NEG_FILL = -1e30
EPSILON = 1e-05


def attend_local(queries, key_cache, value_cache, new_key, new_value, cache_length):
    row_count = queries.shape[0]
    kv_local = new_key.shape[1] // HEAD_DIM
    group = HEADS // KV_HEADS
    length_max = key_cache.shape[1]
    query_heads = queries.reshape(row_count, kv_local, group, HEAD_DIM)
    key_heads = key_cache.reshape(row_count, length_max, kv_local, HEAD_DIM)
    value_heads = value_cache.reshape(row_count, length_max, kv_local, HEAD_DIM)
    own_keys = new_key.reshape(row_count, kv_local, HEAD_DIM)
    own_values = new_value.reshape(row_count, kv_local, HEAD_DIM)
    scale = 1.0 / math.sqrt(HEAD_DIM)
    past = (
        jnp.einsum("rkgd,rlkd->rkgl", query_heads, key_heads, preferred_element_type=jnp.float32)
        * scale
    )
    valid = jnp.arange(length_max, dtype=jnp.int32)[None, :] < cache_length[:, None]
    past = jnp.where(valid[:, None, None, :], past, NEG_FILL)
    own = (
        jnp.einsum("rkgd,rkd->rkg", query_heads, own_keys, preferred_element_type=jnp.float32)
        * scale
    )
    largest = jnp.maximum(jnp.max(past, axis=3), own)
    past_weight = jnp.exp(past - largest[..., None])
    own_weight = jnp.exp(own - largest)
    total = jnp.sum(past_weight, axis=3) + own_weight
    past_prob = (past_weight / total[..., None]).astype(jnp.bfloat16)
    own_prob = (own_weight / total).astype(jnp.bfloat16)
    result = jnp.einsum(
        "rkgl,rlkd->rkgd", past_prob, value_heads, preferred_element_type=jnp.float32
    )
    result = (
        result
        + own_prob.astype(jnp.float32)[..., None] * own_values.astype(jnp.float32)[:, :, None, :]
    )
    return result.reshape(row_count, kv_local * group * HEAD_DIM).astype(jnp.bfloat16)


def selection(routes, route_weight, capacity):
    row_count = routes.shape[0]
    experts = jnp.arange(HELD, dtype=jnp.int32)
    match = routes[None, :, :] == experts[:, None, None]
    hit = jnp.any(match, axis=2)
    row_weight = jnp.sum(jnp.where(match, route_weight[None], 0.0), axis=2)
    earlier = jnp.arange(row_count)[:, None] < jnp.arange(row_count)[None, :]
    slot = jnp.sum(jnp.where(earlier[None] & hit[:, :, None], 1, 0), axis=1)
    taken = hit[:, None, :] & (slot[:, None, :] == jnp.arange(capacity, dtype=jnp.int32)[None, :, None])
    slot_weight = jnp.sum(jnp.where(taken, row_weight[:, None, :], 0.0), axis=2)
    return taken, slot_weight


def gather_attn(block):
    count = lax.axis_size("attn")
    copies = jnp.broadcast_to(block[None], (count,) + block.shape)
    return lax.all_to_all(copies, "attn", split_axis=0, concat_axis=0, tiled=True)


def pair_sum(block):
    return block + lax.ppermute(block, "expert", [(0, 1), (1, 0)])


def shards_plain(
    queries,
    key_cache,
    value_cache,
    new_key,
    new_value,
    cache_length,
    residual,
    out_weight,
    ln_gain,
    gate_weight,
    up_weight,
    down_weight,
    routes,
    route_weight,
):
    attn_count = lax.axis_size("attn")
    core_count = lax.axis_size("expert")
    sharers = attn_count * core_count // HELD
    my_expert = (lax.axis_index("attn") * core_count + lax.axis_index("expert")) // sharers
    dest_expert = [index * core_count // sharers for index in range(attn_count)]
    row_count = routes.shape[0]
    capacity = row_count * TOP // EXPERTS * 2
    cols = residual.shape[1]

    taken, slot_weight = selection(routes, route_weight, capacity)
    pick = taken.astype(jnp.bfloat16)

    gains = gather_attn(ln_gain)

    attended = attend_local(queries, key_cache, value_cache, new_key, new_value, cache_length)
    whole = gather_attn(attended).reshape(row_count, -1)
    partial_proj = jnp.dot(whole, out_weight, preferred_element_type=jnp.float32)
    head_total = pair_sum(partial_proj)
    attn_stream = (residual.astype(jnp.float32) + head_total).astype(jnp.bfloat16)

    chosen = jnp.einsum(
        "esr,rd->esd", pick, attn_stream, preferred_element_type=jnp.float32
    ).astype(jnp.bfloat16)
    outgoing = jnp.stack([chosen[index] for index in dest_expert])
    rows = lax.all_to_all(outgoing, "attn", split_axis=0, concat_axis=0, tiled=True)
    wide = rows.astype(jnp.float32)
    row_mean = jnp.sum(wide, axis=(0, 2)) / D
    row_var = jnp.sum(wide * wide, axis=(0, 2)) / D - row_mean * row_mean
    normed = (
        (wide - row_mean[None, :, None])
        * lax.rsqrt(row_var + EPSILON)[None, :, None]
        * gains.reshape(attn_count, 1, cols)
    ).astype(jnp.bfloat16)
    gate_val = jnp.einsum(
        "asd,adf->sf", normed, gate_weight.reshape(attn_count, cols, -1),
        preferred_element_type=jnp.float32,
    )
    up_val = jnp.einsum(
        "asd,adf->sf", normed, up_weight.reshape(attn_count, cols, -1),
        preferred_element_type=jnp.float32,
    )
    hidden = (jax.nn.silu(gate_val) * up_val).astype(jnp.bfloat16)
    piece = jnp.dot(hidden, down_weight, preferred_element_type=jnp.float32)
    mine = jnp.take(slot_weight, my_expert, axis=0)
    piece = (piece * mine[:, None]).astype(jnp.bfloat16)
    returned = lax.all_to_all(
        piece.reshape(capacity, attn_count, cols).swapaxes(0, 1),
        "attn", split_axis=0, concat_axis=0, tiled=True,
    )
    spread = jnp.stack([pick[index] for index in dest_expert])
    combined = jnp.einsum(
        "asr,asd->rd", spread, returned, preferred_element_type=jnp.float32
    )
    expert_out = pair_sum(combined).astype(jnp.bfloat16)
    return (attn_stream, expert_out)


MIB = 1024 * 1024
EXCHANGE_FLOPS = 10**10
VMEM_SPEC = pl.BlockSpec(memory_space=pltpu.VMEM)
SMEM_SPEC = pl.BlockSpec(memory_space=pltpu.SMEM)
HBM_SPEC = pl.BlockSpec(memory_space=pltpu.HBM)


def call(kernel, outs, in_specs, scratch, flops, nbytes, vmem_mib):
    single = not isinstance(outs, (list, tuple))
    return pl.pallas_call(
        kernel,
        out_shape=outs,
        in_specs=in_specs,
        out_specs=VMEM_SPEC if single else [VMEM_SPEC] * len(outs),
        scratch_shapes=scratch,
        cost_estimate=pl.CostEstimate(flops=flops, bytes_accessed=nbytes, transcendentals=0),
        compiler_params=pltpu.CompilerParams(vmem_limit_bytes=vmem_mib * MIB),
    )


def order_kernel(out_ref):
    rows = out_ref.shape[0]
    before = lax.broadcasted_iota(jnp.int32, (rows, rows), 0) < lax.broadcasted_iota(
        jnp.int32, (rows, rows), 1
    )
    out_ref[...] = jnp.where(before, 1.0, 0.0).astype(jnp.bfloat16)


def order(rows):
    return call(
        order_kernel,
        jax.ShapeDtypeStruct((rows, rows), jnp.bfloat16),
        [],
        [],
        EXCHANGE_FLOPS, rows * rows * 2, 2,
    )()


def expert_rows(routes, earlier, expert, capacity):
    row_count = routes.shape[1]
    hit = jnp.max((routes == expert).astype(jnp.float32), axis=0, keepdims=True)
    slot = jnp.dot(
        jnp.broadcast_to(hit, (8, row_count)).astype(jnp.bfloat16),
        earlier,
        preferred_element_type=jnp.float32,
    )[:1]
    place = lax.broadcasted_iota(jnp.int32, (capacity, row_count), 0).astype(jnp.float32)
    return jnp.where((slot == place) & (hit > 0.5), 1.0, 0.0)


def prepare_kernel(sharers, length_ref, earlier_ref, routes_ref, weight_ref, query_ref,
                   own_key_ref, own_value_ref, gain_ref, spread_ref, own_ref, limit_ref, taken_ref,
                   slot_ref, value_rows, part_ref, query_rows, key_rows):
    row_count = query_ref.shape[0]
    kv_local = own_key_ref.shape[1] // HEAD_DIM
    group = HEADS // KV_HEADS
    heads = kv_local * group
    for g in range(kv_local):
        own_key = own_key_ref[:, g * HEAD_DIM : (g + 1) * HEAD_DIM].astype(jnp.float32)
        for i in range(group):
            index = g * group + i
            rows = pl.ds(index * row_count, row_count)
            query_rows[rows, :] = query_ref[
                :, index * HEAD_DIM : (index + 1) * HEAD_DIM
            ].astype(jnp.float32)
            key_rows[rows, :] = own_key
            value_rows[rows, :] = own_value_ref[
                :, g * HEAD_DIM : (g + 1) * HEAD_DIM
            ].astype(jnp.float32)
    gain_row = gain_ref[...].reshape(1, -1)
    half = gain_row.shape[1] // 2
    row = lax.broadcasted_iota(jnp.int32, (row_count, half), 0)
    left = jnp.broadcast_to(gain_row[:, :half], (row_count, half))
    right = jnp.broadcast_to(gain_row[:, half:], (row_count, half))
    gain = jnp.where(row % 2 == 0, left, right)
    upper = gain.astype(jnp.bfloat16).astype(jnp.float32)
    part_ref[...] = jnp.where(row < 2, upper, gain - upper).astype(jnp.bfloat16)
    scale = 1.0 / math.sqrt(HEAD_DIM)
    lengths = length_ref[...].reshape(1, -1)
    head = lax.broadcasted_iota(jnp.int32, (heads, 1), 0) // group
    for r in range(row_count):
        strided = pl.ds(r, heads, stride=row_count)
        query = query_rows[strided, :]
        own = jnp.sum(query * key_rows[strided, :], axis=1, keepdims=True) * scale
        own_ref[r] = jnp.broadcast_to(own, (heads, HEAD_DIM))
        limit_ref[r] = jnp.broadcast_to(lengths[:, r : r + 1], (heads, HEAD_DIM))
        spread_ref[r] = jnp.concatenate(
            [jnp.where(head == g, query, 0.0) for g in range(kv_local)], axis=1
        ).astype(jnp.bfloat16)
    routes = routes_ref[...]
    capacity = slot_ref.shape[0]
    core = lax.axis_index("expert")
    taken = []
    for e in range(HELD):
        both = expert_rows(routes, earlier_ref[...], e, 2 * capacity)
        taken.append(jnp.where(core == 0, both[:capacity], both[capacity:]))
        taken_ref[e] = taken[e]
    first = lax.axis_index("attn") < sharers
    expert = jnp.where(first, 0, 1)
    row_weight = jnp.sum(
        jnp.where(routes == expert, weight_ref[...], 0.0), axis=0, keepdims=True
    )
    mine = jnp.where(first, taken[0], taken[1])
    slot_ref[...] = jnp.broadcast_to(
        jnp.sum(mine * row_weight, axis=1, keepdims=True), slot_ref.shape
    )


def prepare(
    sharers, capacity, cache_length, earlier, routes, route_weight, queries, new_key, new_value,
    gain,
):
    row_count, width = queries.shape
    heads = width // HEAD_DIM
    table = pltpu.VMEM((heads * row_count, HEAD_DIM), jnp.float32)
    return call(
        functools.partial(prepare_kernel, sharers),
        [
            jax.ShapeDtypeStruct((row_count, heads, new_key.shape[1]), jnp.bfloat16),
            jax.ShapeDtypeStruct((row_count, heads, HEAD_DIM), jnp.float32),
            jax.ShapeDtypeStruct((row_count, heads, HEAD_DIM), jnp.int32),
            jax.ShapeDtypeStruct((HELD, capacity, routes.shape[1]), jnp.float32),
            jax.ShapeDtypeStruct((capacity, HEAD_DIM), jnp.float32),
            jax.ShapeDtypeStruct((heads * row_count, HEAD_DIM), jnp.float32),
            jax.ShapeDtypeStruct((row_count, gain.shape[0] // 2), jnp.bfloat16),
        ],
        [VMEM_SPEC] * 8,
        [table, table],
        queries.size * 8, queries.size * 16, 4,
    )(cache_length, earlier, routes, route_weight, queries, new_key, new_value, gain)


def score_kernel(spread_ref, own_ref, limit_ref, key_ref, probs_ref, own_probs_ref):
    row_count, heads, length_max = probs_ref.shape
    scale = 1.0 / math.sqrt(HEAD_DIM)
    contract = (((1,), (1,)), ((), ()))
    products = [
        lax.dot_general(spread_ref[r], key_ref[r], contract, preferred_element_type=jnp.float32)
        for r in range(row_count)
    ]
    for first in range(0, row_count, 2):
        batch = range(first, min(first + 2, row_count))
        scores = jnp.concatenate([products[r] for r in batch], axis=0)
        position = lax.broadcasted_iota(jnp.int32, scores.shape, 1)
        limit = jnp.concatenate([limit_ref[r, :, :1] for r in batch], axis=0)
        own = jnp.concatenate([own_ref[r, :, :1] for r in batch], axis=0)
        past = jnp.where(position < limit, scores * scale, NEG_FILL)
        largest = jnp.maximum(jnp.max(past, axis=1, keepdims=True), own)
        weight = jnp.exp(past - largest)
        own_weight = jnp.exp(own - largest)
        inverse = 1.0 / (jnp.sum(weight, axis=1, keepdims=True) + own_weight)
        probs = weight * inverse
        own_prob = (own_weight * inverse).astype(jnp.bfloat16).astype(jnp.float32)
        for index, r in enumerate(batch):
            rows = slice(index * heads, (index + 1) * heads)
            probs_ref[r] = probs[rows].astype(jnp.bfloat16)
            own_probs_ref[r] = jnp.broadcast_to(own_prob[rows], own_probs_ref.shape[1:])


def value_kernel(probs_ref, own_ref, value_ref, value_rows, part_ref, out_ref, result_rows):
    row_count, length_max, width = value_ref.shape
    kv_local = width // HEAD_DIM
    group = HEADS // KV_HEADS
    heads = kv_local * group
    head = lax.broadcasted_iota(jnp.int32, (heads, 1), 0) // group
    for r in range(row_count):
        strided = pl.ds(r, heads, stride=row_count)
        product = jnp.dot(probs_ref[r], value_ref[r], preferred_element_type=jnp.float32)
        total = own_ref[r] * value_rows[strided, :]
        for g in range(kv_local):
            lanes = slice(g * HEAD_DIM, (g + 1) * HEAD_DIM)
            total = total + jnp.where(head == g, product[:, lanes], 0.0)
        result_rows[strided, :] = total
    for index in range(heads):
        rows = result_rows[pl.ds(index * row_count, row_count), :].astype(jnp.bfloat16)
        for copy in range(out_ref.shape[0]):
            out_ref[copy, :, index * HEAD_DIM : (index + 1) * HEAD_DIM] = rows
    parts = part_ref[...]
    for copy in range(out_ref.shape[0]):
        out_ref[copy, :, heads * HEAD_DIM :] = parts


def attend(count, spread, own, limit, key_cache, value_cache, value_rows, parts):
    row_count, heads, _ = spread.shape
    length_max = key_cache.shape[1]
    table = pltpu.VMEM((heads * row_count, HEAD_DIM), jnp.float32)
    probs, own_probs = call(
        score_kernel,
        [
            jax.ShapeDtypeStruct((row_count, heads, length_max), jnp.bfloat16),
            jax.ShapeDtypeStruct((row_count, heads, HEAD_DIM), jnp.float32),
        ],
        [VMEM_SPEC] * 4,
        [],
        2 * key_cache.size * heads, key_cache.size * 2, 8,
    )(spread, own, limit, key_cache)
    width = heads * HEAD_DIM + parts.shape[1]
    return call(
        value_kernel,
        jax.ShapeDtypeStruct((count, row_count, width), jnp.bfloat16),
        [VMEM_SPEC] * 5,
        [table],
        EXCHANGE_FLOPS, value_cache.size * 2, 8,
    )(probs, own_probs, value_cache, value_rows, parts)


def project_kernel(pieces, weight_ref, out_ref, gain_ref, stack):
    count, rows, _ = pieces.shape
    width = weight_ref.shape[0]
    half = gain_ref.shape[1] // 2
    for k in range(count):
        parts = pieces[k, :, width:].astype(jnp.float32)
        gain_ref[pl.ds(k, 1), :half] = parts[0:1] + parts[2:3]
        gain_ref[pl.ds(k, 1), half:] = parts[1:2] + parts[3:4]
    total = 0.0
    step = width // 4
    for start in range(0, width, step):
        part = slice(start, start + step)
        for k in range(count):
            stack[pl.ds(k * rows, rows), part] = pieces[k, :, part].astype(jnp.float32)
        total = total + jnp.dot(
            stack[:, part].astype(jnp.bfloat16),
            weight_ref[part, :],
            preferred_element_type=jnp.float32,
        )
    out_ref[...] = total


def project(pieces, out_weight):
    count, rows, _ = pieces.shape
    depth, cols = out_weight.shape
    return call(
        project_kernel,
        [
            jax.ShapeDtypeStruct((rows * count, cols), jnp.float32),
            jax.ShapeDtypeStruct((count, cols), jnp.float32),
        ],
        [VMEM_SPEC, VMEM_SPEC],
        [pltpu.VMEM((rows * count, depth), jnp.float32)],
        2 * rows * count * out_weight.size, out_weight.size * 2, 10,
    )(pieces, out_weight)


def pick_kernel(sharers, mine_ref, other_ref, residual_ref, taken_ref, stream_ref, out_ref):
    stream = (
        residual_ref[...].astype(jnp.float32) + (mine_ref[...] + other_ref[...])
    ).astype(jnp.bfloat16)
    stream_ref[...] = stream
    chosen = [
        jnp.dot(
            taken_ref[e].astype(jnp.bfloat16), stream, preferred_element_type=jnp.float32
        ).astype(jnp.bfloat16)
        for e in range(HELD)
    ]
    for k in range(out_ref.shape[0]):
        out_ref[k] = chosen[k // sharers]


def pick(sharers, count, mine, other, residual, taken):
    rows, cols = mine.shape
    return call(
        functools.partial(pick_kernel, sharers),
        [
            jax.ShapeDtypeStruct((rows, cols), jnp.bfloat16),
            jax.ShapeDtypeStruct((count, taken.shape[1], cols), jnp.bfloat16),
        ],
        [VMEM_SPEC] * 4,
        [],
        2 * HELD * taken.shape[1] * rows * cols, rows * cols * 12, 4,
    )(mine, other, residual, taken)


def expert_kernel(slot_ref, pieces, gains, *refs):
    weights, out_ref, rows_ref = (refs[:3], refs[3:6]), refs[6], refs[7]
    count, capacity, cols = pieces.shape
    first = second = 0.0
    for k in range(count):
        wide = pieces[k].astype(jnp.float32)
        first = first + wide
        second = second + wide * wide
    row_mean = jnp.sum(first, axis=1, keepdims=True) / D
    row_var = jnp.sum(second, axis=1, keepdims=True) / D - row_mean * row_mean
    inverse = lax.rsqrt(row_var + EPSILON)
    for k in range(count):
        wide = pieces[k].astype(jnp.float32)
        normed = (wide - row_mean) * inverse * gains[pl.ds(k, 1), :]
        rows_ref[:, k * cols : (k + 1) * cols] = normed.astype(jnp.bfloat16)
    rows = rows_ref[...]
    contract = (((1,), (1,)), ((), ()))
    hidden = []
    for gate_ref, up_ref, _ in weights:
        gate = lax.dot_general(rows, gate_ref[...], contract, preferred_element_type=jnp.float32)
        up = lax.dot_general(rows, up_ref[...], contract, preferred_element_type=jnp.float32)
        hidden.append((gate / (1.0 + jnp.exp(-gate)) * up).astype(jnp.bfloat16))
    slot_weight = slot_ref[:, :1]
    for k in range(count):
        block = slice(k * cols, (k + 1) * cols)
        piece = sum(
            jnp.dot(part, refs_of[2][:, block], preferred_element_type=jnp.float32)
            for part, refs_of in zip(hidden, weights)
        )
        out_ref[k] = (piece * slot_weight).astype(jnp.bfloat16)


def run_experts(slots, pieces, gains, own, other):
    count, capacity, cols = pieces.shape
    return call(
        expert_kernel,
        jax.ShapeDtypeStruct(pieces.shape, jnp.bfloat16),
        [VMEM_SPEC] * 9,
        [pltpu.VMEM((capacity, count * cols), jnp.bfloat16)],
        12 * capacity * own[0].size, own[0].size * 12, 20,
    )(slots, pieces, gains, *own, *other)


def combine_kernel(sharers, taken_ref, pieces, out_ref):
    count, capacity, cols = pieces.shape
    spread = [taken_ref[k // sharers] for k in range(count)]
    rows = [pieces[k].astype(jnp.float32) for k in range(count)]
    out_ref[...] = lax.dot_general(
        jnp.concatenate(spread, axis=0).astype(jnp.bfloat16),
        jnp.concatenate(rows, axis=0).astype(jnp.bfloat16),
        (((0,), (0,)), ((), ())),
        preferred_element_type=jnp.float32,
    )


def combine(sharers, taken, pieces):
    count, capacity, cols = pieces.shape
    rows = taken.shape[2]
    return call(
        functools.partial(combine_kernel, sharers),
        jax.ShapeDtypeStruct((rows, cols), jnp.float32),
        [VMEM_SPEC] * 2,
        [],
        2 * rows * capacity * count * cols, (count * capacity * 2 + rows * 4) * cols, 4,
    )(taken, pieces)


def finish_kernel(stream_ref, mine_ref, other_ref, stream_out_ref, out_ref):
    stream_out_ref[...] = stream_ref[...]
    out_ref[...] = (mine_ref[...] + other_ref[...]).astype(jnp.bfloat16)


def finish(stream, mine, other):
    return call(
        finish_kernel,
        [jax.ShapeDtypeStruct(stream.shape, jnp.bfloat16)] * 2,
        [VMEM_SPEC] * 3,
        [],
        mine.size, mine.size * 14, 4,
    )(stream, mine, other)


def exchange(blocks):
    return lax.all_to_all(blocks, "attn", split_axis=0, concat_axis=0, tiled=True)


def swap(block):
    return lax.ppermute(block, "expert", [(0, 1), (1, 0)])


def shards(
    queries,
    key_cache,
    value_cache,
    new_key,
    new_value,
    cache_length,
    residual,
    out_weight,
    ln_gain,
    gate_weight,
    up_weight,
    down_weight,
    routes,
    route_weight,
):
    count = lax.axis_size("attn")
    sharers = count // HELD
    capacity = routes.shape[0] * TOP // EXPERTS

    earlier = order(routes.shape[0])
    weights = (gate_weight.T, up_weight.T, down_weight)
    spread, own, limit, taken, slots, value_rows, parts = prepare(
        sharers, capacity, cache_length, earlier, routes.T, route_weight.T, queries, new_key,
        new_value, ln_gain,
    )
    other_weights = [swap(block) for block in lax.optimization_barrier(weights[:2])]
    attended = exchange(
        attend(count, spread, own, limit, key_cache, value_cache, value_rows, parts)
    )
    mine, gains = project(attended, out_weight)
    late_down, mine = lax.optimization_barrier((weights[2], mine))
    other_weights.append(swap(late_down))
    stream, chosen = pick(sharers, count, mine, swap(mine), residual, taken)
    outgoing = run_experts(slots, exchange(chosen), gains, weights, other_weights)
    combined = combine(sharers, taken, exchange(outgoing))
    attn_stream, expert_out = finish(stream, combined, swap(combined))
    return (attn_stream, expert_out)


def solution(mesh):
    count = mesh.shape["attn"]
    fits = D // count % 256 == 0 and count % HELD == 0 and mesh.shape["expert"] == 2
    return jax.shard_map(
        shards if fits else shards_plain,
        mesh=mesh,
        in_specs=(
            P(("group", "attn"), "expert"),
            P(("group", "attn"), None, "expert"),
            P(("group", "attn"), None, "expert"),
            P(("group", "attn"), "expert"),
            P(("group", "attn"), "expert"),
            P(("group", "attn")),
            P("group", "attn"),
            P("expert", "attn"),
            P("attn"),
            P(None, ("attn", "expert")),
            P(None, ("attn", "expert")),
            P(("attn", "expert"), None),
            P("group", None),
            P("group", None),
        ),
        out_specs=(P("group", "attn"), P("group", "attn")),
        check_vma=False,
    )
```
